32 devices in a mesh: dp: 8 (over z, y), heads: 4 (over x, core).
Axes of the slice: x: 2, y: 2, z: 4, core: 2. Of those that a mesh axis runs over, the one named last changes fastest.
Arguments:
- tokens: bfloat16 [16384, 1024], P('dp', 'heads'), may hold values from -6 to 6
- cotangent: bfloat16 [16384, 1024], P('dp', 'heads'), may hold values from -6 to 6
- scan_block_starts: int32 [128], P('dp'), may hold values from 0 to 1, as said below
- scan_block_fill: int32 [128], P('dp'), may hold values from 32 to 128, as said below
- norm_gain: float32 [1024], replicated, may hold values from 0.1 to 1.9
- w_x: bfloat16 [1024, 2048], P('dp', 'heads'), may hold values from -0.1875 to 0.1875
- w_z: bfloat16 [1024, 2048], P('dp', 'heads'), may hold values from -0.1875 to 0.1875
- w_dt: bfloat16 [1024, 32], P('dp', 'heads'), may hold values from -0.1875 to 0.1875
- w_bc: bfloat16 [1024, 256], P('dp'), may hold values from -0.1875 to 0.1875
- conv_x: float32 [4, 2048], P(None, 'heads'), may hold values from -3 to 3
- conv_bc: float32 [4, 256], replicated, may hold values from -3 to 3
- dt_bias: float32 [32], P('heads'), may hold values from -6 to -2
- a_log: float32 [32], P('heads'), may hold values from 0 to 2.77
- skip: float32 [32], P('heads'), may hold values from 0.5 to 1.5
- gate_gain: float32 [2048], P('heads'), may hold values from 0.1 to 1.9
- w_out: bfloat16 [1024, 2048], P('dp', 'heads'), may hold values from -0.125 to 0.125
Outputs:
- block_out: bfloat16 [16384, 1024], P('dp', 'heads')
- grad_tokens: float32 [16384, 1024], P('dp', 'heads')
- grad_norm_gain: float32 [1024], P('heads')
- grad_w_x: float32 [1024, 2048], P('dp', 'heads')
- grad_w_z: float32 [1024, 2048], P('dp', 'heads')
- grad_w_dt: float32 [1024, 32], P('dp', 'heads')
- grad_w_bc: float32 [1024, 256], P('dp')
- grad_conv_x: float32 [4, 2048], P(None, 'heads')
- grad_conv_bc: float32 [4, 256], replicated
- grad_dt_bias: float32 [32], P('heads')
- grad_a_log: float32 [32], P('heads')
- grad_skip: float32 [32], P('heads')
- grad_gate_gain: float32 [2048], P('heads')
- grad_w_out: float32 [1024, 2048], P('dp', 'heads')
The draws below stay inside these ranges and needn't reach their ends.
Inputs may be any that keep to these rules, and one draw needn't show every extreme that they name: `scan_block_starts`: scenes never span two indices of dp: the first block of each 2048 tokens always begins a scene and its second never does. `scan_block_fill`: only the last block of a scene may be partly padded; the first block of every 2048 tokens is full.
All inputs are finite; a program needn't handle non-finite values.
Results may differ from the reference program's by a relative error of at most 0.01.
Values may be sent and summed in bfloat16 or wider, within the bound.
A program may use at most 192 MiB of HBM per device.

```python
import jax
import jax.numpy as jnp
from jax import lax

D = 1024
NH = 32
HD = 64
NS = 128
INNER = 2048
CONV = 4
STRETCH = 128
TOK_DEV = 2048
TOKENS = 16384


def scene_layout(key):
    start_key = jax.random.fold_in(key, 11)
    fill_key = jax.random.fold_in(key, 12)
    devices_n = TOKENS // TOK_DEV
    per_device = TOK_DEV // STRETCH
    environment_beginning = (jax.random.randint(start_key, (devices_n, per_device), 0, 4) == 0).astype(jnp.int32)
    column = jnp.arange(per_device, dtype=jnp.int32)[None, :]
    row_index = jnp.arange(devices_n, dtype=jnp.int32)[:, None]
    environment_beginning = jnp.where(column == 0, 1, jnp.where(column == 1, 0, environment_beginning)).astype(jnp.int32)
    following = jnp.concatenate([environment_beginning[:, 1:], jnp.ones((devices_n, 1), jnp.int32)], axis=1)
    partial_value = jax.random.randint(fill_key, (devices_n, per_device), STRETCH // 4, STRETCH + 1)
    padded_matrix_entries = jnp.where(following == 1, partial_value, STRETCH).astype(jnp.int32)
    padded_matrix_entries = jnp.where((row_index == 0) & (column == per_device - 1), STRETCH // 4, padded_matrix_entries).astype(jnp.int32)
    padded_matrix_entries = jnp.where(column == 0, STRETCH, padded_matrix_entries).astype(jnp.int32)
    return (environment_beginning.reshape(-1), padded_matrix_entries.reshape(-1))


def draw_scan_block_starts(key, part):
    return scene_layout(key)[0]


def draw_scan_block_fill(key, part):
    return scene_layout(key)[1]


def steps_of(key, extent, cuts, smallest, top_value):
    level, own = 1.0, jax.random.fold_in(key, 6)
    for dim, blocks in cuts:
        heights = jnp.exp(jax.random.uniform(jax.random.fold_in(own, dim), (blocks,), jnp.float32, smallest / len(cuts), top_value / len(cuts)))
        level = level * jnp.repeat(heights, extent[dim] // blocks).reshape([-1 if axis == dim else 1 for axis in range(len(extent))])
    return level


def centred(own_key, extent, scale, bound, cuts=(), held_as=jnp.bfloat16):
    loudness = steps_of(own_key, extent, cuts, -0.22, 0.18) if cuts else 1.0
    values = jax.random.normal(own_key, extent, jnp.float32) * scale * loudness
    return jnp.minimum(jnp.maximum(values, -bound), bound).astype(held_as)


def setup_inputs(seed: int = 0) -> dict:
    seeds = jax.random.split(jax.random.key(seed), 17)
    tokens = centred(seeds[0], (TOKENS, D), 1.0, 6.0, ((0, 8), (1, 4)))
    cotangent = centred(seeds[1], (TOKENS, D), 1.0, 6.0, ((0, 8), (1, 4)))
    scan_block_starts = draw_scan_block_starts(jax.random.fold_in(seeds[16], 71), 0)
    scan_block_fill = draw_scan_block_fill(jax.random.fold_in(seeds[16], 71), 0)
    norm_gain = jnp.clip(1.0 + 0.18 * jax.random.normal(seeds[4], (D,), jnp.float32), 0.1, 1.9)
    w_x = centred(seeds[5], (D, INNER), D ** -0.5, 0.1875, ((0, 8), (1, 4)))
    w_z = centred(seeds[6], (D, INNER), D ** -0.5, 0.1875, ((0, 8), (1, 4)))
    w_dt = centred(seeds[7], (D, NH), D ** -0.5, 0.1875, ((0, 8), (1, 4)))
    w_bc = centred(seeds[8], (D, 2 * NS), D ** -0.5, 0.1875, ((0, 8),))
    conv_x = centred(seeds[9], (CONV, INNER), CONV ** -0.5, 3.0, ((1, 4),), jnp.float32)
    conv_bc = centred(seeds[10], (CONV, 2 * NS), CONV ** -0.5, 3.0, (), jnp.float32)
    dt_bias = jnp.clip(-6.0 + 4.0 * jax.random.uniform(seeds[11], (NH,), jnp.float32) ** steps_of(seeds[11], (NH,), ((0, 4),), -0.2, 0.2), -6.0, -2.0)
    a_log = jnp.clip(2.77 * jax.random.uniform(seeds[12], (NH,), jnp.float32) ** steps_of(seeds[12], (NH,), ((0, 4),), -0.2, 0.2), 0.0, 2.77)
    skip = jnp.clip(0.5 + 1.0 * jax.random.uniform(seeds[13], (NH,), jnp.float32) ** steps_of(seeds[13], (NH,), ((0, 4),), -0.2, 0.2), 0.5, 1.5)
    gate_gain = jnp.clip(1.0 + 0.18 * jax.random.normal(seeds[14], (INNER,), jnp.float32), 0.1, 1.9)
    w_out = centred(seeds[15], (D, INNER), INNER ** -0.5, 0.125, ((0, 8), (1, 4)))
    return dict(tokens=tokens, cotangent=cotangent, scan_block_starts=scan_block_starts, scan_block_fill=scan_block_fill, norm_gain=norm_gain, w_x=w_x, w_z=w_z, w_dt=w_dt, w_bc=w_bc, conv_x=conv_x, conv_bc=conv_bc, dt_bias=dt_bias, a_log=a_log, skip=skip, gate_gain=gate_gain, w_out=w_out)


eps_norm = 1e-05
highest = lax.Precision.HIGHEST

@jax.custom_vjp
def low(v):
    return lax.optimization_barrier(v.astype(jnp.bfloat16)).astype(jnp.float32)

@jax.custom_vjp
def low_back(v):
    return v

def low_keep(v):
    return (low(v), None)

def low_pass(kept, grad):
    return (grad,)

def back_keep(v):
    return (v, None)

def back_low(kept, grad):
    return (low(grad),)
low.defvjp(low_keep, low_pass)
low_back.defvjp(back_keep, back_low)

def embedding_index_arrays(environment_boundary_indices, padded_matrix_entries, length):
    blocks = environment_boundary_indices.shape[0]
    span = length // blocks
    inside_segment = (jnp.arange(length, dtype=jnp.int32) % span).astype(jnp.int32)
    environment_beginning = jnp.repeat(environment_boundary_indices, span)
    segment_boundaries = jnp.repeat(padded_matrix_entries, span)
    embedding_validity_mask = (inside_segment < segment_boundaries).astype(jnp.float32)
    return (environment_beginning, inside_segment, embedding_validity_mask)

def leftward_convolution_kernel(signal, kernel_coefficients, environment_beginning, inside_segment):
    taps = kernel_coefficients.shape[0]
    result = kernel_coefficients[taps - 1] * signal
    for distance in range(1, taps):
        moved = jnp.concatenate([jnp.zeros((distance, signal.shape[1]), jnp.float32), signal[:-distance]], axis=0)
        allowed = 1.0 - ((environment_beginning == 1) & (inside_segment < distance)).astype(jnp.float32)
        result = result + kernel_coefficients[taps - 1 - distance] * moved * allowed[:, None]
    return result

def state_space(inputs, interval_widths, rates, b_mat, c_mat, environment_boundary_indices):
    total_rows, head_count, head_dim = inputs.shape
    blocks = environment_boundary_indices.shape[0]
    span = total_rows // blocks
    state_dim = b_mat.shape[1]
    x_blocks = inputs.reshape(blocks, span, head_count, head_dim)
    dt_blocks = interval_widths.reshape(blocks, span, head_count).transpose(0, 2, 1)
    b_blocks = b_mat.reshape(blocks, span, state_dim)
    c_blocks = c_mat.reshape(blocks, span, state_dim)
    running = jnp.cumsum(dt_blocks * rates[None, :, None], axis=2)
    lower = jnp.arange(span)[:, None] >= jnp.arange(span)[None, :]
    spread = running[:, :, :, None] - running[:, :, None, :]
    fading = jnp.exp(jnp.where(lower, spread, -1e+30))
    scores = jnp.einsum('cln,csn->cls', c_blocks, b_blocks, precision=highest)
    mixing = scores[:, None] * fading * dt_blocks[:, :, None, :]
    outputs = jnp.einsum('chls,cshp->clhp', mixing, x_blocks, precision=highest)
    closing = jnp.exp(running[:, :, -1:] - running) * dt_blocks
    weighted = x_blocks * closing.transpose(0, 2, 1)[..., None]
    block_states = jnp.einsum('clhp,cln->chpn', weighted, b_blocks, precision=highest)
    carried = jnp.exp(running[:, :, -1])
    resets = 1.0 - environment_boundary_indices.astype(jnp.float32)

    def advance(state, packed):
        keep_rate, fresh, reset_one = packed
        entering = state * reset_one
        return (keep_rate[:, None, None] * entering + fresh, entering)
    final_state, entering = lax.scan(advance, jnp.zeros((head_count, head_dim, state_dim), jnp.float32), (carried, block_states, resets))
    reading = jnp.einsum('cln,chpn->clhp', c_blocks, entering, precision=highest)
    outputs = outputs + jnp.exp(running).transpose(0, 2, 1)[..., None] * reading
    return outputs.reshape(total_rows, head_count, head_dim)

def leading_state_matrices(mapped_state_matrices, kernel_coefficients_statewise, environment_beginning, inside_segment, embedding_validity_mask):
    return jax.nn.silu(leftward_convolution_kernel(mapped_state_matrices, kernel_coefficients_statewise, environment_beginning, inside_segment)) * embedding_validity_mask[:, None]

def state_space_layer(mapped_input_vector, mapped_multiplier, mapped_interval_width, current_input_state_matrices, kernel_coefficients_inputwise, interval_offset_vector, forgetting_exponent_coefficients, direct_coupling_factors, environment_boundary_indices, environment_beginning, inside_segment, embedding_validity_mask):
    total_rows = mapped_input_vector.shape[0]
    current_input_vector = jax.nn.silu(leftward_convolution_kernel(mapped_input_vector, kernel_coefficients_inputwise, environment_beginning, inside_segment)) * embedding_validity_mask[:, None]
    interval_widths = jax.nn.softplus(mapped_interval_width + interval_offset_vector) * embedding_validity_mask[:, None]
    rates = -jnp.exp(forgetting_exponent_coefficients)
    state_dim = current_input_state_matrices.shape[1] // 2
    x_heads = current_input_vector.reshape(total_rows, -1, HD)
    scanned = state_space(x_heads, interval_widths, rates, current_input_state_matrices[:, :state_dim], current_input_state_matrices[:, state_dim:], environment_boundary_indices)
    scanned = scanned + direct_coupling_factors[None, :, None] * x_heads
    return scanned.reshape(total_rows, -1) * jax.nn.silu(mapped_multiplier)

def reference(tokens, cotangent, scan_block_starts, scan_block_fill, norm_gain, w_x, w_z, w_dt, w_bc, conv_x, conv_bc, dt_bias, a_log, skip, gate_gain, w_out):
    blocks_n = TOKENS // TOK_DEV
    starts_all = scan_block_starts.reshape(blocks_n, -1)
    fill_all = scan_block_fill.reshape(blocks_n, -1)

    def forward(tokens_in, gain_in, weight_x, weight_z, weight_dt, weight_bc, kernel_coefficients_inputwise, kernel_coefficients_statewise, interval_offset_vector, forgetting_exponent_coefficients, direct_coupling_factors, gain_gate, weight_out):

        def one_block(packed):
            carried_hidden_vector, environment_boundary_indices, padded_matrix_entries = packed
            environment_beginning, inside_segment, embedding_validity_mask = embedding_index_arrays(environment_boundary_indices, padded_matrix_entries, carried_hidden_vector.shape[0])
            inverse = lax.rsqrt(lax.optimization_barrier(jnp.mean(carried_hidden_vector * carried_hidden_vector, axis=-1, keepdims=True)) + eps_norm)
            normed = low(carried_hidden_vector * inverse * gain_in)
            mapped_input_vector = low_back(jnp.dot(normed, weight_x, precision=highest))
            mapped_multiplier = low_back(jnp.dot(normed, weight_z, precision=highest))
            mapped_interval_width = low_back(jnp.dot(normed, weight_dt, precision=highest))
            mapped_state_matrices = low_back(jnp.dot(normed, weight_bc, precision=highest))
            current_input_state_matrices = leading_state_matrices(mapped_state_matrices, kernel_coefficients_statewise, environment_beginning, inside_segment, embedding_validity_mask)
            multiplied_result_vector = state_space_layer(mapped_input_vector, mapped_multiplier, mapped_interval_width, current_input_state_matrices, kernel_coefficients_inputwise, interval_offset_vector, forgetting_exponent_coefficients, direct_coupling_factors, environment_boundary_indices, environment_beginning, inside_segment, embedding_validity_mask)
            gate_inverse = lax.rsqrt(lax.optimization_barrier(jnp.mean(multiplied_result_vector * multiplied_result_vector, axis=-1, keepdims=True)) + eps_norm)
            gated_normed = low(multiplied_result_vector * gate_inverse * gain_gate)
            return carried_hidden_vector + jnp.dot(gated_normed, weight_out.T, precision=highest)
        blocks_out = lax.map(jax.checkpoint(one_block), (tokens_in.reshape(blocks_n, TOK_DEV, -1), starts_all, fill_all))
        return blocks_out.reshape(TOKENS, -1)
    floats = (tokens.astype(jnp.float32), norm_gain, w_x.astype(jnp.float32), w_z.astype(jnp.float32), w_dt.astype(jnp.float32), w_bc.astype(jnp.float32), conv_x, conv_bc, dt_bias, a_log, skip, gate_gain, w_out.astype(jnp.float32))
    result, pullback = jax.vjp(forward, *floats)
    grads = pullback(cotangent.astype(jnp.float32))
    return (result.astype(jnp.bfloat16), grads[0], grads[1], grads[2], grads[3], grads[4], grads[5], grads[6], grads[7], grads[8], grads[9], grads[10], grads[11], grads[12])
```

```python
import functools
import jax
import jax.numpy as jnp
import numpy as np
from jax import lax
from jax.experimental import pallas as pl
from jax.experimental.pallas import tpu as pltpu
from jax.sharding import PartitionSpec as P

HD = 64
EPS = 1e-05
F32 = jnp.float32
BF = jnp.bfloat16
NEG = -1e30


def nn(a, b):
    return lax.dot_general(a, b, (((1,), (0,)), ((), ())), preferred_element_type=F32)


def nt(a, b):
    return lax.dot_general(a, b, (((1,), (1,)), ((), ())), preferred_element_type=F32)


def tn(a, b):
    return lax.dot_general(a, b, (((0,), (0,)), ((), ())), preferred_element_type=F32)


def split2(v):
    hi = v.astype(BF).astype(F32)
    return hi, v - hi


def split3(v):
    hi = v.astype(BF).astype(F32)
    rest = v - hi
    mid = rest.astype(BF).astype(F32)
    return hi, mid, rest - mid


def softplus(v):
    return jnp.maximum(v, 0.0) + jnp.log1p(jnp.exp(-jnp.abs(v)))


def sigmoid(v):
    return 1.0 / (1.0 + jnp.exp(-v))


def iota2(rows, cols, axis):
    return lax.broadcasted_iota(jnp.int32, (rows, cols), axis)


def scan_constants(chunk, heads):
    inner = heads * HD
    t = np.arange(chunk)
    upper = (t[:, None] <= t[None, :]).astype(np.float32)
    head_of = np.arange(inner) // HD
    spread = np.zeros((chunk, 3 * inner), np.float32)
    for q in range(3):
        for part in range(2):
            base = heads * (1 + 2 * q + part)
            for h in range(heads):
                spread[base + h, q * inner : (q + 1) * inner] = head_of == h
    gather = np.zeros((3, inner, chunk), np.float32)
    for q in range(3):
        for h in range(heads):
            gather[q, :, q * heads + h] = head_of == h
    return jnp.asarray(upper, BF), jnp.asarray(spread, BF), jnp.asarray(gather, BF)


def conv_from(ext, taps, rows, halo):
    n = taps.shape[0]
    out = taps[n - 1 : n, :] * ext[pl.ds(halo, rows), :]
    for k in range(1, n):
        out = out + taps[n - 1 - k : n - k, :] * ext[pl.ds(halo - k, rows), :]
    return out


def dt_rows(pdt, bias, rate, fill, heads, upper):
    chunk = pdt.shape[0]
    pre = jnp.transpose(pdt)[:heads] + bias
    live = (iota2(heads, chunk, 1) < fill).astype(F32)
    dt = softplus(pre) * live
    hi, mid, low = split3(dt * rate)
    stacked = jnp.concatenate([hi, mid, low], axis=0).astype(BF)
    summed = nn(stacked, upper)
    run = summed[:heads] + summed[heads : 2 * heads] + summed[2 * heads :]
    return pre, live, dt, run


def spread_all(run, dt, heads, chunk, spread):
    last = run[:, chunk - 1 : chunk]
    e_in = jnp.exp(run)
    e_out = jnp.exp(last - run)
    parts = [run]
    for v in (dt, e_in, e_out):
        parts.extend(split2(v))
    used = heads * len(parts)
    if used < chunk:
        parts.append(jnp.zeros((chunk - used, chunk), F32))
    cols = jnp.transpose(jnp.concatenate(parts, axis=0))
    return cols, nn(cols.astype(BF), spread)


def pair_stack(v, low_lanes):
    zero = jnp.zeros_like(v)
    return jnp.concatenate([jnp.where(low_lanes, v, zero), jnp.where(low_lanes, zero, v)], axis=0)


def scan_fwd_kernel(
    heads, starts, fill, px, pbd, convx, convbc, bias, rate, skip, upper, spread,
    y_out, sin_out, state, extx, extb,
):
    c = pl.program_id(0)
    chunk, inner = px.shape
    bc = convbc.shape[1]
    ns = bc // 2
    keep = starts[c] == 0

    @pl.when(c == 0)
    def _():
        state[...] = jnp.zeros_like(state)
        extx[...] = jnp.zeros_like(extx)
        extb[...] = jnp.zeros_like(extb)

    state[...] = jnp.where(keep, state[...], 0.0)
    extx[0:8, :] = jnp.where(keep, extx[chunk : chunk + 8, :], 0.0)
    extb[0:8, :] = jnp.where(keep, extb[chunk : chunk + 8, :], 0.0)
    extx[8 : chunk + 8, :] = px[...]
    extb[8 : chunk + 8, :] = pbd[:, :bc]

    n_live = fill[c]
    u = conv_from(extx, convx[...], chunk, 8)
    x = u * sigmoid(u) * (iota2(chunk, inner, 0) < n_live).astype(F32)
    ub = conv_from(extb, convbc[...], chunk, 8)
    act = (ub * sigmoid(ub) * (iota2(chunk, bc, 0) < n_live).astype(F32)).astype(BF)
    b, cc = act[:, :ns], act[:, ns:]

    _, _, dt, run = dt_rows(pbd[:, bc:], bias[...], rate[...], n_live, heads, upper[...])
    cols, wide = spread_all(run, dt, heads, chunk, spread[...])
    dt_w, ein_w, eout_w = wide[:, :inner], wide[:, inner : 2 * inner], wide[:, 2 * inner :]

    xd = x * dt_w
    xdb = xd.astype(BF)
    scores = nt(cc, b)
    tri = iota2(chunk, chunk, 0) >= iota2(chunk, chunk, 1)
    low_lanes = iota2(chunk, 2 * HD, 1) < HD
    diag = []
    for j in range(heads // 2):
        mix = []
        for h in (2 * j, 2 * j + 1):
            spread_h = cols[:, h : h + 1] - run[h : h + 1, :]
            mix.append((scores * jnp.exp(jnp.where(tri, spread_h, NEG))).astype(BF))
        pair = pair_stack(xdb[:, 2 * HD * j : 2 * HD * (j + 1)], low_lanes)
        diag.append(nn(jnp.concatenate(mix, axis=1), pair))
    enter = state[...]
    enter_b = enter.astype(BF)
    sin_out[0] = enter_b
    y_out[...] = jnp.concatenate(diag, axis=1) + ein_w * nn(cc, enter_b) + skip[...] * x
    state[...] = ein_w[chunk - 1 : chunk, :] * enter + tn(b, (xd * eout_w).astype(BF))


def scan_forward(px, pbd, conv_x, conv_bc, dt_bias, a_log, skip, starts, fill):
    tokens, inner = px.shape
    blocks = starts.shape[0]
    chunk = tokens // blocks
    heads = inner // HD
    bc = conv_bc.shape[1]
    upper, spread, _ = scan_constants(chunk, heads)
    bias = jnp.broadcast_to(dt_bias[:, None], (heads, chunk))
    rate = jnp.broadcast_to(-jnp.exp(a_log)[:, None], (heads, chunk))
    skip_w = jnp.repeat(skip, HD)[None, :]
    fixed = lambda c, *_: (0, 0)
    whole = lambda a: pl.BlockSpec(a.shape, fixed)
    rows = lambda w: pl.BlockSpec((chunk, w), lambda c, *_: (c, 0))
    return pl.pallas_call(
        functools.partial(scan_fwd_kernel, heads),
        grid_spec=pltpu.PrefetchScalarGridSpec(
            num_scalar_prefetch=2,
            grid=(blocks,),
            in_specs=[rows(inner), rows(pbd.shape[1])]
            + [whole(a) for a in (conv_x, conv_bc, bias, rate, skip_w, upper, spread)],
            out_specs=[rows(inner), pl.BlockSpec((1, bc // 2, inner), lambda c, *_: (c, 0, 0))],
            scratch_shapes=[
                pltpu.VMEM((bc // 2, inner), F32),
                pltpu.VMEM((chunk + 8, inner), F32),
                pltpu.VMEM((chunk + 8, bc), F32),
            ],
        ),
        out_shape=[
            jax.ShapeDtypeStruct((tokens, inner), F32),
            jax.ShapeDtypeStruct((blocks, bc // 2, inner), BF),
        ],
        compiler_params=pltpu.CompilerParams(vmem_limit_bytes=48 * 2**20),
        name="scan_forward",
    )(starts, fill, px, pbd, conv_x, conv_bc, bias, rate, skip_w, upper, spread)


def scan_bwd_kernel(
    heads, total_inner, starts, fill, ggn, y, pz, px, px_halo, pbd, pbd_halo, sin, rows, gain, convx, convbc,
    bias, rate, skip, upper, spread, gather, ones_h,
    lpx, lpz, lpbd, acc_x, acc_bc, acc_s, dstate, extx, extb, dux, dub,
):
    i = pl.program_id(0)
    blocks = pl.num_programs(0)
    c = blocks - 1 - i
    chunk, inner = px.shape
    bc = convbc.shape[1]
    ns = bc // 2
    taps_n = convx.shape[0]
    keep = starts[c] == 0
    nxt = jnp.minimum(c + 1, blocks - 1)
    keep_next = jnp.logical_and(starts[nxt] == 0, i > 0)
    n_live = fill[c]

    @pl.when(i == 0)
    def _():
        for ref in (dstate, dux, dub, acc_x, acc_bc, acc_s):
            ref[...] = jnp.zeros_like(ref)

    moved = jnp.transpose(
        jnp.concatenate([rows[0], jnp.zeros((chunk - rows.shape[1], chunk), F32)], axis=0)
    )
    inv = lax.rsqrt(moved[:, 0:1] / total_inner + EPS)
    coef = inv * inv * inv * (moved[:, 1:2] / total_inner)
    z = pz[...]
    sz = sigmoid(z)
    silu_z = z * sz
    yv = y[...]
    gated = yv * silu_z
    g = ggn[...]
    d_gated = inv * (g * gain[...]) - gated * coef
    lpz[...] = (d_gated * yv * (sz * (1.0 + z * (1.0 - sz)))).astype(BF)
    dy = d_gated * silu_z
    acc_x[taps_n : taps_n + 1, :] += jnp.sum(g * gated * inv, axis=0, keepdims=True)

    extx[0:8, :] = jnp.where(keep, px_halo[...], 0.0)
    extb[0:8, :] = jnp.where(keep, pbd_halo[:, :bc], 0.0)
    extx[8 : chunk + 8, :] = px[...]
    extb[8 : chunk + 8, :] = pbd[:, :bc]
    taps = convx[...]
    taps_b = convbc[...]
    live_x = (iota2(chunk, inner, 0) < n_live).astype(F32)
    live_b = (iota2(chunk, bc, 0) < n_live).astype(F32)
    u = conv_from(extx, taps, chunk, 8)
    su = sigmoid(u)
    x = u * su * live_x
    dx_du = su * (1.0 + u * (1.0 - su)) * live_x
    ub = conv_from(extb, taps_b, chunk, 8)
    sb = sigmoid(ub)
    act = (ub * sb * live_b).astype(BF)
    db_du = sb * (1.0 + ub * (1.0 - sb)) * live_b
    b, cc = act[:, :ns], act[:, ns:]

    pre, live, dt, run = dt_rows(pbd[:, bc:], bias[...], rate[...], n_live, heads, upper[...])
    cols, wide = spread_all(run, dt, heads, chunk, spread[...])
    dt_w, ein_w, eout_w = wide[:, :inner], wide[:, inner : 2 * inner], wide[:, 2 * inner :]
    xd = x * dt_w
    xdb = xd.astype(BF)
    dyb = dy.astype(BF)
    acc_x[taps_n + 1 : taps_n + 2, :] += jnp.sum(dy * x, axis=0, keepdims=True)

    scores_t = nt(b, cc)
    tri = iota2(chunk, chunk, 0) <= iota2(chunk, chunk, 1)
    low_lanes = iota2(chunk, 2 * HD, 1) < HD
    d_scores_t = jnp.zeros((chunk, chunk), F32)
    dxd = []
    pulls = []
    read_sums = []
    for j in range(heads // 2):
        span = slice(2 * HD * j, 2 * HD * (j + 1))
        dy_pair = pair_stack(dyb[:, span], low_lanes)
        x_pair = pair_stack(xdb[:, span], low_lanes)
        d_mix = nt(x_pair, dyb[:, span])
        mix = []
        for k in (0, 1):
            h = 2 * j + k
            spread_h = run[h : h + 1, :] - cols[:, h : h + 1]
            fade = jnp.exp(jnp.where(tri, spread_h, NEG))
            m = scores_t * fade
            dm = d_mix[k * chunk : (k + 1) * chunk]
            d_scores_t = d_scores_t + dm * fade
            pull = (dm * m).astype(BF)
            pulls.append(pull)
            read_sums.append(jnp.sum(pull.astype(F32), axis=0, keepdims=True))
            mix.append(m.astype(BF))
        dxd.append(nn(jnp.concatenate(mix, axis=1), dy_pair))
    source_sums = nn(jnp.concatenate(pulls, axis=1), ones_h[...])
    read_rows = jnp.concatenate(read_sums, axis=0)

    d_state = jnp.where(keep_next, dstate[...], 0.0)
    d_state_b = d_state.astype(BF)
    enter_b = sin[0]
    edy = ein_w * dy
    edyb = edy.astype(BF)
    readings = nn(cc, enter_b)
    from_state = nn(b, d_state_b) * eout_w
    d_xd = jnp.concatenate(dxd, axis=1) + from_state
    q1 = edy * readings
    q2 = xd * from_state
    decay = ein_w[chunk - 1 : chunk, :]
    dstate[...] = decay * d_state + tn(cc, edyb)
    d_cb = tn(d_scores_t.astype(BF), b) + nt(edyb, enter_b)
    d_b = nn(d_scores_t.astype(BF), cc) + nt((xd * eout_w).astype(BF), d_state_b)

    sums = (
        nn((d_xd * x).astype(BF), gather[0])
        + nn((q1 - q2).astype(BF), gather[1])
        + nn(q2.astype(BF), gather[2])
        - source_sums
    )
    sums_t = jnp.transpose(sums)
    dt_direct = sums_t[:heads]
    d_run = sums_t[heads : 2 * heads] + read_rows
    whole_q2 = jnp.sum(sums_t[2 * heads : 3 * heads], axis=1, keepdims=True)
    kept = jnp.sum(enter_b.astype(F32) * d_state, axis=0, keepdims=True) * decay
    kept_hi, kept_lo = split2(kept)
    kept_two = jnp.concatenate([kept_hi, kept_lo, jnp.zeros((6, inner), F32)], axis=0).astype(BF)
    kept_cols = nt(gather[3][:, :inner], kept_two)
    d_last = whole_q2 + kept_cols[:heads, 0:1] + kept_cols[:heads, 1:2]
    hi, mid, low = split3(d_run)
    back = nt(jnp.concatenate([hi, mid, low], axis=0).astype(BF), upper[...])
    d_a = back[:heads] + back[heads : 2 * heads] + back[2 * heads :] + d_last
    d_dt = dt_direct + d_a * rate[...]
    d_pre = d_dt * live * sigmoid(pre)
    acc_s[0:heads, :] += d_pre
    acc_s[heads : 2 * heads, :] += d_a * dt * rate[...]

    def conv_back(d_u, du_ref, ext_ref, tap_values, acc):
        du_ref[chunk : chunk + 8, :] = jnp.where(keep_next, du_ref[0:8, :], 0.0)
        du_ref[0:chunk, :] = d_u
        out = tap_values[taps_n - 1 : taps_n, :] * d_u
        acc[taps_n - 1 : taps_n, :] += jnp.sum(d_u * ext_ref[8 : chunk + 8, :], axis=0, keepdims=True)
        for k in range(1, taps_n):
            row = taps_n - 1 - k
            out = out + tap_values[row : row + 1, :] * du_ref[pl.ds(k, chunk), :]
            acc[row : row + 1, :] += jnp.sum(
                d_u * ext_ref[pl.ds(8 - k, chunk), :], axis=0, keepdims=True
            )
        return out

    d_x = d_xd * dt_w + skip[...] * dy
    lpx[...] = conv_back(d_x * dx_du, dux, extx, taps, acc_x).astype(BF)
    d_act = jnp.concatenate([d_b, d_cb], axis=1)
    lpbd[:, :bc] = conv_back(d_act * db_du, dub, extb, taps_b, acc_bc).astype(BF)
    pad = jnp.concatenate([d_pre, jnp.zeros((chunk - heads, chunk), F32)], axis=0)
    lpbd[:, bc:] = jnp.transpose(pad).astype(BF)


def scan_backward(
    ggn, y, pz, px, pbd, sin, rows, gain, conv_x, conv_bc, dt_bias, a_log, skip, starts, fill, total_inner
):
    tokens, inner = px.shape
    blocks = starts.shape[0]
    chunk = tokens // blocks
    heads = inner // HD
    bc = conv_bc.shape[1]
    upper, spread, gather = scan_constants(chunk, heads)
    selector = np.zeros((1, inner, chunk), np.float32)
    lanes = np.zeros((chunk, inner), np.float32)
    for h in range(heads):
        lanes[h, h * HD : (h + 1) * HD] = 1.0
    ones_h = np.zeros((heads * chunk, chunk), np.float32)
    for h in range(heads):
        ones_h[h * chunk : (h + 1) * chunk, heads + h] = 1.0
    ones_h = jnp.asarray(ones_h, BF)
    lanes = jnp.asarray(lanes, BF)
    bias = jnp.broadcast_to(dt_bias[:, None], (heads, chunk))
    rate = jnp.broadcast_to(-jnp.exp(a_log)[:, None], (heads, chunk))
    skip_w = jnp.repeat(skip, HD)[None, :]
    whole = lambda a: pl.BlockSpec(a.shape, lambda i, *_: (0,) * a.ndim)
    back = lambda w: pl.BlockSpec((chunk, w), lambda i, *_: (blocks - 1 - i, 0))
    halo = lambda w: pl.BlockSpec(
        (8, w), lambda i, *_: (jnp.maximum((blocks - 1 - i) * (chunk // 8) - 1, 0), 0)
    )
    width = pbd.shape[1]
    consts = (gain[None, :], conv_x, conv_bc, bias, rate, skip_w, upper, spread, gather, lanes, ones_h)

    def kernel(*refs):
        n_in = 2 + 9
        ins, cons, rest = refs[:n_in], refs[n_in : n_in + 11], refs[n_in + 11 :]
        gain_r, cx, cb, bias_r, rate_r, skip_r, up, sp, ga, la, on = cons

        class Gather:
            def __getitem__(self, k):
                return la[...] if k == 3 else ga[k]

        scan_bwd_kernel(
            heads, total_inner, *ins, gain_r, cx, cb, bias_r, rate_r, skip_r, up, sp, Gather(), on, *rest
        )

    return pl.pallas_call(
        kernel,
        grid_spec=pltpu.PrefetchScalarGridSpec(
            num_scalar_prefetch=2,
            grid=(blocks,),
            in_specs=[
                back(inner), back(inner), back(inner), back(inner), halo(inner), back(width), halo(width),
                pl.BlockSpec((1, bc // 2, inner), lambda i, *_: (blocks - 1 - i, 0, 0)),
                pl.BlockSpec((1, 8, chunk), lambda i, *_: (blocks - 1 - i, 0, 0)),
            ]
            + [whole(a) for a in consts],
            out_specs=[
                back(inner), back(inner), back(width),
                pl.BlockSpec((8, inner), lambda i, *_: (0, 0)),
                pl.BlockSpec((8, bc), lambda i, *_: (0, 0)),
                pl.BlockSpec((2 * heads, chunk), lambda i, *_: (0, 0)),
            ],
            scratch_shapes=[
                pltpu.VMEM((bc // 2, inner), F32),
                pltpu.VMEM((chunk + 8, inner), F32),
                pltpu.VMEM((chunk + 8, bc), F32),
                pltpu.VMEM((chunk + 8, inner), F32),
                pltpu.VMEM((chunk + 8, bc), F32),
            ],
        ),
        out_shape=[
            jax.ShapeDtypeStruct((tokens, inner), BF),
            jax.ShapeDtypeStruct((tokens, inner), BF),
            jax.ShapeDtypeStruct((tokens, width), BF),
            jax.ShapeDtypeStruct((8, inner), F32),
            jax.ShapeDtypeStruct((8, bc), F32),
            jax.ShapeDtypeStruct((2 * heads, chunk), F32),
        ],
        compiler_params=pltpu.CompilerParams(vmem_limit_bytes=48 * 2**20),
        name="scan_backward",
    )(starts, fill, ggn, y, pz, px, px, pbd, pbd, sin, rows, *consts)


def body(
    tokens, cotangent, starts, fill, norm_gain, w_x, w_z, w_dt, w_bc, conv_x, conv_bc, dt_bias, a_log, skip,
    gate_gain, w_out,
):
    heads_n = lax.axis_size("heads")
    head_index = lax.axis_index("heads")
    count, columns = tokens.shape
    width = columns * heads_n
    blocks = starts.shape[0]
    chunk = count // blocks
    inner = w_x.shape[1]
    heads = w_dt.shape[1]
    bc = w_bc.shape[1]
    total_inner = inner * heads_n
    dt_pad = jnp.pad(w_dt, ((0, 0), (0, chunk - heads)))
    packed = jnp.concatenate([w_x, w_z, w_bc, dt_pad, w_out], axis=1)
    rows_all = lax.all_gather(packed, "dp", axis=0, tiled=True)
    rows_x, rows_z = rows_all[:, :inner], rows_all[:, inner : 2 * inner]
    rows_bd, rows_out = rows_all[:, 2 * inner : 2 * inner + bc + chunk], rows_all[:, 2 * inner + bc + chunk :]
    whole = lax.all_gather(tokens, "heads", axis=1, tiled=True).astype(F32)
    inverse = lax.rsqrt(jnp.mean(whole * whole, axis=-1, keepdims=True) + EPS)
    normed = (whole * inverse * norm_gain).astype(BF)
    px, pz, pbd = nn(normed, rows_x), nn(normed, rows_z), nn(normed, rows_bd)
    y, sin = scan_forward(px, pbd, conv_x, conv_bc, dt_bias, a_log, skip, starts, fill)
    g_full = lax.all_gather(cotangent, "heads", axis=1, tiled=True)
    ggn = nn(g_full, rows_out)
    gated = y * jax.nn.silu(pz)
    both = jnp.stack(
        [jnp.sum(gated * gated, axis=-1), jnp.sum(gated * gate_gain * ggn, axis=-1)], axis=0
    )
    both = lax.psum(both, "heads")
    rows = jnp.pad(jnp.transpose(both.reshape(2, blocks, chunk), (1, 0, 2)), ((0, 0), (0, 6), (0, 0)))
    gate_inverse = lax.rsqrt(both[0] / total_inner + EPS)[:, None]
    gated_normed = (gated * gate_inverse * gate_gain).astype(BF)
    partial_out = nt(gated_normed, rows_out)
    out_share = lax.psum_scatter(partial_out, "heads", scatter_dimension=1, tiled=True)
    block_out = (tokens.astype(F32) + out_share).astype(BF)
    lpx, lpz, lpbd, acc_x, acc_bc, acc_s = scan_backward(
        ggn, y, pz, px, pbd, sin, rows, gate_gain, conv_x, conv_bc, dt_bias, a_log, skip, starts, fill,
        total_inner,
    )
    partial_in = nt(lpx, rows_x) + nt(lpz, rows_z) + nt(lpbd, rows_bd)
    in_share = lax.psum_scatter(partial_in, "heads", scatter_dimension=1, tiled=True)
    own = tokens.astype(F32)
    own_gain = lax.dynamic_slice_in_dim(norm_gain, head_index * columns, columns, 0)
    gain_part = jnp.sum(in_share * own * inverse, axis=0)
    norm_dots = lax.psum(jnp.sum(in_share * own_gain * own, axis=-1), "heads")
    grad_tokens = (
        cotangent.astype(F32)
        + inverse * own_gain * in_share
        - own * inverse**3 * (norm_dots / width)[:, None]
    )
    grads = jnp.concatenate(
        [tn(normed, lpx), tn(normed, lpz), tn(normed, lpbd), tn(g_full, gated_normed)], axis=1
    )
    grads = lax.psum_scatter(grads, "dp", scatter_dimension=0, tiled=True)
    grad_w_x, grad_w_z = grads[:, :inner], grads[:, inner : 2 * inner]
    grad_bd = grads[:, 2 * inner : 2 * inner + bc + chunk]
    grad_w_bc = lax.psum(grad_bd[:, :bc], "heads")
    grad_w_dt = grad_bd[:, bc : bc + heads]
    grad_w_out = grads[:, 2 * inner + bc + chunk :]
    taps = conv_x.shape[0]
    small = jnp.concatenate([acc_x.reshape(-1), jnp.sum(acc_s, axis=1), gain_part])
    small = lax.psum(small, "dp")
    grad_conv_bc = lax.psum(acc_bc[:taps], ("dp", "heads"))
    acc_x = small[: acc_x.size].reshape(acc_x.shape)
    acc_s = small[acc_x.size : acc_x.size + 2 * heads]
    return (
        block_out, grad_tokens, small[acc_x.size + 2 * heads :], grad_w_x, grad_w_z, grad_w_dt, grad_w_bc,
        acc_x[:taps], grad_conv_bc, acc_s[:heads], acc_s[heads:],
        jnp.sum(acc_x[taps + 1].reshape(heads, HD), axis=1), acc_x[taps], grad_w_out,
    )


def solution(mesh):
    placed = (
        P("dp", "heads"),
        P("dp", "heads"),
        P("dp"),
        P("dp"),
        P(),
        P("dp", "heads"),
        P("dp", "heads"),
        P("dp", "heads"),
        P("dp", None),
        P(None, "heads"),
        P(),
        P("heads"),
        P("heads"),
        P("heads"),
        P("heads"),
        P("dp", "heads"),
    )
    return jax.shard_map(
        body,
        mesh=mesh,
        in_specs=placed,
        out_specs=(
            P("dp", "heads"),
            P("dp", "heads"),
            P("heads"),
            P("dp", "heads"),
            P("dp", "heads"),
            P("dp", "heads"),
            P("dp", None),
            P(None, "heads"),
            P(),
            P("heads"),
            P("heads"),
            P("heads"),
            P("heads"),
            P("dp", "heads"),
        ),
        check_vma=False,
    )
```

```python
import functools
import jax
import jax.numpy as jnp
import numpy as np
from jax import lax
from jax.experimental import pallas as pl
from jax.experimental.pallas import tpu as pltpu
from jax.sharding import PartitionSpec as P

HD = 64
EPS = 1e-05
F32 = jnp.float32
BF = jnp.bfloat16
NEG = -1e30
MESH = pl.DeviceIdType.MESH


def nn(a, b):
    return lax.dot_general(a, b, (((1,), (0,)), ((), ())), preferred_element_type=F32)


def nt(a, b):
    return lax.dot_general(a, b, (((1,), (1,)), ((), ())), preferred_element_type=F32)


def tn(a, b):
    return lax.dot_general(a, b, (((0,), (0,)), ((), ())), preferred_element_type=F32)


def split2(v):
    hi = v.astype(BF).astype(F32)
    return hi, v - hi


def split3(v):
    hi = v.astype(BF).astype(F32)
    rest = v - hi
    mid = rest.astype(BF).astype(F32)
    return hi, mid, rest - mid


def softplus(v):
    return jnp.maximum(v, 0.0) + jnp.log1p(jnp.exp(-jnp.abs(v)))


def sigmoid(v):
    return 1.0 / (1.0 + jnp.exp(-v))


def iota2(rows, cols, axis):
    return lax.broadcasted_iota(jnp.int32, (rows, cols), axis)


def scan_constants(chunk, heads):
    inner = heads * HD
    t = np.arange(chunk)
    upper = (t[:, None] <= t[None, :]).astype(np.float32)
    head_of = np.arange(inner) // HD
    spread = np.zeros((chunk, 3 * inner), np.float32)
    for q in range(3):
        for part in range(2):
            base = heads * (1 + 2 * q + part)
            for h in range(heads):
                spread[base + h, q * inner : (q + 1) * inner] = head_of == h
    gather = np.zeros((3, inner, chunk), np.float32)
    for q in range(3):
        for h in range(heads):
            gather[q, :, q * heads + h] = head_of == h
    return jnp.asarray(upper, BF), jnp.asarray(spread, BF), jnp.asarray(gather, BF)


def conv_from(ext, taps, rows, halo):
    n = taps.shape[0]
    out = taps[n - 1 : n, :] * ext[pl.ds(halo, rows), :]
    for k in range(1, n):
        out = out + taps[n - 1 - k : n - k, :] * ext[pl.ds(halo - k, rows), :]
    return out


def dt_rows(pdt, bias, rate, fill, heads, upper):
    chunk = pdt.shape[0]
    pre = jnp.transpose(pdt)[:heads] + bias
    live = (iota2(heads, chunk, 1) < fill).astype(F32)
    dt = softplus(pre) * live
    hi, mid, low = split3(dt * rate)
    stacked = jnp.concatenate([hi, mid, low], axis=0).astype(BF)
    summed = nn(stacked, upper)
    run = summed[:heads] + summed[heads : 2 * heads] + summed[2 * heads :]
    return pre, live, dt, run


def spread_all(run, dt, heads, chunk, spread):
    last = run[:, chunk - 1 : chunk]
    e_in = jnp.exp(run)
    e_out = jnp.exp(last - run)
    parts = [run]
    for v in (dt, e_in, e_out):
        parts.extend(split2(v))
    used = heads * len(parts)
    if used < chunk:
        parts.append(jnp.zeros((chunk - used, chunk), F32))
    cols = jnp.transpose(jnp.concatenate(parts, axis=0))
    return cols, nn(cols.astype(BF), spread)


def pair_stack(v, low_lanes):
    zero = jnp.zeros_like(v)
    return jnp.concatenate([jnp.where(low_lanes, v, zero), jnp.where(low_lanes, zero, v)], axis=0)


def scan_fwd_kernel(
    heads, starts, fill, px, pbd, convx, convbc, bias, rate, skip, upper, spread,
    y_out, sin_out, state, extx, extb,
):
    c = pl.program_id(0)
    chunk, inner = px.shape
    bc = convbc.shape[1]
    ns = bc // 2
    keep = starts[c] == 0

    @pl.when(c == 0)
    def _():
        state[...] = jnp.zeros_like(state)
        extx[...] = jnp.zeros_like(extx)
        extb[...] = jnp.zeros_like(extb)

    state[...] = jnp.where(keep, state[...], 0.0)
    extx[0:8, :] = jnp.where(keep, extx[chunk : chunk + 8, :], 0.0)
    extb[0:8, :] = jnp.where(keep, extb[chunk : chunk + 8, :], 0.0)
    extx[8 : chunk + 8, :] = px[...]
    extb[8 : chunk + 8, :] = pbd[:, :bc]

    n_live = fill[c]
    u = conv_from(extx, convx[...], chunk, 8)
    x = u * sigmoid(u) * (iota2(chunk, inner, 0) < n_live).astype(F32)
    ub = conv_from(extb, convbc[...], chunk, 8)
    act = (ub * sigmoid(ub) * (iota2(chunk, bc, 0) < n_live).astype(F32)).astype(BF)
    b, cc = act[:, :ns], act[:, ns:]

    _, _, dt, run = dt_rows(pbd[:, bc:], bias[...], rate[...], n_live, heads, upper[...])
    cols, wide = spread_all(run, dt, heads, chunk, spread[...])
    dt_w, ein_w, eout_w = wide[:, :inner], wide[:, inner : 2 * inner], wide[:, 2 * inner :]

    xd = x * dt_w
    xdb = xd.astype(BF)
    scores = nt(cc, b)
    tri = iota2(chunk, chunk, 0) >= iota2(chunk, chunk, 1)
    low_lanes = iota2(chunk, 2 * HD, 1) < HD
    diag = []
    for j in range(heads // 2):
        mix = []
        for h in (2 * j, 2 * j + 1):
            spread_h = cols[:, h : h + 1] - run[h : h + 1, :]
            mix.append((scores * jnp.exp(jnp.where(tri, spread_h, NEG))).astype(BF))
        pair = pair_stack(xdb[:, 2 * HD * j : 2 * HD * (j + 1)], low_lanes)
        diag.append(nn(jnp.concatenate(mix, axis=1), pair))
    enter = state[...]
    enter_b = enter.astype(BF)
    sin_out[0] = enter_b
    y_out[...] = jnp.concatenate(diag, axis=1) + ein_w * nn(cc, enter_b) + skip[...] * x
    state[...] = ein_w[chunk - 1 : chunk, :] * enter + tn(b, (xd * eout_w).astype(BF))


def scan_forward(px, pbd, conv_x, conv_bc, dt_bias, a_log, skip, starts, fill):
    tokens, inner = px.shape
    blocks = starts.shape[0]
    chunk = tokens // blocks
    heads = inner // HD
    bc = conv_bc.shape[1]
    upper, spread, _ = scan_constants(chunk, heads)
    bias = jnp.broadcast_to(dt_bias[:, None], (heads, chunk))
    rate = jnp.broadcast_to(-jnp.exp(a_log)[:, None], (heads, chunk))
    skip_w = jnp.repeat(skip, HD)[None, :]
    fixed = lambda c, *_: (0, 0)
    whole = lambda a: pl.BlockSpec(a.shape, fixed)
    rows = lambda w: pl.BlockSpec((chunk, w), lambda c, *_: (c, 0))
    return pl.pallas_call(
        functools.partial(scan_fwd_kernel, heads),
        grid_spec=pltpu.PrefetchScalarGridSpec(
            num_scalar_prefetch=2,
            grid=(blocks,),
            in_specs=[rows(inner), rows(pbd.shape[1])]
            + [whole(a) for a in (conv_x, conv_bc, bias, rate, skip_w, upper, spread)],
            out_specs=[rows(inner), pl.BlockSpec((1, bc // 2, inner), lambda c, *_: (c, 0, 0))],
            scratch_shapes=[
                pltpu.VMEM((bc // 2, inner), F32),
                pltpu.VMEM((chunk + 8, inner), F32),
                pltpu.VMEM((chunk + 8, bc), F32),
            ],
        ),
        out_shape=[
            jax.ShapeDtypeStruct((tokens, inner), F32),
            jax.ShapeDtypeStruct((blocks, bc // 2, inner), BF),
        ],
        compiler_params=pltpu.CompilerParams(vmem_limit_bytes=48 * 2**20),
        name="scan_forward",
    )(starts, fill, px, pbd, conv_x, conv_bc, bias, rate, skip_w, upper, spread)


def scan_bwd_kernel(
    heads, total_inner, starts, fill, ggn, y, pz, px, px_halo, pbd, pbd_halo, sin, rows, gain, convx, convbc,
    bias, rate, skip, upper, spread, gather, ones_h,
    lpx, lpz, lpbd, acc_x, acc_bc, acc_s, dstate, extx, extb, dux, dub,
):
    i = pl.program_id(0)
    blocks = pl.num_programs(0)
    c = blocks - 1 - i
    chunk, inner = px.shape
    bc = convbc.shape[1]
    ns = bc // 2
    taps_n = convx.shape[0]
    keep = starts[c] == 0
    nxt = jnp.minimum(c + 1, blocks - 1)
    keep_next = jnp.logical_and(starts[nxt] == 0, i > 0)
    n_live = fill[c]

    @pl.when(i == 0)
    def _():
        for ref in (dstate, dux, dub, acc_x, acc_bc, acc_s):
            ref[...] = jnp.zeros_like(ref)

    moved = jnp.transpose(
        jnp.concatenate([rows[0], jnp.zeros((chunk - rows.shape[1], chunk), F32)], axis=0)
    )
    inv = lax.rsqrt(moved[:, 0:1] / total_inner + EPS)
    coef = inv * inv * inv * (moved[:, 1:2] / total_inner)
    z = pz[...]
    sz = sigmoid(z)
    silu_z = z * sz
    yv = y[...]
    gated = yv * silu_z
    g = ggn[...]
    d_gated = inv * (g * gain[...]) - gated * coef
    lpz[...] = (d_gated * yv * (sz * (1.0 + z * (1.0 - sz)))).astype(BF)
    dy = d_gated * silu_z
    acc_x[taps_n : taps_n + 1, :] += jnp.sum(g * gated * inv, axis=0, keepdims=True)

    extx[0:8, :] = jnp.where(keep, px_halo[...], 0.0)
    extb[0:8, :] = jnp.where(keep, pbd_halo[:, :bc], 0.0)
    extx[8 : chunk + 8, :] = px[...]
    extb[8 : chunk + 8, :] = pbd[:, :bc]
    taps = convx[...]
    taps_b = convbc[...]
    live_x = (iota2(chunk, inner, 0) < n_live).astype(F32)
    live_b = (iota2(chunk, bc, 0) < n_live).astype(F32)
    u = conv_from(extx, taps, chunk, 8)
    su = sigmoid(u)
    x = u * su * live_x
    dx_du = su * (1.0 + u * (1.0 - su)) * live_x
    ub = conv_from(extb, taps_b, chunk, 8)
    sb = sigmoid(ub)
    act = (ub * sb * live_b).astype(BF)
    db_du = sb * (1.0 + ub * (1.0 - sb)) * live_b
    b, cc = act[:, :ns], act[:, ns:]

    pre, live, dt, run = dt_rows(pbd[:, bc:], bias[...], rate[...], n_live, heads, upper[...])
    cols, wide = spread_all(run, dt, heads, chunk, spread[...])
    dt_w, ein_w, eout_w = wide[:, :inner], wide[:, inner : 2 * inner], wide[:, 2 * inner :]
    xd = x * dt_w
    xdb = xd.astype(BF)
    dyb = dy.astype(BF)
    acc_x[taps_n + 1 : taps_n + 2, :] += jnp.sum(dy * x, axis=0, keepdims=True)

    scores_t = nt(b, cc)
    tri = iota2(chunk, chunk, 0) <= iota2(chunk, chunk, 1)
    low_lanes = iota2(chunk, 2 * HD, 1) < HD
    d_scores_t = jnp.zeros((chunk, chunk), F32)
    dxd = []
    pulls = []
    read_sums = []
    for j in range(heads // 2):
        span = slice(2 * HD * j, 2 * HD * (j + 1))
        dy_pair = pair_stack(dyb[:, span], low_lanes)
        x_pair = pair_stack(xdb[:, span], low_lanes)
        d_mix = nt(x_pair, dyb[:, span])
        mix = []
        for k in (0, 1):
            h = 2 * j + k
            spread_h = run[h : h + 1, :] - cols[:, h : h + 1]
            fade = jnp.exp(jnp.where(tri, spread_h, NEG))
            m = scores_t * fade
            dm = d_mix[k * chunk : (k + 1) * chunk]
            d_scores_t = d_scores_t + dm * fade
            pull = (dm * m).astype(BF)
            pulls.append(pull)
            read_sums.append(jnp.sum(pull.astype(F32), axis=0, keepdims=True))
            mix.append(m.astype(BF))
        dxd.append(nn(jnp.concatenate(mix, axis=1), dy_pair))
    source_sums = nn(jnp.concatenate(pulls, axis=1), ones_h[...])
    read_rows = jnp.concatenate(read_sums, axis=0)

    d_state = jnp.where(keep_next, dstate[...], 0.0)
    d_state_b = d_state.astype(BF)
    enter_b = sin[0]
    edy = ein_w * dy
    edyb = edy.astype(BF)
    readings = nn(cc, enter_b)
    from_state = nn(b, d_state_b) * eout_w
    d_xd = jnp.concatenate(dxd, axis=1) + from_state
    q1 = edy * readings
    q2 = xd * from_state
    decay = ein_w[chunk - 1 : chunk, :]
    dstate[...] = decay * d_state + tn(cc, edyb)
    d_cb = tn(d_scores_t.astype(BF), b) + nt(edyb, enter_b)
    d_b = nn(d_scores_t.astype(BF), cc) + nt((xd * eout_w).astype(BF), d_state_b)

    sums = (
        nn((d_xd * x).astype(BF), gather[0])
        + nn((q1 - q2).astype(BF), gather[1])
        + nn(q2.astype(BF), gather[2])
        - source_sums
    )
    sums_t = jnp.transpose(sums)
    dt_direct = sums_t[:heads]
    d_run = sums_t[heads : 2 * heads] + read_rows
    whole_q2 = jnp.sum(sums_t[2 * heads : 3 * heads], axis=1, keepdims=True)
    kept = jnp.sum(enter_b.astype(F32) * d_state, axis=0, keepdims=True) * decay
    kept_hi, kept_lo = split2(kept)
    kept_two = jnp.concatenate([kept_hi, kept_lo, jnp.zeros((6, inner), F32)], axis=0).astype(BF)
    kept_cols = nt(gather[3][:, :inner], kept_two)
    d_last = whole_q2 + kept_cols[:heads, 0:1] + kept_cols[:heads, 1:2]
    hi, mid, low = split3(d_run)
    back = nt(jnp.concatenate([hi, mid, low], axis=0).astype(BF), upper[...])
    d_a = back[:heads] + back[heads : 2 * heads] + back[2 * heads :] + d_last
    d_dt = dt_direct + d_a * rate[...]
    d_pre = d_dt * live * sigmoid(pre)
    acc_s[0:heads, :] += d_pre
    acc_s[heads : 2 * heads, :] += d_a * dt * rate[...]

    def conv_back(d_u, du_ref, ext_ref, tap_values, acc):
        du_ref[chunk : chunk + 8, :] = jnp.where(keep_next, du_ref[0:8, :], 0.0)
        du_ref[0:chunk, :] = d_u
        out = tap_values[taps_n - 1 : taps_n, :] * d_u
        acc[taps_n - 1 : taps_n, :] += jnp.sum(d_u * ext_ref[8 : chunk + 8, :], axis=0, keepdims=True)
        for k in range(1, taps_n):
            row = taps_n - 1 - k
            out = out + tap_values[row : row + 1, :] * du_ref[pl.ds(k, chunk), :]
            acc[row : row + 1, :] += jnp.sum(
                d_u * ext_ref[pl.ds(8 - k, chunk), :], axis=0, keepdims=True
            )
        return out

    d_x = d_xd * dt_w + skip[...] * dy
    lpx[...] = conv_back(d_x * dx_du, dux, extx, taps, acc_x).astype(BF)
    d_act = jnp.concatenate([d_b, d_cb], axis=1)
    lpbd[:, :bc] = conv_back(d_act * db_du, dub, extb, taps_b, acc_bc).astype(BF)
    pad = jnp.concatenate([d_pre, jnp.zeros((chunk - heads, chunk), F32)], axis=0)
    lpbd[:, bc:] = jnp.transpose(pad).astype(BF)


def scan_backward(
    ggn, y, pz, px, pbd, sin, rows, gain, conv_x, conv_bc, dt_bias, a_log, skip, starts, fill, total_inner
):
    tokens, inner = px.shape
    blocks = starts.shape[0]
    chunk = tokens // blocks
    heads = inner // HD
    bc = conv_bc.shape[1]
    upper, spread, gather = scan_constants(chunk, heads)
    selector = np.zeros((1, inner, chunk), np.float32)
    lanes = np.zeros((chunk, inner), np.float32)
    for h in range(heads):
        lanes[h, h * HD : (h + 1) * HD] = 1.0
    ones_h = np.zeros((heads * chunk, chunk), np.float32)
    for h in range(heads):
        ones_h[h * chunk : (h + 1) * chunk, heads + h] = 1.0
    ones_h = jnp.asarray(ones_h, BF)
    lanes = jnp.asarray(lanes, BF)
    bias = jnp.broadcast_to(dt_bias[:, None], (heads, chunk))
    rate = jnp.broadcast_to(-jnp.exp(a_log)[:, None], (heads, chunk))
    skip_w = jnp.repeat(skip, HD)[None, :]
    whole = lambda a: pl.BlockSpec(a.shape, lambda i, *_: (0,) * a.ndim)
    back = lambda w: pl.BlockSpec((chunk, w), lambda i, *_: (blocks - 1 - i, 0))
    halo = lambda w: pl.BlockSpec(
        (8, w), lambda i, *_: (jnp.maximum((blocks - 1 - i) * (chunk // 8) - 1, 0), 0)
    )
    width = pbd.shape[1]
    consts = (gain[None, :], conv_x, conv_bc, bias, rate, skip_w, upper, spread, gather, lanes, ones_h)

    def kernel(*refs):
        n_in = 2 + 9
        ins, cons, rest = refs[:n_in], refs[n_in : n_in + 11], refs[n_in + 11 :]
        gain_r, cx, cb, bias_r, rate_r, skip_r, up, sp, ga, la, on = cons

        class Gather:
            def __getitem__(self, k):
                return la[...] if k == 3 else ga[k]

        scan_bwd_kernel(
            heads, total_inner, *ins, gain_r, cx, cb, bias_r, rate_r, skip_r, up, sp, Gather(), on, *rest
        )

    return pl.pallas_call(
        kernel,
        grid_spec=pltpu.PrefetchScalarGridSpec(
            num_scalar_prefetch=2,
            grid=(blocks,),
            in_specs=[
                back(inner), back(inner), back(inner), back(inner), halo(inner), back(width), halo(width),
                pl.BlockSpec((1, bc // 2, inner), lambda i, *_: (blocks - 1 - i, 0, 0)),
                pl.BlockSpec((1, 8, chunk), lambda i, *_: (blocks - 1 - i, 0, 0)),
            ]
            + [whole(a) for a in consts],
            out_specs=[
                back(inner), back(inner), back(width),
                pl.BlockSpec((8, inner), lambda i, *_: (0, 0)),
                pl.BlockSpec((8, bc), lambda i, *_: (0, 0)),
                pl.BlockSpec((2 * heads, chunk), lambda i, *_: (0, 0)),
            ],
            scratch_shapes=[
                pltpu.VMEM((bc // 2, inner), F32),
                pltpu.VMEM((chunk + 8, inner), F32),
                pltpu.VMEM((chunk + 8, bc), F32),
                pltpu.VMEM((chunk + 8, inner), F32),
                pltpu.VMEM((chunk + 8, bc), F32),
            ],
        ),
        out_shape=[
            jax.ShapeDtypeStruct((tokens, inner), BF),
            jax.ShapeDtypeStruct((tokens, inner), BF),
            jax.ShapeDtypeStruct((tokens, width), BF),
            jax.ShapeDtypeStruct((8, inner), F32),
            jax.ShapeDtypeStruct((8, bc), F32),
            jax.ShapeDtypeStruct((2 * heads, chunk), F32),
        ],
        compiler_params=pltpu.CompilerParams(vmem_limit_bytes=48 * 2**20),
        name="scan_backward",
    )(starts, fill, ggn, y, pz, px, px, pbd, pbd, sin, rows, *consts)
def peers(dp_n):
    dp, hm = lax.axis_index("dp"), lax.axis_index("heads")
    across, core = hm // 2, hm % 2
    pair, line, lines = dp % 2, dp // 2, dp_n // 2
    return dict(
        sib=(dp, 2 * across + 1 - core),
        xn=(dp, 2 * (1 - across) + core),
        dg=(dp, 2 * (1 - across) + 1 - core),
        yn=(2 * line + 1 - pair, hm),
        line=lambda k: (2 * ((line + k) % lines) + pair, hm),
        mine=hm,
        other=2 * (1 - across) + core,
        sib_mine=2 * across + 1 - core,
        sib_other=2 * (1 - across) + 1 - core,
        pair=pair, line_index=line, lines=lines, dp=dp, core=core,
    )


def meet(who):
    barrier = pltpu.get_barrier_semaphore()
    for name in ("sib", "xn", "dg", "yn"):
        pl.semaphore_signal(barrier, inc=1, device_id=who[name], device_id_type=MESH)

    def greet(k, carry):
        pl.semaphore_signal(barrier, inc=1, device_id=who["line"](k), device_id_type=MESH)
        return carry

    lax.fori_loop(1, who["lines"], greet, 0)
    pl.semaphore_wait(barrier, 4 + who["lines"] - 1)


def push(src, dst, send, recv, to):
    return pltpu.make_async_remote_copy(
        src_ref=src, dst_ref=dst, send_sem=send, recv_sem=recv, device_id=to, device_id_type=MESH
    )


def tail_kernel(
    dp_n, units,
    grad_t_in, gn_in, rows_out_in, normed_t_in, lpz_in, rows_z_in, lpx_in, rows_x_in, lpbd_in, rows_bd_in, normed_in,
    tokens, acc_x, acc_bc, acc_s,
    block_out, in_share, row_sums, g_x, g_z, g_out, g_bc, small_out,
    sib_send, sib_recv, x_send, x_recv, part, held,
    y_send, y_recv, z_send, z_recv, g_own, yb_send, yb_recv, zb_send, zb_recv, gb_own, bh_send, bh_recv,
    bx_send, bx_recv, bs_recv, h_send, h_recv, sy_send, sy_recv, sz_send, sz_recv, dy_send, dy_recv, dz_send, dz_recv,
    grad_t, gn, rows_out, normed_t, lpz, rows_z, lpx, rows_x, lpbd, rows_bd, normed,
    s_in, s_sib, r_sib, s_x, r_x, s_y, r_y, s_z, r_z, s_m, r_m, s_sl, r_sl,
):
    loads = [
        pltpu.make_async_copy(src, dst, s_in.at[i])
        for i, (src, dst) in enumerate((
            (grad_t_in, grad_t), (gn_in, gn), (rows_out_in, rows_out), (normed_t_in, normed_t), (lpz_in, lpz),
            (rows_z_in, rows_z), (lpx_in, lpx), (rows_x_in, rows_x), (lpbd_in, lpbd), (rows_bd_in, rows_bd),
            (normed_in, normed),
        ))
    ]
    for load in loads:
        load.start()
    who = peers(dp_n)
    meet(who)
    count = normed.shape[0]
    width = normed.shape[1]
    inner = lpx.shape[1]
    bc = acc_bc.shape[1]
    quarter = width // 4
    span = count // units
    block = width // dp_n
    lines = who["lines"]
    heads = acc_s.shape[0] // 2
    taps_rows = acc_x.shape[0]

    def copy_sib(u):
        return push(sib_send.at[u], sib_recv.at[u], s_sib.at[u], r_sib.at[u], who["sib"])

    def copy_x(u):
        return push(x_send.at[u], x_recv.at[u], s_x.at[u], r_x.at[u], who["xn"])

    def product(u, q):
        cols = pl.ds(pl.multiple_of(q * quarter, quarter), quarter)
        if u < units:
            return nt(gn[u * span : (u + 1) * span, :], rows_out[cols, :])
        at = slice((u - units) * span, (u - units + 1) * span)
        return nt(lpx[at, :], rows_x[cols, :]) + nt(lpz[at, :], rows_z[cols, :]) + nt(lpbd[at, :], rows_bd[cols, :])

    def head_a(u):
        for k, q in enumerate(("sib_mine", "sib_other", "mine", "other")):
            p = product(u, who[q])
            if u >= units:
                at = slice((u - units) * span, (u - units + 1) * span)
                cols = pl.ds(pl.multiple_of(who[q] * quarter, quarter), quarter)
                inner_p = p * normed[at, cols].astype(F32)
                h_send[0:1, cols] += jnp.sum(inner_p, axis=0, keepdims=True)
                first = (u - units) * span
                lanes = slice(first % width, first % width + span)
                h_send[2 + first // width : 3 + first // width, lanes] += nt(
                    jnp.ones((8, quarter), BF), inner_p.astype(BF)
                )[0:1]
            if k < 2:
                sib_send[u, k] = p.astype(BF)
            else:
                part[u % 2, k - 2] = p
        copy_sib(u).start()

    def head_b(u):
        copy_sib(u).wait()
        x_send[u] = (part[u % 2, 1] + sib_recv[u, 1].astype(F32)).astype(BF)
        copy_x(u).start()
        held[u] = part[u % 2, 0] + sib_recv[u, 0].astype(F32)

    def head_c(u):
        copy_x(u).wait()
        total = held[u] + x_recv[u].astype(F32)
        if u < units:
            at = slice(u * span, (u + 1) * span)
            block_out[at, :] = (tokens[at, :].astype(F32) + total).astype(BF)
        else:
            in_share[(u - units) * span : (u - units + 1) * span, :] = total

    def rows_of(line, pair):
        return pl.ds(pl.multiple_of((2 * line + pair) * block, block), block)

    def grad_a(v):
        left, right = ((grad_t, gn), (normed_t, lpz), (normed_t, lpx))[v // 2]
        cols = slice((v % 2) * (inner // 2), (v % 2 + 1) * (inner // 2))
        for side in (0, 1):
            pair = (1 - who["pair"]) if side == 0 else who["pair"]
            stacked = jnp.concatenate([left[rows_of(l, pair), :] for l in range(lines)], axis=0)
            value = nn(stacked, right[:, cols])
            if side == 0:
                y_send[v] = value.astype(BF)
                copy_y(v).start()
            else:
                g_own[v] = value

    def copy_y(v):
        return push(y_send.at[v], y_recv.at[v], s_y.at[v], r_y.at[v], who["yn"])

    def copy_z(v, k):
        to = (who["line_index"] + k) % lines
        return push(
            z_send.at[v, pl.ds(pl.multiple_of(to * block, block), block)],
            z_recv.at[v, k - 1], s_z.at[v, k - 1], r_z.at[v, k - 1], who["line"](k),
        )

    def each_line(fn):
        def step(k, carry):
            fn(k)
            return carry

        lax.fori_loop(1, lines, step, 0)

    def own_rows():
        return pl.ds(pl.multiple_of(who["line_index"] * block, block), block)

    def grad_b(v):
        copy_y(v).wait()
        g_own[v] = g_own[v] + y_recv[v].astype(F32)
        z_send[v] = g_own[v].astype(BF)
        each_line(lambda k: copy_z(v, k).start())

    def grad_c(v):
        each_line(lambda k: copy_z(v, k).wait())
        total = g_own[v, own_rows(), :]
        for k in range(lines - 1):
            total = total + z_recv[v, k].astype(F32)
        cols = slice((v % 2) * (inner // 2), (v % 2 + 1) * (inner // 2))
        (g_out, g_z, g_x)[v // 2][:, cols] = total

    half = bc // 2

    def copy_bh():
        return push(bh_send, bh_recv, s_m.at[0], r_m.at[0], who["sib"])

    def copy_yb():
        return push(yb_send, yb_recv, s_m.at[1], r_m.at[1], who["yn"])

    def copy_zb(k):
        to = (who["line_index"] + k) % lines
        return push(
            zb_send.at[pl.ds(pl.multiple_of(to * block, block), block)],
            zb_recv.at[k - 1], s_sl.at[0, k - 1], r_sl.at[0, k - 1], who["line"](k),
        )

    def copy_bx():
        return push(bx_send, bx_recv, s_m.at[2], r_m.at[2], who["xn"])

    def copy_bs():
        return push(bx_send, bs_recv, s_m.at[3], r_m.at[3], who["sib"])

    def bc_a():
        for side in (0, 1):
            pair = (1 - who["pair"]) if side == 0 else who["pair"]
            stacked = jnp.concatenate([normed_t[rows_of(l, pair), :] for l in range(lines)], axis=0)
            value = nn(stacked, lpbd[:, :bc])
            first = who["core"] == 0
            lo, hi = value[:, :half], value[:, half:]
            at = slice(side * lines * block, (side + 1) * lines * block)
            bh_send[at, :] = jnp.where(first, hi, lo).astype(BF)
            gb_own[at, :] = jnp.where(first, lo, hi)
        copy_bh().start()

    def bc_b():
        copy_bh().wait()
        rows = lines * block
        gb_own[...] = gb_own[...] + bh_recv[...].astype(F32)
        yb_send[...] = gb_own[:rows, :].astype(BF)
        copy_yb().start()

    def bc_c():
        rows = lines * block
        copy_yb().wait()
        gb_own[rows:, :] = gb_own[rows:, :] + yb_recv[...].astype(F32)
        zb_send[...] = gb_own[rows:, :].astype(BF)
        each_line(lambda k: copy_zb(k).start())

    def bc_d():
        each_line(lambda k: copy_zb(k).wait())
        at = pl.ds(pl.multiple_of(lines * block + who["line_index"] * block, block), block)
        total = gb_own[at, :]
        for k in range(lines - 1):
            total = total + zb_recv[k].astype(F32)
        bx_send[...] = total
        copy_bx().start()

    def bc_e():
        copy_bx().wait()
        bx_send[...] = bx_send[...] + bx_recv[...]
        copy_bs().start()

    def bc_f():
        copy_bs().wait()
        mine, theirs = bx_send[...], bs_recv[...]
        first = who["core"] == 0
        g_bc[:, :half] = jnp.where(first, mine, theirs)
        g_bc[:, half:] = jnp.where(first, theirs, mine)

    three = (("sib", 4), ("xn", 5), ("dg", 6))
    taps = width // bc
    token_rows = count // width

    def copy_h(k):
        name, sem = three[k]
        return push(h_send, h_recv.at[k], s_m.at[sem], r_m.at[sem], who[name])

    def small_a():
        for k in range(taps):
            h_send[1:2, k * bc : (k + 1) * bc] = acc_bc[k : k + 1, :]
        for k in range(3):
            copy_h(k).start()

    def copy_sy():
        return push(sy_send, sy_recv, s_m.at[7], r_m.at[7], who["yn"])

    def copy_dy():
        return push(dy_send, dy_recv, s_m.at[8], r_m.at[8], who["yn"])

    def copy_sz(k):
        return push(sz_send, sz_recv.at[k - 1], s_sl.at[1, k - 1], r_sl.at[1, k - 1], who["line"](k))

    def copy_dz(k):
        return push(dz_send, dz_recv.at[k - 1], s_sl.at[2, k - 1], r_sl.at[2, k - 1], who["line"](k))

    def dt_a():
        dy_send[...] = tn(lpbd[:, bc:], normed[...])[0:16, :].astype(BF)
        copy_dy().start()

    def dt_b():
        copy_dy().wait()
        dz_send[...] = (dy_send[...].astype(F32) + dy_recv[...].astype(F32)).astype(BF)
        each_line(lambda k: copy_dz(k).start())

    def dt_c():
        each_line(lambda k: copy_dz(k).wait())
        total = dz_send[...].astype(F32)
        for k in range(lines - 1):
            total = total + dz_recv[k].astype(F32)
        small_out[8:24, :] = total

    def small_b():
        for k in range(3):
            copy_h(k).wait()
        over_heads = h_send[...] + h_recv[0] + h_recv[1] + h_recv[2]
        row_sums[...] = over_heads[2 : 2 + token_rows, :]
        sy_send[...] = jnp.zeros_like(sy_send)
        sy_send[0:2, :] = over_heads[0:2, :]
        per = width // inner
        for k in range(taps + 2):
            sy_send[2 + k // per : 3 + k // per, (k % per) * inner : (k % per + 1) * inner] = acc_x[k : k + 1, :]
        lanes = acc_s.shape[1]
        at = 2 + -(-(taps + 2) // per)
        fit = width // lanes
        for k in range(2 * heads):
            sy_send[at + k // fit : at + k // fit + 1, (k % fit) * lanes : (k % fit + 1) * lanes] = acc_s[k : k + 1, :]
        copy_sy().start()

    def small_c():
        copy_sy().wait()
        sz_send[...] = sy_send[...] + sy_recv[...]
        each_line(lambda k: copy_sz(k).start())

    def small_d():
        each_line(lambda k: copy_sz(k).wait())
        total = sz_send[...]
        for k in range(lines - 1):
            total = total + sz_recv[k]
        small_out[0:8, :] = total

    h_send[...] = jnp.zeros_like(h_send)

    def seq(*steps):
        for fn, *args in steps:
            fn(*args)

    assert units == 4

    def load(*which):
        for i in which:
            loads[i].wait()

    load(0, 1)
    seq((grad_a, 0), (grad_a, 1))
    load(2)
    seq((head_a, 0), (head_a, 1), (head_b, 0), (head_a, 2), (head_b, 1), (head_a, 3), (head_b, 2))
    load(3, 8)
    seq((bc_a,), (head_b, 3))
    load(4)
    seq((grad_a, 2), (bc_b,), (grad_a, 3))
    load(5, 6, 7, 9, 10)
    seq((grad_b, 0), (head_a, 4), (dt_a,), (grad_b, 1), (grad_a, 4), (head_b, 4), (head_a, 5), (bc_c,), (head_b, 5))
    seq((grad_a, 5), (head_a, 6), (grad_b, 2), (head_b, 6), (head_a, 7), (small_a,), (grad_b, 3), (head_b, 7))
    seq((dt_b,), (small_b,), (head_c, 0), (head_c, 1), (head_c, 2), (head_c, 3), (bc_d,), (grad_c, 0), (grad_c, 1))
    seq((grad_b, 4), (small_c,), (grad_b, 5), (dt_c,), (bc_e,), (head_c, 4), (head_c, 5), (grad_c, 2), (grad_c, 3))
    seq((small_d,), (head_c, 6), (grad_c, 4), (bc_f,), (head_c, 7), (grad_c, 5))


def tail(dp_n, units, normed_t, normed, grad_t, gn, lpx, lpz, lpbd, rows_x, rows_z, rows_bd, rows_out, tokens, acc_x, acc_bc, acc_s):
    count, width = normed.shape
    inner = lpx.shape[1]
    bc = acc_bc.shape[1]
    quarter = width // 4
    span = count // units
    block = width // dp_n
    lines = dp_n // 2
    half_rows = lines * block
    more = max(lines - 1, 1)
    vm = pltpu.VMEM
    dma = pltpu.SemaphoreType.DMA
    operands = (
        grad_t, gn, rows_out, normed_t, lpz, rows_z, lpx, rows_x, lpbd, rows_bd, normed, tokens, acc_x, acc_bc, acc_s,
    )
    sds = jax.ShapeDtypeStruct
    spec = pl.BlockSpec(memory_space=pltpu.VMEM)
    return pl.pallas_call(
        functools.partial(tail_kernel, dp_n, units),
        out_shape=[
            sds((count, quarter), BF), sds((count, quarter), F32), sds((count // width, width), F32),
            sds((block, inner), F32), sds((block, inner), F32), sds((block, inner), F32), sds((block, bc), F32),
            sds((24, width), F32),
        ],
        in_specs=[pl.BlockSpec(memory_space=pl.ANY)] * 11 + [spec] * 4,
        out_specs=[spec] * 8,
        scratch_shapes=[
            vm((2 * units, 2, span, quarter), BF), vm((2 * units, 2, span, quarter), BF),
            vm((2 * units, span, quarter), BF), vm((2 * units, span, quarter), BF),
            vm((2, 2, span, quarter), F32), vm((2 * units, span, quarter), F32),
            vm((6, half_rows, inner // 2), BF), vm((6, half_rows, inner // 2), BF),
            vm((6, half_rows, inner // 2), BF), vm((6, more, block, inner // 2), BF),
            vm((6, half_rows, inner // 2), F32),
            vm((half_rows, bc // 2), BF), vm((half_rows, bc // 2), BF),
            vm((half_rows, bc // 2), BF), vm((more, block, bc // 2), BF),
            vm((2 * half_rows, bc // 2), F32),
            vm((2 * half_rows, bc // 2), BF), vm((2 * half_rows, bc // 2), BF),
            vm((block, bc // 2), F32), vm((block, bc // 2), F32), vm((block, bc // 2), F32),
            vm((8, width), F32), vm((3, 8, width), F32),
            vm((8, width), F32), vm((8, width), F32), vm((8, width), F32), vm((more, 8, width), F32),
            vm((16, width), BF), vm((16, width), BF), vm((16, width), BF), vm((more, 16, width), BF),
        ]
        + [vm(a.shape, a.dtype) for a in operands[:11]]
        + [
            dma((11,)), dma((2 * units,)), dma((2 * units,)), dma((2 * units,)), dma((2 * units,)),
            dma((6,)), dma((6,)), dma((6, more)), dma((6, more)), dma((9,)), dma((9,)),
            dma((3, more)), dma((3, more)),
        ],
        compiler_params=pltpu.CompilerParams(
            collective_id=1, has_side_effects=True, vmem_limit_bytes=62 * 2**20
        ),
        name="tail",
    )(*operands)
def shares(ref_in, block_of, dp_n, width, send, recv, who):
    rows = ref_in.shape[0]
    lines = who["lines"]

    def at(dp):
        return block_of.at[pl.ds(pl.multiple_of(dp * rows, rows), rows), width]

    def own():
        return push(ref_in.at[:, width], at(who["dp"]), send.at[0], recv.at[0], who["yn"])

    def along(k):
        return push(ref_in.at[:, width], at(who["dp"]), send.at[k], recv.at[k], who["line"](k))

    def onward(k):
        source = at(2 * ((who["line_index"] - k + lines) % lines) + who["pair"])
        return push(source, source, send.at[lines - 1 + k], recv.at[lines - 1 + k], who["yn"])

    return own, along, onward


def loop_line(lines, fn):
    def step(k, carry):
        fn(k)
        return carry

    lax.fori_loop(1, lines, step, 0)


def front_kernel(
    dp_n, units,
    tokens, w_bd, w_x, gain,
    px_out, pbd_out, normed_out, normed_t_out, q_out, rows_x, rows_bd,
    tok, wx, wbd, px, pbd, normed, normed_t, q,
    s_loc, s_sib, r_sib, s_x, r_x, s_f, r_f, s_b, r_b, s_w, r_w, s_out,
):
    who = peers(dp_n)
    count, quarter = tokens.shape
    width = 4 * quarter
    span = count // units
    lines = who["lines"]
    block = w_x.shape[0]
    here = pl.ds(pl.multiple_of(who["dp"] * block, block), block)
    local = [
        pltpu.make_async_copy(tokens, tok.at[who["mine"]], s_loc.at[0]),
        pltpu.make_async_copy(w_bd, wbd.at[here], s_loc.at[1]),
        pltpu.make_async_copy(w_x, wx.at[here], s_loc.at[2]),
    ]
    for copy in local:
        copy.start()
    meet(who)

    def rows(s):
        return pl.ds(s * span, span)

    def to_x(s):
        return push(tokens.at[rows(s)], tok.at[who["mine"], rows(s)], s_x.at[s], r_x.at[s], who["xn"])

    def to_sib():
        return push(tokens, tok.at[who["mine"]], s_sib.at[0], r_sib.at[0], who["sib"])

    def forward(s):
        here = tok.at[who["other"], rows(s)]
        return push(here, here, s_f.at[s], r_f.at[s], who["sib"])

    every = slice(None)
    bd_own, bd_along, bd_onward = shares(w_bd, wbd, dp_n, every, s_b, r_b, who)
    x_own, x_along, x_onward = shares(w_x, wx, dp_n, every, s_w, r_w, who)
    to_x(0).start()
    loop_line(lines, lambda k: bd_along(k).start())
    bd_own().start()
    for s in range(1, units):
        to_x(s).start()
    to_sib().start()
    loop_line(lines, lambda k: x_along(k).start())
    x_own().start()

    def pass_on(along, onward, k):
        along(k).wait()
        onward(k).start()

    def norm(s):
        at = slice(s * span, (s + 1) * span)
        parts = [tok[h, at, :].astype(F32) for h in range(4)]
        total = sum(jnp.sum(p * p, axis=1, keepdims=True) for p in parts)
        inv = lax.rsqrt(total / width + EPS)
        q[at, :] = jnp.broadcast_to(inv, (span, q.shape[1]))
        for h in range(4):
            cols = slice(h * quarter, (h + 1) * quarter)
            value = (parts[h] * inv * gain[:, cols]).astype(BF)
            normed[at, cols] = value
            normed_t[cols, at] = jnp.transpose(value)

    def outward(ref, out, i, at):
        return pltpu.make_async_copy(ref.at[at], out.at[at], s_out.at[i])

    def send_norm(s):
        at = (slice(s * span, (s + 1) * span),)
        copies = [
            outward(normed, normed_out, 3 * s, at),
            outward(normed_t, normed_t_out, 3 * s + 1, (slice(None),) + at),
            outward(q, q_out, 3 * s + 2, at),
        ]
        return copies

    def project(s):
        at = slice(s * span, (s + 1) * span)
        pbd[at, :] = nn(normed[at, :], wbd[...])
        px[at, :] = nn(normed[at, :], wx[...])

    def send_proj(s):
        at = (slice(s * span, (s + 1) * span),)
        base = 3 * units + 2 * s
        return [outward(px, px_out, base, at), outward(pbd, pbd_out, base + 1, at)]

    outs = []

    def go(copies):
        for copy in copies:
            copy.start()
        outs.extend(copies)

    local[0].wait()
    to_x(0).wait()
    forward(0).start()
    loop_line(lines, lambda k: pass_on(bd_along, bd_onward, k))
    to_sib().wait()
    for s in range(units):
        forward(s).wait()
        norm(s)
        go(send_norm(s))
        if s + 1 < units:
            to_x(s + 1).wait()
            forward(s + 1).start()
        if s == 1:
            bd_own().wait()
            loop_line(lines, lambda k: bd_onward(k).wait())
            local[1].wait()
            copy = pltpu.make_async_copy(wbd, rows_bd, s_out.at[5 * units])
            go([copy])
        if s == units - 2:
            loop_line(lines, lambda k: pass_on(x_along, x_onward, k))
    x_own().wait()
    loop_line(lines, lambda k: x_onward(k).wait())
    local[2].wait()
    go([pltpu.make_async_copy(wx, rows_x, s_out.at[5 * units + 1])])
    for s in range(units):
        project(s)
        go(send_proj(s))
    for copy in outs:
        copy.wait()


def front(dp_n, units, tokens, w_bd, w_x, gain):
    count, quarter = tokens.shape
    width = 4 * quarter
    inner, wide = w_x.shape[1], w_bd.shape[1]
    vm, dma, sds = pltpu.VMEM, pltpu.SemaphoreType.DMA, jax.ShapeDtypeStruct
    hbm = pl.BlockSpec(memory_space=pl.ANY)
    lines = dp_n // 2
    ways = 2 * lines - 1
    outs = [
        sds((count, inner), F32), sds((count, wide), F32), sds((count, width), BF), sds((width, count), BF),
        sds((count, 128), F32), sds((width, inner), BF), sds((width, wide), BF),
    ]
    return pl.pallas_call(
        functools.partial(front_kernel, dp_n, units),
        out_shape=outs,
        in_specs=[hbm] * 3 + [pl.BlockSpec(memory_space=pltpu.VMEM)],
        out_specs=[hbm] * 7,
        scratch_shapes=[
            vm((4, count, quarter), BF), vm((width, inner), BF), vm((width, wide), BF),
            vm((count, inner), F32), vm((count, wide), F32), vm((count, width), BF), vm((width, count), BF),
            vm((count, 128), F32),
            dma((3,)), dma((1,)), dma((1,)), dma((units,)), dma((units,)), dma((units,)), dma((units,)),
            dma((ways,)), dma((ways,)), dma((ways,)), dma((ways,)), dma((5 * units + 2,)),
        ],
        compiler_params=pltpu.CompilerParams(
            collective_id=2, has_side_effects=True, vmem_limit_bytes=58 * 2**20
        ),
        name="front",
    )(tokens, w_bd, w_x, gain)


def body(
    tokens, cotangent, starts, fill, norm_gain, w_x, w_z, w_dt, w_bc, conv_x, conv_bc, dt_bias, a_log, skip,
    gate_gain, w_out,
):
    heads_n = lax.axis_size("heads")
    dp_n = lax.axis_size("dp")
    head_index = lax.axis_index("heads")
    dp_index = lax.axis_index("dp")
    count, columns = tokens.shape
    width = columns * heads_n
    blocks = starts.shape[0]
    chunk = count // blocks
    inner = w_x.shape[1]
    heads = w_dt.shape[1]
    bc = w_bc.shape[1]
    total_inner = inner * heads_n
    w_bd = jnp.concatenate([w_bc, jnp.pad(w_dt, ((0, 0), (0, chunk - heads)))], axis=1)
    px, pbd, normed, normed_t, q_wide, rows_x, rows_bd = front(dp_n, 4, tokens, w_bd, w_x, norm_gain[None, :])
    rows_z, rows_out = (lax.all_gather(w, "dp", axis=0, tiled=True) for w in (w_z, w_out))
    y, sin = scan_forward(px, pbd, conv_x, conv_bc, dt_bias, a_log, skip, starts, fill)
    pz = nn(normed, rows_z)
    g_full = lax.all_gather(cotangent, "heads", axis=1, tiled=True)
    ggn = nn(g_full, rows_out)
    gated = y * jax.nn.silu(pz)
    both = jnp.stack(
        [jnp.sum(gated * gated, axis=-1), jnp.sum(gated * gate_gain * ggn, axis=-1)], axis=0
    )
    both = lax.psum(both, "heads")
    rows = jnp.pad(jnp.transpose(both.reshape(2, blocks, chunk), (1, 0, 2)), ((0, 0), (0, 6), (0, 0)))
    gate_inverse = lax.rsqrt(both[0] / total_inner + EPS)[:, None]
    gated_normed = (gated * gate_inverse * gate_gain).astype(BF)
    lpx, lpz, lpbd, acc_x, acc_bc, acc_s = scan_backward(
        ggn, y, pz, px, pbd, sin, rows, gate_gain, conv_x, conv_bc, dt_bias, a_log, skip, starts, fill,
        total_inner,
    )
    block_out, in_share, row_sums, grad_w_x, grad_w_z, grad_w_out, grad_w_bc, small = tail(
        dp_n, 4, normed_t, normed, g_full.T, gated_normed, lpx, lpz, lpbd, rows_x, rows_z, rows_bd, rows_out,
        tokens, acc_x, acc_bc, acc_s,
    )
    own = tokens.astype(F32)
    own_gain = lax.dynamic_slice_in_dim(norm_gain, head_index * columns, columns, 0)
    inverse = q_wide[:, 0:1]
    grad_tokens = (
        cotangent.astype(F32)
        + inverse * own_gain * in_share
        - own * (inverse * inverse) * (row_sums.reshape(-1) / width)[:, None]
    )
    return (block_out, grad_tokens) + outputs(
        small, dp_index, head_index, own_gain, conv_x, bc, heads, inner, width // dp_n, chunk,
        grad_w_x, grad_w_z, grad_w_bc, grad_w_out,
    )


def outputs(small, dp_index, head_index, own_gain, conv_x, bc, heads, inner, block, chunk, g_x, g_z, g_bc, g_out):
    taps = conv_x.shape[0]
    width = small.shape[1]
    columns = own_gain.shape[0]
    grad_w_dt = lax.dynamic_slice_in_dim(small[8 : 8 + heads], dp_index * block, block, 1).T
    gain_sum = lax.dynamic_slice_in_dim(small[0], head_index * columns, columns, 0)
    per = width // inner
    scans = small[2 : 2 + -(-(taps + 2) // per)].reshape(-1, inner)
    at = 2 + -(-(taps + 2) // per)
    lanes = jnp.sum(small[at:8].reshape(-1, chunk)[: 2 * heads], axis=1)
    return (
        gain_sum / own_gain, g_x, g_z, grad_w_dt, g_bc, scans[:taps], small[1].reshape(taps, bc), lanes[:heads],
        lanes[heads:], jnp.sum(scans[taps + 1].reshape(heads, HD), axis=1), scans[taps], g_out,
    )


def solution(mesh):
    placed = (
        P("dp", "heads"),
        P("dp", "heads"),
        P("dp"),
        P("dp"),
        P(),
        P("dp", "heads"),
        P("dp", "heads"),
        P("dp", "heads"),
        P("dp", None),
        P(None, "heads"),
        P(),
        P("heads"),
        P("heads"),
        P("heads"),
        P("heads"),
        P("dp", "heads"),
    )
    return jax.shard_map(
        body,
        mesh=mesh,
        in_specs=placed,
        out_specs=(
            P("dp", "heads"),
            P("dp", "heads"),
            P("heads"),
            P("dp", "heads"),
            P("dp", "heads"),
            P("dp", "heads"),
            P("dp", None),
            P(None, "heads"),
            P(),
            P("heads"),
            P("heads"),
            P("heads"),
            P("heads"),
            P("dp", "heads"),
        ),
        check_vma=False,
    )
```

```python
import functools
import jax
import jax.numpy as jnp
import numpy as np
from jax import lax
from jax.experimental import pallas as pl
from jax.experimental.pallas import tpu as pltpu
from jax.sharding import PartitionSpec as P

HD = 64
EPS = 1e-05
F32 = jnp.float32
BF = jnp.bfloat16
NEG = -1e30
MESH = pl.DeviceIdType.MESH


def nn(a, b):
    return lax.dot_general(a, b, (((1,), (0,)), ((), ())), preferred_element_type=F32)


def nt(a, b):
    return lax.dot_general(a, b, (((1,), (1,)), ((), ())), preferred_element_type=F32)


def tn(a, b):
    return lax.dot_general(a, b, (((0,), (0,)), ((), ())), preferred_element_type=F32)


def split2(v):
    hi = v.astype(BF).astype(F32)
    return hi, v - hi


def split3(v):
    hi = v.astype(BF).astype(F32)
    rest = v - hi
    mid = rest.astype(BF).astype(F32)
    return hi, mid, rest - mid


def softplus(v):
    return jnp.maximum(v, 0.0) + jnp.log1p(jnp.exp(-jnp.abs(v)))


def sigmoid(v):
    return 1.0 / (1.0 + jnp.exp(-v))


def iota2(rows, cols, axis):
    return lax.broadcasted_iota(jnp.int32, (rows, cols), axis)


def scan_constants(chunk, heads):
    inner = heads * HD
    t = np.arange(chunk)
    upper = (t[:, None] <= t[None, :]).astype(np.float32)
    head_of = np.arange(inner) // HD
    spread = np.zeros((chunk, 3 * inner), np.float32)
    for q in range(3):
        for part in range(2):
            base = heads * (1 + 2 * q + part)
            for h in range(heads):
                spread[base + h, q * inner : (q + 1) * inner] = head_of == h
    gather = np.zeros((3, inner, chunk), np.float32)
    for q in range(3):
        for h in range(heads):
            gather[q, :, q * heads + h] = head_of == h
    return jnp.asarray(upper, BF), jnp.asarray(spread, BF), jnp.asarray(gather, BF)


def conv_from(ext, taps, rows, halo):
    n = taps.shape[0]
    out = taps[n - 1 : n, :] * ext[pl.ds(halo, rows), :]
    for k in range(1, n):
        out = out + taps[n - 1 - k : n - k, :] * ext[pl.ds(halo - k, rows), :]
    return out


def dt_rows(pdt, bias, rate, fill, heads, upper):
    chunk = pdt.shape[0]
    pre = jnp.transpose(pdt)[:heads] + bias
    live = (iota2(heads, chunk, 1).astype(F32) < fill).astype(F32)
    dt = softplus(pre) * live
    hi, mid, low = split3(dt * rate)
    stacked = jnp.concatenate([hi, mid, low], axis=0).astype(BF)
    summed = nn(stacked, upper)
    run = summed[:heads] + summed[heads : 2 * heads] + summed[2 * heads :]
    return pre, live, dt, run


def spread_all(run, dt, heads, chunk, spread):
    last = run[:, chunk - 1 : chunk]
    e_in = jnp.exp(run)
    e_out = jnp.exp(last - run)
    parts = [run]
    for v in (dt, e_in, e_out):
        parts.extend(split2(v))
    used = heads * len(parts)
    if used < chunk:
        parts.append(jnp.zeros((chunk - used, chunk), F32))
    cols = jnp.transpose(jnp.concatenate(parts, axis=0))
    return cols, nn(cols.astype(BF), spread)


def pair_stack(v, low_lanes):
    zero = jnp.zeros_like(v)
    return jnp.concatenate([jnp.where(low_lanes, v, zero), jnp.where(low_lanes, zero, v)], axis=0)


def scan_fwd_kernel(
    heads, dp_n, meta, px, pbd, convx, convbc, bias, rate, skip, upper, spread, cot, w_z, w_out,
    y_out, sin_out, parts, rows_z, rows_out, state, extx, extb,
    s_loc, s_sib, r_sib, s_x, r_x, s_f, r_f, s_w, r_w,
):
    c = pl.program_id(0)
    chunk, inner = px.shape
    bc = convbc.shape[1]
    ns = bc // 2
    keep = meta[0, 0:1, 0:1] > 0.5
    finish = gather_beside_scan(
        dp_n, cot, w_z, w_out, parts, rows_z, rows_out, s_loc, s_sib, r_sib, s_x, r_x, s_f, r_f, s_w, r_w
    )

    @pl.when(c == 0)
    def _():
        state[...] = jnp.zeros_like(state)
        extx[...] = jnp.zeros_like(extx)
        extb[...] = jnp.zeros_like(extb)

    state[...] = jnp.where(keep, state[...], 0.0)
    extx[0:8, :] = jnp.where(keep, extx[chunk : chunk + 8, :], 0.0)
    extb[0:8, :] = jnp.where(keep, extb[chunk : chunk + 8, :], 0.0)
    extx[8 : chunk + 8, :] = px[...]
    extb[8 : chunk + 8, :] = pbd[:, :bc]

    n_live = meta[0, 1:2, 0:1]
    u = conv_from(extx, convx[...], chunk, 8)
    x = u * sigmoid(u) * (iota2(chunk, inner, 0).astype(F32) < n_live).astype(F32)
    ub = conv_from(extb, convbc[...], chunk, 8)
    act = (ub * sigmoid(ub) * (iota2(chunk, bc, 0).astype(F32) < n_live).astype(F32)).astype(BF)
    b, cc = act[:, :ns], act[:, ns:]

    _, _, dt, run = dt_rows(pbd[:, bc:], bias[...], rate[...], n_live, heads, upper[...])
    cols, wide = spread_all(run, dt, heads, chunk, spread[...])
    dt_w, ein_w, eout_w = wide[:, :inner], wide[:, inner : 2 * inner], wide[:, 2 * inner :]

    xd = x * dt_w
    xdb = xd.astype(BF)
    scores = nt(cc, b)
    tri = iota2(chunk, chunk, 0) >= iota2(chunk, chunk, 1)
    low_lanes = iota2(chunk, 2 * HD, 1) < HD
    diag = []
    for j in range(heads // 2):
        mix = []
        for h in (2 * j, 2 * j + 1):
            spread_h = cols[:, h : h + 1] - run[h : h + 1, :]
            mix.append((scores * jnp.exp(jnp.where(tri, spread_h, NEG))).astype(BF))
        pair = pair_stack(xdb[:, 2 * HD * j : 2 * HD * (j + 1)], low_lanes)
        diag.append(nn(jnp.concatenate(mix, axis=1), pair))
    enter = state[...]
    enter_b = enter.astype(BF)
    sin_out[0] = enter_b
    y_out[...] = jnp.concatenate(diag, axis=1) + ein_w * nn(cc, enter_b) + skip[...] * x
    state[...] = ein_w[chunk - 1 : chunk, :] * enter + tn(b, (xd * eout_w).astype(BF))
    pl.when(c == pl.num_programs(0) - 1)(finish)


def gather_beside_scan(
    dp_n, cot, w_z, w_out, parts, rows_z, rows_out, s_loc, s_sib, r_sib, s_x, r_x, s_f, r_f, s_w, r_w
):
    c = pl.program_id(0)
    last = pl.num_programs(0) - 1
    who = peers(dp_n)
    count = cot.shape[0]
    pieces = s_x.shape[0]
    span = count // pieces
    block, inner = w_z.shape
    here = pl.ds(pl.multiple_of(who["dp"] * block, block), block)
    local = [
        pltpu.make_async_copy(cot, parts.at[who["mine"]], s_loc.at[0]),
        pltpu.make_async_copy(w_z, rows_z.at[here], s_loc.at[1]),
        pltpu.make_async_copy(w_out, rows_out.at[here], s_loc.at[2]),
    ]

    def to_x(j):
        at = pl.ds(j * span, span)
        return push(cot.at[at], parts.at[who["mine"], at], s_x.at[j], r_x.at[j], who["xn"])

    def to_sib():
        return push(cot, parts.at[who["mine"]], s_sib.at[0], r_sib.at[0], who["sib"])

    def forward(j):
        there = parts.at[who["other"], pl.ds(j * span, span)]
        return push(there, there, s_f.at[j], r_f.at[j], who["sib"])

    cuts = [
        shares(ref, rows, dp_n, pl.ds(h * (inner // 2), inner // 2), s_w.at[2 * i + h], r_w.at[2 * i + h], who)
        for i, (ref, rows) in enumerate(((w_z, rows_z), (w_out, rows_out)))
        for h in (0, 1)
    ]

    @pl.when(c == 0)
    def _():
        for copy in local:
            copy.start()
        meet(who)
        for j in range(pieces):
            to_x(j).start()
        for own, along, onward in cuts:
            loop_line(who["lines"], lambda k: along(k).start())
            own().start()
        to_sib().start()

    def pass_cot(j):
        to_x(j).wait()
        forward(j).start()

    def pass_rows(p):
        own, along, onward = cuts[p]

        def one(k):
            along(k).wait()
            onward(k).start()

        loop_line(who["lines"], one)

    events = {}
    for p, at in enumerate((5, 10, 14)):
        events.setdefault(at, []).append((pass_rows, p))
    for j, at in enumerate((3, 6, 8, 11, 13)):
        if j < pieces:
            events.setdefault(at, []).append((pass_cot, j))
    late = [(pass_rows, 3)] + [(pass_cot, j) for j in range(5, pieces)]
    for at, steps in events.items():

        @pl.when(c == at)
        def _(steps=steps):
            for fn, k in steps:
                fn(k)

    def finish():
        for fn, k in late:
            fn(k)
        for copy in local:
            copy.wait()
        to_sib().wait()
        for j in range(pieces):
            forward(j).wait()
        for own, along, onward in cuts:
            own().wait()
            loop_line(who["lines"], lambda k: onward(k).wait())

    return finish


def scan_forward(dp_n, px, pbd, conv_x, conv_bc, dt_bias, a_log, skip, meta, cot, w_z, w_out):
    tokens, inner = px.shape
    blocks = meta.shape[0]
    chunk = tokens // blocks
    heads = inner // HD
    bc = conv_bc.shape[1]
    upper, spread, _ = scan_constants(chunk, heads)
    bias = jnp.broadcast_to(dt_bias[:, None], (heads, chunk))
    rate = jnp.broadcast_to(-jnp.exp(a_log)[:, None], (heads, chunk))
    skip_w = jnp.repeat(skip, HD)[None, :]
    whole = lambda a: pl.BlockSpec(a.shape, lambda c: (0, 0))
    rows = lambda w: pl.BlockSpec((chunk, w), lambda c: (c, 0))
    hbm = pl.BlockSpec(memory_space=pl.ANY)
    dma = pltpu.SemaphoreType.DMA
    sds = jax.ShapeDtypeStruct
    pieces = 8
    ways = dp_n - 1
    return pl.pallas_call(
        functools.partial(scan_fwd_kernel, heads, dp_n),
        grid=(blocks,),
        in_specs=[pl.BlockSpec((1, 8, chunk), lambda c: (c, 0, 0)), rows(inner), rows(pbd.shape[1])]
        + [whole(a) for a in (conv_x, conv_bc, bias, rate, skip_w, upper, spread)]
        + [hbm] * 3,
        out_specs=[rows(inner), pl.BlockSpec((1, bc // 2, inner), lambda c: (c, 0, 0))] + [hbm] * 3,
        scratch_shapes=[
            pltpu.VMEM((bc // 2, inner), F32),
            pltpu.VMEM((chunk + 8, inner), F32),
            pltpu.VMEM((chunk + 8, bc), F32),
            dma((3,)), dma((1,)), dma((1,)), dma((pieces,)), dma((pieces,)), dma((pieces,)), dma((pieces,)),
            dma((4, ways)), dma((4, ways)),
        ],
        out_shape=[
            sds((tokens, inner), F32), sds((blocks, bc // 2, inner), BF),
            sds((4,) + cot.shape, BF), sds((w_z.shape[0] * dp_n, inner), BF), sds((w_z.shape[0] * dp_n, inner), BF),
        ],
        compiler_params=pltpu.CompilerParams(
            collective_id=3, has_side_effects=True, vmem_limit_bytes=48 * 2**20
        ),
        name="scan_forward",
    )(meta, px, pbd, conv_x, conv_bc, bias, rate, skip_w, upper, spread, cot, w_z, w_out)


def gate_kernel(
    dp_n, normed, rows_z, rows_out, parts, y, gain, pz, ggn, grad_t, sums, h_send, h_recv, s_h, r_h,
):
    i = pl.program_id(0)
    who = peers(dp_n)
    names = ("sib", "xn", "dg")
    barrier = pltpu.get_barrier_semaphore()
    span, quarter = parts.shape[1:]
    chunk = h_send.shape[2]

    @pl.when(i == 0)
    def _():
        for name in names:
            pl.semaphore_signal(barrier, inc=1, device_id=who[name], device_id_type=MESH)

    z = nn(normed[...], rows_z[...])
    pz[...] = z
    g = nn(parts[0], rows_out[0:quarter, :])
    for k in range(1, 4):
        g = g + nn(parts[k], rows_out[k * quarter : (k + 1) * quarter, :])
    ggn[...] = g
    for k in range(4):
        grad_t[k * quarter : (k + 1) * quarter, :] = jnp.transpose(parts[k])
    gated = y[...] * (z * sigmoid(z))
    ones = jnp.ones((8, gated.shape[1]), BF)
    for k, value in enumerate((gated * gated, gated * gain[...] * g)):
        row = nt(ones, value.astype(BF))
        for j in range(span // chunk):
            h_send[k, pl.ds(i * (span // chunk) + j, 1), :] = row[0:1, j * chunk : (j + 1) * chunk]

    @pl.when(i == pl.num_programs(0) - 1)
    def _():
        pl.semaphore_wait(barrier, 3)
        copies = [push(h_send, h_recv.at[k], s_h.at[k], r_h.at[k], who[name]) for k, name in enumerate(names)]
        for copy in copies:
            copy.start()
        for copy in copies:
            copy.wait()
        sums[...] = h_send[...] + h_recv[0] + h_recv[1] + h_recv[2]


def gate(dp_n, blocks, normed, rows_z, rows_out, parts, y, gain):
    count, width = normed.shape
    inner = y.shape[1]
    chunk = count // blocks
    steps = 8
    span = count // steps
    quarter = width // 4
    sds = jax.ShapeDtypeStruct
    rows = lambda w: pl.BlockSpec((span, w), lambda i: (i, 0))
    whole = lambda a: pl.BlockSpec(a.shape, lambda i: (0, 0))
    return pl.pallas_call(
        functools.partial(gate_kernel, dp_n),
        grid=(steps,),
        in_specs=[
            rows(width), whole(rows_z), whole(rows_out),
            pl.BlockSpec((4, span, quarter), lambda i: (0, i, 0)), rows(inner), whole(gain),
        ],
        out_specs=[
            rows(inner), rows(inner), pl.BlockSpec((width, span), lambda i: (0, i)),
            pl.BlockSpec((2, blocks, chunk), lambda i: (0, 0, 0)),
        ],
        out_shape=[
            sds((count, inner), F32), sds((count, inner), F32), sds((width, count), BF), sds((2, blocks, chunk), F32),
        ],
        scratch_shapes=[
            pltpu.VMEM((2, blocks, chunk), F32), pltpu.VMEM((3, 2, blocks, chunk), F32),
            pltpu.SemaphoreType.DMA((3,)), pltpu.SemaphoreType.DMA((3,)),
        ],
        compiler_params=pltpu.CompilerParams(
            collective_id=4, has_side_effects=True, vmem_limit_bytes=48 * 2**20
        ),
        name="gate",
    )(normed, rows_z, rows_out, parts, y, gain)


def scan_bwd_kernel(
    heads, total_inner, starts, fill, ggn, y, pz, px, px_halo, pbd, pbd_halo, sin, rows, gain, convx, convbc,
    bias, rate, skip, upper, spread, gather, ones_h,
    lpx, lpz, lpbd, gn, acc_x, acc_bc, acc_s, dstate, extx, extb, dux, dub,
):
    i = pl.program_id(0)
    blocks = pl.num_programs(0)
    c = blocks - 1 - i
    chunk, inner = px.shape
    bc = convbc.shape[1]
    ns = bc // 2
    taps_n = convx.shape[0]
    keep = starts[c] == 0
    nxt = jnp.minimum(c + 1, blocks - 1)
    keep_next = jnp.logical_and(starts[nxt] == 0, i > 0)
    n_live = fill[c]

    @pl.when(i == 0)
    def _():
        for ref in (dstate, dux, dub, acc_x, acc_bc, acc_s):
            ref[...] = jnp.zeros_like(ref)

    moved = jnp.transpose(
        jnp.concatenate(
            [rows[0, pl.ds(c, 1), :], rows[1, pl.ds(c, 1), :], jnp.zeros((chunk - 2, chunk), F32)], axis=0
        )
    )
    inv = lax.rsqrt(moved[:, 0:1] / total_inner + EPS)
    coef = inv * inv * inv * (moved[:, 1:2] / total_inner)
    z = pz[...]
    sz = sigmoid(z)
    silu_z = z * sz
    yv = y[...]
    gated = yv * silu_z
    g = ggn[...]
    d_gated = inv * (g * gain[...]) - gated * coef
    lpz[...] = (d_gated * yv * (sz * (1.0 + z * (1.0 - sz)))).astype(BF)
    dy = d_gated * silu_z
    gn[...] = (gated * inv * gain[...]).astype(BF)
    acc_x[taps_n : taps_n + 1, :] += jnp.sum(g * gated * inv, axis=0, keepdims=True)

    extx[0:8, :] = jnp.where(keep, px_halo[...], 0.0)
    extb[0:8, :] = jnp.where(keep, pbd_halo[:, :bc], 0.0)
    extx[8 : chunk + 8, :] = px[...]
    extb[8 : chunk + 8, :] = pbd[:, :bc]
    taps = convx[...]
    taps_b = convbc[...]
    live_x = (iota2(chunk, inner, 0) < n_live).astype(F32)
    live_b = (iota2(chunk, bc, 0) < n_live).astype(F32)
    u = conv_from(extx, taps, chunk, 8)
    su = sigmoid(u)
    x = u * su * live_x
    dx_du = su * (1.0 + u * (1.0 - su)) * live_x
    ub = conv_from(extb, taps_b, chunk, 8)
    sb = sigmoid(ub)
    act = (ub * sb * live_b).astype(BF)
    db_du = sb * (1.0 + ub * (1.0 - sb)) * live_b
    b, cc = act[:, :ns], act[:, ns:]

    pre, live, dt, run = dt_rows(pbd[:, bc:], bias[...], rate[...], n_live, heads, upper[...])
    cols, wide = spread_all(run, dt, heads, chunk, spread[...])
    dt_w, ein_w, eout_w = wide[:, :inner], wide[:, inner : 2 * inner], wide[:, 2 * inner :]
    xd = x * dt_w
    xdb = xd.astype(BF)
    dyb = dy.astype(BF)
    acc_x[taps_n + 1 : taps_n + 2, :] += jnp.sum(dy * x, axis=0, keepdims=True)

    scores_t = nt(b, cc)
    tri = iota2(chunk, chunk, 0) <= iota2(chunk, chunk, 1)
    low_lanes = iota2(chunk, 2 * HD, 1) < HD
    d_scores_t = jnp.zeros((chunk, chunk), F32)
    dxd = []
    pulls = []
    read_sums = []
    for j in range(heads // 2):
        span = slice(2 * HD * j, 2 * HD * (j + 1))
        dy_pair = pair_stack(dyb[:, span], low_lanes)
        x_pair = pair_stack(xdb[:, span], low_lanes)
        d_mix = nt(x_pair, dyb[:, span])
        mix = []
        for k in (0, 1):
            h = 2 * j + k
            spread_h = run[h : h + 1, :] - cols[:, h : h + 1]
            fade = jnp.exp(jnp.where(tri, spread_h, NEG))
            m = scores_t * fade
            dm = d_mix[k * chunk : (k + 1) * chunk]
            d_scores_t = d_scores_t + dm * fade
            pull = (dm * m).astype(BF)
            pulls.append(pull)
            read_sums.append(jnp.sum(pull.astype(F32), axis=0, keepdims=True))
            mix.append(m.astype(BF))
        dxd.append(nn(jnp.concatenate(mix, axis=1), dy_pair))
    source_sums = nn(jnp.concatenate(pulls, axis=1), ones_h[...])
    read_rows = jnp.concatenate(read_sums, axis=0)

    d_state = jnp.where(keep_next, dstate[...], 0.0)
    d_state_b = d_state.astype(BF)
    enter_b = sin[0]
    edy = ein_w * dy
    edyb = edy.astype(BF)
    readings = nn(cc, enter_b)
    from_state = nn(b, d_state_b) * eout_w
    d_xd = jnp.concatenate(dxd, axis=1) + from_state
    q1 = edy * readings
    q2 = xd * from_state
    decay = ein_w[chunk - 1 : chunk, :]
    dstate[...] = decay * d_state + tn(cc, edyb)
    d_cb = tn(d_scores_t.astype(BF), b) + nt(edyb, enter_b)
    d_b = nn(d_scores_t.astype(BF), cc) + nt((xd * eout_w).astype(BF), d_state_b)

    sums = (
        nn((d_xd * x).astype(BF), gather[0])
        + nn((q1 - q2).astype(BF), gather[1])
        + nn(q2.astype(BF), gather[2])
        - source_sums
    )
    sums_t = jnp.transpose(sums)
    dt_direct = sums_t[:heads]
    d_run = sums_t[heads : 2 * heads] + read_rows
    whole_q2 = jnp.sum(sums_t[2 * heads : 3 * heads], axis=1, keepdims=True)
    kept = jnp.sum(enter_b.astype(F32) * d_state, axis=0, keepdims=True) * decay
    kept_hi, kept_lo = split2(kept)
    kept_two = jnp.concatenate([kept_hi, kept_lo, jnp.zeros((6, inner), F32)], axis=0).astype(BF)
    kept_cols = nt(gather[3][:, :inner], kept_two)
    d_last = whole_q2 + kept_cols[:heads, 0:1] + kept_cols[:heads, 1:2]
    hi, mid, low = split3(d_run)
    back = nt(jnp.concatenate([hi, mid, low], axis=0).astype(BF), upper[...])
    d_a = back[:heads] + back[heads : 2 * heads] + back[2 * heads :] + d_last
    d_dt = dt_direct + d_a * rate[...]
    d_pre = d_dt * live * sigmoid(pre)
    acc_s[0:heads, :] += d_pre
    acc_s[heads : 2 * heads, :] += d_a * dt * rate[...]

    def conv_back(d_u, du_ref, ext_ref, tap_values, acc):
        du_ref[chunk : chunk + 8, :] = jnp.where(keep_next, du_ref[0:8, :], 0.0)
        du_ref[0:chunk, :] = d_u
        out = tap_values[taps_n - 1 : taps_n, :] * d_u
        acc[taps_n - 1 : taps_n, :] += jnp.sum(d_u * ext_ref[8 : chunk + 8, :], axis=0, keepdims=True)
        for k in range(1, taps_n):
            row = taps_n - 1 - k
            out = out + tap_values[row : row + 1, :] * du_ref[pl.ds(k, chunk), :]
            acc[row : row + 1, :] += jnp.sum(
                d_u * ext_ref[pl.ds(8 - k, chunk), :], axis=0, keepdims=True
            )
        return out

    d_x = d_xd * dt_w + skip[...] * dy
    lpx[...] = conv_back(d_x * dx_du, dux, extx, taps, acc_x).astype(BF)
    d_act = jnp.concatenate([d_b, d_cb], axis=1)
    lpbd[:, :bc] = conv_back(d_act * db_du, dub, extb, taps_b, acc_bc).astype(BF)
    pad = jnp.concatenate([d_pre, jnp.zeros((chunk - heads, chunk), F32)], axis=0)
    lpbd[:, bc:] = jnp.transpose(pad).astype(BF)


def scan_backward(
    ggn, y, pz, px, pbd, sin, rows, gain, conv_x, conv_bc, dt_bias, a_log, skip, starts, fill, total_inner
):
    tokens, inner = px.shape
    blocks = starts.shape[0]
    chunk = tokens // blocks
    heads = inner // HD
    bc = conv_bc.shape[1]
    upper, spread, gather = scan_constants(chunk, heads)
    selector = np.zeros((1, inner, chunk), np.float32)
    lanes = np.zeros((chunk, inner), np.float32)
    for h in range(heads):
        lanes[h, h * HD : (h + 1) * HD] = 1.0
    ones_h = np.zeros((heads * chunk, chunk), np.float32)
    for h in range(heads):
        ones_h[h * chunk : (h + 1) * chunk, heads + h] = 1.0
    ones_h = jnp.asarray(ones_h, BF)
    lanes = jnp.asarray(lanes, BF)
    bias = jnp.broadcast_to(dt_bias[:, None], (heads, chunk))
    rate = jnp.broadcast_to(-jnp.exp(a_log)[:, None], (heads, chunk))
    skip_w = jnp.repeat(skip, HD)[None, :]
    whole = lambda a: pl.BlockSpec(a.shape, lambda i, *_: (0,) * a.ndim)
    back = lambda w: pl.BlockSpec((chunk, w), lambda i, *_: (blocks - 1 - i, 0))
    halo = lambda w: pl.BlockSpec(
        (8, w), lambda i, *_: (jnp.maximum((blocks - 1 - i) * (chunk // 8) - 1, 0), 0)
    )
    width = pbd.shape[1]
    consts = (gain[None, :], conv_x, conv_bc, bias, rate, skip_w, upper, spread, gather, lanes, ones_h)

    def kernel(*refs):
        n_in = 2 + 9
        ins, cons, rest = refs[:n_in], refs[n_in : n_in + 11], refs[n_in + 11 :]
        gain_r, cx, cb, bias_r, rate_r, skip_r, up, sp, ga, la, on = cons

        class Gather:
            def __getitem__(self, k):
                return la[...] if k == 3 else ga[k]

        scan_bwd_kernel(
            heads, total_inner, *ins, gain_r, cx, cb, bias_r, rate_r, skip_r, up, sp, Gather(), on, *rest
        )

    return pl.pallas_call(
        kernel,
        grid_spec=pltpu.PrefetchScalarGridSpec(
            num_scalar_prefetch=2,
            grid=(blocks,),
            in_specs=[
                back(inner), back(inner), back(inner), back(inner), halo(inner), back(width), halo(width),
                pl.BlockSpec((1, bc // 2, inner), lambda i, *_: (blocks - 1 - i, 0, 0)),
                pl.BlockSpec(rows.shape, lambda i, *_: (0, 0, 0)),
            ]
            + [whole(a) for a in consts],
            out_specs=[
                back(inner), back(inner), back(width), back(inner),
                pl.BlockSpec((8, inner), lambda i, *_: (0, 0)),
                pl.BlockSpec((8, bc), lambda i, *_: (0, 0)),
                pl.BlockSpec((2 * heads, chunk), lambda i, *_: (0, 0)),
            ],
            scratch_shapes=[
                pltpu.VMEM((bc // 2, inner), F32),
                pltpu.VMEM((chunk + 8, inner), F32),
                pltpu.VMEM((chunk + 8, bc), F32),
                pltpu.VMEM((chunk + 8, inner), F32),
                pltpu.VMEM((chunk + 8, bc), F32),
            ],
        ),
        out_shape=[
            jax.ShapeDtypeStruct((tokens, inner), BF),
            jax.ShapeDtypeStruct((tokens, inner), BF),
            jax.ShapeDtypeStruct((tokens, width), BF),
            jax.ShapeDtypeStruct((tokens, inner), BF),
            jax.ShapeDtypeStruct((8, inner), F32),
            jax.ShapeDtypeStruct((8, bc), F32),
            jax.ShapeDtypeStruct((2 * heads, chunk), F32),
        ],
        compiler_params=pltpu.CompilerParams(vmem_limit_bytes=48 * 2**20),
        name="scan_backward",
    )(starts, fill, ggn, y, pz, px, px, pbd, pbd, sin, rows, *consts)
def peers(dp_n):
    dp, hm = lax.axis_index("dp"), lax.axis_index("heads")
    across, core = hm // 2, hm % 2
    pair, line, lines = dp % 2, dp // 2, dp_n // 2
    return dict(
        sib=(dp, 2 * across + 1 - core),
        xn=(dp, 2 * (1 - across) + core),
        dg=(dp, 2 * (1 - across) + 1 - core),
        yn=(2 * line + 1 - pair, hm),
        line=lambda k: (2 * ((line + k) % lines) + pair, hm),
        mine=hm,
        other=2 * (1 - across) + core,
        sib_mine=2 * across + 1 - core,
        sib_other=2 * (1 - across) + 1 - core,
        pair=pair, line_index=line, lines=lines, dp=dp, core=core,
    )


def meet(who):
    barrier = pltpu.get_barrier_semaphore()
    for name in ("sib", "xn", "dg", "yn"):
        pl.semaphore_signal(barrier, inc=1, device_id=who[name], device_id_type=MESH)

    def greet(k, carry):
        pl.semaphore_signal(barrier, inc=1, device_id=who["line"](k), device_id_type=MESH)
        return carry

    lax.fori_loop(1, who["lines"], greet, 0)
    pl.semaphore_wait(barrier, 4 + who["lines"] - 1)


def push(src, dst, send, recv, to):
    return pltpu.make_async_remote_copy(
        src_ref=src, dst_ref=dst, send_sem=send, recv_sem=recv, device_id=to, device_id_type=MESH
    )


def tail_kernel(
    dp_n, units,
    grad_t_in, gn_in, rows_out_in, normed_t_in, lpz_in, rows_z_in, lpx_in, rows_x_in, lpbd_in, rows_bd_in, normed_in,
    tokens, acc_x, acc_bc, acc_s, cot, q_wide, gain,
    block_out, grad_tokens, g_x, g_z, g_out, g_bc, small_out,
    sib_send, sib_recv, x_send, x_recv, part, held,
    y_send, y_recv, z_send, z_recv, g_own, yb_send, yb_recv, zb_send, zb_recv, gb_own, bh_send, bh_recv,
    bx_send, bx_recv, bs_recv, h_send, h_recv, sy_send, sy_recv, sz_send, sz_recv, dy_send, dy_recv, dz_send, dz_recv, row_sums,
    grad_t, gn, rows_out, normed_t, lpz, rows_z, lpx, rows_x, lpbd, rows_bd, normed,
    s_in, s_sib, r_sib, s_x, r_x, s_y, r_y, s_z, r_z, s_m, r_m, s_sl, r_sl,
):
    loads = [
        pltpu.make_async_copy(src, dst, s_in.at[i])
        for i, (src, dst) in enumerate((
            (grad_t_in, grad_t), (gn_in, gn), (rows_out_in, rows_out), (normed_t_in, normed_t), (lpz_in, lpz),
            (rows_z_in, rows_z), (lpx_in, lpx), (rows_x_in, rows_x), (lpbd_in, lpbd), (rows_bd_in, rows_bd),
            (normed_in, normed),
        ))
    ]
    for load in loads:
        load.start()
    who = peers(dp_n)
    meet(who)
    count = normed.shape[0]
    width = normed.shape[1]
    inner = lpx.shape[1]
    bc = acc_bc.shape[1]
    quarter = width // 4
    span = count // units
    block = width // dp_n
    lines = who["lines"]
    heads = acc_s.shape[0] // 2
    taps_rows = acc_x.shape[0]

    def copy_sib(u):
        return push(sib_send.at[u], sib_recv.at[u], s_sib.at[u], r_sib.at[u], who["sib"])

    def copy_x(u):
        return push(x_send.at[u], x_recv.at[u], s_x.at[u], r_x.at[u], who["xn"])

    def product(u, q):
        cols = pl.ds(pl.multiple_of(q * quarter, quarter), quarter)
        if u < units:
            return nt(gn[u * span : (u + 1) * span, :], rows_out[cols, :])
        at = slice((u - units) * span, (u - units + 1) * span)
        return nt(lpx[at, :], rows_x[cols, :]) + nt(lpz[at, :], rows_z[cols, :]) + nt(lpbd[at, :], rows_bd[cols, :])

    def head_a(u):
        for k, q in enumerate(("sib_mine", "sib_other", "mine", "other")):
            p = product(u, who[q])
            if u >= units:
                at = slice((u - units) * span, (u - units + 1) * span)
                cols = pl.ds(pl.multiple_of(who[q] * quarter, quarter), quarter)
                inner_p = p * normed[at, cols].astype(F32)
                h_send[0:1, cols] += jnp.sum(inner_p, axis=0, keepdims=True)
                first = (u - units) * span
                lanes = slice(first % width, first % width + span)
                h_send[2 + first // width : 3 + first // width, lanes] += nt(
                    jnp.ones((8, quarter), BF), inner_p.astype(BF)
                )[0:1]
            if k < 2:
                sib_send[u, k] = p.astype(BF)
            else:
                part[u % 2, k - 2] = p
        copy_sib(u).start()

    def head_b(u):
        copy_sib(u).wait()
        x_send[u] = (part[u % 2, 1] + sib_recv[u, 1].astype(F32)).astype(BF)
        copy_x(u).start()
        held[u] = part[u % 2, 0] + sib_recv[u, 0].astype(F32)

    def head_c(u):
        copy_x(u).wait()
        total = held[u] + x_recv[u].astype(F32)
        if u < units:
            at = slice(u * span, (u + 1) * span)
            block_out[at, :] = (tokens[at, :].astype(F32) + total).astype(BF)
        else:
            first = (u - units) * span
            lanes = q_wide.shape[1]
            cols = pl.ds(pl.multiple_of(who["mine"] * quarter, quarter), quarter)
            for j in range(span // lanes):
                at = slice(first + j * lanes, first + (j + 1) * lanes)
                row, lane = (first + j * lanes) // width, (first + j * lanes) % width
                dots = jnp.transpose(jnp.broadcast_to(row_sums[row : row + 1, lane : lane + lanes], (lanes, lanes)))
                q = q_wide[at, :]
                coef = q * q * (dots / width)
                grad_tokens[at, :] = (
                    cot[at, :].astype(F32)
                    + q[:, 0:1] * gain[:, cols] * total[j * lanes : (j + 1) * lanes]
                    - tokens[at, :].astype(F32) * coef[:, 0:1]
                )

    def rows_of(line, pair):
        return pl.ds(pl.multiple_of((2 * line + pair) * block, block), block)

    def grad_a(v):
        left, right = ((grad_t, gn), (normed_t, lpz), (normed_t, lpx))[v // 2]
        cols = slice((v % 2) * (inner // 2), (v % 2 + 1) * (inner // 2))
        for side in (0, 1):
            pair = (1 - who["pair"]) if side == 0 else who["pair"]
            stacked = jnp.concatenate([left[rows_of(l, pair), :] for l in range(lines)], axis=0)
            value = nn(stacked, right[:, cols])
            if side == 0:
                y_send[v] = value.astype(BF)
                copy_y(v).start()
            else:
                g_own[v] = value

    def copy_y(v):
        return push(y_send.at[v], y_recv.at[v], s_y.at[v], r_y.at[v], who["yn"])

    def copy_z(v, k):
        to = (who["line_index"] + k) % lines
        return push(
            z_send.at[v, pl.ds(pl.multiple_of(to * block, block), block)],
            z_recv.at[v, k - 1], s_z.at[v, k - 1], r_z.at[v, k - 1], who["line"](k),
        )

    def each_line(fn):
        def step(k, carry):
            fn(k)
            return carry

        lax.fori_loop(1, lines, step, 0)

    def own_rows():
        return pl.ds(pl.multiple_of(who["line_index"] * block, block), block)

    def grad_b(v):
        copy_y(v).wait()
        g_own[v] = g_own[v] + y_recv[v].astype(F32)
        z_send[v] = g_own[v].astype(BF)
        each_line(lambda k: copy_z(v, k).start())

    def grad_c(v):
        each_line(lambda k: copy_z(v, k).wait())
        total = g_own[v, own_rows(), :]
        for k in range(lines - 1):
            total = total + z_recv[v, k].astype(F32)
        cols = slice((v % 2) * (inner // 2), (v % 2 + 1) * (inner // 2))
        (g_out, g_z, g_x)[v // 2][:, cols] = total

    half = bc // 2

    def copy_bh():
        return push(bh_send, bh_recv, s_m.at[0], r_m.at[0], who["sib"])

    def copy_yb():
        return push(yb_send, yb_recv, s_m.at[1], r_m.at[1], who["yn"])

    def copy_zb(k):
        to = (who["line_index"] + k) % lines
        return push(
            zb_send.at[pl.ds(pl.multiple_of(to * block, block), block)],
            zb_recv.at[k - 1], s_sl.at[0, k - 1], r_sl.at[0, k - 1], who["line"](k),
        )

    def copy_bx():
        return push(bx_send, bx_recv, s_m.at[2], r_m.at[2], who["xn"])

    def copy_bs():
        return push(bx_send, bs_recv, s_m.at[3], r_m.at[3], who["sib"])

    def bc_a():
        for side in (0, 1):
            pair = (1 - who["pair"]) if side == 0 else who["pair"]
            stacked = jnp.concatenate([normed_t[rows_of(l, pair), :] for l in range(lines)], axis=0)
            value = nn(stacked, lpbd[:, :bc])
            first = who["core"] == 0
            lo, hi = value[:, :half], value[:, half:]
            at = slice(side * lines * block, (side + 1) * lines * block)
            bh_send[at, :] = jnp.where(first, hi, lo).astype(BF)
            gb_own[at, :] = jnp.where(first, lo, hi)
        copy_bh().start()

    def bc_b():
        copy_bh().wait()
        rows = lines * block
        gb_own[...] = gb_own[...] + bh_recv[...].astype(F32)
        yb_send[...] = gb_own[:rows, :].astype(BF)
        copy_yb().start()

    def bc_c():
        rows = lines * block
        copy_yb().wait()
        gb_own[rows:, :] = gb_own[rows:, :] + yb_recv[...].astype(F32)
        zb_send[...] = gb_own[rows:, :].astype(BF)
        each_line(lambda k: copy_zb(k).start())

    def bc_d():
        each_line(lambda k: copy_zb(k).wait())
        at = pl.ds(pl.multiple_of(lines * block + who["line_index"] * block, block), block)
        total = gb_own[at, :]
        for k in range(lines - 1):
            total = total + zb_recv[k].astype(F32)
        bx_send[...] = total
        copy_bx().start()

    def bc_e():
        copy_bx().wait()
        bx_send[...] = bx_send[...] + bx_recv[...]
        copy_bs().start()

    def bc_f():
        copy_bs().wait()
        mine, theirs = bx_send[...], bs_recv[...]
        first = who["core"] == 0
        g_bc[:, :half] = jnp.where(first, mine, theirs)
        g_bc[:, half:] = jnp.where(first, theirs, mine)

    three = (("sib", 4), ("xn", 5), ("dg", 6))
    taps = width // bc
    token_rows = count // width

    def copy_h(k):
        name, sem = three[k]
        return push(h_send, h_recv.at[k], s_m.at[sem], r_m.at[sem], who[name])

    def small_a():
        for k in range(taps):
            h_send[1:2, k * bc : (k + 1) * bc] = acc_bc[k : k + 1, :]
        for k in range(3):
            copy_h(k).start()

    def copy_sy():
        return push(sy_send, sy_recv, s_m.at[7], r_m.at[7], who["yn"])

    def copy_dy():
        return push(dy_send, dy_recv, s_m.at[8], r_m.at[8], who["yn"])

    def copy_sz(k):
        return push(sz_send, sz_recv.at[k - 1], s_sl.at[1, k - 1], r_sl.at[1, k - 1], who["line"](k))

    def copy_dz(k):
        return push(dz_send, dz_recv.at[k - 1], s_sl.at[2, k - 1], r_sl.at[2, k - 1], who["line"](k))

    def dt_a():
        dy_send[...] = tn(lpbd[:, bc:], normed[...])[0:16, :].astype(BF)
        copy_dy().start()

    def dt_b():
        copy_dy().wait()
        dz_send[...] = (dy_send[...].astype(F32) + dy_recv[...].astype(F32)).astype(BF)
        each_line(lambda k: copy_dz(k).start())

    def dt_c():
        each_line(lambda k: copy_dz(k).wait())
        total = dz_send[...].astype(F32)
        for k in range(lines - 1):
            total = total + dz_recv[k].astype(F32)
        small_out[8:24, :] = total

    def small_b():
        for k in range(3):
            copy_h(k).wait()
        over_heads = h_send[...] + h_recv[0] + h_recv[1] + h_recv[2]
        row_sums[0:token_rows, :] = over_heads[2 : 2 + token_rows, :]
        sy_send[...] = jnp.zeros_like(sy_send)
        sy_send[0:2, :] = over_heads[0:2, :]
        per = width // inner
        for k in range(taps + 2):
            sy_send[2 + k // per : 3 + k // per, (k % per) * inner : (k % per + 1) * inner] = acc_x[k : k + 1, :]
        lanes = acc_s.shape[1]
        at = 2 + -(-(taps + 2) // per)
        fit = width // lanes
        for k in range(2 * heads):
            sy_send[at + k // fit : at + k // fit + 1, (k % fit) * lanes : (k % fit + 1) * lanes] = acc_s[k : k + 1, :]
        copy_sy().start()

    def small_c():
        copy_sy().wait()
        sz_send[...] = sy_send[...] + sy_recv[...]
        each_line(lambda k: copy_sz(k).start())

    def small_d():
        each_line(lambda k: copy_sz(k).wait())
        total = sz_send[...]
        for k in range(lines - 1):
            total = total + sz_recv[k]
        small_out[0:8, :] = total

    h_send[...] = jnp.zeros_like(h_send)

    def seq(*steps):
        for fn, *args in steps:
            fn(*args)

    assert units == 4

    def load(*which):
        for i in which:
            loads[i].wait()

    load(0, 1)
    seq((grad_a, 0), (grad_a, 1))
    load(2)
    seq((head_a, 0), (head_a, 1), (head_b, 0), (head_a, 2), (head_b, 1), (head_a, 3), (head_b, 2))
    load(3, 8)
    seq((bc_a,), (head_b, 3))
    load(4)
    seq((grad_a, 2), (bc_b,), (grad_a, 3))
    load(5, 6, 7, 9, 10)
    seq((grad_b, 0), (head_a, 4), (dt_a,), (grad_b, 1), (grad_a, 4), (head_b, 4), (head_a, 5), (bc_c,), (head_b, 5))
    seq((grad_a, 5), (head_a, 6), (grad_b, 2), (head_b, 6), (head_a, 7), (small_a,), (grad_b, 3), (head_b, 7))
    seq((dt_b,), (small_b,), (head_c, 0), (head_c, 1), (head_c, 2), (head_c, 3), (bc_d,), (grad_c, 0), (grad_c, 1))
    seq((grad_b, 4), (small_c,), (grad_b, 5), (dt_c,), (bc_e,), (head_c, 4), (head_c, 5), (grad_c, 2), (grad_c, 3))
    seq((small_d,), (head_c, 6), (grad_c, 4), (bc_f,), (head_c, 7), (grad_c, 5))


def tail(dp_n, units, normed_t, normed, grad_t, gn, lpx, lpz, lpbd, rows_x, rows_z, rows_bd, rows_out, tokens, acc_x, acc_bc, acc_s, cot, q_wide, gain):
    count, width = normed.shape
    inner = lpx.shape[1]
    bc = acc_bc.shape[1]
    quarter = width // 4
    span = count // units
    block = width // dp_n
    lines = dp_n // 2
    half_rows = lines * block
    more = max(lines - 1, 1)
    vm = pltpu.VMEM
    dma = pltpu.SemaphoreType.DMA
    operands = (
        grad_t, gn, rows_out, normed_t, lpz, rows_z, lpx, rows_x, lpbd, rows_bd, normed, tokens, acc_x, acc_bc, acc_s,
        cot, q_wide, gain,
    )
    sds = jax.ShapeDtypeStruct
    spec = pl.BlockSpec(memory_space=pltpu.VMEM)
    return pl.pallas_call(
        functools.partial(tail_kernel, dp_n, units),
        out_shape=[
            sds((count, quarter), BF), sds((count, quarter), F32),
            sds((block, inner), F32), sds((block, inner), F32), sds((block, inner), F32), sds((block, bc), F32),
            sds((24, width), F32),
        ],
        in_specs=[pl.BlockSpec(memory_space=pl.ANY)] * 11 + [spec] * 7,
        out_specs=[spec] * 7,
        scratch_shapes=[
            vm((2 * units, 2, span, quarter), BF), vm((2 * units, 2, span, quarter), BF),
            vm((2 * units, span, quarter), BF), vm((2 * units, span, quarter), BF),
            vm((2, 2, span, quarter), F32), vm((2 * units, span, quarter), F32),
            vm((6, half_rows, inner // 2), BF), vm((6, half_rows, inner // 2), BF),
            vm((6, half_rows, inner // 2), BF), vm((6, more, block, inner // 2), BF),
            vm((6, half_rows, inner // 2), F32),
            vm((half_rows, bc // 2), BF), vm((half_rows, bc // 2), BF),
            vm((half_rows, bc // 2), BF), vm((more, block, bc // 2), BF),
            vm((2 * half_rows, bc // 2), F32),
            vm((2 * half_rows, bc // 2), BF), vm((2 * half_rows, bc // 2), BF),
            vm((block, bc // 2), F32), vm((block, bc // 2), F32), vm((block, bc // 2), F32),
            vm((8, width), F32), vm((3, 8, width), F32),
            vm((8, width), F32), vm((8, width), F32), vm((8, width), F32), vm((more, 8, width), F32),
            vm((16, width), BF), vm((16, width), BF), vm((16, width), BF), vm((more, 16, width), BF),
            vm((8, width), F32),
        ]
        + [vm(a.shape, a.dtype) for a in operands[:11]]
        + [
            dma((11,)), dma((2 * units,)), dma((2 * units,)), dma((2 * units,)), dma((2 * units,)),
            dma((6,)), dma((6,)), dma((6, more)), dma((6, more)), dma((9,)), dma((9,)),
            dma((3, more)), dma((3, more)),
        ],
        compiler_params=pltpu.CompilerParams(
            collective_id=1, has_side_effects=True, vmem_limit_bytes=62 * 2**20
        ),
        name="tail",
    )(*operands)
def shares(ref_in, block_of, dp_n, width, send, recv, who):
    rows = ref_in.shape[0]
    lines = who["lines"]

    def at(dp):
        return block_of.at[pl.ds(pl.multiple_of(dp * rows, rows), rows), width]

    def own():
        return push(ref_in.at[:, width], at(who["dp"]), send.at[0], recv.at[0], who["yn"])

    def along(k):
        return push(ref_in.at[:, width], at(who["dp"]), send.at[k], recv.at[k], who["line"](k))

    def onward(k):
        source = at(2 * ((who["line_index"] - k + lines) % lines) + who["pair"])
        return push(source, source, send.at[lines - 1 + k], recv.at[lines - 1 + k], who["yn"])

    return own, along, onward


def loop_line(lines, fn):
    def step(k, carry):
        fn(k)
        return carry

    lax.fori_loop(1, lines, step, 0)


def front_kernel(
    dp_n, units,
    tokens, w_bd, w_x, gain,
    px_out, pbd_out, normed_out, normed_t_out, q_out, rows_x, rows_bd,
    tok, wx, wbd, px, pbd, normed, normed_t, q,
    s_loc, s_sib, r_sib, s_x, r_x, s_f, r_f, s_b, r_b, s_w, r_w, s_out,
):
    who = peers(dp_n)
    count, quarter = tokens.shape
    width = 4 * quarter
    span = count // units
    lines = who["lines"]
    block = w_x.shape[0]
    here = pl.ds(pl.multiple_of(who["dp"] * block, block), block)
    local = [
        pltpu.make_async_copy(tokens, tok.at[who["mine"]], s_loc.at[0]),
        pltpu.make_async_copy(w_bd, wbd.at[here], s_loc.at[1]),
        pltpu.make_async_copy(w_x, wx.at[here], s_loc.at[2]),
    ]
    for copy in local:
        copy.start()
    meet(who)

    def rows(s):
        return pl.ds(s * span, span)

    def to_x(s):
        return push(tokens.at[rows(s)], tok.at[who["mine"], rows(s)], s_x.at[s], r_x.at[s], who["xn"])

    def to_sib():
        return push(tokens, tok.at[who["mine"]], s_sib.at[0], r_sib.at[0], who["sib"])

    def forward(s):
        here = tok.at[who["other"], rows(s)]
        return push(here, here, s_f.at[s], r_f.at[s], who["sib"])

    every = slice(None)
    bd_own, bd_along, bd_onward = shares(w_bd, wbd, dp_n, every, s_b, r_b, who)
    x_own, x_along, x_onward = shares(w_x, wx, dp_n, every, s_w, r_w, who)
    to_x(0).start()
    loop_line(lines, lambda k: bd_along(k).start())
    bd_own().start()
    for s in range(1, units):
        to_x(s).start()
    to_sib().start()
    loop_line(lines, lambda k: x_along(k).start())
    x_own().start()

    def pass_on(along, onward, k):
        along(k).wait()
        onward(k).start()

    def norm(s):
        at = slice(s * span, (s + 1) * span)
        parts = [tok[h, at, :].astype(F32) for h in range(4)]
        total = sum(jnp.sum(p * p, axis=1, keepdims=True) for p in parts)
        inv = lax.rsqrt(total / width + EPS)
        q[at, :] = jnp.broadcast_to(inv, (span, q.shape[1]))
        for h in range(4):
            cols = slice(h * quarter, (h + 1) * quarter)
            value = (parts[h] * inv * gain[:, cols]).astype(BF)
            normed[at, cols] = value
            normed_t[cols, at] = jnp.transpose(value)

    def outward(ref, out, i, at):
        return pltpu.make_async_copy(ref.at[at], out.at[at], s_out.at[i])

    def send_norm(s):
        at = (slice(s * span, (s + 1) * span),)
        copies = [
            outward(normed, normed_out, 3 * s, at),
            outward(normed_t, normed_t_out, 3 * s + 1, (slice(None),) + at),
            outward(q, q_out, 3 * s + 2, at),
        ]
        return copies

    def project(s):
        at = slice(s * span, (s + 1) * span)
        pbd[at, :] = nn(normed[at, :], wbd[...])
        px[at, :] = nn(normed[at, :], wx[...])

    def send_proj(s):
        at = (slice(s * span, (s + 1) * span),)
        base = 3 * units + 2 * s
        return [outward(px, px_out, base, at), outward(pbd, pbd_out, base + 1, at)]

    outs = []

    def go(copies):
        for copy in copies:
            copy.start()
        outs.extend(copies)

    local[0].wait()
    to_x(0).wait()
    forward(0).start()
    loop_line(lines, lambda k: pass_on(bd_along, bd_onward, k))
    to_sib().wait()
    for s in range(units):
        forward(s).wait()
        norm(s)
        go(send_norm(s))
        if s + 1 < units:
            to_x(s + 1).wait()
            forward(s + 1).start()
        if s == 1:
            bd_own().wait()
            loop_line(lines, lambda k: bd_onward(k).wait())
            local[1].wait()
            copy = pltpu.make_async_copy(wbd, rows_bd, s_out.at[5 * units])
            go([copy])
        if s == units - 2:
            loop_line(lines, lambda k: pass_on(x_along, x_onward, k))
    x_own().wait()
    loop_line(lines, lambda k: x_onward(k).wait())
    local[2].wait()
    go([pltpu.make_async_copy(wx, rows_x, s_out.at[5 * units + 1])])
    for s in range(units):
        project(s)
        go(send_proj(s))
    for copy in outs:
        copy.wait()


def front(dp_n, units, tokens, w_bd, w_x, gain):
    count, quarter = tokens.shape
    width = 4 * quarter
    inner, wide = w_x.shape[1], w_bd.shape[1]
    vm, dma, sds = pltpu.VMEM, pltpu.SemaphoreType.DMA, jax.ShapeDtypeStruct
    hbm = pl.BlockSpec(memory_space=pl.ANY)
    lines = dp_n // 2
    ways = 2 * lines - 1
    outs = [
        sds((count, inner), F32), sds((count, wide), F32), sds((count, width), BF), sds((width, count), BF),
        sds((count, 128), F32), sds((width, inner), BF), sds((width, wide), BF),
    ]
    return pl.pallas_call(
        functools.partial(front_kernel, dp_n, units),
        out_shape=outs,
        in_specs=[hbm] * 3 + [pl.BlockSpec(memory_space=pltpu.VMEM)],
        out_specs=[hbm] * 7,
        scratch_shapes=[
            vm((4, count, quarter), BF), vm((width, inner), BF), vm((width, wide), BF),
            vm((count, inner), F32), vm((count, wide), F32), vm((count, width), BF), vm((width, count), BF),
            vm((count, 128), F32),
            dma((3,)), dma((1,)), dma((1,)), dma((units,)), dma((units,)), dma((units,)), dma((units,)),
            dma((ways,)), dma((ways,)), dma((ways,)), dma((ways,)), dma((5 * units + 2,)),
        ],
        compiler_params=pltpu.CompilerParams(
            collective_id=2, has_side_effects=True, vmem_limit_bytes=58 * 2**20
        ),
        name="front",
    )(tokens, w_bd, w_x, gain)


def body(
    tokens, cotangent, starts, fill, norm_gain, w_x, w_z, w_dt, w_bc, conv_x, conv_bc, dt_bias, a_log, skip,
    gate_gain, w_out,
):
    heads_n = lax.axis_size("heads")
    dp_n = lax.axis_size("dp")
    head_index = lax.axis_index("heads")
    dp_index = lax.axis_index("dp")
    count, columns = tokens.shape
    width = columns * heads_n
    blocks = starts.shape[0]
    chunk = count // blocks
    inner = w_x.shape[1]
    heads = w_dt.shape[1]
    bc = w_bc.shape[1]
    total_inner = inner * heads_n
    w_bd = jnp.concatenate([w_bc, jnp.pad(w_dt, ((0, 0), (0, chunk - heads)))], axis=1)
    px, pbd, normed, normed_t, q_wide, rows_x, rows_bd = front(dp_n, 4, tokens, w_bd, w_x, norm_gain[None, :])
    keep = jnp.where(starts == 0, 1.0, 0.0).astype(F32)
    meta = jnp.stack([keep, fill.astype(F32)] + [keep] * 6, axis=1)
    meta = jnp.broadcast_to(meta[:, :, None], (blocks, 8, chunk))
    y, sin, parts, rows_z, rows_out = scan_forward(
        dp_n, px, pbd, conv_x, conv_bc, dt_bias, a_log, skip, meta, cotangent, w_z, w_out
    )
    pz, ggn, grad_t, sums = gate(dp_n, blocks, normed, rows_z, rows_out, parts, y, gate_gain[None, :])
    lpx, lpz, lpbd, gn, acc_x, acc_bc, acc_s = scan_backward(
        ggn, y, pz, px, pbd, sin, sums, gate_gain, conv_x, conv_bc, dt_bias, a_log, skip, starts, fill,
        total_inner,
    )
    block_out, grad_tokens, grad_w_x, grad_w_z, grad_w_out, grad_w_bc, small = tail(
        dp_n, 4, normed_t, normed, grad_t, gn, lpx, lpz, lpbd, rows_x, rows_z, rows_bd, rows_out,
        tokens, acc_x, acc_bc, acc_s, cotangent, q_wide, norm_gain[None, :],
    )
    own_gain = lax.dynamic_slice_in_dim(norm_gain, head_index * columns, columns, 0)
    return (block_out, grad_tokens) + outputs(
        small, dp_index, head_index, own_gain, conv_x, bc, heads, inner, width // dp_n, chunk,
        grad_w_x, grad_w_z, grad_w_bc, grad_w_out,
    )


def outputs(small, dp_index, head_index, own_gain, conv_x, bc, heads, inner, block, chunk, g_x, g_z, g_bc, g_out):
    taps = conv_x.shape[0]
    width = small.shape[1]
    columns = own_gain.shape[0]
    grad_w_dt = lax.dynamic_slice_in_dim(small[8 : 8 + heads], dp_index * block, block, 1).T
    gain_sum = lax.dynamic_slice_in_dim(small[0], head_index * columns, columns, 0)
    per = width // inner
    scans = small[2 : 2 + -(-(taps + 2) // per)].reshape(-1, inner)
    at = 2 + -(-(taps + 2) // per)
    lanes = jnp.sum(small[at:8].reshape(-1, chunk)[: 2 * heads], axis=1)
    return (
        gain_sum / own_gain, g_x, g_z, grad_w_dt, g_bc, scans[:taps], small[1].reshape(taps, bc), lanes[:heads],
        lanes[heads:], jnp.sum(scans[taps + 1].reshape(heads, HD), axis=1), scans[taps], g_out,
    )


def solution(mesh):
    placed = (
        P("dp", "heads"),
        P("dp", "heads"),
        P("dp"),
        P("dp"),
        P(),
        P("dp", "heads"),
        P("dp", "heads"),
        P("dp", "heads"),
        P("dp", None),
        P(None, "heads"),
        P(),
        P("heads"),
        P("heads"),
        P("heads"),
        P("heads"),
        P("dp", "heads"),
    )
    return jax.shard_map(
        body,
        mesh=mesh,
        in_specs=placed,
        out_specs=(
            P("dp", "heads"),
            P("dp", "heads"),
            P("heads"),
            P("dp", "heads"),
            P("dp", "heads"),
            P("dp", "heads"),
            P("dp", None),
            P(None, "heads"),
            P(),
            P("heads"),
            P("heads"),
            P("heads"),
            P("heads"),
            P("dp", "heads"),
        ),
        check_vma=False,
    )
```

```python
import functools
import jax
import jax.numpy as jnp
from jax import lax
from jax.experimental import pallas as pl
from jax.experimental.pallas import tpu as pltpu
from jax.sharding import PartitionSpec as P

HD = 64
EPS = 1e-05
F32 = jnp.float32
BF = jnp.bfloat16
NEG = -1e30
MESH = pl.DeviceIdType.MESH


def nn(a, b):
    return lax.dot_general(a, b, (((1,), (0,)), ((), ())), preferred_element_type=F32)


def nt(a, b):
    return lax.dot_general(a, b, (((1,), (1,)), ((), ())), preferred_element_type=F32)


def tn(a, b):
    return lax.dot_general(a, b, (((0,), (0,)), ((), ())), preferred_element_type=F32)


def split2(v):
    hi = v.astype(BF).astype(F32)
    return hi, v - hi


def split3(v):
    hi = v.astype(BF).astype(F32)
    rest = v - hi
    mid = rest.astype(BF).astype(F32)
    return hi, mid, rest - mid


def softplus(v):
    return jnp.maximum(v, 0.0) + jnp.log1p(jnp.exp(-jnp.abs(v)))


def sigmoid(v):
    return 1.0 / (1.0 + jnp.exp(-v))


def iota2(rows, cols, axis):
    return lax.broadcasted_iota(jnp.int32, (rows, cols), axis)


def zero_one(cond):
    return jnp.where(cond, 1.0, 0.0).astype(BF)


def set_upper(upper):
    upper[...] = zero_one(iota2(*upper.shape, 0) <= iota2(*upper.shape, 1))


def set_spread(spread, heads):
    rows, lanes = iota2(*spread.shape, 0), iota2(*spread.shape, 1)
    inner = heads * HD
    base = heads * (1 + 2 * (lanes // inner)) + (lanes % inner) // HD
    spread[...] = zero_one(jnp.logical_or(rows == base, rows == base + heads))


def set_gather(gather, ones_h, heads):
    for q in range(3):
        rows, lanes = iota2(*gather.shape[1:], 0), iota2(*gather.shape[1:], 1)
        gather[q] = zero_one(lanes == q * heads + rows // HD)
    rows, lanes = iota2(*ones_h.shape, 0), iota2(*ones_h.shape, 1)
    ones_h[...] = zero_one(lanes == heads + rows // ones_h.shape[1])


def conv_from(ext, taps, rows, halo):
    n = taps.shape[0]
    out = taps[n - 1 : n, :] * ext[pl.ds(halo, rows), :]
    for k in range(1, n):
        out = out + taps[n - 1 - k : n - k, :] * ext[pl.ds(halo - k, rows), :]
    return out


def dt_rows(pdt, bias, rate, fill, heads, upper):
    chunk = pdt.shape[0]
    pre = jnp.transpose(pdt)[:heads] + bias
    live = (iota2(heads, chunk, 1).astype(F32) < fill).astype(F32)
    dt = softplus(pre) * live
    hi, mid, low = split3(dt * rate)
    stacked = jnp.concatenate([hi, mid, low], axis=0).astype(BF)
    summed = nn(stacked, upper)
    run = summed[:heads] + summed[heads : 2 * heads] + summed[2 * heads :]
    return pre, live, dt, run


def spread_all(run, dt, heads, chunk, spread):
    last = run[:, chunk - 1 : chunk]
    e_in = jnp.exp(run)
    e_out = jnp.exp(last - run)
    parts = [run]
    for v in (dt, e_in, e_out):
        parts.extend(split2(v))
    used = heads * len(parts)
    if used < chunk:
        parts.append(jnp.zeros((chunk - used, chunk), F32))
    cols = jnp.transpose(jnp.concatenate(parts, axis=0))
    return cols, nn(cols.astype(BF), spread)


def pair_stack(v, low_lanes):
    zero = jnp.zeros_like(v)
    return jnp.concatenate([jnp.where(low_lanes, v, zero), jnp.where(low_lanes, zero, v)], axis=0)


def read_vec(vec, heads, chunk, inner, bc, taps):
    return dict(
        convx=vec[0:taps, :inner], skip=vec[4:5, :inner], gain=vec[5:6, :inner],
        bias=vec[8 : 8 + heads, :chunk], rate=vec[8 : 8 + heads, chunk : 2 * chunk], convbc=vec[16 : 16 + taps, :bc],
    )


def read_block(vec, c, chunk):
    row = vec[pl.ds(24 + c, 1), :]
    return row[:, 0:1] > 0.5, row[:, chunk : chunk + 1], row[:, 2 * chunk : 2 * chunk + 1] > 0.5


def pack_vec(conv_x, skip, gate_gain, norm_gain, dt_bias, a_log, conv_bc, starts, fill, chunk):
    width = norm_gain.shape[0]
    wide = lambda a: jnp.pad(a, ((0, 0), (0, width - a.shape[1])))
    down = lambda a, rows: jnp.pad(a, ((0, rows - a.shape[0]), (0, 0)))
    cols = lambda *vs: jnp.concatenate([jnp.broadcast_to(v[:, None], (v.shape[0], chunk)) for v in vs], axis=1)
    keep = jnp.where(starts == 0, 1.0, 0.0).astype(F32)
    keep_next = jnp.concatenate([keep[1:], jnp.zeros((1,), F32)])
    rows = [
        wide(conv_x), wide(jnp.repeat(skip, HD)[None]), wide(gate_gain[None]), norm_gain[None],
        jnp.zeros((1, width), F32), down(wide(cols(dt_bias, -jnp.exp(a_log))), 8), down(wide(conv_bc), 8),
        wide(cols(keep, fill.astype(F32), keep_next)),
    ]
    return jnp.concatenate(rows, axis=0)


def scan_step(heads, par, block, px, pbd, upper, spread, state, extx, extb):
    chunk, inner = px.shape
    bc = par["convbc"].shape[1]
    ns = bc // 2
    keep, n_live, _ = block
    state[...] = jnp.where(keep, state[...], 0.0)
    extx[0:8, :] = jnp.where(keep, extx[chunk : chunk + 8, :], 0.0)
    extb[0:8, :] = jnp.where(keep, extb[chunk : chunk + 8, :], 0.0)
    extx[8 : chunk + 8, :] = px[...]
    extb[8 : chunk + 8, :] = pbd[:, :bc]

    u = conv_from(extx, par["convx"], chunk, 8)
    x = u * sigmoid(u) * (iota2(chunk, inner, 0).astype(F32) < n_live).astype(F32)
    ub = conv_from(extb, par["convbc"], chunk, 8)
    act = (ub * sigmoid(ub) * (iota2(chunk, bc, 0).astype(F32) < n_live).astype(F32)).astype(BF)
    b, cc = act[:, :ns], act[:, ns:]

    _, _, dt, run = dt_rows(pbd[:, bc:], par["bias"], par["rate"], n_live, heads, upper[...])
    cols, wide = spread_all(run, dt, heads, chunk, spread[...])
    dt_w, ein_w, eout_w = wide[:, :inner], wide[:, inner : 2 * inner], wide[:, 2 * inner :]

    xd = x * dt_w
    xdb = xd.astype(BF)
    scores = nt(cc, b)
    tri = iota2(chunk, chunk, 0) >= iota2(chunk, chunk, 1)
    low_lanes = iota2(chunk, 2 * HD, 1) < HD
    diag = []
    for j in range(heads // 2):
        mix = []
        for h in (2 * j, 2 * j + 1):
            spread_h = cols[:, h : h + 1] - run[h : h + 1, :]
            mix.append((scores * jnp.exp(jnp.where(tri, spread_h, NEG))).astype(BF))
        pair = pair_stack(xdb[:, 2 * HD * j : 2 * HD * (j + 1)], low_lanes)
        diag.append(nn(jnp.concatenate(mix, axis=1), pair))
    enter = state[...]
    enter_b = enter.astype(BF)
    y = jnp.concatenate(diag, axis=1) + ein_w * nn(cc, enter_b) + par["skip"] * x
    state[...] = ein_w[chunk - 1 : chunk, :] * enter + tn(b, (xd * eout_w).astype(BF))
    return y, enter_b


def gate_kernel(
    dp_n, normed, rows_z, rows_out, parts, y, vec, pz, ggn, grad_t, sums, h_send, h_recv, s_h, r_h,
):
    i = pl.program_id(0)
    who = peers(dp_n)
    names = ("sib", "xn", "dg")
    barrier = pltpu.get_barrier_semaphore()
    span, quarter = parts.shape[1:]
    chunk = h_send.shape[2]

    @pl.when(i == 0)
    def _():
        for name in names:
            pl.semaphore_signal(barrier, inc=1, device_id=who[name], device_id_type=MESH)

    z = nn(normed[...], rows_z[...])
    pz[...] = z
    g = nn(parts[0], rows_out[0:quarter, :])
    for k in range(1, 4):
        g = g + nn(parts[k], rows_out[k * quarter : (k + 1) * quarter, :])
    ggn[...] = g
    for k in range(4):
        grad_t[k * quarter : (k + 1) * quarter, :] = jnp.transpose(parts[k])
    gated = y[...] * (z * sigmoid(z))
    ones = jnp.ones((8, gated.shape[1]), BF)
    for k, value in enumerate((gated * gated, gated * vec[5:6, : gated.shape[1]] * g)):
        row = nt(ones, value.astype(BF))
        for j in range(span // chunk):
            h_send[k, pl.ds(i * (span // chunk) + j, 1), :] = row[0:1, j * chunk : (j + 1) * chunk]

    @pl.when(i == pl.num_programs(0) - 1)
    def _():
        pl.semaphore_wait(barrier, 3)
        copies = [push(h_send, h_recv.at[k], s_h.at[k], r_h.at[k], who[name]) for k, name in enumerate(names)]
        for copy in copies:
            copy.start()
        for copy in copies:
            copy.wait()
        sums[...] = h_send[...] + h_recv[0] + h_recv[1] + h_recv[2]


def gate(dp_n, blocks, normed, rows_z, rows_out, parts, y, vec):
    count, width = normed.shape
    inner = y.shape[1]
    chunk = count // blocks
    steps = 8
    span = count // steps
    quarter = width // 4
    sds = jax.ShapeDtypeStruct
    rows = lambda w: pl.BlockSpec((span, w), lambda i: (i, 0))
    whole = lambda a: pl.BlockSpec(a.shape, lambda i: (0, 0))
    return pl.pallas_call(
        functools.partial(gate_kernel, dp_n),
        grid=(steps,),
        in_specs=[
            rows(width), whole(rows_z), whole(rows_out),
            pl.BlockSpec((4, span, quarter), lambda i: (0, i, 0)), rows(inner), whole(vec),
        ],
        out_specs=[
            rows(inner), rows(inner), pl.BlockSpec((width, span), lambda i: (0, i)),
            pl.BlockSpec((2, blocks, chunk), lambda i: (0, 0, 0)),
        ],
        out_shape=[
            sds((count, inner), F32), sds((count, inner), F32), sds((width, count), BF), sds((2, blocks, chunk), F32),
        ],
        scratch_shapes=[
            pltpu.VMEM((2, blocks, chunk), F32), pltpu.VMEM((3, 2, blocks, chunk), F32),
            pltpu.SemaphoreType.DMA((3,)), pltpu.SemaphoreType.DMA((3,)),
        ],
        compiler_params=pltpu.CompilerParams(
            collective_id=4, has_side_effects=True, vmem_limit_bytes=48 * 2**20
        ),
        name="gate",
    )(normed, rows_z, rows_out, parts, y, vec)


def scan_bwd_kernel(
    heads, total_inner, taps_n, bc, ggn, y, pz, px, px_halo, pbd, pbd_halo, sin, rows, vec,
    lpx, lpz, lpbd, gn, acc, dstate, extx, extb, dux, dub, acc_x, acc_bc, acc_s, upper, spread, gather, ones_h,
):
    i = pl.program_id(0)
    blocks = pl.num_programs(0)
    c = blocks - 1 - i
    chunk, inner = px.shape
    ns = bc // 2
    par = read_vec(vec, heads, chunk, inner, bc, taps_n)
    keep, n_live, keep_next = read_block(vec, c, chunk)
    taps, taps_b, bias, rate, skip, gain = (par[k] for k in ("convx", "convbc", "bias", "rate", "skip", "gain"))

    @pl.when(i == 0)
    def _():
        for ref in (dstate, dux, dub, acc_x, acc_bc, acc_s):
            ref[...] = jnp.zeros_like(ref)
        set_upper(upper)
        set_spread(spread, heads)
        set_gather(gather, ones_h, heads)

    moved = jnp.transpose(
        jnp.concatenate(
            [rows[0, pl.ds(c, 1), :], rows[1, pl.ds(c, 1), :], jnp.zeros((chunk - 2, chunk), F32)], axis=0
        )
    )
    inv = lax.rsqrt(moved[:, 0:1] / total_inner + EPS)
    coef = inv * inv * inv * (moved[:, 1:2] / total_inner)
    z = pz[...]
    sz = sigmoid(z)
    silu_z = z * sz
    yv = y[...]
    gated = yv * silu_z
    g = ggn[...]
    d_gated = inv * (g * gain) - gated * coef
    lpz[...] = (d_gated * yv * (sz * (1.0 + z * (1.0 - sz)))).astype(BF)
    dy = d_gated * silu_z
    gn[...] = (gated * inv * gain).astype(BF)
    acc_x[taps_n : taps_n + 1, :] += jnp.sum(g * gated * inv, axis=0, keepdims=True)

    extx[0:8, :] = jnp.where(keep, px_halo[...], 0.0)
    extb[0:8, :] = jnp.where(keep, pbd_halo[:, :bc], 0.0)
    extx[8 : chunk + 8, :] = px[...]
    extb[8 : chunk + 8, :] = pbd[:, :bc]
    live_x = (iota2(chunk, inner, 0).astype(F32) < n_live).astype(F32)
    live_b = (iota2(chunk, bc, 0).astype(F32) < n_live).astype(F32)
    u = conv_from(extx, taps, chunk, 8)
    su = sigmoid(u)
    x = u * su * live_x
    dx_du = su * (1.0 + u * (1.0 - su)) * live_x
    ub = conv_from(extb, taps_b, chunk, 8)
    sb = sigmoid(ub)
    act = (ub * sb * live_b).astype(BF)
    db_du = sb * (1.0 + ub * (1.0 - sb)) * live_b
    b, cc = act[:, :ns], act[:, ns:]

    pre, live, dt, run = dt_rows(pbd[:, bc:], bias, rate, n_live, heads, upper[...])
    cols, wide = spread_all(run, dt, heads, chunk, spread[...])
    dt_w, ein_w, eout_w = wide[:, :inner], wide[:, inner : 2 * inner], wide[:, 2 * inner :]
    xd = x * dt_w
    xdb = xd.astype(BF)
    dyb = dy.astype(BF)
    acc_x[taps_n + 1 : taps_n + 2, :] += jnp.sum(dy * x, axis=0, keepdims=True)

    scores_t = nt(b, cc)
    tri = iota2(chunk, chunk, 0) <= iota2(chunk, chunk, 1)
    low_lanes = iota2(chunk, 2 * HD, 1) < HD
    d_scores_t = jnp.zeros((chunk, chunk), F32)
    dxd = []
    pulls = []
    read_sums = []
    for j in range(heads // 2):
        span = slice(2 * HD * j, 2 * HD * (j + 1))
        dy_pair = pair_stack(dyb[:, span], low_lanes)
        x_pair = pair_stack(xdb[:, span], low_lanes)
        d_mix = nt(x_pair, dyb[:, span])
        mix = []
        for k in (0, 1):
            h = 2 * j + k
            spread_h = run[h : h + 1, :] - cols[:, h : h + 1]
            fade = jnp.exp(jnp.where(tri, spread_h, NEG))
            m = scores_t * fade
            dm = d_mix[k * chunk : (k + 1) * chunk]
            d_scores_t = d_scores_t + dm * fade
            pull = (dm * m).astype(BF)
            pulls.append(pull)
            read_sums.append(jnp.sum(pull.astype(F32), axis=0, keepdims=True))
            mix.append(m.astype(BF))
        dxd.append(nn(jnp.concatenate(mix, axis=1), dy_pair))
    source_sums = nn(jnp.concatenate(pulls, axis=1), ones_h[...])
    read_rows = jnp.concatenate(read_sums, axis=0)

    d_state = jnp.where(keep_next, dstate[...], 0.0)
    d_state_b = d_state.astype(BF)
    enter_b = sin[0]
    edy = ein_w * dy
    edyb = edy.astype(BF)
    readings = nn(cc, enter_b)
    from_state = nn(b, d_state_b) * eout_w
    d_xd = jnp.concatenate(dxd, axis=1) + from_state
    q1 = edy * readings
    q2 = xd * from_state
    decay = ein_w[chunk - 1 : chunk, :]
    dstate[...] = decay * d_state + tn(cc, edyb)
    d_cb = tn(d_scores_t.astype(BF), b) + nt(edyb, enter_b)
    d_b = nn(d_scores_t.astype(BF), cc) + nt((xd * eout_w).astype(BF), d_state_b)

    sums = (
        nn((d_xd * x).astype(BF), gather[0])
        + nn((q1 - q2).astype(BF), gather[1])
        + nn(q2.astype(BF), gather[2])
        - source_sums
    )
    sums_t = jnp.transpose(sums)
    dt_direct = sums_t[:heads]
    d_run = sums_t[heads : 2 * heads] + read_rows
    whole_q2 = jnp.sum(sums_t[2 * heads : 3 * heads], axis=1, keepdims=True)
    kept = jnp.sum(enter_b.astype(F32) * d_state, axis=0, keepdims=True) * decay
    kept_hi, kept_lo = split2(kept)
    kept_two = jnp.concatenate([kept_hi, kept_lo, jnp.zeros((6, inner), F32)], axis=0).astype(BF)
    kept_rows = nn(kept_two, gather[0])
    kept_cols = jnp.transpose(
        jnp.concatenate([kept_rows[0:1] + kept_rows[1:2], jnp.zeros((chunk - 1, chunk), F32)], axis=0)
    )
    d_last = whole_q2 + kept_cols[:heads, 0:1]
    hi, mid, low = split3(d_run)
    back = nt(jnp.concatenate([hi, mid, low], axis=0).astype(BF), upper[...])
    d_a = back[:heads] + back[heads : 2 * heads] + back[2 * heads :] + d_last
    d_dt = dt_direct + d_a * rate
    d_pre = d_dt * live * sigmoid(pre)
    acc_s[0:heads, :] += d_pre
    acc_s[heads : 2 * heads, :] += d_a * dt * rate

    def conv_back(d_u, du_ref, ext_ref, tap_values, acc):
        du_ref[chunk : chunk + 8, :] = jnp.where(keep_next, du_ref[0:8, :], 0.0)
        du_ref[0:chunk, :] = d_u
        out = tap_values[taps_n - 1 : taps_n, :] * d_u
        acc[taps_n - 1 : taps_n, :] += jnp.sum(d_u * ext_ref[8 : chunk + 8, :], axis=0, keepdims=True)
        for k in range(1, taps_n):
            row = taps_n - 1 - k
            out = out + tap_values[row : row + 1, :] * du_ref[pl.ds(k, chunk), :]
            acc[row : row + 1, :] += jnp.sum(
                d_u * ext_ref[pl.ds(8 - k, chunk), :], axis=0, keepdims=True
            )
        return out

    d_x = d_xd * dt_w + skip * dy
    lpx[...] = conv_back(d_x * dx_du, dux, extx, taps, acc_x).astype(BF)
    d_act = jnp.concatenate([d_b, d_cb], axis=1)
    lpbd[:, :bc] = conv_back(d_act * db_du, dub, extb, taps_b, acc_bc).astype(BF)
    pad = jnp.concatenate([d_pre, jnp.zeros((chunk - heads, chunk), F32)], axis=0)
    lpbd[:, bc:] = jnp.transpose(pad).astype(BF)

    @pl.when(i == blocks - 1)
    def _():
        acc[...] = jnp.zeros_like(acc)
        for k in range(taps_n):
            acc[1:2, k * bc : (k + 1) * bc] = acc_bc[k : k + 1, :]
        per = acc.shape[1] // inner
        for k in range(taps_n + 1):
            acc[2 + k // per : 3 + k // per, (k % per) * inner : (k % per + 1) * inner] = acc_x[k : k + 1, :]
        per_head = jnp.sum(
            jnp.transpose(jnp.concatenate([acc_s[...], jnp.zeros((chunk - 2 * heads, chunk), F32)], axis=0)),
            axis=0, keepdims=True,
        )
        three = jnp.concatenate(split3(acc_x[taps_n + 1 : taps_n + 2, :]) + (jnp.zeros((5, inner), F32),), axis=0)
        skips = jnp.sum(nn(three.astype(BF), gather[2]), axis=0, keepdims=True)
        acc[5:6, 0:chunk] = per_head + skips


def scan_backward(ggn, y, pz, px, pbd, sin, rows, vec, heads, taps, bc, total_inner):
    tokens, inner = px.shape
    blocks = sin.shape[0]
    chunk = tokens // blocks
    whole = lambda a: pl.BlockSpec(a.shape, lambda i: (0,) * a.ndim)
    back = lambda w: pl.BlockSpec((chunk, w), lambda i: (blocks - 1 - i, 0))
    halo = lambda w: pl.BlockSpec((8, w), lambda i: (jnp.maximum((blocks - 1 - i) * (chunk // 8) - 1, 0), 0))
    width = pbd.shape[1]
    vm, sds = pltpu.VMEM, jax.ShapeDtypeStruct
    return pl.pallas_call(
        functools.partial(scan_bwd_kernel, heads, total_inner, taps, bc),
        grid=(blocks,),
        in_specs=[
            back(inner), back(inner), back(inner), back(inner), halo(inner), back(width), halo(width),
            pl.BlockSpec((1, bc // 2, inner), lambda i: (blocks - 1 - i, 0, 0)), whole(rows), whole(vec),
        ],
        out_specs=[
            back(inner), back(inner), back(width), back(inner), pl.BlockSpec((8, vec.shape[1]), lambda i: (0, 0)),
        ],
        scratch_shapes=[
            vm((bc // 2, inner), F32), vm((chunk + 8, inner), F32), vm((chunk + 8, bc), F32),
            vm((chunk + 8, inner), F32), vm((chunk + 8, bc), F32),
            vm((8, inner), F32), vm((8, bc), F32), vm((2 * heads, chunk), F32),
            vm((chunk, chunk), BF), vm((chunk, 3 * inner), BF), vm((3, inner, chunk), BF), vm((heads * chunk, chunk), BF),
        ],
        out_shape=[
            sds((tokens, inner), BF), sds((tokens, inner), BF), sds((tokens, width), BF), sds((tokens, inner), BF),
            sds((8, vec.shape[1]), F32),
        ],
        compiler_params=pltpu.CompilerParams(vmem_limit_bytes=48 * 2**20),
        name="scan_backward",
    )(ggn, y, pz, px, px, pbd, pbd, sin, rows, vec)
def peers(dp_n):
    dp, hm = lax.axis_index("dp"), lax.axis_index("heads")
    across, core = hm // 2, hm % 2
    pair, line, lines = dp % 2, dp // 2, dp_n // 2
    return dict(
        sib=(dp, 2 * across + 1 - core),
        xn=(dp, 2 * (1 - across) + core),
        dg=(dp, 2 * (1 - across) + 1 - core),
        yn=(2 * line + 1 - pair, hm),
        line=lambda k: (2 * ((line + k) % lines) + pair, hm),
        mine=hm,
        other=2 * (1 - across) + core,
        sib_mine=2 * across + 1 - core,
        sib_other=2 * (1 - across) + 1 - core,
        pair=pair, line_index=line, lines=lines, dp=dp, core=core,
    )


def meet(who):
    barrier = pltpu.get_barrier_semaphore()
    for name in ("sib", "xn", "dg", "yn"):
        pl.semaphore_signal(barrier, inc=1, device_id=who[name], device_id_type=MESH)

    def greet(k, carry):
        pl.semaphore_signal(barrier, inc=1, device_id=who["line"](k), device_id_type=MESH)
        return carry

    lax.fori_loop(1, who["lines"], greet, 0)
    pl.semaphore_wait(barrier, 4 + who["lines"] - 1)


def push(src, dst, send, recv, to):
    return pltpu.make_async_remote_copy(
        src_ref=src, dst_ref=dst, send_sem=send, recv_sem=recv, device_id=to, device_id_type=MESH
    )


def tail_kernel(
    dp_n, units,
    grad_t_in, gn_in, rows_out_in, normed_t_in, lpz_in, rows_z_in, lpx_in, rows_x_in, lpbd_in, rows_bd_in, normed_in,
    tokens, acc, cot, q_wide, vec,
    block_out, grad_tokens, g_x, g_z, g_out, g_bc, small_out,
    sib_send, sib_recv, x_send, x_recv, part, held,
    y_send, y_recv, z_send, z_recv, g_own, yb_send, yb_recv, zb_send, zb_recv, gb_own, bh_send, bh_recv,
    bx_send, bx_recv, bs_recv, h_send, h_recv, sy_send, sy_recv, sz_send, sz_recv, dy_send, dy_recv, dz_send, dz_recv, row_sums,
    grad_t, gn, rows_out, normed_t, lpz, rows_z, lpx, rows_x, lpbd, rows_bd, normed,
    s_in, s_sib, r_sib, s_x, r_x, s_y, r_y, s_z, r_z, s_m, r_m, s_sl, r_sl,
):
    loads = [
        pltpu.make_async_copy(src, dst, s_in.at[i])
        for i, (src, dst) in enumerate((
            (grad_t_in, grad_t), (gn_in, gn), (rows_out_in, rows_out), (normed_t_in, normed_t), (lpz_in, lpz),
            (rows_z_in, rows_z), (lpx_in, lpx), (rows_x_in, rows_x), (lpbd_in, lpbd), (rows_bd_in, rows_bd),
            (normed_in, normed),
        ))
    ]
    for load in loads:
        load.start()
    who = peers(dp_n)
    meet(who)
    count = normed.shape[0]
    width = normed.shape[1]
    inner = lpx.shape[1]
    bc = 2 * bh_send.shape[1]
    quarter = width // 4
    span = count // units
    block = width // dp_n
    lines = who["lines"]

    def copy_sib(u):
        return push(sib_send.at[u], sib_recv.at[u], s_sib.at[u], r_sib.at[u], who["sib"])

    def copy_x(u):
        return push(x_send.at[u], x_recv.at[u], s_x.at[u], r_x.at[u], who["xn"])

    def product(u, q):
        cols = pl.ds(pl.multiple_of(q * quarter, quarter), quarter)
        if u < units:
            return nt(gn[u * span : (u + 1) * span, :], rows_out[cols, :])
        at = slice((u - units) * span, (u - units + 1) * span)
        return nt(lpx[at, :], rows_x[cols, :]) + nt(lpz[at, :], rows_z[cols, :]) + nt(lpbd[at, :], rows_bd[cols, :])

    def head_a(u):
        for k, q in enumerate(("sib_mine", "sib_other", "mine", "other")):
            p = product(u, who[q])
            if u >= units:
                at = slice((u - units) * span, (u - units + 1) * span)
                cols = pl.ds(pl.multiple_of(who[q] * quarter, quarter), quarter)
                inner_p = p * normed[at, cols].astype(F32)
                h_send[0:1, cols] += jnp.sum(inner_p, axis=0, keepdims=True)
                first = (u - units) * span
                lanes = slice(first % width, first % width + span)
                h_send[2 + first // width : 3 + first // width, lanes] += nt(
                    jnp.ones((8, quarter), BF), inner_p.astype(BF)
                )[0:1]
            if k < 2:
                sib_send[u, k] = p.astype(BF)
            else:
                part[u % 2, k - 2] = p
        copy_sib(u).start()

    def head_b(u):
        copy_sib(u).wait()
        x_send[u] = (part[u % 2, 1] + sib_recv[u, 1].astype(F32)).astype(BF)
        copy_x(u).start()
        held[u] = part[u % 2, 0] + sib_recv[u, 0].astype(F32)

    def head_c(u):
        copy_x(u).wait()
        total = held[u] + x_recv[u].astype(F32)
        if u < units:
            at = slice(u * span, (u + 1) * span)
            block_out[at, :] = (tokens[at, :].astype(F32) + total).astype(BF)
        else:
            first = (u - units) * span
            lanes = q_wide.shape[1]
            cols = pl.ds(pl.multiple_of(who["mine"] * quarter, quarter), quarter)
            for j in range(span // lanes):
                at = slice(first + j * lanes, first + (j + 1) * lanes)
                row, lane = (first + j * lanes) // width, (first + j * lanes) % width
                dots = jnp.transpose(jnp.broadcast_to(row_sums[row : row + 1, lane : lane + lanes], (lanes, lanes)))
                q = q_wide[at, :]
                coef = q * q * (dots / width)
                grad_tokens[at, :] = (
                    cot[at, :].astype(F32)
                    + q[:, 0:1] * vec[6:7, cols] * total[j * lanes : (j + 1) * lanes]
                    - tokens[at, :].astype(F32) * coef[:, 0:1]
                )

    def rows_of(line, pair):
        return pl.ds(pl.multiple_of((2 * line + pair) * block, block), block)

    def grad_a(v):
        left, right = ((grad_t, gn), (normed_t, lpz), (normed_t, lpx))[v // 2]
        cols = slice((v % 2) * (inner // 2), (v % 2 + 1) * (inner // 2))
        for side in (0, 1):
            pair = (1 - who["pair"]) if side == 0 else who["pair"]
            stacked = jnp.concatenate([left[rows_of(l, pair), :] for l in range(lines)], axis=0)
            value = nn(stacked, right[:, cols])
            if side == 0:
                y_send[v] = value.astype(BF)
                copy_y(v).start()
            else:
                g_own[v] = value

    def copy_y(v):
        return push(y_send.at[v], y_recv.at[v], s_y.at[v], r_y.at[v], who["yn"])

    def copy_z(v, k):
        to = (who["line_index"] + k) % lines
        return push(
            z_send.at[v, pl.ds(pl.multiple_of(to * block, block), block)],
            z_recv.at[v, k - 1], s_z.at[v, k - 1], r_z.at[v, k - 1], who["line"](k),
        )

    def each_line(fn):
        def step(k, carry):
            fn(k)
            return carry

        lax.fori_loop(1, lines, step, 0)

    def own_rows():
        return pl.ds(pl.multiple_of(who["line_index"] * block, block), block)

    def grad_b(v):
        copy_y(v).wait()
        g_own[v] = g_own[v] + y_recv[v].astype(F32)
        z_send[v] = g_own[v].astype(BF)
        each_line(lambda k: copy_z(v, k).start())

    def grad_c(v):
        each_line(lambda k: copy_z(v, k).wait())
        total = g_own[v, own_rows(), :]
        for k in range(lines - 1):
            total = total + z_recv[v, k].astype(F32)
        cols = slice((v % 2) * (inner // 2), (v % 2 + 1) * (inner // 2))
        (g_out, g_z, g_x)[v // 2][:, cols] = total

    half = bc // 2

    def copy_bh():
        return push(bh_send, bh_recv, s_m.at[0], r_m.at[0], who["sib"])

    def copy_yb():
        return push(yb_send, yb_recv, s_m.at[1], r_m.at[1], who["yn"])

    def copy_zb(k):
        to = (who["line_index"] + k) % lines
        return push(
            zb_send.at[pl.ds(pl.multiple_of(to * block, block), block)],
            zb_recv.at[k - 1], s_sl.at[0, k - 1], r_sl.at[0, k - 1], who["line"](k),
        )

    def copy_bx():
        return push(bx_send, bx_recv, s_m.at[2], r_m.at[2], who["xn"])

    def copy_bs():
        return push(bx_send, bs_recv, s_m.at[3], r_m.at[3], who["sib"])

    def bc_a():
        for side in (0, 1):
            pair = (1 - who["pair"]) if side == 0 else who["pair"]
            stacked = jnp.concatenate([normed_t[rows_of(l, pair), :] for l in range(lines)], axis=0)
            value = nn(stacked, lpbd[:, :bc])
            first = who["core"] == 0
            lo, hi = value[:, :half], value[:, half:]
            at = slice(side * lines * block, (side + 1) * lines * block)
            bh_send[at, :] = jnp.where(first, hi, lo).astype(BF)
            gb_own[at, :] = jnp.where(first, lo, hi)
        copy_bh().start()

    def bc_b():
        copy_bh().wait()
        rows = lines * block
        gb_own[...] = gb_own[...] + bh_recv[...].astype(F32)
        yb_send[...] = gb_own[:rows, :].astype(BF)
        copy_yb().start()

    def bc_c():
        rows = lines * block
        copy_yb().wait()
        gb_own[rows:, :] = gb_own[rows:, :] + yb_recv[...].astype(F32)
        zb_send[...] = gb_own[rows:, :].astype(BF)
        each_line(lambda k: copy_zb(k).start())

    def bc_d():
        each_line(lambda k: copy_zb(k).wait())
        at = pl.ds(pl.multiple_of(lines * block + who["line_index"] * block, block), block)
        total = gb_own[at, :]
        for k in range(lines - 1):
            total = total + zb_recv[k].astype(F32)
        bx_send[...] = total
        copy_bx().start()

    def bc_e():
        copy_bx().wait()
        bx_send[...] = bx_send[...] + bx_recv[...]
        copy_bs().start()

    def bc_f():
        copy_bs().wait()
        mine, theirs = bx_send[...], bs_recv[...]
        first = who["core"] == 0
        g_bc[:, :half] = jnp.where(first, mine, theirs)
        g_bc[:, half:] = jnp.where(first, theirs, mine)

    three = (("sib", 4), ("xn", 5), ("dg", 6))
    token_rows = count // width

    def copy_h(k):
        name, sem = three[k]
        return push(h_send, h_recv.at[k], s_m.at[sem], r_m.at[sem], who[name])

    def small_a():
        h_send[1:2, :] = acc[1:2, :]
        for k in range(3):
            copy_h(k).start()

    def copy_sy():
        return push(sy_send, sy_recv, s_m.at[7], r_m.at[7], who["yn"])

    def copy_dy():
        return push(dy_send, dy_recv, s_m.at[8], r_m.at[8], who["yn"])

    def copy_sz(k):
        return push(sz_send, sz_recv.at[k - 1], s_sl.at[1, k - 1], r_sl.at[1, k - 1], who["line"](k))

    def copy_dz(k):
        return push(dz_send, dz_recv.at[k - 1], s_sl.at[2, k - 1], r_sl.at[2, k - 1], who["line"](k))

    def dt_a():
        dy_send[...] = tn(lpbd[:, bc:], normed[...])[0:16, :].astype(BF)
        copy_dy().start()

    def dt_b():
        copy_dy().wait()
        dz_send[...] = (dy_send[...].astype(F32) + dy_recv[...].astype(F32)).astype(BF)
        each_line(lambda k: copy_dz(k).start())

    def dt_c():
        each_line(lambda k: copy_dz(k).wait())
        total = dz_send[...].astype(F32)
        for k in range(lines - 1):
            total = total + dz_recv[k].astype(F32)
        small_out[8:24, :] = total

    def small_b():
        for k in range(3):
            copy_h(k).wait()
        over_heads = h_send[...] + h_recv[0] + h_recv[1] + h_recv[2]
        row_sums[0:token_rows, :] = over_heads[2 : 2 + token_rows, :]
        sy_send[0:2, :] = over_heads[0:2, :]
        sy_send[2:8, :] = acc[2:8, :]
        copy_sy().start()

    def small_c():
        copy_sy().wait()
        sz_send[...] = sy_send[...] + sy_recv[...]
        each_line(lambda k: copy_sz(k).start())

    def small_d():
        each_line(lambda k: copy_sz(k).wait())
        total = sz_send[...]
        for k in range(lines - 1):
            total = total + sz_recv[k]
        small_out[0:8, :] = total

    h_send[...] = jnp.zeros_like(h_send)

    def seq(*steps):
        for fn, *args in steps:
            fn(*args)

    assert units == 4

    def load(*which):
        for i in which:
            loads[i].wait()

    load(0, 1)
    seq((grad_a, 0), (grad_a, 1))
    load(2)
    seq((head_a, 0), (head_a, 1), (head_b, 0), (head_a, 2), (head_b, 1), (head_a, 3), (head_b, 2))
    load(3, 8)
    seq((bc_a,), (head_b, 3))
    load(4)
    seq((grad_a, 2), (bc_b,), (grad_a, 3))
    load(5, 6, 7, 9, 10)
    seq((grad_b, 0), (head_a, 4), (dt_a,), (grad_b, 1), (grad_a, 4), (head_b, 4), (head_a, 5), (bc_c,), (head_b, 5))
    seq((grad_a, 5), (head_a, 6), (grad_b, 2), (head_b, 6), (head_a, 7), (small_a,), (grad_b, 3), (head_b, 7))
    seq((dt_b,), (small_b,), (head_c, 0), (head_c, 1), (head_c, 2), (head_c, 3), (bc_d,), (grad_c, 0), (grad_c, 1))
    seq((grad_b, 4), (small_c,), (grad_b, 5), (dt_c,), (bc_e,), (head_c, 4), (head_c, 5), (grad_c, 2), (grad_c, 3))
    seq((small_d,), (head_c, 6), (grad_c, 4), (bc_f,), (head_c, 7), (grad_c, 5))


def tail(dp_n, units, normed_t, normed, grad_t, gn, lpx, lpz, lpbd, rows_x, rows_z, rows_bd, rows_out, tokens, acc, cot, q_wide, vec, bc):
    count, width = normed.shape
    inner = lpx.shape[1]
    quarter = width // 4
    span = count // units
    block = width // dp_n
    lines = dp_n // 2
    half_rows = lines * block
    more = max(lines - 1, 1)
    vm = pltpu.VMEM
    dma = pltpu.SemaphoreType.DMA
    operands = (
        grad_t, gn, rows_out, normed_t, lpz, rows_z, lpx, rows_x, lpbd, rows_bd, normed, tokens, acc, cot, q_wide, vec,
    )
    sds = jax.ShapeDtypeStruct
    spec = pl.BlockSpec(memory_space=pltpu.VMEM)
    return pl.pallas_call(
        functools.partial(tail_kernel, dp_n, units),
        out_shape=[
            sds((count, quarter), BF), sds((count, quarter), F32),
            sds((block, inner), F32), sds((block, inner), F32), sds((block, inner), F32), sds((block, bc), F32),
            sds((24, width), F32),
        ],
        in_specs=[pl.BlockSpec(memory_space=pl.ANY)] * 11 + [spec] * 5,
        out_specs=[spec] * 7,
        scratch_shapes=[
            vm((2 * units, 2, span, quarter), BF), vm((2 * units, 2, span, quarter), BF),
            vm((2 * units, span, quarter), BF), vm((2 * units, span, quarter), BF),
            vm((2, 2, span, quarter), F32), vm((2 * units, span, quarter), F32),
            vm((6, half_rows, inner // 2), BF), vm((6, half_rows, inner // 2), BF),
            vm((6, half_rows, inner // 2), BF), vm((6, more, block, inner // 2), BF),
            vm((6, half_rows, inner // 2), F32),
            vm((half_rows, bc // 2), BF), vm((half_rows, bc // 2), BF),
            vm((half_rows, bc // 2), BF), vm((more, block, bc // 2), BF),
            vm((2 * half_rows, bc // 2), F32),
            vm((2 * half_rows, bc // 2), BF), vm((2 * half_rows, bc // 2), BF),
            vm((block, bc // 2), F32), vm((block, bc // 2), F32), vm((block, bc // 2), F32),
            vm((8, width), F32), vm((3, 8, width), F32),
            vm((8, width), F32), vm((8, width), F32), vm((8, width), F32), vm((more, 8, width), F32),
            vm((16, width), BF), vm((16, width), BF), vm((16, width), BF), vm((more, 16, width), BF),
            vm((8, width), F32),
        ]
        + [vm(a.shape, a.dtype) for a in operands[:11]]
        + [
            dma((11,)), dma((2 * units,)), dma((2 * units,)), dma((2 * units,)), dma((2 * units,)),
            dma((6,)), dma((6,)), dma((6, more)), dma((6, more)), dma((9,)), dma((9,)),
            dma((3, more)), dma((3, more)),
        ],
        compiler_params=pltpu.CompilerParams(
            collective_id=1, has_side_effects=True, vmem_limit_bytes=62 * 2**20
        ),
        name="tail",
    )(*operands)
def shares(ref_in, block_of, dp_n, width, send, recv, who):
    rows = ref_in.shape[0]
    lines = who["lines"]

    def at(dp):
        return block_of.at[pl.ds(pl.multiple_of(dp * rows, rows), rows), width]

    def own():
        return push(ref_in.at[:, width], at(who["dp"]), send.at[0], recv.at[0], who["yn"])

    def along(k):
        return push(ref_in.at[:, width], at(who["dp"]), send.at[k], recv.at[k], who["line"](k))

    def onward(k):
        source = at(2 * ((who["line_index"] - k + lines) % lines) + who["pair"])
        return push(source, source, send.at[lines - 1 + k], recv.at[lines - 1 + k], who["yn"])

    return own, along, onward


def loop_line(lines, fn):
    def step(k, carry):
        fn(k)
        return carry

    lax.fori_loop(1, lines, step, 0)


def front_kernel(
    dp_n, heads, units, taps, bc,
    tokens, cot, w_x, w_bd, w_z, w_out, vec,
    px_out, pbd_out, normed_out, normed_t_out, q_out, y_out, sin_out, parts, rows_x, rows_bd, rows_z, rows_out,
    tok, wx, wbd, px, pbd, normed, normed_t, q, y, sin, state, extx, extb, upper, spread,
    s_loc, s_sib, r_sib, s_x, r_x, s_f, r_f, s_cx, r_cx, s_cf, r_cf, s_w, r_w, s_out, s_y,
):
    who = peers(dp_n)
    count, quarter = tokens.shape
    width = 4 * quarter
    span = count // units
    lines = who["lines"]
    block, inner = w_x.shape
    blocks = sin.shape[0]
    chunk = count // blocks
    per = blocks // units
    pieces = s_cx.shape[0]
    cot_span = count // pieces
    here = pl.ds(pl.multiple_of(who["dp"] * block, block), block)
    local = [
        pltpu.make_async_copy(src, dst, s_loc.at[k])
        for k, (src, dst) in enumerate((
            (tokens, tok.at[who["mine"]]), (w_x, wx.at[here]), (w_bd, wbd.at[here]),
            (w_z, rows_z.at[here]), (w_out, rows_out.at[here]), (cot, parts.at[who["mine"]]),
        ))
    ]
    for copy in local[:3]:
        copy.start()
    meet(who)

    def rows(s, n=span):
        return pl.ds(pl.multiple_of(s * n, n), n)

    def to_x(s):
        return push(tokens.at[rows(s)], tok.at[who["mine"], rows(s)], s_x.at[s], r_x.at[s], who["xn"])

    def to_sib():
        return push(tokens, tok.at[who["mine"]], s_sib.at[0], r_sib.at[0], who["sib"])

    def forward(s):
        at = tok.at[who["other"], rows(s)]
        return push(at, at, s_f.at[s], r_f.at[s], who["sib"])

    def cot_x(j):
        at = rows(j, cot_span)
        return push(cot.at[at], parts.at[who["mine"], at], s_cx.at[j], r_cx.at[j], who["xn"])

    def cot_sib():
        return push(cot, parts.at[who["mine"]], s_sib.at[1], r_sib.at[1], who["sib"])

    def cot_forward(j):
        at = parts.at[who["other"], rows(j, cot_span)]
        return push(at, at, s_cf.at[j], r_cf.at[j], who["sib"])

    half = inner // 2
    cuts = [
        shares(ref, to, dp_n, cols, s_w.at[n], r_w.at[n], who)
        for n, (ref, to, cols) in enumerate((
            (w_x, wx, pl.ds(0, half)), (w_x, wx, pl.ds(half, half)), (w_bd, wbd, slice(None)),
            (w_z, rows_z, pl.ds(0, half)), (w_z, rows_z, pl.ds(half, half)),
            (w_out, rows_out, pl.ds(0, half)), (w_out, rows_out, pl.ds(half, half)),
        ))
    ]

    def offer(n):
        own, along, onward = cuts[n]
        loop_line(lines, lambda k: along(k).start())
        own().start()

    def pass_rows(n):
        own, along, onward = cuts[n]

        def one(k):
            along(k).wait()
            onward(k).start()

        loop_line(lines, one)

    def have(n):
        own, along, onward = cuts[n]
        own().wait()
        loop_line(lines, lambda k: onward(k).wait())

    def pass_cot(j):
        cot_x(j).wait()
        cot_forward(j).start()

    to_x(0).start()
    offer(0)
    for s in range(1, units):
        to_x(s).start()
    to_sib().start()
    for n in (1, 2):
        offer(n)
    for j in range(pieces):
        cot_x(j).start()
    for n in (3, 4, 5, 6):
        offer(n)
    set_upper(upper)
    set_spread(spread, heads)
    state[...] = jnp.zeros_like(state)
    extx[...] = jnp.zeros_like(extx)
    extb[...] = jnp.zeros_like(extb)
    par = read_vec(vec, heads, chunk, inner, bc, taps)
    gain = vec[6:7, :width]

    def out_copies(s):
        at = rows(s)
        every = slice(None)
        return [
            pltpu.make_async_copy(ref.at[to], out.at[to], s_out.at[n, s])
            for n, (ref, out, to) in enumerate((
                (normed, normed_out, (at,)), (normed_t, normed_t_out, (every, at)), (q, q_out, (at,)),
                (px, px_out, (at,)), (pbd, pbd_out, (at,)),
            ))
        ]

    def norm(s):
        at = rows(s)
        values = [tok[h, at, :].astype(F32) for h in range(4)]
        total = sum(jnp.sum(p * p, axis=1, keepdims=True) for p in values)
        inv = lax.rsqrt(total / width + EPS)
        q[at, :] = jnp.broadcast_to(inv, (span, q.shape[1]))
        for h in range(4):
            cols = slice(h * quarter, (h + 1) * quarter)
            value = (values[h] * inv * gain[:, cols]).astype(BF)
            normed[at, cols] = value
            normed_t[cols, at] = jnp.transpose(value)
        for copy in out_copies(s)[:3]:
            copy.start()

    def project(s):
        at = rows(s)
        pbd[at, :] = nn(normed[at, :], wbd[...])
        px[at, :] = nn(normed[at, :], wx[...])
        for copy in out_copies(s)[3:]:
            copy.start()

    local[0].wait()
    to_x(0).wait()
    forward(0).start()
    pass_rows(0)
    to_sib().wait()
    forward(0).wait()
    norm(0)
    to_x(1).wait()
    forward(1).start()
    pass_rows(1)
    forward(1).wait()
    norm(1)
    pass_rows(2)
    to_x(2).wait()
    forward(2).start()
    for copy in local[3:]:
        copy.start()
    cot_sib().start()
    forward(2).wait()
    norm(2)
    for copy in local[1:3]:
        copy.wait()
    for n in (0, 1, 2):
        have(n)
    keep_rows = [
        pltpu.make_async_copy(wx, rows_x, s_loc.at[6]), pltpu.make_async_copy(wbd, rows_bd, s_loc.at[7]),
    ]
    for copy in keep_rows:
        copy.start()

    def last_tokens(s):
        to_x(s).wait()
        forward(s).start()

    def last_norm(s):
        forward(s).wait()
        norm(s)

    events = {1: [(last_tokens, units - 1)], 2: [(last_norm, units - 1)]}
    late = []
    plan = [(pass_rows, 3, 4), (pass_rows, 4, 8), (pass_rows, 5, 12)]
    plan += [(pass_cot, j, 5 + 2 * j) for j in range(pieces)] + [(pass_rows, 6, blocks)]
    for fn, k, at in plan:
        if at < blocks:
            events.setdefault(at, []).append((fn, k))
        else:
            late.append((fn, k))

    def y_copies(c):
        at = rows(c, chunk)
        return (
            pltpu.make_async_copy(y.at[at], y_out.at[at], s_y.at[0, c]),
            pltpu.make_async_copy(sin.at[c], sin_out.at[c], s_y.at[1, c]),
        )

    def step(c, carry):
        for at, fns in events.items():

            @pl.when(c == at)
            def _(fns=fns):
                for fn, k in fns:
                    fn(k)

        @pl.when(c % per == 0)
        def _():
            project(c // per)

        at = rows(c, chunk)
        y_c, enter = scan_step(
            heads, par, read_block(vec, c, chunk), px.at[at], pbd.at[at], upper, spread, state, extx, extb
        )
        y[at, :] = y_c
        sin[c] = enter
        for copy in y_copies(c):
            copy.start()
        return carry

    lax.fori_loop(0, blocks, step, 0)
    for fn, k in late:
        fn(k)

    def end_y(c, carry):
        for copy in y_copies(c):
            copy.wait()
        return carry

    lax.fori_loop(0, blocks, end_y, 0)
    for s in range(units):
        for copy in out_copies(s):
            copy.wait()
    for copy in local[3:] + keep_rows:
        copy.wait()
    cot_sib().wait()
    for j in range(pieces):
        cot_forward(j).wait()
    for n in (3, 4, 5, 6):
        have(n)


def front(dp_n, heads, taps, bc, blocks, tokens, cot, w_x, w_bd, w_z, w_out, vec):
    count, quarter = tokens.shape
    width = 4 * quarter
    inner, wide = w_x.shape[1], w_bd.shape[1]
    chunk = count // blocks
    units, pieces = 4, 8
    vm, dma, sds = pltpu.VMEM, pltpu.SemaphoreType.DMA, jax.ShapeDtypeStruct
    hbm = pl.BlockSpec(memory_space=pl.ANY)
    ways = dp_n - 1
    outs = [
        sds((count, inner), F32), sds((count, wide), F32), sds((count, width), BF), sds((width, count), BF),
        sds((count, 128), F32), sds((count, inner), F32), sds((blocks, bc // 2, inner), BF),
        sds((4, count, quarter), BF), sds((width, inner), BF), sds((width, wide), BF), sds((width, inner), BF),
        sds((width, inner), BF),
    ]
    return pl.pallas_call(
        functools.partial(front_kernel, dp_n, heads, units, taps, bc),
        out_shape=outs,
        in_specs=[hbm] * 6 + [pl.BlockSpec(memory_space=pltpu.VMEM)],
        out_specs=[hbm] * len(outs),
        scratch_shapes=[
            vm((4, count, quarter), BF), vm((width, inner), BF), vm((width, wide), BF),
            vm((count, inner), F32), vm((count, wide), F32), vm((count, width), BF), vm((width, count), BF),
            vm((count, 128), F32), vm((count, inner), F32), vm((blocks, bc // 2, inner), BF),
            vm((bc // 2, inner), F32), vm((chunk + 8, inner), F32), vm((chunk + 8, bc), F32),
            vm((chunk, chunk), BF), vm((chunk, 3 * inner), BF),
            dma((8,)), dma((2,)), dma((2,)), dma((units,)), dma((units,)), dma((units,)), dma((units,)),
            dma((pieces,)), dma((pieces,)), dma((pieces,)), dma((pieces,)),
            dma((7, ways)), dma((7, ways)), dma((5, units)), dma((2, blocks)),
        ],
        compiler_params=pltpu.CompilerParams(
            collective_id=2, has_side_effects=True, vmem_limit_bytes=58 * 2**20
        ),
        name="front",
    )(tokens, cot, w_x, w_bd, w_z, w_out, vec)


def body(
    tokens, cotangent, starts, fill, norm_gain, w_x, w_z, w_dt, w_bc, conv_x, conv_bc, dt_bias, a_log, skip,
    gate_gain, w_out,
):
    heads_n = lax.axis_size("heads")
    dp_n = lax.axis_size("dp")
    head_index = lax.axis_index("heads")
    dp_index = lax.axis_index("dp")
    count, columns = tokens.shape
    width = columns * heads_n
    blocks = starts.shape[0]
    chunk = count // blocks
    inner = w_x.shape[1]
    heads = w_dt.shape[1]
    taps, bc = conv_bc.shape
    w_bd = jnp.concatenate([w_bc, jnp.pad(w_dt, ((0, 0), (0, chunk - heads)))], axis=1)
    vec = pack_vec(conv_x, skip, gate_gain, norm_gain, dt_bias, a_log, conv_bc, starts, fill, chunk)
    px, pbd, normed, normed_t, q_wide, y, sin, parts, rows_x, rows_bd, rows_z, rows_out = front(
        dp_n, heads, taps, bc, blocks, tokens, cotangent, w_x, w_bd, w_z, w_out, vec
    )
    pz, ggn, grad_t, sums = gate(dp_n, blocks, normed, rows_z, rows_out, parts, y, vec)
    lpx, lpz, lpbd, gn, acc = scan_backward(
        ggn, y, pz, px, pbd, sin, sums, vec, heads, taps, bc, inner * heads_n
    )
    block_out, grad_tokens, grad_w_x, grad_w_z, grad_w_out, grad_w_bc, small = tail(
        dp_n, 4, normed_t, normed, grad_t, gn, lpx, lpz, lpbd, rows_x, rows_z, rows_bd, rows_out,
        tokens, acc, cotangent, q_wide, vec, bc,
    )
    block = width // dp_n
    own_gain = lax.dynamic_slice_in_dim(norm_gain, head_index * columns, columns, 0)
    gain_sum = lax.dynamic_slice_in_dim(small[0], head_index * columns, columns, 0)
    grad_w_dt = lax.dynamic_slice_in_dim(small[8 : 8 + heads], dp_index * block, block, 1).T
    return (
        block_out, grad_tokens, gain_sum / own_gain, grad_w_x, grad_w_z, grad_w_dt, grad_w_bc,
        small[2:4].reshape(taps, inner), small[1].reshape(taps, bc), small[5, :heads], small[5, heads : 2 * heads],
        small[5, 2 * heads : 3 * heads], small[4, :inner], grad_w_out,
    )


def solution(mesh):
    placed = (
        P("dp", "heads"),
        P("dp", "heads"),
        P("dp"),
        P("dp"),
        P(),
        P("dp", "heads"),
        P("dp", "heads"),
        P("dp", "heads"),
        P("dp", None),
        P(None, "heads"),
        P(),
        P("heads"),
        P("heads"),
        P("heads"),
        P("heads"),
        P("dp", "heads"),
    )
    return jax.shard_map(
        body,
        mesh=mesh,
        in_specs=placed,
        out_specs=(
            P("dp", "heads"),
            P("dp", "heads"),
            P("heads"),
            P("dp", "heads"),
            P("dp", "heads"),
            P("dp", "heads"),
            P("dp", None),
            P(None, "heads"),
            P(),
            P("heads"),
            P("heads"),
            P("heads"),
            P("heads"),
            P("dp", "heads"),
        ),
        check_vma=False,
    )
```

```python
import functools
import jax
import jax.numpy as jnp
from jax import lax
from jax.experimental import pallas as pl
from jax.experimental.pallas import tpu as pltpu
from jax.sharding import PartitionSpec as P

HD = 64
EPS = 1e-05
F32 = jnp.float32
BF = jnp.bfloat16
NEG = -1e30
MESH = pl.DeviceIdType.MESH


def nn(a, b):
    return lax.dot_general(a, b, (((1,), (0,)), ((), ())), preferred_element_type=F32)


def nt(a, b):
    return lax.dot_general(a, b, (((1,), (1,)), ((), ())), preferred_element_type=F32)


def tn(a, b):
    return lax.dot_general(a, b, (((0,), (0,)), ((), ())), preferred_element_type=F32)


def split2(v):
    hi = v.astype(BF).astype(F32)
    return hi, v - hi


def split3(v):
    hi = v.astype(BF).astype(F32)
    rest = v - hi
    mid = rest.astype(BF).astype(F32)
    return hi, mid, rest - mid


def softplus(v):
    return jnp.maximum(v, 0.0) + jnp.log1p(jnp.exp(-jnp.abs(v)))


def sigmoid(v):
    return 1.0 / (1.0 + jnp.exp(-v))


def iota2(rows, cols, axis):
    return lax.broadcasted_iota(jnp.int32, (rows, cols), axis)


def zero_one(cond):
    return jnp.where(cond, 1.0, 0.0).astype(BF)


def set_upper(upper):
    upper[...] = zero_one(iota2(*upper.shape, 0) <= iota2(*upper.shape, 1))


def set_spread(spread, heads):
    rows, lanes = iota2(*spread.shape, 0), iota2(*spread.shape, 1)
    inner = heads * HD
    base = heads * (1 + 2 * (lanes // inner)) + (lanes % inner) // HD
    spread[...] = zero_one(jnp.logical_or(rows == base, rows == base + heads))


def set_gather(gather, ones_h, heads):
    for q in range(3):
        rows, lanes = iota2(*gather.shape[1:], 0), iota2(*gather.shape[1:], 1)
        gather[q] = zero_one(lanes == q * heads + rows // HD)
    rows, lanes = iota2(*ones_h.shape, 0), iota2(*ones_h.shape, 1)
    ones_h[...] = zero_one(lanes == heads + rows // ones_h.shape[1])


def conv_from(ext, taps, rows, halo):
    n = taps.shape[0]
    out = taps[n - 1 : n, :] * ext[pl.ds(halo, rows), :]
    for k in range(1, n):
        out = out + taps[n - 1 - k : n - k, :] * ext[pl.ds(halo - k, rows), :]
    return out


def dt_rows(pdt, bias, rate, fill, heads, upper):
    chunk = pdt.shape[0]
    pre = jnp.transpose(pdt)[:heads] + bias
    live = (iota2(heads, chunk, 1).astype(F32) < fill).astype(F32)
    dt = softplus(pre) * live
    hi, mid, low = split3(dt * rate)
    stacked = jnp.concatenate([hi, mid, low], axis=0).astype(BF)
    summed = nn(stacked, upper)
    run = summed[:heads] + summed[heads : 2 * heads] + summed[2 * heads :]
    return pre, live, dt, run


def spread_all(run, dt, heads, chunk, spread):
    last = run[:, chunk - 1 : chunk]
    e_in = jnp.exp(run)
    e_out = jnp.exp(last - run)
    parts = [run]
    for v in (dt, e_in, e_out):
        parts.extend(split2(v))
    used = heads * len(parts)
    if used < chunk:
        parts.append(jnp.zeros((chunk - used, chunk), F32))
    cols = jnp.transpose(jnp.concatenate(parts, axis=0))
    return cols, nn(cols.astype(BF), spread)


def pair_stack(v, low_lanes):
    zero = jnp.zeros_like(v)
    return jnp.concatenate([jnp.where(low_lanes, v, zero), jnp.where(low_lanes, zero, v)], axis=0)


def read_vec(vec, heads, chunk, inner, bc, taps):
    return dict(
        convx=vec[0:taps, :inner], skip=vec[4:5, :inner], gain=vec[5:6, :inner],
        bias=vec[8 : 8 + heads, :chunk], rate=vec[8 : 8 + heads, chunk : 2 * chunk], convbc=vec[16 : 16 + taps, :bc],
    )


def read_block(vec, c, chunk):
    row = vec[pl.ds(24 + c, 1), :]
    return row[:, 0:1] > 0.5, row[:, chunk : chunk + 1], row[:, 2 * chunk : 2 * chunk + 1] > 0.5


def pack_vec(vec, conv_x, conv_bc, norm_gain, gate_gain, dt_bias, a_log, skip, starts, fill, chunk):
    taps, inner = conv_x.shape
    vec[...] = jnp.zeros_like(vec)
    vec[0:taps, :inner] = conv_x[...]
    vec[16 : 16 + taps, : conv_bc.shape[1]] = conv_bc[...]
    vec[5:6, :inner] = gate_gain[...]
    vec[6:7, :] = norm_gain[...]
    head = iota2(1, inner, 1) // HD
    skips = jnp.zeros((1, inner), F32)
    for h in range(dt_bias.shape[0]):
        skips = jnp.where(head == h, skip[h], skips)
        vec[8 + h : 9 + h, 0:chunk] = jnp.full((1, chunk), dt_bias[h], F32)
        vec[8 + h : 9 + h, chunk : 2 * chunk] = -jnp.exp(jnp.full((1, chunk), a_log[h], F32))
    vec[4:5, :inner] = skips
    blocks = starts.shape[0]
    for c in range(blocks):
        row = slice(24 + c, 25 + c)
        vec[row, 0:chunk] = jnp.full((1, chunk), 1 - starts[c], jnp.int32).astype(F32)
        vec[row, chunk : 2 * chunk] = jnp.full((1, chunk), fill[c], jnp.int32).astype(F32)
        if c + 1 < blocks:
            vec[row, 2 * chunk : 3 * chunk] = jnp.full((1, chunk), 1 - starts[c + 1], jnp.int32).astype(F32)


def scan_step(heads, par, block, px, pbd, upper, spread, state, extx, extb):
    chunk, inner = px.shape
    bc = par["convbc"].shape[1]
    ns = bc // 2
    keep, n_live, _ = block
    state[...] = jnp.where(keep, state[...], 0.0)
    extx[0:8, :] = jnp.where(keep, extx[chunk : chunk + 8, :], 0.0)
    extb[0:8, :] = jnp.where(keep, extb[chunk : chunk + 8, :], 0.0)
    extx[8 : chunk + 8, :] = px[...]
    extb[8 : chunk + 8, :] = pbd[:, :bc]

    u = conv_from(extx, par["convx"], chunk, 8)
    x = u * sigmoid(u) * (iota2(chunk, inner, 0).astype(F32) < n_live).astype(F32)
    ub = conv_from(extb, par["convbc"], chunk, 8)
    act = (ub * sigmoid(ub) * (iota2(chunk, bc, 0).astype(F32) < n_live).astype(F32)).astype(BF)
    b, cc = act[:, :ns], act[:, ns:]

    _, _, dt, run = dt_rows(pbd[:, bc:], par["bias"], par["rate"], n_live, heads, upper[...])
    cols, wide = spread_all(run, dt, heads, chunk, spread[...])
    dt_w, ein_w, eout_w = wide[:, :inner], wide[:, inner : 2 * inner], wide[:, 2 * inner :]

    xd = x * dt_w
    xdb = xd.astype(BF)
    scores = nt(cc, b)
    tri = iota2(chunk, chunk, 0) >= iota2(chunk, chunk, 1)
    low_lanes = iota2(chunk, 2 * HD, 1) < HD
    diag = []
    for j in range(heads // 2):
        mix = []
        for h in (2 * j, 2 * j + 1):
            spread_h = cols[:, h : h + 1] - run[h : h + 1, :]
            mix.append((scores * jnp.exp(jnp.where(tri, spread_h, NEG))).astype(BF))
        pair = pair_stack(xdb[:, 2 * HD * j : 2 * HD * (j + 1)], low_lanes)
        diag.append(nn(jnp.concatenate(mix, axis=1), pair))
    enter = state[...]
    enter_b = enter.astype(BF)
    y = jnp.concatenate(diag, axis=1) + ein_w * nn(cc, enter_b) + par["skip"] * x
    state[...] = ein_w[chunk - 1 : chunk, :] * enter + tn(b, (xd * eout_w).astype(BF))
    return y, enter_b


def gate_kernel(
    dp_n, normed, rows_z, rows_out, parts, y, vec, pz, ggn, grad_t, sums, h_send, h_recv, s_h, r_h,
):
    i = pl.program_id(0)
    who = peers(dp_n)
    names = ("sib", "xn", "dg")
    barrier = pltpu.get_barrier_semaphore()
    span, quarter = parts.shape[1:]
    chunk = h_send.shape[2]

    @pl.when(i == 0)
    def _():
        for name in names:
            pl.semaphore_signal(barrier, inc=1, device_id=who[name], device_id_type=MESH)

    z = nn(normed[...], rows_z[...])
    pz[...] = z
    g = nn(parts[0], rows_out[0:quarter, :])
    for k in range(1, 4):
        g = g + nn(parts[k], rows_out[k * quarter : (k + 1) * quarter, :])
    ggn[...] = g
    for k in range(4):
        grad_t[k * quarter : (k + 1) * quarter, :] = jnp.transpose(parts[k])
    gated = y[...] * (z * sigmoid(z))
    ones = jnp.ones((8, gated.shape[1]), BF)
    for k, value in enumerate((gated * gated, gated * vec[5:6, : gated.shape[1]] * g)):
        row = nt(ones, value.astype(BF))
        for j in range(span // chunk):
            h_send[k, pl.ds(i * (span // chunk) + j, 1), :] = row[0:1, j * chunk : (j + 1) * chunk]

    @pl.when(i == pl.num_programs(0) - 1)
    def _():
        pl.semaphore_wait(barrier, 3)
        copies = [push(h_send, h_recv.at[k], s_h.at[k], r_h.at[k], who[name]) for k, name in enumerate(names)]
        for copy in copies:
            copy.start()
        for copy in copies:
            copy.wait()
        sums[...] = h_send[...] + h_recv[0] + h_recv[1] + h_recv[2]


def gate(dp_n, blocks, normed, rows_z, rows_out, parts, y, vec):
    count, width = normed.shape
    inner = y.shape[1]
    chunk = count // blocks
    steps = 8
    span = count // steps
    quarter = width // 4
    sds = jax.ShapeDtypeStruct
    rows = lambda w: pl.BlockSpec((span, w), lambda i: (i, 0))
    whole = lambda a: pl.BlockSpec(a.shape, lambda i: (0, 0))
    return pl.pallas_call(
        functools.partial(gate_kernel, dp_n),
        grid=(steps,),
        in_specs=[
            rows(width), whole(rows_z), whole(rows_out),
            pl.BlockSpec((4, span, quarter), lambda i: (0, i, 0)), rows(inner), whole(vec),
        ],
        out_specs=[
            rows(inner), rows(inner), pl.BlockSpec((width, span), lambda i: (0, i)),
            pl.BlockSpec((2, blocks, chunk), lambda i: (0, 0, 0)),
        ],
        out_shape=[
            sds((count, inner), F32), sds((count, inner), F32), sds((width, count), BF), sds((2, blocks, chunk), F32),
        ],
        scratch_shapes=[
            pltpu.VMEM((2, blocks, chunk), F32), pltpu.VMEM((3, 2, blocks, chunk), F32),
            pltpu.SemaphoreType.DMA((3,)), pltpu.SemaphoreType.DMA((3,)),
        ],
        compiler_params=pltpu.CompilerParams(
            collective_id=4, has_side_effects=True, vmem_limit_bytes=48 * 2**20
        ),
        name="gate",
    )(normed, rows_z, rows_out, parts, y, vec)


def scan_bwd_kernel(
    heads, total_inner, taps_n, bc, ggn, y, pz, px, px_halo, pbd, pbd_halo, sin, rows, vec,
    lpx, lpz, lpbd, gn, acc, dstate, extx, extb, dux, dub, acc_x, acc_bc, acc_s, upper, spread, gather, ones_h,
):
    i = pl.program_id(0)
    blocks = pl.num_programs(0)
    c = blocks - 1 - i
    chunk, inner = px.shape
    ns = bc // 2
    par = read_vec(vec, heads, chunk, inner, bc, taps_n)
    keep, n_live, keep_next = read_block(vec, c, chunk)
    taps, taps_b, bias, rate, skip, gain = (par[k] for k in ("convx", "convbc", "bias", "rate", "skip", "gain"))

    @pl.when(i == 0)
    def _():
        for ref in (dstate, dux, dub, acc_x, acc_bc, acc_s):
            ref[...] = jnp.zeros_like(ref)
        set_upper(upper)
        set_spread(spread, heads)
        set_gather(gather, ones_h, heads)

    moved = jnp.transpose(
        jnp.concatenate(
            [rows[0, pl.ds(c, 1), :], rows[1, pl.ds(c, 1), :], jnp.zeros((chunk - 2, chunk), F32)], axis=0
        )
    )
    inv = lax.rsqrt(moved[:, 0:1] / total_inner + EPS)
    coef = inv * inv * inv * (moved[:, 1:2] / total_inner)
    z = pz[...]
    sz = sigmoid(z)
    silu_z = z * sz
    yv = y[...]
    gated = yv * silu_z
    g = ggn[...]
    d_gated = inv * (g * gain) - gated * coef
    lpz[...] = (d_gated * yv * (sz * (1.0 + z * (1.0 - sz)))).astype(BF)
    dy = d_gated * silu_z
    gn[...] = (gated * inv * gain).astype(BF)
    acc_x[taps_n : taps_n + 1, :] += jnp.sum(g * gated * inv, axis=0, keepdims=True)

    extx[0:8, :] = jnp.where(keep, px_halo[...], 0.0)
    extb[0:8, :] = jnp.where(keep, pbd_halo[:, :bc], 0.0)
    extx[8 : chunk + 8, :] = px[...]
    extb[8 : chunk + 8, :] = pbd[:, :bc]
    live_x = (iota2(chunk, inner, 0).astype(F32) < n_live).astype(F32)
    live_b = (iota2(chunk, bc, 0).astype(F32) < n_live).astype(F32)
    u = conv_from(extx, taps, chunk, 8)
    su = sigmoid(u)
    x = u * su * live_x
    dx_du = su * (1.0 + u * (1.0 - su)) * live_x
    ub = conv_from(extb, taps_b, chunk, 8)
    sb = sigmoid(ub)
    act = (ub * sb * live_b).astype(BF)
    db_du = sb * (1.0 + ub * (1.0 - sb)) * live_b
    b, cc = act[:, :ns], act[:, ns:]

    pre, live, dt, run = dt_rows(pbd[:, bc:], bias, rate, n_live, heads, upper[...])
    cols, wide = spread_all(run, dt, heads, chunk, spread[...])
    dt_w, ein_w, eout_w = wide[:, :inner], wide[:, inner : 2 * inner], wide[:, 2 * inner :]
    xd = x * dt_w
    xdb = xd.astype(BF)
    dyb = dy.astype(BF)
    acc_x[taps_n + 1 : taps_n + 2, :] += jnp.sum(dy * x, axis=0, keepdims=True)

    scores_t = nt(b, cc)
    tri = iota2(chunk, chunk, 0) <= iota2(chunk, chunk, 1)
    low_lanes = iota2(chunk, 2 * HD, 1) < HD
    d_scores_t = jnp.zeros((chunk, chunk), F32)
    dxd = []
    pulls = []
    read_sums = []
    for j in range(heads // 2):
        span = slice(2 * HD * j, 2 * HD * (j + 1))
        dy_pair = pair_stack(dyb[:, span], low_lanes)
        x_pair = pair_stack(xdb[:, span], low_lanes)
        d_mix = nt(x_pair, dyb[:, span])
        mix = []
        for k in (0, 1):
            h = 2 * j + k
            spread_h = run[h : h + 1, :] - cols[:, h : h + 1]
            fade = jnp.exp(jnp.where(tri, spread_h, NEG))
            m = scores_t * fade
            dm = d_mix[k * chunk : (k + 1) * chunk]
            d_scores_t = d_scores_t + dm * fade
            pull = (dm * m).astype(BF)
            pulls.append(pull)
            read_sums.append(jnp.sum(pull.astype(F32), axis=0, keepdims=True))
            mix.append(m.astype(BF))
        dxd.append(nn(jnp.concatenate(mix, axis=1), dy_pair))
    source_sums = nn(jnp.concatenate(pulls, axis=1), ones_h[...])
    read_rows = jnp.concatenate(read_sums, axis=0)

    d_state = jnp.where(keep_next, dstate[...], 0.0)
    d_state_b = d_state.astype(BF)
    enter_b = sin[0]
    edy = ein_w * dy
    edyb = edy.astype(BF)
    readings = nn(cc, enter_b)
    from_state = nn(b, d_state_b) * eout_w
    d_xd = jnp.concatenate(dxd, axis=1) + from_state
    q1 = edy * readings
    q2 = xd * from_state
    decay = ein_w[chunk - 1 : chunk, :]
    dstate[...] = decay * d_state + tn(cc, edyb)
    d_cb = tn(d_scores_t.astype(BF), b) + nt(edyb, enter_b)
    d_b = nn(d_scores_t.astype(BF), cc) + nt((xd * eout_w).astype(BF), d_state_b)

    sums = (
        nn((d_xd * x).astype(BF), gather[0])
        + nn((q1 - q2).astype(BF), gather[1])
        + nn(q2.astype(BF), gather[2])
        - source_sums
    )
    sums_t = jnp.transpose(sums)
    dt_direct = sums_t[:heads]
    d_run = sums_t[heads : 2 * heads] + read_rows
    whole_q2 = jnp.sum(sums_t[2 * heads : 3 * heads], axis=1, keepdims=True)
    kept = jnp.sum(enter_b.astype(F32) * d_state, axis=0, keepdims=True) * decay
    kept_hi, kept_lo = split2(kept)
    kept_two = jnp.concatenate([kept_hi, kept_lo, jnp.zeros((6, inner), F32)], axis=0).astype(BF)
    kept_rows = nn(kept_two, gather[0])
    kept_cols = jnp.transpose(
        jnp.concatenate([kept_rows[0:1] + kept_rows[1:2], jnp.zeros((chunk - 1, chunk), F32)], axis=0)
    )
    d_last = whole_q2 + kept_cols[:heads, 0:1]
    hi, mid, low = split3(d_run)
    back = nt(jnp.concatenate([hi, mid, low], axis=0).astype(BF), upper[...])
    d_a = back[:heads] + back[heads : 2 * heads] + back[2 * heads :] + d_last
    d_dt = dt_direct + d_a * rate
    d_pre = d_dt * live * sigmoid(pre)
    acc_s[0:heads, :] += d_pre
    acc_s[heads : 2 * heads, :] += d_a * dt * rate

    def conv_back(d_u, du_ref, ext_ref, tap_values, acc):
        du_ref[chunk : chunk + 8, :] = jnp.where(keep_next, du_ref[0:8, :], 0.0)
        du_ref[0:chunk, :] = d_u
        out = tap_values[taps_n - 1 : taps_n, :] * d_u
        acc[taps_n - 1 : taps_n, :] += jnp.sum(d_u * ext_ref[8 : chunk + 8, :], axis=0, keepdims=True)
        for k in range(1, taps_n):
            row = taps_n - 1 - k
            out = out + tap_values[row : row + 1, :] * du_ref[pl.ds(k, chunk), :]
            acc[row : row + 1, :] += jnp.sum(
                d_u * ext_ref[pl.ds(8 - k, chunk), :], axis=0, keepdims=True
            )
        return out

    d_x = d_xd * dt_w + skip * dy
    lpx[...] = conv_back(d_x * dx_du, dux, extx, taps, acc_x).astype(BF)
    d_act = jnp.concatenate([d_b, d_cb], axis=1)
    lpbd[:, :bc] = conv_back(d_act * db_du, dub, extb, taps_b, acc_bc).astype(BF)
    pad = jnp.concatenate([d_pre, jnp.zeros((chunk - heads, chunk), F32)], axis=0)
    lpbd[:, bc:] = jnp.transpose(pad).astype(BF)

    @pl.when(i == blocks - 1)
    def _():
        acc[...] = jnp.zeros_like(acc)
        for k in range(taps_n):
            acc[1:2, k * bc : (k + 1) * bc] = acc_bc[k : k + 1, :]
        per = acc.shape[1] // inner
        for k in range(taps_n + 1):
            acc[2 + k // per : 3 + k // per, (k % per) * inner : (k % per + 1) * inner] = acc_x[k : k + 1, :]
        per_head = jnp.sum(
            jnp.transpose(jnp.concatenate([acc_s[...], jnp.zeros((chunk - 2 * heads, chunk), F32)], axis=0)),
            axis=0, keepdims=True,
        )
        three = jnp.concatenate(split3(acc_x[taps_n + 1 : taps_n + 2, :]) + (jnp.zeros((5, inner), F32),), axis=0)
        skips = jnp.sum(nn(three.astype(BF), gather[2]), axis=0, keepdims=True)
        acc[5:6, 0:chunk] = per_head + skips


def scan_backward(ggn, y, pz, px, pbd, sin, rows, vec, heads, taps, bc, total_inner):
    tokens, inner = px.shape
    blocks = sin.shape[0]
    chunk = tokens // blocks
    whole = lambda a: pl.BlockSpec(a.shape, lambda i: (0,) * a.ndim)
    back = lambda w: pl.BlockSpec((chunk, w), lambda i: (blocks - 1 - i, 0))
    halo = lambda w: pl.BlockSpec((8, w), lambda i: (jnp.maximum((blocks - 1 - i) * (chunk // 8) - 1, 0), 0))
    width = pbd.shape[1]
    vm, sds = pltpu.VMEM, jax.ShapeDtypeStruct
    return pl.pallas_call(
        functools.partial(scan_bwd_kernel, heads, total_inner, taps, bc),
        grid=(blocks,),
        in_specs=[
            back(inner), back(inner), back(inner), back(inner), halo(inner), back(width), halo(width),
            pl.BlockSpec((1, bc // 2, inner), lambda i: (blocks - 1 - i, 0, 0)), whole(rows), whole(vec),
        ],
        out_specs=[
            back(inner), back(inner), back(width), back(inner), pl.BlockSpec((8, vec.shape[1]), lambda i: (0, 0)),
        ],
        scratch_shapes=[
            vm((bc // 2, inner), F32), vm((chunk + 8, inner), F32), vm((chunk + 8, bc), F32),
            vm((chunk + 8, inner), F32), vm((chunk + 8, bc), F32),
            vm((8, inner), F32), vm((8, bc), F32), vm((2 * heads, chunk), F32),
            vm((chunk, chunk), BF), vm((chunk, 3 * inner), BF), vm((3, inner, chunk), BF), vm((heads * chunk, chunk), BF),
        ],
        out_shape=[
            sds((tokens, inner), BF), sds((tokens, inner), BF), sds((tokens, width), BF), sds((tokens, inner), BF),
            sds((8, vec.shape[1]), F32),
        ],
        compiler_params=pltpu.CompilerParams(vmem_limit_bytes=48 * 2**20),
        name="scan_backward",
    )(ggn, y, pz, px, px, pbd, pbd, sin, rows, vec)
def peers(dp_n):
    dp, hm = lax.axis_index("dp"), lax.axis_index("heads")
    across, core = hm // 2, hm % 2
    pair, line, lines = dp % 2, dp // 2, dp_n // 2
    return dict(
        sib=(dp, 2 * across + 1 - core),
        xn=(dp, 2 * (1 - across) + core),
        dg=(dp, 2 * (1 - across) + 1 - core),
        yn=(2 * line + 1 - pair, hm),
        line=lambda k: (2 * ((line + k) % lines) + pair, hm),
        mine=hm,
        other=2 * (1 - across) + core,
        sib_mine=2 * across + 1 - core,
        sib_other=2 * (1 - across) + 1 - core,
        pair=pair, line_index=line, lines=lines, dp=dp, core=core,
    )


def meet(who):
    barrier = pltpu.get_barrier_semaphore()
    for name in ("sib", "xn", "dg", "yn"):
        pl.semaphore_signal(barrier, inc=1, device_id=who[name], device_id_type=MESH)

    def greet(k, carry):
        pl.semaphore_signal(barrier, inc=1, device_id=who["line"](k), device_id_type=MESH)
        return carry

    lax.fori_loop(1, who["lines"], greet, 0)
    pl.semaphore_wait(barrier, 4 + who["lines"] - 1)


def push(src, dst, send, recv, to):
    return pltpu.make_async_remote_copy(
        src_ref=src, dst_ref=dst, send_sem=send, recv_sem=recv, device_id=to, device_id_type=MESH
    )


def tail_kernel(
    dp_n, units,
    grad_t_in, gn_in, rows_out_in, normed_t_in, lpz_in, rows_z_in, lpx_in, rows_x_in, lpbd_in, rows_bd_in, normed_in,
    tokens, acc, cot, q_wide, vec,
    block_out, grad_tokens, g_x, g_z, g_out, g_bc, small_out,
    sib_send, sib_recv, x_send, x_recv, part, held,
    y_send, y_recv, z_send, z_recv, g_own, yb_send, yb_recv, zb_send, zb_recv, gb_own, bh_send, bh_recv,
    bx_send, bx_recv, bs_recv, h_send, h_recv, sy_send, sy_recv, sz_send, sz_recv, dy_send, dy_recv, dz_send, dz_recv, row_sums,
    grad_t, gn, rows_out, normed_t, lpz, rows_z, lpx, rows_x, lpbd, rows_bd, normed,
    s_in, s_sib, r_sib, s_x, r_x, s_y, r_y, s_z, r_z, s_m, r_m, s_sl, r_sl,
):
    loads = [
        pltpu.make_async_copy(src, dst, s_in.at[i])
        for i, (src, dst) in enumerate((
            (grad_t_in, grad_t), (gn_in, gn), (rows_out_in, rows_out), (normed_t_in, normed_t), (lpz_in, lpz),
            (rows_z_in, rows_z), (lpx_in, lpx), (rows_x_in, rows_x), (lpbd_in, lpbd), (rows_bd_in, rows_bd),
            (normed_in, normed),
        ))
    ]
    for load in loads:
        load.start()
    who = peers(dp_n)
    meet(who)
    count = normed.shape[0]
    width = normed.shape[1]
    inner = lpx.shape[1]
    bc = 2 * bh_send.shape[1]
    quarter = width // 4
    span = count // units
    block = width // dp_n
    lines = who["lines"]

    def copy_sib(u):
        return push(sib_send.at[u], sib_recv.at[u], s_sib.at[u], r_sib.at[u], who["sib"])

    def copy_x(u):
        return push(x_send.at[u], x_recv.at[u], s_x.at[u], r_x.at[u], who["xn"])

    def product(u, q):
        cols = pl.ds(pl.multiple_of(q * quarter, quarter), quarter)
        if u < units:
            return nt(gn[u * span : (u + 1) * span, :], rows_out[cols, :])
        at = slice((u - units) * span, (u - units + 1) * span)
        return nt(lpx[at, :], rows_x[cols, :]) + nt(lpz[at, :], rows_z[cols, :]) + nt(lpbd[at, :], rows_bd[cols, :])

    def head_a(u):
        for k, q in enumerate(("sib_mine", "sib_other", "mine", "other")):
            p = product(u, who[q])
            if u >= units:
                at = slice((u - units) * span, (u - units + 1) * span)
                cols = pl.ds(pl.multiple_of(who[q] * quarter, quarter), quarter)
                inner_p = p * normed[at, cols].astype(F32)
                h_send[0:1, cols] += jnp.sum(inner_p, axis=0, keepdims=True)
                first = (u - units) * span
                lanes = slice(first % width, first % width + span)
                h_send[2 + first // width : 3 + first // width, lanes] += nt(
                    jnp.ones((8, quarter), BF), inner_p.astype(BF)
                )[0:1]
            if k < 2:
                sib_send[u, k] = p.astype(BF)
            else:
                part[u % 2, k - 2] = p
        copy_sib(u).start()

    def head_b(u):
        copy_sib(u).wait()
        x_send[u] = (part[u % 2, 1] + sib_recv[u, 1].astype(F32)).astype(BF)
        copy_x(u).start()
        held[u] = part[u % 2, 0] + sib_recv[u, 0].astype(F32)

    def head_c(u):
        copy_x(u).wait()
        total = held[u] + x_recv[u].astype(F32)
        if u < units:
            at = slice(u * span, (u + 1) * span)
            block_out[at, :] = (tokens[at, :].astype(F32) + total).astype(BF)
        else:
            first = (u - units) * span
            lanes = q_wide.shape[1]
            cols = pl.ds(pl.multiple_of(who["mine"] * quarter, quarter), quarter)
            for j in range(span // lanes):
                at = slice(first + j * lanes, first + (j + 1) * lanes)
                row, lane = (first + j * lanes) // width, (first + j * lanes) % width
                dots = jnp.transpose(jnp.broadcast_to(row_sums[row : row + 1, lane : lane + lanes], (lanes, lanes)))
                q = q_wide[at, :]
                coef = q * q * (dots / width)
                grad_tokens[at, :] = (
                    cot[at, :].astype(F32)
                    + q[:, 0:1] * vec[6:7, cols] * total[j * lanes : (j + 1) * lanes]
                    - tokens[at, :].astype(F32) * coef[:, 0:1]
                )

    def rows_of(line, pair):
        return pl.ds(pl.multiple_of((2 * line + pair) * block, block), block)

    def grad_a(v):
        left, right = ((grad_t, gn), (normed_t, lpz), (normed_t, lpx))[v // 2]
        cols = slice((v % 2) * (inner // 2), (v % 2 + 1) * (inner // 2))
        for side in (0, 1):
            pair = (1 - who["pair"]) if side == 0 else who["pair"]
            stacked = jnp.concatenate([left[rows_of(l, pair), :] for l in range(lines)], axis=0)
            value = nn(stacked, right[:, cols])
            if side == 0:
                y_send[v] = value.astype(BF)
                copy_y(v).start()
            else:
                g_own[v] = value

    def copy_y(v):
        return push(y_send.at[v], y_recv.at[v], s_y.at[v], r_y.at[v], who["yn"])

    def copy_z(v, k):
        to = (who["line_index"] + k) % lines
        return push(
            z_send.at[v, pl.ds(pl.multiple_of(to * block, block), block)],
            z_recv.at[v, k - 1], s_z.at[v, k - 1], r_z.at[v, k - 1], who["line"](k),
        )

    def each_line(fn):
        def step(k, carry):
            fn(k)
            return carry

        lax.fori_loop(1, lines, step, 0)

    def own_rows():
        return pl.ds(pl.multiple_of(who["line_index"] * block, block), block)

    def grad_b(v):
        copy_y(v).wait()
        g_own[v] = g_own[v] + y_recv[v].astype(F32)
        z_send[v] = g_own[v].astype(BF)
        each_line(lambda k: copy_z(v, k).start())

    def grad_c(v):
        each_line(lambda k: copy_z(v, k).wait())
        total = g_own[v, own_rows(), :]
        for k in range(lines - 1):
            total = total + z_recv[v, k].astype(F32)
        cols = slice((v % 2) * (inner // 2), (v % 2 + 1) * (inner // 2))
        (g_out, g_z, g_x)[v // 2][:, cols] = total

    half = bc // 2

    def copy_bh():
        return push(bh_send, bh_recv, s_m.at[0], r_m.at[0], who["sib"])

    def copy_yb():
        return push(yb_send, yb_recv, s_m.at[1], r_m.at[1], who["yn"])

    def copy_zb(k):
        to = (who["line_index"] + k) % lines
        return push(
            zb_send.at[pl.ds(pl.multiple_of(to * block, block), block)],
            zb_recv.at[k - 1], s_sl.at[0, k - 1], r_sl.at[0, k - 1], who["line"](k),
        )

    def copy_bx():
        return push(bx_send, bx_recv, s_m.at[2], r_m.at[2], who["xn"])

    def copy_bs():
        return push(bx_send, bs_recv, s_m.at[3], r_m.at[3], who["sib"])

    def bc_a():
        for side in (0, 1):
            pair = (1 - who["pair"]) if side == 0 else who["pair"]
            stacked = jnp.concatenate([normed_t[rows_of(l, pair), :] for l in range(lines)], axis=0)
            value = nn(stacked, lpbd[:, :bc])
            first = who["core"] == 0
            lo, hi = value[:, :half], value[:, half:]
            at = slice(side * lines * block, (side + 1) * lines * block)
            bh_send[at, :] = jnp.where(first, hi, lo).astype(BF)
            gb_own[at, :] = jnp.where(first, lo, hi)
        copy_bh().start()

    def bc_b():
        copy_bh().wait()
        rows = lines * block
        gb_own[...] = gb_own[...] + bh_recv[...].astype(F32)
        yb_send[...] = gb_own[:rows, :].astype(BF)
        copy_yb().start()

    def bc_c():
        rows = lines * block
        copy_yb().wait()
        gb_own[rows:, :] = gb_own[rows:, :] + yb_recv[...].astype(F32)
        zb_send[...] = gb_own[rows:, :].astype(BF)
        each_line(lambda k: copy_zb(k).start())

    def bc_d():
        each_line(lambda k: copy_zb(k).wait())
        at = pl.ds(pl.multiple_of(lines * block + who["line_index"] * block, block), block)
        total = gb_own[at, :]
        for k in range(lines - 1):
            total = total + zb_recv[k].astype(F32)
        bx_send[...] = total
        copy_bx().start()

    def bc_e():
        copy_bx().wait()
        bx_send[...] = bx_send[...] + bx_recv[...]
        copy_bs().start()

    def bc_f():
        copy_bs().wait()
        mine, theirs = bx_send[...], bs_recv[...]
        first = who["core"] == 0
        g_bc[:, :half] = jnp.where(first, mine, theirs)
        g_bc[:, half:] = jnp.where(first, theirs, mine)

    three = (("sib", 4), ("xn", 5), ("dg", 6))
    token_rows = count // width

    def copy_h(k):
        name, sem = three[k]
        return push(h_send, h_recv.at[k], s_m.at[sem], r_m.at[sem], who[name])

    def small_a():
        h_send[1:2, :] = acc[1:2, :]
        for k in range(3):
            copy_h(k).start()

    def copy_sy():
        return push(sy_send, sy_recv, s_m.at[7], r_m.at[7], who["yn"])

    def copy_dy():
        return push(dy_send, dy_recv, s_m.at[8], r_m.at[8], who["yn"])

    def copy_sz(k):
        return push(sz_send, sz_recv.at[k - 1], s_sl.at[1, k - 1], r_sl.at[1, k - 1], who["line"](k))

    def copy_dz(k):
        return push(dz_send, dz_recv.at[k - 1], s_sl.at[2, k - 1], r_sl.at[2, k - 1], who["line"](k))

    def dt_a():
        dy_send[...] = tn(lpbd[:, bc:], normed[...])[0:16, :].astype(BF)
        copy_dy().start()

    def dt_b():
        copy_dy().wait()
        dz_send[...] = (dy_send[...].astype(F32) + dy_recv[...].astype(F32)).astype(BF)
        each_line(lambda k: copy_dz(k).start())

    def dt_c():
        each_line(lambda k: copy_dz(k).wait())
        total = dz_send[...].astype(F32)
        for k in range(lines - 1):
            total = total + dz_recv[k].astype(F32)
        small_out[8:24, :] = total

    def small_b():
        for k in range(3):
            copy_h(k).wait()
        over_heads = h_send[...] + h_recv[0] + h_recv[1] + h_recv[2]
        row_sums[0:token_rows, :] = over_heads[2 : 2 + token_rows, :]
        sy_send[0:2, :] = over_heads[0:2, :]
        sy_send[2:8, :] = acc[2:8, :]
        copy_sy().start()

    def small_c():
        copy_sy().wait()
        sz_send[...] = sy_send[...] + sy_recv[...]
        each_line(lambda k: copy_sz(k).start())

    def small_d():
        each_line(lambda k: copy_sz(k).wait())
        total = sz_send[...]
        for k in range(lines - 1):
            total = total + sz_recv[k]
        small_out[0:8, :] = total

    h_send[...] = jnp.zeros_like(h_send)

    def seq(*steps):
        for fn, *args in steps:
            fn(*args)

    assert units == 4

    def load(*which):
        for i in which:
            loads[i].wait()

    load(0, 1)
    seq((grad_a, 0), (grad_a, 1))
    load(2)
    seq((head_a, 0), (head_a, 1), (head_b, 0), (head_a, 2), (head_b, 1), (head_a, 3), (head_b, 2))
    load(3, 8)
    seq((bc_a,), (head_b, 3))
    load(4)
    seq((grad_a, 2), (bc_b,), (grad_a, 3))
    load(5, 6, 7, 9, 10)
    seq((grad_b, 0), (head_a, 4), (dt_a,), (grad_b, 1), (grad_a, 4), (head_b, 4), (head_a, 5), (bc_c,), (head_b, 5))
    seq((grad_a, 5), (head_a, 6), (grad_b, 2), (head_b, 6), (head_a, 7), (small_a,), (grad_b, 3), (head_b, 7))
    seq((dt_b,), (small_b,), (head_c, 0), (head_c, 1), (head_c, 2), (head_c, 3), (bc_d,), (grad_c, 0), (grad_c, 1))
    seq((grad_b, 4), (small_c,), (grad_b, 5), (dt_c,), (bc_e,), (head_c, 4), (head_c, 5), (grad_c, 2), (grad_c, 3))
    seq((small_d,), (head_c, 6), (grad_c, 4), (bc_f,), (head_c, 7), (grad_c, 5))


def tail(dp_n, units, normed_t, normed, grad_t, gn, lpx, lpz, lpbd, rows_x, rows_z, rows_bd, rows_out, tokens, acc, cot, q_wide, vec, bc):
    count, width = normed.shape
    inner = lpx.shape[1]
    quarter = width // 4
    span = count // units
    block = width // dp_n
    lines = dp_n // 2
    half_rows = lines * block
    more = max(lines - 1, 1)
    vm = pltpu.VMEM
    dma = pltpu.SemaphoreType.DMA
    operands = (
        grad_t, gn, rows_out, normed_t, lpz, rows_z, lpx, rows_x, lpbd, rows_bd, normed, tokens, acc, cot, q_wide, vec,
    )
    sds = jax.ShapeDtypeStruct
    spec = pl.BlockSpec(memory_space=pltpu.VMEM)
    return pl.pallas_call(
        functools.partial(tail_kernel, dp_n, units),
        out_shape=[
            sds((count, quarter), BF), sds((count, quarter), F32),
            sds((block, inner), F32), sds((block, inner), F32), sds((block, inner), F32), sds((block, bc), F32),
            sds((24, width), F32),
        ],
        in_specs=[pl.BlockSpec(memory_space=pl.ANY)] * 11 + [spec] * 5,
        out_specs=[spec] * 7,
        scratch_shapes=[
            vm((2 * units, 2, span, quarter), BF), vm((2 * units, 2, span, quarter), BF),
            vm((2 * units, span, quarter), BF), vm((2 * units, span, quarter), BF),
            vm((2, 2, span, quarter), F32), vm((2 * units, span, quarter), F32),
            vm((6, half_rows, inner // 2), BF), vm((6, half_rows, inner // 2), BF),
            vm((6, half_rows, inner // 2), BF), vm((6, more, block, inner // 2), BF),
            vm((6, half_rows, inner // 2), F32),
            vm((half_rows, bc // 2), BF), vm((half_rows, bc // 2), BF),
            vm((half_rows, bc // 2), BF), vm((more, block, bc // 2), BF),
            vm((2 * half_rows, bc // 2), F32),
            vm((2 * half_rows, bc // 2), BF), vm((2 * half_rows, bc // 2), BF),
            vm((block, bc // 2), F32), vm((block, bc // 2), F32), vm((block, bc // 2), F32),
            vm((8, width), F32), vm((3, 8, width), F32),
            vm((8, width), F32), vm((8, width), F32), vm((8, width), F32), vm((more, 8, width), F32),
            vm((16, width), BF), vm((16, width), BF), vm((16, width), BF), vm((more, 16, width), BF),
            vm((8, width), F32),
        ]
        + [vm(a.shape, a.dtype) for a in operands[:11]]
        + [
            dma((11,)), dma((2 * units,)), dma((2 * units,)), dma((2 * units,)), dma((2 * units,)),
            dma((6,)), dma((6,)), dma((6, more)), dma((6, more)), dma((9,)), dma((9,)),
            dma((3, more)), dma((3, more)),
        ],
        compiler_params=pltpu.CompilerParams(
            collective_id=1, has_side_effects=True, vmem_limit_bytes=62 * 2**20
        ),
        name="tail",
    )(*operands)
def shares(ref_in, block_of, dp_n, width, send, recv, who):
    rows = ref_in.shape[0]
    lines = who["lines"]
    source = ref_in.at[:, width] if ref_in.shape[1] != width.size else ref_in

    def at(dp):
        return block_of.at[pl.ds(pl.multiple_of(dp * rows, rows), rows), width]

    def own():
        return push(source, at(who["dp"]), send.at[0], recv.at[0], who["yn"])

    def along(k):
        return push(source, at(who["dp"]), send.at[k], recv.at[k], who["line"](k))

    def onward(k):
        there = at(2 * ((who["line_index"] - k + lines) % lines) + who["pair"])
        return push(there, there, send.at[lines - 1 + k], recv.at[lines - 1 + k], who["yn"])

    return own, along, onward


def loop_line(lines, fn):
    def step(k, carry):
        fn(k)
        return carry

    lax.fori_loop(1, lines, step, 0)


def front_kernel(
    dp_n, heads, units, taps, bc,
    tokens, cot, w_x, w_bc, w_z, w_out, w_dt, conv_x, conv_bc, norm_gain, gate_gain, dt_bias, a_log, skip, starts, fill,
    vec, px_out, pbd_out, normed_out, normed_t_out, q_out, y_out, sin_out, parts, rows_x, rows_bd, rows_z, rows_out,
    own_dt, tok, wx, wbd, px, pbd, normed, normed_t, q, y, sin, own_w, own_cot, state, extx, extb, upper, spread,
    s_loc, s_sib, r_sib, s_x, r_x, s_f, r_f, s_cx, r_cx, s_cf, r_cf, s_w, r_w, s_out, s_y,
):
    who = peers(dp_n)
    count, quarter = tokens.shape
    width = 4 * quarter
    span = count // units
    lines = who["lines"]
    block, inner = w_x.shape
    blocks = sin.shape[0]
    chunk = count // blocks
    per = blocks // units
    pieces = s_cx.shape[0]
    cot_span = count // pieces
    here = pl.ds(pl.multiple_of(who["dp"] * block, block), block)
    own_half = pl.ds(pl.multiple_of(who["core"] * (bc // 2), bc // 2), bc // 2)
    dt_cols = pl.ds(bc, chunk)
    local = [
        pltpu.make_async_copy(src, dst, s_loc.at[k])
        for k, (src, dst) in enumerate((
            (tokens, tok.at[who["mine"]]), (w_x, wx.at[here]), (w_bc.at[:, own_half], wbd.at[here, own_half]),
            (w_z, own_w.at[0]), (w_out, own_w.at[1]), (cot, own_cot),
        ))
    ]
    for copy in local:
        copy.start()
    own_dt[...] = jnp.zeros_like(own_dt)
    own_dt[:, :heads] = w_dt[...]
    wbd[here, dt_cols] = own_dt[...]
    onto = [
        pltpu.make_async_copy(src, dst, s_loc.at[8 + k])
        for k, (src, dst) in enumerate((
            (own_w.at[0], rows_z.at[here]), (own_w.at[1], rows_out.at[here]), (own_cot, parts.at[who["mine"]]),
        ))
    ]
    meet(who)

    def rows(s, n=span):
        return pl.ds(pl.multiple_of(s * n, n), n)

    def to_x(s):
        return push(tokens.at[rows(s)], tok.at[who["mine"], rows(s)], s_x.at[s], r_x.at[s], who["xn"])

    def to_sib():
        return push(tokens, tok.at[who["mine"]], s_sib.at[0], r_sib.at[0], who["sib"])

    def forward(s):
        at = tok.at[who["other"], rows(s)]
        return push(at, at, s_f.at[s], r_f.at[s], who["sib"])

    def cot_x(j):
        at = rows(j, cot_span)
        return push(cot.at[at], parts.at[who["mine"], at], s_cx.at[j], r_cx.at[j], who["xn"])

    def cot_sib():
        return push(cot, parts.at[who["mine"]], s_sib.at[1], r_sib.at[1], who["sib"])

    def cot_forward(j):
        at = parts.at[who["other"], rows(j, cot_span)]
        return push(at, at, s_cf.at[j], r_cf.at[j], who["sib"])

    half = inner // 2
    cuts = [
        shares(ref, to, dp_n, cols, s_w.at[n], r_w.at[n], who)
        for n, (ref, to, cols) in enumerate((
            (w_x, wx, pl.ds(0, half)), (w_x, wx, pl.ds(half, half)), (w_bc, wbd, own_half), (own_dt, wbd, dt_cols),
            (w_z, rows_z, pl.ds(0, half)), (w_z, rows_z, pl.ds(half, half)),
            (w_out, rows_out, pl.ds(0, half)), (w_out, rows_out, pl.ds(half, half)),
        ))
    ]

    def offer(n):
        loop_line(lines, lambda k: cuts[n][1](k).start())

    def other_half():
        cols = wbd.at[:, own_half]
        return push(cols, cols, s_sib.at[2], r_sib.at[2], who["sib"])

    def pass_rows(n):
        own, along, onward = cuts[n]
        own().start()

        def one(k):
            along(k).wait()
            onward(k).start()

        loop_line(lines, one)

    def have(n):
        own, along, onward = cuts[n]
        own().wait()
        loop_line(lines, lambda k: onward(k).wait())

    def pass_cot(j):
        cot_x(j).wait()
        cot_forward(j).start()

    to_x(0).start()
    offer(0)
    for s in range(1, units):
        to_x(s).start()
    to_sib().start()
    for n in (1, 2, 3):
        offer(n)
    for j in range(pieces):
        cot_x(j).start()
    for n in (4, 5, 6, 7):
        offer(n)
    pack_vec(vec, conv_x, conv_bc, norm_gain, gate_gain, dt_bias, a_log, skip, starts, fill, chunk)
    set_upper(upper)
    set_spread(spread, heads)
    state[...] = jnp.zeros_like(state)
    extx[...] = jnp.zeros_like(extx)
    extb[...] = jnp.zeros_like(extb)
    par = read_vec(vec, heads, chunk, inner, bc, taps)
    gain = vec[6:7, :width]

    def out_copies(s):
        at = rows(s)
        every = slice(None)
        return [
            pltpu.make_async_copy(ref.at[to], out.at[to], s_out.at[n, s])
            for n, (ref, out, to) in enumerate((
                (normed, normed_out, (at,)), (normed_t, normed_t_out, (every, at)), (q, q_out, (at,)),
                (px, px_out, (at,)), (pbd, pbd_out, (at,)),
            ))
        ]

    def norm(s):
        at = rows(s)
        values = [tok[h, at, :].astype(F32) for h in range(4)]
        total = sum(jnp.sum(p * p, axis=1, keepdims=True) for p in values)
        inv = lax.rsqrt(total / width + EPS)
        q[at, :] = jnp.broadcast_to(inv, (span, q.shape[1]))
        for h in range(4):
            cols = slice(h * quarter, (h + 1) * quarter)
            value = (values[h] * inv * gain[:, cols]).astype(BF)
            normed[at, cols] = value
            normed_t[cols, at] = jnp.transpose(value)
        for copy in out_copies(s)[:3]:
            copy.start()

    def project(s):
        at = rows(s)
        pbd[at, :] = nn(normed[at, :], wbd[...])
        px[at, :] = nn(normed[at, :], wx[...])
        for copy in out_copies(s)[3:]:
            copy.start()

    local[0].wait()
    to_x(0).wait()
    forward(0).start()
    pass_rows(0)
    to_sib().wait()
    forward(0).wait()
    norm(0)
    to_x(1).wait()
    forward(1).start()
    pass_rows(1)
    forward(1).wait()
    norm(1)
    pass_rows(2)
    pass_rows(3)
    have(2)
    local[2].wait()
    other_half().start()
    to_x(2).wait()
    forward(2).start()
    for copy in local[3:]:
        copy.wait()
    for copy in onto:
        copy.start()
    cot_sib().start()
    forward(2).wait()
    norm(2)
    local[1].wait()
    for n in (0, 1, 3):
        have(n)
    other_half().wait()
    keep_rows = [
        pltpu.make_async_copy(wx, rows_x, s_loc.at[6]), pltpu.make_async_copy(wbd, rows_bd, s_loc.at[7]),
    ]
    for copy in keep_rows:
        copy.start()

    def last_tokens(s):
        to_x(s).wait()
        forward(s).start()

    def last_norm(s):
        forward(s).wait()
        norm(s)

    events = {1: [(last_tokens, units - 1)], 2: [(last_norm, units - 1)]}
    late = []
    plan = [(pass_rows, 4, 3), (pass_rows, 5, 7), (pass_rows, 6, 11)]
    plan += [(pass_cot, j, 5 + 2 * j) for j in range(pieces)] + [(pass_rows, 7, 15)]
    for fn, k, at in plan:
        if at < blocks:
            events.setdefault(at, []).append((fn, k))
        else:
            late.append((fn, k))

    def y_copies(c):
        at = rows(c, chunk)
        return (
            pltpu.make_async_copy(y.at[at], y_out.at[at], s_y.at[0, c]),
            pltpu.make_async_copy(sin.at[c], sin_out.at[c], s_y.at[1, c]),
        )

    def step(c, carry):
        for at, fns in events.items():

            @pl.when(c == at)
            def _(fns=fns):
                for fn, k in fns:
                    fn(k)

        @pl.when(c % per == 0)
        def _():
            project(c // per)

        at = rows(c, chunk)
        y_c, enter = scan_step(
            heads, par, read_block(vec, c, chunk), px.at[at], pbd.at[at], upper, spread, state, extx, extb
        )
        y[at, :] = y_c
        sin[c] = enter
        for copy in y_copies(c):
            copy.start()
        return carry

    lax.fori_loop(0, blocks, step, 0)
    for fn, k in late:
        fn(k)

    def end_y(c, carry):
        for copy in y_copies(c):
            copy.wait()
        return carry

    lax.fori_loop(0, blocks, end_y, 0)
    for s in range(units):
        for copy in out_copies(s):
            copy.wait()
    for copy in onto + keep_rows:
        copy.wait()
    cot_sib().wait()
    for j in range(pieces):
        cot_forward(j).wait()
    for n in (4, 5, 6, 7):
        have(n)


def front(dp_n, tokens, cot, w_x, w_bc, w_z, w_out, w_dt, conv_x, conv_bc, norm_gain, gate_gain, *scalars):
    count, quarter = tokens.shape
    width = 4 * quarter
    inner, heads = w_x.shape[1], w_dt.shape[1]
    taps, bc = conv_bc.shape
    blocks = scalars[-1].shape[0]
    chunk = count // blocks
    wide = bc + chunk
    units, pieces = 4, 8
    vm, dma, sds = pltpu.VMEM, pltpu.SemaphoreType.DMA, jax.ShapeDtypeStruct
    hbm, vmem = pl.BlockSpec(memory_space=pl.ANY), pl.BlockSpec(memory_space=pltpu.VMEM)
    ways = dp_n - 1
    outs = [
        sds((24 + blocks, width), F32),
        sds((count, inner), F32), sds((count, wide), F32), sds((count, width), BF), sds((width, count), BF),
        sds((count, 128), F32), sds((count, inner), F32), sds((blocks, bc // 2, inner), BF),
        sds((4, count, quarter), BF), sds((width, inner), BF), sds((width, wide), BF), sds((width, inner), BF),
        sds((width, inner), BF),
    ]
    return pl.pallas_call(
        functools.partial(front_kernel, dp_n, heads, units, taps, bc),
        out_shape=outs,
        in_specs=[hbm] * 6 + [vmem] * 5 + [pl.BlockSpec(memory_space=pltpu.SMEM)] * 5,
        out_specs=[vmem] + [hbm] * (len(outs) - 1),
        scratch_shapes=[
            vm((w_x.shape[0], chunk), BF),
            vm((4, count, quarter), BF), vm((width, inner), BF), vm((width, wide), BF),
            vm((count, inner), F32), vm((count, wide), F32), vm((count, width), BF), vm((width, count), BF),
            vm((count, 128), F32), vm((count, inner), F32), vm((blocks, bc // 2, inner), BF),
            vm((2,) + w_z.shape, BF), vm(cot.shape, BF),
            vm((bc // 2, inner), F32), vm((chunk + 8, inner), F32), vm((chunk + 8, bc), F32),
            vm((chunk, chunk), BF), vm((chunk, 3 * inner), BF),
            dma((11,)), dma((3,)), dma((3,)), dma((units,)), dma((units,)), dma((units,)), dma((units,)),
            dma((pieces,)), dma((pieces,)), dma((pieces,)), dma((pieces,)),
            dma((8, ways)), dma((8, ways)), dma((5, units)), dma((2, blocks)),
        ],
        compiler_params=pltpu.CompilerParams(
            collective_id=2, has_side_effects=True, vmem_limit_bytes=58 * 2**20
        ),
        name="front",
    )(
        tokens, cot, w_x, w_bc, w_z, w_out, w_dt, conv_x, conv_bc, norm_gain[None, :], gate_gain[None, :], *scalars
    )


def body(
    tokens, cotangent, starts, fill, norm_gain, w_x, w_z, w_dt, w_bc, conv_x, conv_bc, dt_bias, a_log, skip,
    gate_gain, w_out,
):
    heads_n = lax.axis_size("heads")
    dp_n = lax.axis_size("dp")
    head_index = lax.axis_index("heads")
    dp_index = lax.axis_index("dp")
    count, columns = tokens.shape
    width = columns * heads_n
    blocks = starts.shape[0]
    chunk = count // blocks
    inner = w_x.shape[1]
    heads = w_dt.shape[1]
    taps, bc = conv_bc.shape
    vec, px, pbd, normed, normed_t, q_wide, y, sin, parts, rows_x, rows_bd, rows_z, rows_out = front(
        dp_n, tokens, cotangent, w_x, w_bc, w_z, w_out, w_dt, conv_x, conv_bc, norm_gain, gate_gain, dt_bias, a_log,
        skip, starts, fill,
    )
    pz, ggn, grad_t, sums = gate(dp_n, blocks, normed, rows_z, rows_out, parts, y, vec)
    lpx, lpz, lpbd, gn, acc = scan_backward(
        ggn, y, pz, px, pbd, sin, sums, vec, heads, taps, bc, inner * heads_n
    )
    block_out, grad_tokens, grad_w_x, grad_w_z, grad_w_out, grad_w_bc, small = tail(
        dp_n, 4, normed_t, normed, grad_t, gn, lpx, lpz, lpbd, rows_x, rows_z, rows_bd, rows_out,
        tokens, acc, cotangent, q_wide, vec, bc,
    )
    block = width // dp_n
    own_gain = lax.dynamic_slice_in_dim(norm_gain, head_index * columns, columns, 0)
    gain_sum = lax.dynamic_slice_in_dim(small[0], head_index * columns, columns, 0)
    grad_w_dt = lax.dynamic_slice_in_dim(small[8 : 8 + heads], dp_index * block, block, 1).T
    return (
        block_out, grad_tokens, gain_sum / own_gain, grad_w_x, grad_w_z, grad_w_dt, grad_w_bc,
        small[2:4].reshape(taps, inner), small[1].reshape(taps, bc), small[5, :heads], small[5, heads : 2 * heads],
        small[5, 2 * heads : 3 * heads], small[4, :inner], grad_w_out,
    )


def solution(mesh):
    placed = (
        P("dp", "heads"),
        P("dp", "heads"),
        P("dp"),
        P("dp"),
        P(),
        P("dp", "heads"),
        P("dp", "heads"),
        P("dp", "heads"),
        P("dp", None),
        P(None, "heads"),
        P(),
        P("heads"),
        P("heads"),
        P("heads"),
        P("heads"),
        P("dp", "heads"),
    )
    return jax.shard_map(
        body,
        mesh=mesh,
        in_specs=placed,
        out_specs=(
            P("dp", "heads"),
            P("dp", "heads"),
            P("heads"),
            P("dp", "heads"),
            P("dp", "heads"),
            P("dp", "heads"),
            P("dp", None),
            P(None, "heads"),
            P(),
            P("heads"),
            P("heads"),
            P("heads"),
            P("heads"),
            P("dp", "heads"),
        ),
        check_vma=False,
    )
```

```python
import functools
import jax
import jax.numpy as jnp
from jax import lax
from jax.experimental import pallas as pl
from jax.experimental.pallas import tpu as pltpu
from jax.sharding import PartitionSpec as P

HD = 64
EPS = 1e-05
F32 = jnp.float32
BF = jnp.bfloat16
NEG = -1e30
MESH = pl.DeviceIdType.MESH


def nn(a, b):
    return lax.dot_general(a, b, (((1,), (0,)), ((), ())), preferred_element_type=F32)


def nt(a, b):
    return lax.dot_general(a, b, (((1,), (1,)), ((), ())), preferred_element_type=F32)


def tn(a, b):
    return lax.dot_general(a, b, (((0,), (0,)), ((), ())), preferred_element_type=F32)


def split2(v):
    hi = v.astype(BF).astype(F32)
    return hi, v - hi


def split3(v):
    hi = v.astype(BF).astype(F32)
    rest = v - hi
    mid = rest.astype(BF).astype(F32)
    return hi, mid, rest - mid


def softplus(v):
    return jnp.maximum(v, 0.0) + jnp.log1p(jnp.exp(-jnp.abs(v)))


def sigmoid(v):
    return 1.0 / (1.0 + jnp.exp(-v))


def iota2(rows, cols, axis):
    return lax.broadcasted_iota(jnp.int32, (rows, cols), axis)


def zero_one(cond):
    return jnp.where(cond, 1.0, 0.0).astype(BF)


def set_upper(upper):
    upper[...] = zero_one(iota2(*upper.shape, 0) <= iota2(*upper.shape, 1))


def set_spread(spread, heads):
    rows, lanes = iota2(*spread.shape, 0), iota2(*spread.shape, 1)
    inner = heads * HD
    base = heads * (1 + 2 * (lanes // inner)) + (lanes % inner) // HD
    spread[...] = zero_one(jnp.logical_or(rows == base, rows == base + heads))


def set_gather(gather, ones_h, heads):
    for q in range(3):
        rows, lanes = iota2(*gather.shape[1:], 0), iota2(*gather.shape[1:], 1)
        gather[q] = zero_one(lanes == q * heads + rows // HD)
    rows, lanes = iota2(*ones_h.shape, 0), iota2(*ones_h.shape, 1)
    ones_h[...] = zero_one(lanes == heads + rows // ones_h.shape[1])


def conv_from(ext, taps, rows, halo):
    n = taps.shape[0]
    out = taps[n - 1 : n, :] * ext[pl.ds(halo, rows), :]
    for k in range(1, n):
        out = out + taps[n - 1 - k : n - k, :] * ext[pl.ds(halo - k, rows), :]
    return out


def dt_rows(pdt, bias, rate, fill, heads, upper):
    chunk = pdt.shape[0]
    pre = jnp.transpose(pdt)[:heads] + bias
    live = (iota2(heads, chunk, 1).astype(F32) < fill).astype(F32)
    dt = softplus(pre) * live
    hi, mid, low = split3(dt * rate)
    stacked = jnp.concatenate([hi, mid, low], axis=0).astype(BF)
    summed = nn(stacked, upper)
    run = summed[:heads] + summed[heads : 2 * heads] + summed[2 * heads :]
    return pre, live, dt, run


def spread_all(run, dt, heads, chunk, spread):
    last = run[:, chunk - 1 : chunk]
    e_in = jnp.exp(run)
    e_out = jnp.exp(last - run)
    parts = [run]
    for v in (dt, e_in, e_out):
        parts.extend(split2(v))
    used = heads * len(parts)
    if used < chunk:
        parts.append(jnp.zeros((chunk - used, chunk), F32))
    cols = jnp.transpose(jnp.concatenate(parts, axis=0))
    return cols, nn(cols.astype(BF), spread)


def pair_stack(v, low_lanes):
    zero = jnp.zeros_like(v)
    return jnp.concatenate([jnp.where(low_lanes, v, zero), jnp.where(low_lanes, zero, v)], axis=0)


def read_vec(vec, heads, chunk, inner, bc, taps):
    return dict(
        convx=vec[0:taps, :inner], skip=vec[4:5, :inner], gain=vec[5:6, :inner],
        bias=vec[8 : 8 + heads, :chunk], rate=vec[8 : 8 + heads, chunk : 2 * chunk], convbc=vec[16 : 16 + taps, :bc],
    )


def read_block(vec, c, chunk):
    row = vec[pl.ds(24 + c, 1), :]
    return row[:, 0:1] > 0.5, row[:, chunk : chunk + 1], row[:, 2 * chunk : 2 * chunk + 1] > 0.5


def pack_vec(vec, conv_x, conv_bc, norm_gain, gate_gain, dt_bias, a_log, skip, starts, fill, chunk):
    taps, inner = conv_x.shape
    vec[...] = jnp.zeros_like(vec)
    vec[0:taps, :inner] = conv_x[...]
    vec[16 : 16 + taps, : conv_bc.shape[1]] = conv_bc[...]
    vec[5:6, :inner] = gate_gain[...]
    vec[6:7, :] = norm_gain[...]
    head = iota2(1, inner, 1) // HD
    skips = jnp.zeros((1, inner), F32)
    for h in range(dt_bias.shape[0]):
        skips = jnp.where(head == h, skip[h], skips)
        vec[8 + h : 9 + h, 0:chunk] = jnp.full((1, chunk), dt_bias[h], F32)
        vec[8 + h : 9 + h, chunk : 2 * chunk] = -jnp.exp(jnp.full((1, chunk), a_log[h], F32))
    vec[4:5, :inner] = skips
    blocks = starts.shape[0]
    for c in range(blocks):
        row = slice(24 + c, 25 + c)
        vec[row, 0:chunk] = jnp.full((1, chunk), 1 - starts[c], jnp.int32).astype(F32)
        vec[row, chunk : 2 * chunk] = jnp.full((1, chunk), fill[c], jnp.int32).astype(F32)
        if c + 1 < blocks:
            vec[row, 2 * chunk : 3 * chunk] = jnp.full((1, chunk), 1 - starts[c + 1], jnp.int32).astype(F32)


def scan_step(heads, par, block, px, pbd, upper, spread, state, extx, extb):
    chunk, inner = px.shape
    bc = par["convbc"].shape[1]
    ns = bc // 2
    keep, n_live, _ = block
    state[...] = jnp.where(keep, state[...], 0.0)
    extx[0:8, :] = jnp.where(keep, extx[chunk : chunk + 8, :], 0.0)
    extb[0:8, :] = jnp.where(keep, extb[chunk : chunk + 8, :], 0.0)
    extx[8 : chunk + 8, :] = px[...]
    extb[8 : chunk + 8, :] = pbd[:, :bc]

    u = conv_from(extx, par["convx"], chunk, 8)
    x = u * sigmoid(u) * (iota2(chunk, inner, 0).astype(F32) < n_live).astype(F32)
    ub = conv_from(extb, par["convbc"], chunk, 8)
    act = (ub * sigmoid(ub) * (iota2(chunk, bc, 0).astype(F32) < n_live).astype(F32)).astype(BF)
    b, cc = act[:, :ns], act[:, ns:]

    _, _, dt, run = dt_rows(pbd[:, bc:], par["bias"], par["rate"], n_live, heads, upper[...])
    cols, wide = spread_all(run, dt, heads, chunk, spread[...])
    dt_w, ein_w, eout_w = wide[:, :inner], wide[:, inner : 2 * inner], wide[:, 2 * inner :]

    xd = x * dt_w
    xdb = xd.astype(BF)
    scores = nt(cc, b)
    tri = iota2(chunk, chunk, 0) >= iota2(chunk, chunk, 1)
    low_lanes = iota2(chunk, 2 * HD, 1) < HD
    diag = []
    for j in range(heads // 2):
        mix = []
        for h in (2 * j, 2 * j + 1):
            spread_h = cols[:, h : h + 1] - run[h : h + 1, :]
            mix.append((scores * jnp.exp(jnp.where(tri, spread_h, NEG))).astype(BF))
        pair = pair_stack(xdb[:, 2 * HD * j : 2 * HD * (j + 1)], low_lanes)
        diag.append(nn(jnp.concatenate(mix, axis=1), pair))
    enter = state[...]
    enter_b = enter.astype(BF)
    y = jnp.concatenate(diag, axis=1) + ein_w * nn(cc, enter_b) + par["skip"] * x
    state[...] = ein_w[chunk - 1 : chunk, :] * enter + tn(b, (xd * eout_w).astype(BF))
    return y, enter_b


def pair_rows(dp_n, block, pair, values):
    return jnp.concatenate(
        [values[pl.ds(pl.multiple_of((2 * l + pair) * block, block), block), :] for l in range(dp_n // 2)], axis=0
    )


def gate_kernel(
    dp_n, normed, rows_z, rows_out, parts, y, vec, pz, ggn, sums, gn, y_send, g_own,
    h_send, h_recv, gated_all, grad_t, s_h, r_h,
):
    i = pl.program_id(0)
    who = peers(dp_n)
    names = ("sib", "xn", "dg")
    barrier = pltpu.get_barrier_semaphore()
    span, quarter = parts.shape[1:]
    blocks, chunk = h_send.shape[1:]
    inner = y.shape[1]
    here = pl.ds(pl.multiple_of(i * span, span), span)

    @pl.when(i == 0)
    def _():
        for name in names:
            pl.semaphore_signal(barrier, inc=1, device_id=who[name], device_id_type=MESH)

    z = nn(normed[...], rows_z[...])
    pz[...] = z
    g = nn(parts[0], rows_out[0:quarter, :])
    for k in range(1, 4):
        g = g + nn(parts[k], rows_out[k * quarter : (k + 1) * quarter, :])
    ggn[...] = g
    for k in range(4):
        grad_t[k * quarter : (k + 1) * quarter, here] = jnp.transpose(parts[k])
    gated = y[...] * (z * sigmoid(z))
    gated_all[here, :] = gated
    ones = jnp.ones((8, inner), BF)
    for k, value in enumerate((gated * gated, gated * vec[5:6, :inner] * g)):
        row = nt(ones, value.astype(BF))
        for j in range(span // chunk):
            h_send[k, pl.ds(i * (span // chunk) + j, 1), :] = row[0:1, j * chunk : (j + 1) * chunk]

    @pl.when(i == pl.num_programs(0) - 1)
    def _():
        pl.semaphore_wait(barrier, 3)
        copies = [push(h_send, h_recv.at[k], s_h.at[k], r_h.at[k], who[name]) for k, name in enumerate(names)]
        for copy in copies:
            copy.start()
        for copy in copies:
            copy.wait()
        sums[...] = h_send[...] + h_recv[0] + h_recv[1] + h_recv[2]
        gain = vec[5:6, :inner]
        squares = jnp.transpose(
            jnp.concatenate([sums[0], jnp.zeros((chunk - blocks, chunk), F32)], axis=0)
        )
        inv = lax.rsqrt(squares / (4 * inner) + EPS)
        for b in range(blocks):
            at = slice(b * chunk, (b + 1) * chunk)
            gn[at, :] = (gated_all[at, :] * inv[:, b : b + 1] * gain).astype(BF)
        block = grad_t.shape[0] // dp_n
        for v in range(2):
            cols = slice(v * (inner // 2), (v + 1) * (inner // 2))
            y_send[v] = nn(pair_rows(dp_n, block, 1 - who["pair"], grad_t), gn[:, cols]).astype(BF)
            g_own[v] = nn(pair_rows(dp_n, block, who["pair"], grad_t), gn[:, cols])


def gate(dp_n, blocks, normed, rows_z, rows_out, parts, y, vec):
    count, width = normed.shape
    inner = y.shape[1]
    chunk = count // blocks
    steps = 8
    span = count // steps
    quarter = width // 4
    sds = jax.ShapeDtypeStruct
    rows = lambda w: pl.BlockSpec((span, w), lambda i: (i, 0))
    whole = lambda shape: pl.BlockSpec(shape, lambda i: (0,) * len(shape))
    halves = (2, width // 2, inner // 2)
    return pl.pallas_call(
        functools.partial(gate_kernel, dp_n),
        grid=(steps,),
        in_specs=[
            rows(width), whole(rows_z.shape), whole(rows_out.shape),
            pl.BlockSpec((4, span, quarter), lambda i: (0, i, 0)), rows(inner), whole(vec.shape),
        ],
        out_specs=[
            rows(inner), rows(inner), whole((2, blocks, chunk)), whole((count, inner)), whole(halves), whole(halves),
        ],
        out_shape=[
            sds((count, inner), F32), sds((count, inner), F32), sds((2, blocks, chunk), F32), sds((count, inner), BF),
            sds(halves, BF), sds(halves, F32),
        ],
        scratch_shapes=[
            pltpu.VMEM((2, blocks, chunk), F32), pltpu.VMEM((3, 2, blocks, chunk), F32),
            pltpu.VMEM((count, inner), F32), pltpu.VMEM((width, count), BF),
            pltpu.SemaphoreType.DMA((3,)), pltpu.SemaphoreType.DMA((3,)),
        ],
        compiler_params=pltpu.CompilerParams(
            collective_id=4, has_side_effects=True, vmem_limit_bytes=58 * 2**20
        ),
        name="gate",
    )(normed, rows_z, rows_out, parts, y, vec)


def sums_beside_scan(
    dp_n, gn, rows_out, tokens, y_send, g_in, block_out, g_out,
    sib_send, sib_recv, x_send, x_recv, part, held, y_recv, z_send, z_recv, g_own,
    s_sib, r_sib, s_x, r_x, s_y, r_y, s_z, r_z,
):
    i = pl.program_id(0)
    blocks = pl.num_programs(0)
    who = peers(dp_n)
    lines = who["lines"]
    chunk = gn.shape[0]
    quarter = tokens.shape[1]
    block = g_out.shape[0]
    half = g_out.shape[1] // 2

    def copy_sib(k):
        return push(sib_send.at[k], sib_recv.at[k], s_sib.at[k], r_sib.at[k], who["sib"])

    def copy_x(k):
        return push(x_send.at[k], x_recv.at[k], s_x.at[k], r_x.at[k], who["xn"])

    def copy_y(v):
        return push(y_send.at[v], y_recv.at[v], s_y.at[v], r_y.at[v], who["yn"])

    def copy_z(v, k):
        to = (who["line_index"] + k) % lines
        return push(
            z_send.at[v, pl.ds(pl.multiple_of(to * block, block), block)],
            z_recv.at[v, k - 1], s_z.at[v, k - 1], r_z.at[v, k - 1], who["line"](k),
        )

    @pl.when(i == 0)
    def _():
        meet(who)
        for v in range(2):
            copy_y(v).start()

    def first(k):
        for n, q in enumerate(("sib_mine", "sib_other", "mine", "other")):
            cols = pl.ds(pl.multiple_of(who[q] * quarter, quarter), quarter)
            p = nt(gn[...], rows_out[cols, :])
            if n < 2:
                sib_send[k, n] = p.astype(BF)
            else:
                part[k % 2, n - 2] = p
        copy_sib(k).start()

    def second(k):
        copy_sib(k).wait()
        x_send[k] = (part[k % 2, 1] + sib_recv[k, 1].astype(F32)).astype(BF)
        copy_x(k).start()
        held[k] = part[k % 2, 0] + sib_recv[k, 0].astype(F32)

    def third(k):
        copy_x(k).wait()
        at = pl.ds(pl.multiple_of((blocks - 1 - k) * chunk, chunk), chunk)
        block_out[at, :] = (tokens[at, :].astype(F32) + held[k] + x_recv[k].astype(F32)).astype(BF)

    def grad_b(v):
        copy_y(v).wait()
        g_own[v] = g_in[v] + y_recv[v].astype(F32)
        z_send[v] = g_own[v].astype(BF)
        loop_line(lines, lambda k: copy_z(v, k).start())

    def grad_c(v):
        loop_line(lines, lambda k: copy_z(v, k).wait())
        total = g_own[v, pl.ds(pl.multiple_of(who["line_index"] * block, block), block), :]
        for k in range(lines - 1):
            total = total + z_recv[v, k].astype(F32)
        g_out[:, v * half : (v + 1) * half] = total

    for v, at in ((0, 4), (1, 7)):

        @pl.when(i == at)
        def _(v=v):
            grad_b(v)

    @pl.when(i >= 1)
    def _():
        second(i - 1)

    @pl.when(i >= 4)
    def _():
        third(i - 4)

    first(i)

    def finish():
        last = blocks - 1
        second(last)
        for v in range(2):
            grad_c(v)
        for k in range(3, -1, -1):
            third(last - k)

    return finish


def scan_bwd_kernel(
    heads, total_inner, taps_n, bc, dp_n, ggn, y, pz, px, px_halo, pbd, pbd_halo, sin, rows, vec, gn, rows_out, tokens,
    y_send, g_in,
    lpx, lpz, lpbd, acc, block_out, g_out, dstate, extx, extb, dux, dub, acc_x, acc_bc, acc_s, upper, spread, gather, ones_h,
    *beside,
):
    finish = sums_beside_scan(dp_n, gn, rows_out, tokens, y_send, g_in, block_out, g_out, *beside)
    i = pl.program_id(0)
    blocks = pl.num_programs(0)
    c = blocks - 1 - i
    chunk, inner = px.shape
    ns = bc // 2
    par = read_vec(vec, heads, chunk, inner, bc, taps_n)
    keep, n_live, keep_next = read_block(vec, c, chunk)
    taps, taps_b, bias, rate, skip, gain = (par[k] for k in ("convx", "convbc", "bias", "rate", "skip", "gain"))

    @pl.when(i == 0)
    def _():
        for ref in (dstate, dux, dub, acc_x, acc_bc, acc_s):
            ref[...] = jnp.zeros_like(ref)
        set_upper(upper)
        set_spread(spread, heads)
        set_gather(gather, ones_h, heads)

    moved = jnp.transpose(
        jnp.concatenate(
            [rows[0, pl.ds(c, 1), :], rows[1, pl.ds(c, 1), :], jnp.zeros((chunk - 2, chunk), F32)], axis=0
        )
    )
    inv = lax.rsqrt(moved[:, 0:1] / total_inner + EPS)
    coef = inv * inv * inv * (moved[:, 1:2] / total_inner)
    z = pz[...]
    sz = sigmoid(z)
    silu_z = z * sz
    yv = y[...]
    gated = yv * silu_z
    g = ggn[...]
    d_gated = inv * (g * gain) - gated * coef
    lpz[...] = (d_gated * yv * (sz * (1.0 + z * (1.0 - sz)))).astype(BF)
    dy = d_gated * silu_z
    acc_x[taps_n : taps_n + 1, :] += jnp.sum(g * gated * inv, axis=0, keepdims=True)

    extx[0:8, :] = jnp.where(keep, px_halo[...], 0.0)
    extb[0:8, :] = jnp.where(keep, pbd_halo[:, :bc], 0.0)
    extx[8 : chunk + 8, :] = px[...]
    extb[8 : chunk + 8, :] = pbd[:, :bc]
    live_x = (iota2(chunk, inner, 0).astype(F32) < n_live).astype(F32)
    live_b = (iota2(chunk, bc, 0).astype(F32) < n_live).astype(F32)
    u = conv_from(extx, taps, chunk, 8)
    su = sigmoid(u)
    x = u * su * live_x
    dx_du = su * (1.0 + u * (1.0 - su)) * live_x
    ub = conv_from(extb, taps_b, chunk, 8)
    sb = sigmoid(ub)
    act = (ub * sb * live_b).astype(BF)
    db_du = sb * (1.0 + ub * (1.0 - sb)) * live_b
    b, cc = act[:, :ns], act[:, ns:]

    pre, live, dt, run = dt_rows(pbd[:, bc:], bias, rate, n_live, heads, upper[...])
    cols, wide = spread_all(run, dt, heads, chunk, spread[...])
    dt_w, ein_w, eout_w = wide[:, :inner], wide[:, inner : 2 * inner], wide[:, 2 * inner :]
    xd = x * dt_w
    xdb = xd.astype(BF)
    dyb = dy.astype(BF)
    acc_x[taps_n + 1 : taps_n + 2, :] += jnp.sum(dy * x, axis=0, keepdims=True)

    scores_t = nt(b, cc)
    tri = iota2(chunk, chunk, 0) <= iota2(chunk, chunk, 1)
    low_lanes = iota2(chunk, 2 * HD, 1) < HD
    d_scores_t = jnp.zeros((chunk, chunk), F32)
    dxd = []
    pulls = []
    read_sums = []
    for j in range(heads // 2):
        span = slice(2 * HD * j, 2 * HD * (j + 1))
        dy_pair = pair_stack(dyb[:, span], low_lanes)
        x_pair = pair_stack(xdb[:, span], low_lanes)
        d_mix = nt(x_pair, dyb[:, span])
        mix = []
        for k in (0, 1):
            h = 2 * j + k
            spread_h = run[h : h + 1, :] - cols[:, h : h + 1]
            fade = jnp.exp(jnp.where(tri, spread_h, NEG))
            m = scores_t * fade
            dm = d_mix[k * chunk : (k + 1) * chunk]
            d_scores_t = d_scores_t + dm * fade
            pull = (dm * m).astype(BF)
            pulls.append(pull)
            read_sums.append(jnp.sum(pull.astype(F32), axis=0, keepdims=True))
            mix.append(m.astype(BF))
        dxd.append(nn(jnp.concatenate(mix, axis=1), dy_pair))
    source_sums = nn(jnp.concatenate(pulls, axis=1), ones_h[...])
    read_rows = jnp.concatenate(read_sums, axis=0)

    d_state = jnp.where(keep_next, dstate[...], 0.0)
    d_state_b = d_state.astype(BF)
    enter_b = sin[0]
    edy = ein_w * dy
    edyb = edy.astype(BF)
    readings = nn(cc, enter_b)
    from_state = nn(b, d_state_b) * eout_w
    d_xd = jnp.concatenate(dxd, axis=1) + from_state
    q1 = edy * readings
    q2 = xd * from_state
    decay = ein_w[chunk - 1 : chunk, :]
    dstate[...] = decay * d_state + tn(cc, edyb)
    d_cb = tn(d_scores_t.astype(BF), b) + nt(edyb, enter_b)
    d_b = nn(d_scores_t.astype(BF), cc) + nt((xd * eout_w).astype(BF), d_state_b)

    sums = (
        nn((d_xd * x).astype(BF), gather[0])
        + nn((q1 - q2).astype(BF), gather[1])
        + nn(q2.astype(BF), gather[2])
        - source_sums
    )
    sums_t = jnp.transpose(sums)
    dt_direct = sums_t[:heads]
    d_run = sums_t[heads : 2 * heads] + read_rows
    whole_q2 = jnp.sum(sums_t[2 * heads : 3 * heads], axis=1, keepdims=True)
    kept = jnp.sum(enter_b.astype(F32) * d_state, axis=0, keepdims=True) * decay
    kept_hi, kept_lo = split2(kept)
    kept_two = jnp.concatenate([kept_hi, kept_lo, jnp.zeros((6, inner), F32)], axis=0).astype(BF)
    kept_rows = nn(kept_two, gather[0])
    kept_cols = jnp.transpose(
        jnp.concatenate([kept_rows[0:1] + kept_rows[1:2], jnp.zeros((chunk - 1, chunk), F32)], axis=0)
    )
    d_last = whole_q2 + kept_cols[:heads, 0:1]
    hi, mid, low = split3(d_run)
    back = nt(jnp.concatenate([hi, mid, low], axis=0).astype(BF), upper[...])
    d_a = back[:heads] + back[heads : 2 * heads] + back[2 * heads :] + d_last
    d_dt = dt_direct + d_a * rate
    d_pre = d_dt * live * sigmoid(pre)
    acc_s[0:heads, :] += d_pre
    acc_s[heads : 2 * heads, :] += d_a * dt * rate

    def conv_back(d_u, du_ref, ext_ref, tap_values, acc):
        du_ref[chunk : chunk + 8, :] = jnp.where(keep_next, du_ref[0:8, :], 0.0)
        du_ref[0:chunk, :] = d_u
        out = tap_values[taps_n - 1 : taps_n, :] * d_u
        acc[taps_n - 1 : taps_n, :] += jnp.sum(d_u * ext_ref[8 : chunk + 8, :], axis=0, keepdims=True)
        for k in range(1, taps_n):
            row = taps_n - 1 - k
            out = out + tap_values[row : row + 1, :] * du_ref[pl.ds(k, chunk), :]
            acc[row : row + 1, :] += jnp.sum(
                d_u * ext_ref[pl.ds(8 - k, chunk), :], axis=0, keepdims=True
            )
        return out

    d_x = d_xd * dt_w + skip * dy
    lpx[...] = conv_back(d_x * dx_du, dux, extx, taps, acc_x).astype(BF)
    d_act = jnp.concatenate([d_b, d_cb], axis=1)
    lpbd[:, :bc] = conv_back(d_act * db_du, dub, extb, taps_b, acc_bc).astype(BF)
    pad = jnp.concatenate([d_pre, jnp.zeros((chunk - heads, chunk), F32)], axis=0)
    lpbd[:, bc:] = jnp.transpose(pad).astype(BF)

    @pl.when(i == blocks - 1)
    def _():
        acc[...] = jnp.zeros_like(acc)
        for k in range(taps_n):
            acc[1:2, k * bc : (k + 1) * bc] = acc_bc[k : k + 1, :]
        per = acc.shape[1] // inner
        for k in range(taps_n + 1):
            acc[2 + k // per : 3 + k // per, (k % per) * inner : (k % per + 1) * inner] = acc_x[k : k + 1, :]
        per_head = jnp.sum(
            jnp.transpose(jnp.concatenate([acc_s[...], jnp.zeros((chunk - 2 * heads, chunk), F32)], axis=0)),
            axis=0, keepdims=True,
        )
        three = jnp.concatenate(split3(acc_x[taps_n + 1 : taps_n + 2, :]) + (jnp.zeros((5, inner), F32),), axis=0)
        skips = jnp.sum(nn(three.astype(BF), gather[2]), axis=0, keepdims=True)
        acc[5:6, 0:chunk] = per_head + skips
        finish()


def scan_backward(
    dp_n, ggn, y, pz, px, pbd, sin, rows, vec, gn, rows_out, tokens, y_send, g_own, heads, taps, bc, total_inner
):
    count, inner = px.shape
    blocks = sin.shape[0]
    chunk = count // blocks
    whole = lambda a: pl.BlockSpec(a.shape, lambda i: (0,) * a.ndim)
    back = lambda w: pl.BlockSpec((chunk, w), lambda i: (blocks - 1 - i, 0))
    halo = lambda w: pl.BlockSpec((8, w), lambda i: (jnp.maximum((blocks - 1 - i) * (chunk // 8) - 1, 0), 0))
    width = pbd.shape[1]
    lines = dp_n // 2
    more = max(lines - 1, 1)
    block = rows_out.shape[0] // dp_n
    quarter = tokens.shape[1]
    dma = pltpu.SemaphoreType.DMA
    vm, sds = pltpu.VMEM, jax.ShapeDtypeStruct
    return pl.pallas_call(
        functools.partial(scan_bwd_kernel, heads, total_inner, taps, bc, dp_n),
        grid=(blocks,),
        in_specs=[
            back(inner), back(inner), back(inner), back(inner), halo(inner), back(width), halo(width),
            pl.BlockSpec((1, bc // 2, inner), lambda i: (blocks - 1 - i, 0, 0)), whole(rows), whole(vec),
            back(inner), whole(rows_out), whole(tokens), whole(y_send), whole(g_own),
        ],
        out_specs=[
            back(inner), back(inner), back(width), pl.BlockSpec((8, vec.shape[1]), lambda i: (0, 0)),
            whole(tokens), pl.BlockSpec((block, inner), lambda i: (0, 0)),
        ],
        scratch_shapes=[
            vm((bc // 2, inner), F32), vm((chunk + 8, inner), F32), vm((chunk + 8, bc), F32),
            vm((chunk + 8, inner), F32), vm((chunk + 8, bc), F32),
            vm((8, inner), F32), vm((8, bc), F32), vm((2 * heads, chunk), F32),
            vm((chunk, chunk), BF), vm((chunk, 3 * inner), BF), vm((3, inner, chunk), BF), vm((heads * chunk, chunk), BF),
            vm((blocks, 2, chunk, quarter), BF), vm((blocks, 2, chunk, quarter), BF),
            vm((blocks, chunk, quarter), BF), vm((blocks, chunk, quarter), BF),
            vm((2, 2, chunk, quarter), F32), vm((blocks, chunk, quarter), F32),
            vm(y_send.shape, BF), vm(y_send.shape, BF), vm((2, more, block, inner // 2), BF), vm(y_send.shape, F32),
            dma((blocks,)), dma((blocks,)), dma((blocks,)), dma((blocks,)), dma((2,)), dma((2,)),
            dma((2, more)), dma((2, more)),
        ],
        out_shape=[
            sds((count, inner), BF), sds((count, inner), BF), sds((count, width), BF),
            sds((8, vec.shape[1]), F32), sds(tokens.shape, BF), sds((block, inner), F32),
        ],
        compiler_params=pltpu.CompilerParams(
            collective_id=3, has_side_effects=True, vmem_limit_bytes=58 * 2**20
        ),
        name="scan_backward",
    )(ggn, y, pz, px, px, pbd, pbd, sin, rows, vec, gn, rows_out, tokens, y_send, g_own)
def peers(dp_n):
    dp, hm = lax.axis_index("dp"), lax.axis_index("heads")
    across, core = hm // 2, hm % 2
    pair, line, lines = dp % 2, dp // 2, dp_n // 2
    return dict(
        sib=(dp, 2 * across + 1 - core),
        xn=(dp, 2 * (1 - across) + core),
        dg=(dp, 2 * (1 - across) + 1 - core),
        yn=(2 * line + 1 - pair, hm),
        line=lambda k: (2 * ((line + k) % lines) + pair, hm),
        mine=hm,
        other=2 * (1 - across) + core,
        sib_mine=2 * across + 1 - core,
        sib_other=2 * (1 - across) + 1 - core,
        pair=pair, line_index=line, lines=lines, dp=dp, core=core,
    )


def meet(who):
    barrier = pltpu.get_barrier_semaphore()
    for name in ("sib", "xn", "dg", "yn"):
        pl.semaphore_signal(barrier, inc=1, device_id=who[name], device_id_type=MESH)

    def greet(k, carry):
        pl.semaphore_signal(barrier, inc=1, device_id=who["line"](k), device_id_type=MESH)
        return carry

    lax.fori_loop(1, who["lines"], greet, 0)
    pl.semaphore_wait(barrier, 4 + who["lines"] - 1)


def push(src, dst, send, recv, to):
    return pltpu.make_async_remote_copy(
        src_ref=src, dst_ref=dst, send_sem=send, recv_sem=recv, device_id=to, device_id_type=MESH
    )


def tail_kernel(
    dp_n, units,
    normed_t_in, lpz_in, rows_z_in, lpx_in, rows_x_in, lpbd_in, rows_bd_in, normed_in,
    tokens, acc, cot, q_wide, vec,
    grad_tokens, g_x, g_z, g_bc, small_out,
    sib_send, sib_recv, x_send, x_recv, part, held,
    y_send, y_recv, z_send, z_recv, g_own, yb_send, yb_recv, zb_send, zb_recv, gb_own, bh_send, bh_recv,
    bx_send, bx_recv, bs_recv, h_send, h_recv, sy_send, sy_recv, sz_send, sz_recv, dy_send, dy_recv, dz_send, dz_recv, row_sums,
    normed_t, lpz, rows_z, lpx, rows_x, lpbd, rows_bd, normed,
    s_in, s_sib, r_sib, s_x, r_x, s_y, r_y, s_z, r_z, s_m, r_m, s_sl, r_sl,
):
    loads = [
        pltpu.make_async_copy(src, dst, s_in.at[i])
        for i, (src, dst) in enumerate((
            (normed_t_in, normed_t), (lpz_in, lpz), (rows_z_in, rows_z), (lpx_in, lpx), (rows_x_in, rows_x),
            (lpbd_in, lpbd), (rows_bd_in, rows_bd), (normed_in, normed),
        ))
    ]
    for load in loads:
        load.start()
    who = peers(dp_n)
    meet(who)
    count = normed.shape[0]
    width = normed.shape[1]
    inner = lpx.shape[1]
    bc = 2 * bh_send.shape[1]
    quarter = width // 4
    span = count // units
    block = width // dp_n
    lines = who["lines"]

    def copy_sib(u):
        return push(sib_send.at[u], sib_recv.at[u], s_sib.at[u], r_sib.at[u], who["sib"])

    def copy_x(u):
        return push(x_send.at[u], x_recv.at[u], s_x.at[u], r_x.at[u], who["xn"])

    def product(u, q):
        cols = pl.ds(pl.multiple_of(q * quarter, quarter), quarter)
        at = slice(u * span, (u + 1) * span)
        return nt(lpx[at, :], rows_x[cols, :]) + nt(lpz[at, :], rows_z[cols, :]) + nt(lpbd[at, :], rows_bd[cols, :])

    def head_a(u):
        for k, q in enumerate(("sib_mine", "sib_other", "mine", "other")):
            p = product(u, who[q])
            at = slice(u * span, (u + 1) * span)
            cols = pl.ds(pl.multiple_of(who[q] * quarter, quarter), quarter)
            inner_p = p * normed[at, cols].astype(F32)
            h_send[0:1, cols] += jnp.sum(inner_p, axis=0, keepdims=True)
            first = u * span
            lanes = slice(first % width, first % width + span)
            h_send[2 + first // width : 3 + first // width, lanes] += nt(
                jnp.ones((8, quarter), BF), inner_p.astype(BF)
            )[0:1]
            if k < 2:
                sib_send[u, k] = p.astype(BF)
            else:
                part[u % 2, k - 2] = p
        copy_sib(u).start()

    def head_b(u):
        copy_sib(u).wait()
        x_send[u] = (part[u % 2, 1] + sib_recv[u, 1].astype(F32)).astype(BF)
        copy_x(u).start()
        held[u] = part[u % 2, 0] + sib_recv[u, 0].astype(F32)

    def head_c(u):
        copy_x(u).wait()
        total = held[u] + x_recv[u].astype(F32)
        first = u * span
        lanes = q_wide.shape[1]
        cols = pl.ds(pl.multiple_of(who["mine"] * quarter, quarter), quarter)
        for j in range(span // lanes):
            at = slice(first + j * lanes, first + (j + 1) * lanes)
            row, lane = (first + j * lanes) // width, (first + j * lanes) % width
            dots = jnp.transpose(jnp.broadcast_to(row_sums[row : row + 1, lane : lane + lanes], (lanes, lanes)))
            q = q_wide[at, :]
            coef = q * q * (dots / width)
            grad_tokens[at, :] = (
                cot[at, :].astype(F32)
                + q[:, 0:1] * vec[6:7, cols] * total[j * lanes : (j + 1) * lanes]
                - tokens[at, :].astype(F32) * coef[:, 0:1]
            )

    def rows_of(line, pair):
        return pl.ds(pl.multiple_of((2 * line + pair) * block, block), block)

    def grad_a(v):
        left, right = ((normed_t, lpz), (normed_t, lpx))[v // 2]
        cols = slice((v % 2) * (inner // 2), (v % 2 + 1) * (inner // 2))
        for side in (0, 1):
            pair = (1 - who["pair"]) if side == 0 else who["pair"]
            stacked = jnp.concatenate([left[rows_of(l, pair), :] for l in range(lines)], axis=0)
            value = nn(stacked, right[:, cols])
            if side == 0:
                y_send[v] = value.astype(BF)
                copy_y(v).start()
            else:
                g_own[v] = value

    def copy_y(v):
        return push(y_send.at[v], y_recv.at[v], s_y.at[v], r_y.at[v], who["yn"])

    def copy_z(v, k):
        to = (who["line_index"] + k) % lines
        return push(
            z_send.at[v, pl.ds(pl.multiple_of(to * block, block), block)],
            z_recv.at[v, k - 1], s_z.at[v, k - 1], r_z.at[v, k - 1], who["line"](k),
        )

    def each_line(fn):
        def step(k, carry):
            fn(k)
            return carry

        lax.fori_loop(1, lines, step, 0)

    def own_rows():
        return pl.ds(pl.multiple_of(who["line_index"] * block, block), block)

    def grad_b(v):
        copy_y(v).wait()
        g_own[v] = g_own[v] + y_recv[v].astype(F32)
        z_send[v] = g_own[v].astype(BF)
        each_line(lambda k: copy_z(v, k).start())

    def grad_c(v):
        each_line(lambda k: copy_z(v, k).wait())
        total = g_own[v, own_rows(), :]
        for k in range(lines - 1):
            total = total + z_recv[v, k].astype(F32)
        cols = slice((v % 2) * (inner // 2), (v % 2 + 1) * (inner // 2))
        (g_z, g_x)[v // 2][:, cols] = total

    half = bc // 2

    def copy_bh():
        return push(bh_send, bh_recv, s_m.at[0], r_m.at[0], who["sib"])

    def copy_yb():
        return push(yb_send, yb_recv, s_m.at[1], r_m.at[1], who["yn"])

    def copy_zb(k):
        to = (who["line_index"] + k) % lines
        return push(
            zb_send.at[pl.ds(pl.multiple_of(to * block, block), block)],
            zb_recv.at[k - 1], s_sl.at[0, k - 1], r_sl.at[0, k - 1], who["line"](k),
        )

    def copy_bx():
        return push(bx_send, bx_recv, s_m.at[2], r_m.at[2], who["xn"])

    def copy_bs():
        return push(bx_send, bs_recv, s_m.at[3], r_m.at[3], who["sib"])

    def bc_a():
        for side in (0, 1):
            pair = (1 - who["pair"]) if side == 0 else who["pair"]
            stacked = jnp.concatenate([normed_t[rows_of(l, pair), :] for l in range(lines)], axis=0)
            value = nn(stacked, lpbd[:, :bc])
            first = who["core"] == 0
            lo, hi = value[:, :half], value[:, half:]
            at = slice(side * lines * block, (side + 1) * lines * block)
            bh_send[at, :] = jnp.where(first, hi, lo).astype(BF)
            gb_own[at, :] = jnp.where(first, lo, hi)
        copy_bh().start()

    def bc_b():
        copy_bh().wait()
        rows = lines * block
        gb_own[...] = gb_own[...] + bh_recv[...].astype(F32)
        yb_send[...] = gb_own[:rows, :].astype(BF)
        copy_yb().start()

    def bc_c():
        rows = lines * block
        copy_yb().wait()
        gb_own[rows:, :] = gb_own[rows:, :] + yb_recv[...].astype(F32)
        zb_send[...] = gb_own[rows:, :].astype(BF)
        each_line(lambda k: copy_zb(k).start())

    def bc_d():
        each_line(lambda k: copy_zb(k).wait())
        at = pl.ds(pl.multiple_of(lines * block + who["line_index"] * block, block), block)
        total = gb_own[at, :]
        for k in range(lines - 1):
            total = total + zb_recv[k].astype(F32)
        bx_send[...] = total
        copy_bx().start()

    def bc_e():
        copy_bx().wait()
        bx_send[...] = bx_send[...] + bx_recv[...]
        copy_bs().start()

    def bc_f():
        copy_bs().wait()
        mine, theirs = bx_send[...], bs_recv[...]
        first = who["core"] == 0
        g_bc[:, :half] = jnp.where(first, mine, theirs)
        g_bc[:, half:] = jnp.where(first, theirs, mine)

    three = (("sib", 4), ("xn", 5), ("dg", 6))
    token_rows = count // width

    def copy_h(k):
        name, sem = three[k]
        return push(h_send, h_recv.at[k], s_m.at[sem], r_m.at[sem], who[name])

    def small_a():
        h_send[1:2, :] = acc[1:2, :]
        for k in range(3):
            copy_h(k).start()

    def copy_sy():
        return push(sy_send, sy_recv, s_m.at[7], r_m.at[7], who["yn"])

    def copy_dy():
        return push(dy_send, dy_recv, s_m.at[8], r_m.at[8], who["yn"])

    def copy_sz(k):
        return push(sz_send, sz_recv.at[k - 1], s_sl.at[1, k - 1], r_sl.at[1, k - 1], who["line"](k))

    def copy_dz(k):
        return push(dz_send, dz_recv.at[k - 1], s_sl.at[2, k - 1], r_sl.at[2, k - 1], who["line"](k))

    def dt_a():
        dy_send[...] = tn(lpbd[:, bc:], normed[...])[0:16, :].astype(BF)
        copy_dy().start()

    def dt_b():
        copy_dy().wait()
        dz_send[...] = (dy_send[...].astype(F32) + dy_recv[...].astype(F32)).astype(BF)
        each_line(lambda k: copy_dz(k).start())

    def dt_c():
        each_line(lambda k: copy_dz(k).wait())
        total = dz_send[...].astype(F32)
        for k in range(lines - 1):
            total = total + dz_recv[k].astype(F32)
        small_out[8:24, :] = total

    def small_b():
        for k in range(3):
            copy_h(k).wait()
        over_heads = h_send[...] + h_recv[0] + h_recv[1] + h_recv[2]
        row_sums[0:token_rows, :] = over_heads[2 : 2 + token_rows, :]
        sy_send[0:2, :] = over_heads[0:2, :]
        sy_send[2:8, :] = acc[2:8, :]
        copy_sy().start()

    def small_c():
        copy_sy().wait()
        sz_send[...] = sy_send[...] + sy_recv[...]
        each_line(lambda k: copy_sz(k).start())

    def small_d():
        each_line(lambda k: copy_sz(k).wait())
        total = sz_send[...]
        for k in range(lines - 1):
            total = total + sz_recv[k]
        small_out[0:8, :] = total

    h_send[...] = jnp.zeros_like(h_send)

    def seq(*steps):
        for fn, *args in steps:
            fn(*args)

    assert units == 4

    def load(*which):
        for i in which:
            loads[i].wait()

    load(0, 1)
    seq((grad_a, 0), (grad_a, 1))
    load(2, 3, 4, 5, 6, 7)
    seq((head_a, 0), (bc_a,), (head_a, 1), (head_b, 0), (grad_a, 2), (bc_b,), (head_b, 1), (grad_b, 0), (head_a, 2))
    seq((grad_a, 3), (head_b, 2), (dt_a,), (grad_b, 1), (head_a, 3), (small_a,), (bc_c,), (head_b, 3), (dt_b,))
    seq((small_b,), (grad_b, 2), (grad_c, 0), (small_c,), (bc_d,), (dt_c,), (head_c, 0), (grad_b, 3), (grad_c, 1))
    seq((bc_e,), (head_c, 1), (small_d,), (head_c, 2), (grad_c, 2), (bc_f,), (head_c, 3), (grad_c, 3))


def tail(dp_n, units, normed_t, normed, lpx, lpz, lpbd, rows_x, rows_z, rows_bd, tokens, acc, cot, q_wide, vec, bc):
    count, width = normed.shape
    inner = lpx.shape[1]
    quarter = width // 4
    span = count // units
    block = width // dp_n
    lines = dp_n // 2
    half_rows = lines * block
    more = max(lines - 1, 1)
    vm = pltpu.VMEM
    dma = pltpu.SemaphoreType.DMA
    operands = (
        normed_t, lpz, rows_z, lpx, rows_x, lpbd, rows_bd, normed, tokens, acc, cot, q_wide, vec,
    )
    sds = jax.ShapeDtypeStruct
    spec = pl.BlockSpec(memory_space=pltpu.VMEM)
    return pl.pallas_call(
        functools.partial(tail_kernel, dp_n, units),
        out_shape=[
            sds((count, quarter), F32), sds((block, inner), F32), sds((block, inner), F32), sds((block, bc), F32),
            sds((24, width), F32),
        ],
        in_specs=[pl.BlockSpec(memory_space=pl.ANY)] * 8 + [spec] * 5,
        out_specs=[spec] * 5,
        scratch_shapes=[
            vm((units, 2, span, quarter), BF), vm((units, 2, span, quarter), BF),
            vm((units, span, quarter), BF), vm((units, span, quarter), BF),
            vm((2, 2, span, quarter), F32), vm((units, span, quarter), F32),
            vm((4, half_rows, inner // 2), BF), vm((4, half_rows, inner // 2), BF),
            vm((4, half_rows, inner // 2), BF), vm((4, more, block, inner // 2), BF),
            vm((4, half_rows, inner // 2), F32),
            vm((half_rows, bc // 2), BF), vm((half_rows, bc // 2), BF),
            vm((half_rows, bc // 2), BF), vm((more, block, bc // 2), BF),
            vm((2 * half_rows, bc // 2), F32),
            vm((2 * half_rows, bc // 2), BF), vm((2 * half_rows, bc // 2), BF),
            vm((block, bc // 2), F32), vm((block, bc // 2), F32), vm((block, bc // 2), F32),
            vm((8, width), F32), vm((3, 8, width), F32),
            vm((8, width), F32), vm((8, width), F32), vm((8, width), F32), vm((more, 8, width), F32),
            vm((16, width), BF), vm((16, width), BF), vm((16, width), BF), vm((more, 16, width), BF),
            vm((8, width), F32),
        ]
        + [vm(a.shape, a.dtype) for a in operands[:8]]
        + [
            dma((8,)), dma((units,)), dma((units,)), dma((units,)), dma((units,)),
            dma((4,)), dma((4,)), dma((4, more)), dma((4, more)), dma((9,)), dma((9,)),
            dma((3, more)), dma((3, more)),
        ],
        compiler_params=pltpu.CompilerParams(
            collective_id=1, has_side_effects=True, vmem_limit_bytes=62 * 2**20
        ),
        name="tail",
    )(*operands)
def shares(ref_in, block_of, dp_n, width, send, recv, who):
    rows = ref_in.shape[0]
    lines = who["lines"]
    source = ref_in.at[:, width] if ref_in.shape[1] != width.size else ref_in

    def at(dp):
        return block_of.at[pl.ds(pl.multiple_of(dp * rows, rows), rows), width]

    def own():
        return push(source, at(who["dp"]), send.at[0], recv.at[0], who["yn"])

    def along(k):
        return push(source, at(who["dp"]), send.at[k], recv.at[k], who["line"](k))

    def onward(k):
        there = at(2 * ((who["line_index"] - k + lines) % lines) + who["pair"])
        return push(there, there, send.at[lines - 1 + k], recv.at[lines - 1 + k], who["yn"])

    return own, along, onward


def loop_line(lines, fn):
    def step(k, carry):
        fn(k)
        return carry

    lax.fori_loop(1, lines, step, 0)


def front_kernel(
    dp_n, heads, units, taps, bc,
    tokens, cot, w_x, w_bc, w_z, w_out, w_dt, conv_x, conv_bc, norm_gain, gate_gain, dt_bias, a_log, skip, starts, fill,
    vec, px_out, pbd_out, normed_out, normed_t_out, q_out, y_out, sin_out, parts, rows_x, rows_bd, rows_z, rows_out,
    own_dt, tok, wx, wbd, px, pbd, normed, normed_t, q, y, sin, own_w, own_cot, state, extx, extb, upper, spread,
    s_loc, s_sib, r_sib, s_x, r_x, s_f, r_f, s_cx, r_cx, s_cf, r_cf, s_w, r_w, s_out, s_y,
):
    who = peers(dp_n)
    count, quarter = tokens.shape
    width = 4 * quarter
    span = count // units
    lines = who["lines"]
    block, inner = w_x.shape
    blocks = sin.shape[0]
    chunk = count // blocks
    per = blocks // units
    pieces = s_cx.shape[0]
    cot_span = count // pieces
    here = pl.ds(pl.multiple_of(who["dp"] * block, block), block)
    own_half = pl.ds(pl.multiple_of(who["core"] * (bc // 2), bc // 2), bc // 2)
    dt_cols = pl.ds(bc, chunk)
    local = [
        pltpu.make_async_copy(src, dst, s_loc.at[k])
        for k, (src, dst) in enumerate((
            (tokens, tok.at[who["mine"]]), (w_x, wx.at[here]), (w_bc.at[:, own_half], wbd.at[here, own_half]),
            (w_z, own_w.at[0]), (w_out, own_w.at[1]), (cot, own_cot),
        ))
    ]
    for copy in local:
        copy.start()
    own_dt[...] = jnp.zeros_like(own_dt)
    own_dt[:, :heads] = w_dt[...]
    wbd[here, dt_cols] = own_dt[...]
    onto = [
        pltpu.make_async_copy(src, dst, s_loc.at[8 + k])
        for k, (src, dst) in enumerate((
            (own_w.at[0], rows_z.at[here]), (own_w.at[1], rows_out.at[here]), (own_cot, parts.at[who["mine"]]),
        ))
    ]
    meet(who)

    def rows(s, n=span):
        return pl.ds(pl.multiple_of(s * n, n), n)

    def to_x(s):
        return push(tokens.at[rows(s)], tok.at[who["mine"], rows(s)], s_x.at[s], r_x.at[s], who["xn"])

    def to_sib():
        return push(tokens, tok.at[who["mine"]], s_sib.at[0], r_sib.at[0], who["sib"])

    def forward(s):
        at = tok.at[who["other"], rows(s)]
        return push(at, at, s_f.at[s], r_f.at[s], who["sib"])

    def cot_x(j):
        at = rows(j, cot_span)
        return push(cot.at[at], parts.at[who["mine"], at], s_cx.at[j], r_cx.at[j], who["xn"])

    def cot_sib():
        return push(cot, parts.at[who["mine"]], s_sib.at[1], r_sib.at[1], who["sib"])

    def cot_forward(j):
        at = parts.at[who["other"], rows(j, cot_span)]
        return push(at, at, s_cf.at[j], r_cf.at[j], who["sib"])

    half = inner // 2
    cuts = [
        shares(ref, to, dp_n, cols, s_w.at[n], r_w.at[n], who)
        for n, (ref, to, cols) in enumerate((
            (w_x, wx, pl.ds(0, half)), (w_x, wx, pl.ds(half, half)), (w_bc, wbd, own_half), (own_dt, wbd, dt_cols),
            (w_z, rows_z, pl.ds(0, half)), (w_z, rows_z, pl.ds(half, half)),
            (w_out, rows_out, pl.ds(0, half)), (w_out, rows_out, pl.ds(half, half)),
        ))
    ]

    def offer(n):
        loop_line(lines, lambda k: cuts[n][1](k).start())

    def other_half():
        cols = wbd.at[:, own_half]
        return push(cols, cols, s_sib.at[2], r_sib.at[2], who["sib"])

    def pass_rows(n):
        own, along, onward = cuts[n]
        own().start()

        def one(k):
            along(k).wait()
            onward(k).start()

        loop_line(lines, one)

    def have(n):
        own, along, onward = cuts[n]
        own().wait()
        loop_line(lines, lambda k: onward(k).wait())

    def pass_cot(j):
        cot_x(j).wait()
        cot_forward(j).start()

    to_x(0).start()
    offer(0)
    for s in range(1, units):
        to_x(s).start()
    to_sib().start()
    for n in (1, 2, 3):
        offer(n)
    for j in range(pieces):
        cot_x(j).start()
    for n in (4, 5, 6, 7):
        offer(n)
    pack_vec(vec, conv_x, conv_bc, norm_gain, gate_gain, dt_bias, a_log, skip, starts, fill, chunk)
    set_upper(upper)
    set_spread(spread, heads)
    state[...] = jnp.zeros_like(state)
    extx[...] = jnp.zeros_like(extx)
    extb[...] = jnp.zeros_like(extb)
    par = read_vec(vec, heads, chunk, inner, bc, taps)
    gain = vec[6:7, :width]

    def out_copies(s):
        at = rows(s)
        every = slice(None)
        return [
            pltpu.make_async_copy(ref.at[to], out.at[to], s_out.at[n, s])
            for n, (ref, out, to) in enumerate((
                (normed, normed_out, (at,)), (normed_t, normed_t_out, (every, at)), (q, q_out, (at,)),
                (px, px_out, (at,)), (pbd, pbd_out, (at,)),
            ))
        ]

    def norm(s):
        at = rows(s)
        values = [tok[h, at, :].astype(F32) for h in range(4)]
        total = sum(jnp.sum(p * p, axis=1, keepdims=True) for p in values)
        inv = lax.rsqrt(total / width + EPS)
        q[at, :] = jnp.broadcast_to(inv, (span, q.shape[1]))
        for h in range(4):
            cols = slice(h * quarter, (h + 1) * quarter)
            value = (values[h] * inv * gain[:, cols]).astype(BF)
            normed[at, cols] = value
            normed_t[cols, at] = jnp.transpose(value)
        for copy in out_copies(s)[:3]:
            copy.start()

    def project(s):
        at = rows(s)
        pbd[at, :] = nn(normed[at, :], wbd[...])
        px[at, :] = nn(normed[at, :], wx[...])
        for copy in out_copies(s)[3:]:
            copy.start()

    local[0].wait()
    to_x(0).wait()
    forward(0).start()
    pass_rows(0)
    to_sib().wait()
    forward(0).wait()
    norm(0)
    to_x(1).wait()
    forward(1).start()
    pass_rows(1)
    forward(1).wait()
    norm(1)
    pass_rows(2)
    pass_rows(3)
    have(2)
    local[2].wait()
    other_half().start()
    to_x(2).wait()
    forward(2).start()
    for copy in local[3:]:
        copy.wait()
    for copy in onto:
        copy.start()
    cot_sib().start()
    forward(2).wait()
    norm(2)
    local[1].wait()
    for n in (0, 1, 3):
        have(n)
    other_half().wait()
    keep_rows = [
        pltpu.make_async_copy(wx, rows_x, s_loc.at[6]), pltpu.make_async_copy(wbd, rows_bd, s_loc.at[7]),
    ]
    for copy in keep_rows:
        copy.start()

    def last_tokens(s):
        to_x(s).wait()
        forward(s).start()

    def last_norm(s):
        forward(s).wait()
        norm(s)

    events = {1: [(last_tokens, units - 1)], 2: [(last_norm, units - 1)]}
    late = []
    plan = [(pass_rows, 4, 3), (pass_rows, 5, 7), (pass_rows, 6, 11)]
    plan += [(pass_cot, j, 5 + 2 * j) for j in range(pieces)] + [(pass_rows, 7, 15)]
    for fn, k, at in plan:
        if at < blocks:
            events.setdefault(at, []).append((fn, k))
        else:
            late.append((fn, k))

    def y_copies(c):
        at = rows(c, chunk)
        return (
            pltpu.make_async_copy(y.at[at], y_out.at[at], s_y.at[0, c]),
            pltpu.make_async_copy(sin.at[c], sin_out.at[c], s_y.at[1, c]),
        )

    def step(c, carry):
        for at, fns in events.items():

            @pl.when(c == at)
            def _(fns=fns):
                for fn, k in fns:
                    fn(k)

        @pl.when(c % per == 0)
        def _():
            project(c // per)

        at = rows(c, chunk)
        y_c, enter = scan_step(
            heads, par, read_block(vec, c, chunk), px.at[at], pbd.at[at], upper, spread, state, extx, extb
        )
        y[at, :] = y_c
        sin[c] = enter
        for copy in y_copies(c):
            copy.start()
        return carry

    lax.fori_loop(0, blocks, step, 0)
    for fn, k in late:
        fn(k)

    def end_y(c, carry):
        for copy in y_copies(c):
            copy.wait()
        return carry

    lax.fori_loop(0, blocks, end_y, 0)
    for s in range(units):
        for copy in out_copies(s):
            copy.wait()
    for copy in onto + keep_rows:
        copy.wait()
    cot_sib().wait()
    for j in range(pieces):
        cot_forward(j).wait()
    for n in (4, 5, 6, 7):
        have(n)


def front(dp_n, tokens, cot, w_x, w_bc, w_z, w_out, w_dt, conv_x, conv_bc, norm_gain, gate_gain, *scalars):
    count, quarter = tokens.shape
    width = 4 * quarter
    inner, heads = w_x.shape[1], w_dt.shape[1]
    taps, bc = conv_bc.shape
    blocks = scalars[-1].shape[0]
    chunk = count // blocks
    wide = bc + chunk
    units, pieces = 4, 8
    vm, dma, sds = pltpu.VMEM, pltpu.SemaphoreType.DMA, jax.ShapeDtypeStruct
    hbm, vmem = pl.BlockSpec(memory_space=pl.ANY), pl.BlockSpec(memory_space=pltpu.VMEM)
    ways = dp_n - 1
    outs = [
        sds((24 + blocks, width), F32),
        sds((count, inner), F32), sds((count, wide), F32), sds((count, width), BF), sds((width, count), BF),
        sds((count, 128), F32), sds((count, inner), F32), sds((blocks, bc // 2, inner), BF),
        sds((4, count, quarter), BF), sds((width, inner), BF), sds((width, wide), BF), sds((width, inner), BF),
        sds((width, inner), BF),
    ]
    return pl.pallas_call(
        functools.partial(front_kernel, dp_n, heads, units, taps, bc),
        out_shape=outs,
        in_specs=[hbm] * 6 + [vmem] * 5 + [pl.BlockSpec(memory_space=pltpu.SMEM)] * 5,
        out_specs=[vmem] + [hbm] * (len(outs) - 1),
        scratch_shapes=[
            vm((w_x.shape[0], chunk), BF),
            vm((4, count, quarter), BF), vm((width, inner), BF), vm((width, wide), BF),
            vm((count, inner), F32), vm((count, wide), F32), vm((count, width), BF), vm((width, count), BF),
            vm((count, 128), F32), vm((count, inner), F32), vm((blocks, bc // 2, inner), BF),
            vm((2,) + w_z.shape, BF), vm(cot.shape, BF),
            vm((bc // 2, inner), F32), vm((chunk + 8, inner), F32), vm((chunk + 8, bc), F32),
            vm((chunk, chunk), BF), vm((chunk, 3 * inner), BF),
            dma((11,)), dma((3,)), dma((3,)), dma((units,)), dma((units,)), dma((units,)), dma((units,)),
            dma((pieces,)), dma((pieces,)), dma((pieces,)), dma((pieces,)),
            dma((8, ways)), dma((8, ways)), dma((5, units)), dma((2, blocks)),
        ],
        compiler_params=pltpu.CompilerParams(
            collective_id=2, has_side_effects=True, vmem_limit_bytes=58 * 2**20
        ),
        name="front",
    )(
        tokens, cot, w_x, w_bc, w_z, w_out, w_dt, conv_x, conv_bc, norm_gain[None, :], gate_gain[None, :], *scalars
    )


def body(
    tokens, cotangent, starts, fill, norm_gain, w_x, w_z, w_dt, w_bc, conv_x, conv_bc, dt_bias, a_log, skip,
    gate_gain, w_out,
):
    heads_n = lax.axis_size("heads")
    dp_n = lax.axis_size("dp")
    head_index = lax.axis_index("heads")
    dp_index = lax.axis_index("dp")
    count, columns = tokens.shape
    width = columns * heads_n
    blocks = starts.shape[0]
    chunk = count // blocks
    inner = w_x.shape[1]
    heads = w_dt.shape[1]
    taps, bc = conv_bc.shape
    vec, px, pbd, normed, normed_t, q_wide, y, sin, parts, rows_x, rows_bd, rows_z, rows_out = front(
        dp_n, tokens, cotangent, w_x, w_bc, w_z, w_out, w_dt, conv_x, conv_bc, norm_gain, gate_gain, dt_bias, a_log,
        skip, starts, fill,
    )
    pz, ggn, sums, gn, y_send, g_own = gate(dp_n, blocks, normed, rows_z, rows_out, parts, y, vec)
    lpx, lpz, lpbd, acc, block_out, grad_w_out = scan_backward(
        dp_n, ggn, y, pz, px, pbd, sin, sums, vec, gn, rows_out, tokens, y_send, g_own, heads, taps, bc,
        inner * heads_n,
    )
    grad_tokens, grad_w_x, grad_w_z, grad_w_bc, small = tail(
        dp_n, 4, normed_t, normed, lpx, lpz, lpbd, rows_x, rows_z, rows_bd, tokens, acc, cotangent, q_wide, vec, bc,
    )
    block = width // dp_n
    own_gain = lax.dynamic_slice_in_dim(norm_gain, head_index * columns, columns, 0)
    gain_sum = lax.dynamic_slice_in_dim(small[0], head_index * columns, columns, 0)
    grad_w_dt = lax.dynamic_slice_in_dim(small[8 : 8 + heads], dp_index * block, block, 1).T
    return (
        block_out, grad_tokens, gain_sum / own_gain, grad_w_x, grad_w_z, grad_w_dt, grad_w_bc,
        small[2:4].reshape(taps, inner), small[1].reshape(taps, bc), small[5, :heads], small[5, heads : 2 * heads],
        small[5, 2 * heads : 3 * heads], small[4, :inner], grad_w_out,
    )


def solution(mesh):
    placed = (
        P("dp", "heads"),
        P("dp", "heads"),
        P("dp"),
        P("dp"),
        P(),
        P("dp", "heads"),
        P("dp", "heads"),
        P("dp", "heads"),
        P("dp", None),
        P(None, "heads"),
        P(),
        P("heads"),
        P("heads"),
        P("heads"),
        P("heads"),
        P("dp", "heads"),
    )
    return jax.shard_map(
        body,
        mesh=mesh,
        in_specs=placed,
        out_specs=(
            P("dp", "heads"),
            P("dp", "heads"),
            P("heads"),
            P("dp", "heads"),
            P("dp", "heads"),
            P("dp", "heads"),
            P("dp", None),
            P(None, "heads"),
            P(),
            P("heads"),
            P("heads"),
            P("heads"),
            P("heads"),
            P("dp", "heads"),
        ),
        check_vma=False,
    )
```

```python
import functools
import jax
import jax.numpy as jnp
from jax import lax
from jax.experimental import pallas as pl
from jax.experimental.pallas import tpu as pltpu
from jax.sharding import PartitionSpec as P

HD = 64
EPS = 1e-05
F32 = jnp.float32
BF = jnp.bfloat16
NEG = -1e30
MESH = pl.DeviceIdType.MESH


def nn(a, b):
    return lax.dot_general(a, b, (((1,), (0,)), ((), ())), preferred_element_type=F32)


def nt(a, b):
    return lax.dot_general(a, b, (((1,), (1,)), ((), ())), preferred_element_type=F32)


def tn(a, b):
    return lax.dot_general(a, b, (((0,), (0,)), ((), ())), preferred_element_type=F32)


def split2(v):
    hi = v.astype(BF).astype(F32)
    return hi, v - hi


def split3(v):
    hi = v.astype(BF).astype(F32)
    rest = v - hi
    mid = rest.astype(BF).astype(F32)
    return hi, mid, rest - mid


def softplus(v):
    return jnp.maximum(v, 0.0) + jnp.log1p(jnp.exp(-jnp.abs(v)))


def sigmoid(v):
    return 1.0 / (1.0 + jnp.exp(-v))


def iota2(rows, cols, axis):
    return lax.broadcasted_iota(jnp.int32, (rows, cols), axis)


def zero_one(cond):
    return jnp.where(cond, 1.0, 0.0).astype(BF)


def set_upper(upper):
    upper[...] = zero_one(iota2(*upper.shape, 0) <= iota2(*upper.shape, 1))


def set_spread(spread, heads):
    rows, lanes = iota2(*spread.shape, 0), iota2(*spread.shape, 1)
    inner = heads * HD
    base = heads * (1 + 2 * (lanes // inner)) + (lanes % inner) // HD
    spread[...] = zero_one(jnp.logical_or(rows == base, rows == base + heads))


def set_gather(gather, ones_h, heads):
    for q in range(3):
        rows, lanes = iota2(*gather.shape[1:], 0), iota2(*gather.shape[1:], 1)
        gather[q] = zero_one(lanes == q * heads + rows // HD)
    rows, lanes = iota2(*ones_h.shape, 0), iota2(*ones_h.shape, 1)
    ones_h[...] = zero_one(lanes == heads + rows // ones_h.shape[1])


def conv_from(ext, taps, rows, halo):
    n = taps.shape[0]
    out = taps[n - 1 : n, :] * ext[pl.ds(halo, rows), :]
    for k in range(1, n):
        out = out + taps[n - 1 - k : n - k, :] * ext[pl.ds(halo - k, rows), :]
    return out


def dt_rows(pdt, bias, rate, fill, heads, upper):
    chunk = pdt.shape[0]
    pre = jnp.transpose(pdt)[:heads] + bias
    live = (iota2(heads, chunk, 1).astype(F32) < fill).astype(F32)
    dt = softplus(pre) * live
    hi, mid, low = split3(dt * rate)
    stacked = jnp.concatenate([hi, mid, low], axis=0).astype(BF)
    summed = nn(stacked, upper)
    run = summed[:heads] + summed[heads : 2 * heads] + summed[2 * heads :]
    return pre, live, dt, run


def spread_all(run, dt, heads, chunk, spread):
    last = run[:, chunk - 1 : chunk]
    e_in = jnp.exp(run)
    e_out = jnp.exp(last - run)
    parts = [run]
    for v in (dt, e_in, e_out):
        parts.extend(split2(v))
    used = heads * len(parts)
    if used < chunk:
        parts.append(jnp.zeros((chunk - used, chunk), F32))
    cols = jnp.transpose(jnp.concatenate(parts, axis=0))
    return cols, nn(cols.astype(BF), spread)


def pair_stack(v, low_lanes):
    zero = jnp.zeros_like(v)
    return jnp.concatenate([jnp.where(low_lanes, v, zero), jnp.where(low_lanes, zero, v)], axis=0)


def read_vec(vec, heads, chunk, inner, bc, taps):
    return dict(
        convx=vec[0:taps, :inner], skip=vec[4:5, :inner], gain=vec[5:6, :inner],
        bias=vec[8 : 8 + heads, :chunk], rate=vec[8 : 8 + heads, chunk : 2 * chunk], convbc=vec[16 : 16 + taps, :bc],
    )


def read_block(vec, c, chunk):
    row = vec[pl.ds(24 + c, 1), :]
    return row[:, 0:1] > 0.5, row[:, chunk : chunk + 1], row[:, 2 * chunk : 2 * chunk + 1] > 0.5


def pack_vec(vec, conv_x, conv_bc, norm_gain, gate_gain, dt_bias, a_log, skip, starts, fill, chunk):
    taps, inner = conv_x.shape
    vec[...] = jnp.zeros_like(vec)
    vec[0:taps, :inner] = conv_x[...]
    vec[16 : 16 + taps, : conv_bc.shape[1]] = conv_bc[...]
    vec[5:6, :inner] = gate_gain[...]
    vec[6:7, :] = norm_gain[...]
    head = iota2(1, inner, 1) // HD
    skips = jnp.zeros((1, inner), F32)
    for h in range(dt_bias.shape[0]):
        skips = jnp.where(head == h, skip[h], skips)
        vec[8 + h : 9 + h, 0:chunk] = jnp.full((1, chunk), dt_bias[h], F32)
        vec[8 + h : 9 + h, chunk : 2 * chunk] = -jnp.exp(jnp.full((1, chunk), a_log[h], F32))
    vec[4:5, :inner] = skips
    blocks = starts.shape[0]
    for c in range(blocks):
        row = slice(24 + c, 25 + c)
        vec[row, 0:chunk] = jnp.full((1, chunk), 1 - starts[c], jnp.int32).astype(F32)
        vec[row, chunk : 2 * chunk] = jnp.full((1, chunk), fill[c], jnp.int32).astype(F32)
        if c + 1 < blocks:
            vec[row, 2 * chunk : 3 * chunk] = jnp.full((1, chunk), 1 - starts[c + 1], jnp.int32).astype(F32)


def scan_step(heads, par, block, px, pbd, upper, spread, state, extx, extb):
    chunk, inner = px.shape
    bc = par["convbc"].shape[1]
    ns = bc // 2
    keep, n_live, _ = block
    state[...] = jnp.where(keep, state[...], 0.0)
    extx[0:8, :] = jnp.where(keep, extx[chunk : chunk + 8, :], 0.0)
    extb[0:8, :] = jnp.where(keep, extb[chunk : chunk + 8, :], 0.0)
    extx[8 : chunk + 8, :] = px[...]
    extb[8 : chunk + 8, :] = pbd[:, :bc]

    u = conv_from(extx, par["convx"], chunk, 8)
    x = u * sigmoid(u) * (iota2(chunk, inner, 0).astype(F32) < n_live).astype(F32)
    ub = conv_from(extb, par["convbc"], chunk, 8)
    act = (ub * sigmoid(ub) * (iota2(chunk, bc, 0).astype(F32) < n_live).astype(F32)).astype(BF)
    b, cc = act[:, :ns], act[:, ns:]

    _, _, dt, run = dt_rows(pbd[:, bc:], par["bias"], par["rate"], n_live, heads, upper[...])
    cols, wide = spread_all(run, dt, heads, chunk, spread[...])
    dt_w, ein_w, eout_w = wide[:, :inner], wide[:, inner : 2 * inner], wide[:, 2 * inner :]

    xd = x * dt_w
    xdb = xd.astype(BF)
    scores = nt(cc, b)
    tri = iota2(chunk, chunk, 0) >= iota2(chunk, chunk, 1)
    low_lanes = iota2(chunk, 2 * HD, 1) < HD
    diag = []
    for j in range(heads // 2):
        mix = []
        for h in (2 * j, 2 * j + 1):
            spread_h = cols[:, h : h + 1] - run[h : h + 1, :]
            mix.append((scores * jnp.exp(jnp.where(tri, spread_h, NEG))).astype(BF))
        pair = pair_stack(xdb[:, 2 * HD * j : 2 * HD * (j + 1)], low_lanes)
        diag.append(nn(jnp.concatenate(mix, axis=1), pair))
    enter = state[...]
    enter_b = enter.astype(BF)
    y = jnp.concatenate(diag, axis=1) + ein_w * nn(cc, enter_b) + par["skip"] * x
    state[...] = ein_w[chunk - 1 : chunk, :] * enter + tn(b, (xd * eout_w).astype(BF))
    return y, enter_b


def pair_rows(dp_n, block, pair, values):
    return jnp.concatenate(
        [values[pl.ds(pl.multiple_of((2 * l + pair) * block, block), block), :] for l in range(dp_n // 2)], axis=0
    )


def gate_kernel(
    dp_n, normed, rows_z, rows_out, parts, y, vec, pz, ggn, sums, gn, y_send, g_own,
    h_send, h_recv, gated_all, grad_t, s_h, r_h,
):
    i = pl.program_id(0)
    who = peers(dp_n)
    names = ("sib", "xn", "dg")
    barrier = pltpu.get_barrier_semaphore()
    span, quarter = parts.shape[1:]
    blocks, chunk = h_send.shape[1:]
    inner = y.shape[1]
    here = pl.ds(pl.multiple_of(i * span, span), span)

    @pl.when(i == 0)
    def _():
        for name in names:
            pl.semaphore_signal(barrier, inc=1, device_id=who[name], device_id_type=MESH)

    z = nn(normed[...], rows_z[...])
    pz[...] = z
    g = nn(parts[0], rows_out[0:quarter, :])
    for k in range(1, 4):
        g = g + nn(parts[k], rows_out[k * quarter : (k + 1) * quarter, :])
    ggn[...] = g
    for k in range(4):
        grad_t[k * quarter : (k + 1) * quarter, here] = jnp.transpose(parts[k])
    gated = y[...] * (z * sigmoid(z))
    gated_all[here, :] = gated
    ones = jnp.ones((8, inner), BF)
    for k, value in enumerate((gated * gated, gated * vec[5:6, :inner] * g)):
        row = nt(ones, value.astype(BF))
        for j in range(span // chunk):
            h_send[k, pl.ds(i * (span // chunk) + j, 1), :] = row[0:1, j * chunk : (j + 1) * chunk]

    @pl.when(i == pl.num_programs(0) - 1)
    def _():
        pl.semaphore_wait(barrier, 3)
        copies = [push(h_send, h_recv.at[k], s_h.at[k], r_h.at[k], who[name]) for k, name in enumerate(names)]
        for copy in copies:
            copy.start()
        for copy in copies:
            copy.wait()
        sums[...] = h_send[...] + h_recv[0] + h_recv[1] + h_recv[2]
        gain = vec[5:6, :inner]
        squares = jnp.transpose(
            jnp.concatenate([sums[0], jnp.zeros((chunk - blocks, chunk), F32)], axis=0)
        )
        inv = lax.rsqrt(squares / (4 * inner) + EPS)
        for b in range(blocks):
            at = slice(b * chunk, (b + 1) * chunk)
            gn[at, :] = (gated_all[at, :] * inv[:, b : b + 1] * gain).astype(BF)
        block = grad_t.shape[0] // dp_n
        for v in range(2):
            cols = slice(v * (inner // 2), (v + 1) * (inner // 2))
            y_send[v] = nn(pair_rows(dp_n, block, 1 - who["pair"], grad_t), gn[:, cols]).astype(BF)
            g_own[v] = nn(pair_rows(dp_n, block, who["pair"], grad_t), gn[:, cols])


def gate(dp_n, blocks, normed, rows_z, rows_out, parts, y, vec):
    count, width = normed.shape
    inner = y.shape[1]
    chunk = count // blocks
    steps = 8
    span = count // steps
    quarter = width // 4
    sds = jax.ShapeDtypeStruct
    rows = lambda w: pl.BlockSpec((span, w), lambda i: (i, 0))
    whole = lambda shape: pl.BlockSpec(shape, lambda i: (0,) * len(shape))
    halves = (2, width // 2, inner // 2)
    return pl.pallas_call(
        functools.partial(gate_kernel, dp_n),
        grid=(steps,),
        in_specs=[
            rows(width), whole(rows_z.shape), whole(rows_out.shape),
            pl.BlockSpec((4, span, quarter), lambda i: (0, i, 0)), rows(inner), whole(vec.shape),
        ],
        out_specs=[
            rows(inner), rows(inner), whole((2, blocks, chunk)), whole((count, inner)), whole(halves), whole(halves),
        ],
        out_shape=[
            sds((count, inner), F32), sds((count, inner), F32), sds((2, blocks, chunk), F32), sds((count, inner), BF),
            sds(halves, BF), sds(halves, F32),
        ],
        scratch_shapes=[
            pltpu.VMEM((2, blocks, chunk), F32), pltpu.VMEM((3, 2, blocks, chunk), F32),
            pltpu.VMEM((count, inner), F32), pltpu.VMEM((width, count), BF),
            pltpu.SemaphoreType.DMA((3,)), pltpu.SemaphoreType.DMA((3,)),
        ],
        compiler_params=pltpu.CompilerParams(
            collective_id=4, has_side_effects=True, vmem_limit_bytes=58 * 2**20
        ),
        name="gate",
    )(normed, rows_z, rows_out, parts, y, vec)


def sums_beside_scan(
    dp_n, gn, rows_out, tokens, y_send, g_in, block_out, g_out,
    sib_send, sib_recv, x_send, x_recv, part, held, y_recv, z_send, z_recv, g_own,
    s_sib, r_sib, s_x, r_x, s_y, r_y, s_z, r_z,
):
    i = pl.program_id(0)
    who = peers(dp_n)
    lines = who["lines"]
    units, span, quarter = held.shape
    block = g_out.shape[0]
    half = g_out.shape[1] // 2

    def copy_sib(k):
        return push(sib_send.at[k], sib_recv.at[k], s_sib.at[k], r_sib.at[k], who["sib"])

    def copy_x(k):
        return push(x_send.at[k], x_recv.at[k], s_x.at[k], r_x.at[k], who["xn"])

    def copy_y(v):
        return push(y_send.at[v], y_recv.at[v], s_y.at[v], r_y.at[v], who["yn"])

    def copy_z(v, k):
        to = (who["line_index"] + k) % lines
        return push(
            z_send.at[v, pl.ds(pl.multiple_of(to * block, block), block)],
            z_recv.at[v, k - 1], s_z.at[v, k - 1], r_z.at[v, k - 1], who["line"](k),
        )

    @pl.when(i == 0)
    def _():
        meet(who)
        for v in range(2):
            copy_y(v).start()

    def first(k):
        for n, q in enumerate(("sib_mine", "sib_other", "mine", "other")):
            cols = pl.ds(pl.multiple_of(who[q] * quarter, quarter), quarter)
            p = nt(gn[k * span : (k + 1) * span, :], rows_out[cols, :])
            if n < 2:
                sib_send[k, n] = p.astype(BF)
            else:
                part[n - 2] = p
        copy_sib(k).start()

    def second(k):
        copy_sib(k).wait()
        x_send[k] = (part[1] + sib_recv[k, 1].astype(F32)).astype(BF)
        copy_x(k).start()
        held[k] = part[0] + sib_recv[k, 0].astype(F32)

    def third(k):
        copy_x(k).wait()
        at = slice(k * span, (k + 1) * span)
        block_out[at, :] = (tokens[at, :].astype(F32) + held[k] + x_recv[k].astype(F32)).astype(BF)

    def grad_b(v):
        copy_y(v).wait()
        g_own[v] = g_in[v] + y_recv[v].astype(F32)
        z_send[v] = g_own[v].astype(BF)
        loop_line(lines, lambda k: copy_z(v, k).start())

    def grad_c(v):
        loop_line(lines, lambda k: copy_z(v, k).wait())
        total = g_own[v, pl.ds(pl.multiple_of(who["line_index"] * block, block), block), :]
        for k in range(lines - 1):
            total = total + z_recv[v, k].astype(F32)
        g_out[:, v * half : (v + 1) * half] = total

    events = [(grad_b, 0, 4), (grad_b, 1, 7)]
    for k in range(units):
        events += [(first, k, 2 * k), (second, k, 2 * k + 1), (third, k, 2 * k + 6)]
    for at in sorted({e[2] for e in events}):

        @pl.when(i == at)
        def _(at=at):
            for fn, k, when in events:
                if when == at:
                    fn(k)

    def finish():
        for v in range(2):
            grad_c(v)

    return finish


def scan_bwd_kernel(
    heads, total_inner, taps_n, bc, dp_n, ggn, y, pz, px, px_halo, pbd, pbd_halo, sin, rows, vec, gn, rows_out, tokens,
    y_send, g_in,
    lpx, lpz, lpbd, acc, block_out, g_out, dstate, extx, extb, dux, dub, acc_x, acc_bc, acc_s, upper, spread, gather, ones_h,
    *beside,
):
    finish = sums_beside_scan(dp_n, gn, rows_out, tokens, y_send, g_in, block_out, g_out, *beside)
    i = pl.program_id(0)
    blocks = pl.num_programs(0)
    c = blocks - 1 - i
    chunk, inner = px.shape
    ns = bc // 2
    par = read_vec(vec, heads, chunk, inner, bc, taps_n)
    keep, n_live, keep_next = read_block(vec, c, chunk)
    taps, taps_b, bias, rate, skip, gain = (par[k] for k in ("convx", "convbc", "bias", "rate", "skip", "gain"))

    @pl.when(i == 0)
    def _():
        for ref in (dstate, dux, dub, acc_x, acc_bc, acc_s):
            ref[...] = jnp.zeros_like(ref)
        set_upper(upper)
        set_spread(spread, heads)
        set_gather(gather, ones_h, heads)

    moved = jnp.transpose(
        jnp.concatenate(
            [rows[0, pl.ds(c, 1), :], rows[1, pl.ds(c, 1), :], jnp.zeros((chunk - 2, chunk), F32)], axis=0
        )
    )
    inv = lax.rsqrt(moved[:, 0:1] / total_inner + EPS)
    coef = inv * inv * inv * (moved[:, 1:2] / total_inner)
    z = pz[...]
    sz = sigmoid(z)
    silu_z = z * sz
    yv = y[...]
    gated = yv * silu_z
    g = ggn[...]
    d_gated = inv * (g * gain) - gated * coef
    lpz[...] = (d_gated * yv * (sz * (1.0 + z * (1.0 - sz)))).astype(BF)
    dy = d_gated * silu_z
    acc_x[taps_n : taps_n + 1, :] += jnp.sum(g * gated * inv, axis=0, keepdims=True)

    extx[0:8, :] = jnp.where(keep, px_halo[...], 0.0)
    extb[0:8, :] = jnp.where(keep, pbd_halo[:, :bc], 0.0)
    extx[8 : chunk + 8, :] = px[...]
    extb[8 : chunk + 8, :] = pbd[:, :bc]
    live_x = (iota2(chunk, inner, 0).astype(F32) < n_live).astype(F32)
    live_b = (iota2(chunk, bc, 0).astype(F32) < n_live).astype(F32)
    u = conv_from(extx, taps, chunk, 8)
    su = sigmoid(u)
    x = u * su * live_x
    dx_du = su * (1.0 + u * (1.0 - su)) * live_x
    ub = conv_from(extb, taps_b, chunk, 8)
    sb = sigmoid(ub)
    act = (ub * sb * live_b).astype(BF)
    db_du = sb * (1.0 + ub * (1.0 - sb)) * live_b
    b, cc = act[:, :ns], act[:, ns:]

    pre, live, dt, run = dt_rows(pbd[:, bc:], bias, rate, n_live, heads, upper[...])
    cols, wide = spread_all(run, dt, heads, chunk, spread[...])
    dt_w, ein_w, eout_w = wide[:, :inner], wide[:, inner : 2 * inner], wide[:, 2 * inner :]
    xd = x * dt_w
    xdb = xd.astype(BF)
    dyb = dy.astype(BF)
    acc_x[taps_n + 1 : taps_n + 2, :] += jnp.sum(dy * x, axis=0, keepdims=True)

    scores_t = nt(b, cc)
    tri = iota2(chunk, chunk, 0) <= iota2(chunk, chunk, 1)
    low_lanes = iota2(chunk, 2 * HD, 1) < HD
    d_scores_t = jnp.zeros((chunk, chunk), F32)
    dxd = []
    pulls = []
    read_sums = []
    for j in range(heads // 2):
        span = slice(2 * HD * j, 2 * HD * (j + 1))
        dy_pair = pair_stack(dyb[:, span], low_lanes)
        x_pair = pair_stack(xdb[:, span], low_lanes)
        d_mix = nt(x_pair, dyb[:, span])
        mix = []
        for k in (0, 1):
            h = 2 * j + k
            spread_h = run[h : h + 1, :] - cols[:, h : h + 1]
            fade = jnp.exp(jnp.where(tri, spread_h, NEG))
            m = scores_t * fade
            dm = d_mix[k * chunk : (k + 1) * chunk]
            d_scores_t = d_scores_t + dm * fade
            pull = (dm * m).astype(BF)
            pulls.append(pull)
            read_sums.append(jnp.sum(pull.astype(F32), axis=0, keepdims=True))
            mix.append(m.astype(BF))
        dxd.append(nn(jnp.concatenate(mix, axis=1), dy_pair))
    source_sums = nn(jnp.concatenate(pulls, axis=1), ones_h[...])
    read_rows = jnp.concatenate(read_sums, axis=0)

    d_state = jnp.where(keep_next, dstate[...], 0.0)
    d_state_b = d_state.astype(BF)
    enter_b = sin[0]
    edy = ein_w * dy
    edyb = edy.astype(BF)
    readings = nn(cc, enter_b)
    from_state = nn(b, d_state_b) * eout_w
    d_xd = jnp.concatenate(dxd, axis=1) + from_state
    q1 = edy * readings
    q2 = xd * from_state
    decay = ein_w[chunk - 1 : chunk, :]
    dstate[...] = decay * d_state + tn(cc, edyb)
    d_cb = tn(d_scores_t.astype(BF), b) + nt(edyb, enter_b)
    d_b = nn(d_scores_t.astype(BF), cc) + nt((xd * eout_w).astype(BF), d_state_b)

    sums = (
        nn((d_xd * x).astype(BF), gather[0])
        + nn((q1 - q2).astype(BF), gather[1])
        + nn(q2.astype(BF), gather[2])
        - source_sums
    )
    sums_t = jnp.transpose(sums)
    dt_direct = sums_t[:heads]
    d_run = sums_t[heads : 2 * heads] + read_rows
    whole_q2 = jnp.sum(sums_t[2 * heads : 3 * heads], axis=1, keepdims=True)
    kept = jnp.sum(enter_b.astype(F32) * d_state, axis=0, keepdims=True) * decay
    kept_hi, kept_lo = split2(kept)
    kept_two = jnp.concatenate([kept_hi, kept_lo, jnp.zeros((6, inner), F32)], axis=0).astype(BF)
    kept_rows = nn(kept_two, gather[0])
    kept_cols = jnp.transpose(
        jnp.concatenate([kept_rows[0:1] + kept_rows[1:2], jnp.zeros((chunk - 1, chunk), F32)], axis=0)
    )
    d_last = whole_q2 + kept_cols[:heads, 0:1]
    hi, mid, low = split3(d_run)
    back = nt(jnp.concatenate([hi, mid, low], axis=0).astype(BF), upper[...])
    d_a = back[:heads] + back[heads : 2 * heads] + back[2 * heads :] + d_last
    d_dt = dt_direct + d_a * rate
    d_pre = d_dt * live * sigmoid(pre)
    acc_s[0:heads, :] += d_pre
    acc_s[heads : 2 * heads, :] += d_a * dt * rate

    def conv_back(d_u, du_ref, ext_ref, tap_values, acc):
        du_ref[chunk : chunk + 8, :] = jnp.where(keep_next, du_ref[0:8, :], 0.0)
        du_ref[0:chunk, :] = d_u
        out = tap_values[taps_n - 1 : taps_n, :] * d_u
        acc[taps_n - 1 : taps_n, :] += jnp.sum(d_u * ext_ref[8 : chunk + 8, :], axis=0, keepdims=True)
        for k in range(1, taps_n):
            row = taps_n - 1 - k
            out = out + tap_values[row : row + 1, :] * du_ref[pl.ds(k, chunk), :]
            acc[row : row + 1, :] += jnp.sum(
                d_u * ext_ref[pl.ds(8 - k, chunk), :], axis=0, keepdims=True
            )
        return out

    d_x = d_xd * dt_w + skip * dy
    lpx[...] = conv_back(d_x * dx_du, dux, extx, taps, acc_x).astype(BF)
    d_act = jnp.concatenate([d_b, d_cb], axis=1)
    lpbd[:, :bc] = conv_back(d_act * db_du, dub, extb, taps_b, acc_bc).astype(BF)
    pad = jnp.concatenate([d_pre, jnp.zeros((chunk - heads, chunk), F32)], axis=0)
    lpbd[:, bc:] = jnp.transpose(pad).astype(BF)

    @pl.when(i == blocks - 1)
    def _():
        acc[...] = jnp.zeros_like(acc)
        for k in range(taps_n):
            acc[1:2, k * bc : (k + 1) * bc] = acc_bc[k : k + 1, :]
        per = acc.shape[1] // inner
        for k in range(taps_n + 1):
            acc[2 + k // per : 3 + k // per, (k % per) * inner : (k % per + 1) * inner] = acc_x[k : k + 1, :]
        per_head = jnp.sum(
            jnp.transpose(jnp.concatenate([acc_s[...], jnp.zeros((chunk - 2 * heads, chunk), F32)], axis=0)),
            axis=0, keepdims=True,
        )
        three = jnp.concatenate(split3(acc_x[taps_n + 1 : taps_n + 2, :]) + (jnp.zeros((5, inner), F32),), axis=0)
        skips = jnp.sum(nn(three.astype(BF), gather[2]), axis=0, keepdims=True)
        acc[5:6, 0:chunk] = per_head + skips
        finish()


def scan_backward(
    dp_n, ggn, y, pz, px, pbd, sin, rows, vec, gn, rows_out, tokens, y_send, g_own, heads, taps, bc, total_inner
):
    count, inner = px.shape
    blocks = sin.shape[0]
    chunk = count // blocks
    whole = lambda a: pl.BlockSpec(a.shape, lambda i: (0,) * a.ndim)
    back = lambda w: pl.BlockSpec((chunk, w), lambda i: (blocks - 1 - i, 0))
    halo = lambda w: pl.BlockSpec((8, w), lambda i: (jnp.maximum((blocks - 1 - i) * (chunk // 8) - 1, 0), 0))
    width = pbd.shape[1]
    lines = dp_n // 2
    more = max(lines - 1, 1)
    block = rows_out.shape[0] // dp_n
    quarter = tokens.shape[1]
    units = 4
    span = count // units
    dma = pltpu.SemaphoreType.DMA
    vm, sds = pltpu.VMEM, jax.ShapeDtypeStruct
    return pl.pallas_call(
        functools.partial(scan_bwd_kernel, heads, total_inner, taps, bc, dp_n),
        grid=(blocks,),
        in_specs=[
            back(inner), back(inner), back(inner), back(inner), halo(inner), back(width), halo(width),
            pl.BlockSpec((1, bc // 2, inner), lambda i: (blocks - 1 - i, 0, 0)), whole(rows), whole(vec),
            whole(gn), whole(rows_out), whole(tokens), whole(y_send), whole(g_own),
        ],
        out_specs=[
            back(inner), back(inner), back(width), pl.BlockSpec((8, vec.shape[1]), lambda i: (0, 0)),
            whole(tokens), pl.BlockSpec((block, inner), lambda i: (0, 0)),
        ],
        scratch_shapes=[
            vm((bc // 2, inner), F32), vm((chunk + 8, inner), F32), vm((chunk + 8, bc), F32),
            vm((chunk + 8, inner), F32), vm((chunk + 8, bc), F32),
            vm((8, inner), F32), vm((8, bc), F32), vm((2 * heads, chunk), F32),
            vm((chunk, chunk), BF), vm((chunk, 3 * inner), BF), vm((3, inner, chunk), BF), vm((heads * chunk, chunk), BF),
            vm((units, 2, span, quarter), BF), vm((units, 2, span, quarter), BF),
            vm((units, span, quarter), BF), vm((units, span, quarter), BF),
            vm((2, span, quarter), F32), vm((units, span, quarter), F32),
            vm(y_send.shape, BF), vm(y_send.shape, BF), vm((2, more, block, inner // 2), BF), vm(y_send.shape, F32),
            dma((units,)), dma((units,)), dma((units,)), dma((units,)), dma((2,)), dma((2,)),
            dma((2, more)), dma((2, more)),
        ],
        out_shape=[
            sds((count, inner), BF), sds((count, inner), BF), sds((count, width), BF),
            sds((8, vec.shape[1]), F32), sds(tokens.shape, BF), sds((block, inner), F32),
        ],
        compiler_params=pltpu.CompilerParams(
            collective_id=3, has_side_effects=True, vmem_limit_bytes=58 * 2**20
        ),
        name="scan_backward",
    )(ggn, y, pz, px, px, pbd, pbd, sin, rows, vec, gn, rows_out, tokens, y_send, g_own)
def peers(dp_n):
    dp, hm = lax.axis_index("dp"), lax.axis_index("heads")
    across, core = hm // 2, hm % 2
    pair, line, lines = dp % 2, dp // 2, dp_n // 2
    return dict(
        sib=(dp, 2 * across + 1 - core),
        xn=(dp, 2 * (1 - across) + core),
        dg=(dp, 2 * (1 - across) + 1 - core),
        yn=(2 * line + 1 - pair, hm),
        line=lambda k: (2 * ((line + k) % lines) + pair, hm),
        mine=hm,
        other=2 * (1 - across) + core,
        sib_mine=2 * across + 1 - core,
        sib_other=2 * (1 - across) + 1 - core,
        pair=pair, line_index=line, lines=lines, dp=dp, core=core,
    )


def meet(who):
    barrier = pltpu.get_barrier_semaphore()
    for name in ("sib", "xn", "dg", "yn"):
        pl.semaphore_signal(barrier, inc=1, device_id=who[name], device_id_type=MESH)

    def greet(k, carry):
        pl.semaphore_signal(barrier, inc=1, device_id=who["line"](k), device_id_type=MESH)
        return carry

    lax.fori_loop(1, who["lines"], greet, 0)
    pl.semaphore_wait(barrier, 4 + who["lines"] - 1)


def push(src, dst, send, recv, to):
    return pltpu.make_async_remote_copy(
        src_ref=src, dst_ref=dst, send_sem=send, recv_sem=recv, device_id=to, device_id_type=MESH
    )


def tail_kernel(
    dp_n, units,
    normed_t_in, lpz_in, rows_z_in, lpx_in, rows_x_in, lpbd_in, rows_bd_in, normed_in,
    tokens, acc, cot, q_wide, vec,
    grad_tokens, g_x, g_z, g_bc, small_out,
    sib_send, sib_recv, x_send, x_recv, part, held,
    y_send, y_recv, z_send, z_recv, g_own, yb_send, yb_recv, zb_send, zb_recv, gb_own, bh_send, bh_recv,
    bx_send, bx_recv, bs_recv, h_send, h_recv, sy_send, sy_recv, sz_send, sz_recv, dy_send, dy_recv, dz_send, dz_recv, row_sums,
    normed_t, lpz, rows_z, lpx, rows_x, lpbd, rows_bd, normed,
    s_in, s_sib, r_sib, s_x, r_x, s_y, r_y, s_z, r_z, s_m, r_m, s_sl, r_sl,
):
    loads = [
        pltpu.make_async_copy(src, dst, s_in.at[i])
        for i, (src, dst) in enumerate((
            (normed_t_in, normed_t), (lpz_in, lpz), (rows_z_in, rows_z), (lpx_in, lpx), (rows_x_in, rows_x),
            (lpbd_in, lpbd), (rows_bd_in, rows_bd), (normed_in, normed),
        ))
    ]
    for load in loads:
        load.start()
    who = peers(dp_n)
    meet(who)
    count = normed.shape[0]
    width = normed.shape[1]
    inner = lpx.shape[1]
    bc = 2 * bh_send.shape[1]
    quarter = width // 4
    span = count // units
    block = width // dp_n
    lines = who["lines"]

    def copy_sib(u):
        return push(sib_send.at[u], sib_recv.at[u], s_sib.at[u], r_sib.at[u], who["sib"])

    def copy_x(u):
        return push(x_send.at[u], x_recv.at[u], s_x.at[u], r_x.at[u], who["xn"])

    def product(u, q):
        cols = pl.ds(pl.multiple_of(q * quarter, quarter), quarter)
        at = slice(u * span, (u + 1) * span)
        return nt(lpx[at, :], rows_x[cols, :]) + nt(lpz[at, :], rows_z[cols, :]) + nt(lpbd[at, :], rows_bd[cols, :])

    def head_a(u):
        for k, q in enumerate(("sib_mine", "sib_other", "mine", "other")):
            p = product(u, who[q])
            at = slice(u * span, (u + 1) * span)
            cols = pl.ds(pl.multiple_of(who[q] * quarter, quarter), quarter)
            inner_p = p * normed[at, cols].astype(F32)
            h_send[0:1, cols] += jnp.sum(inner_p, axis=0, keepdims=True)
            first = u * span
            lanes = slice(first % width, first % width + span)
            h_send[2 + first // width : 3 + first // width, lanes] += nt(
                jnp.ones((8, quarter), BF), inner_p.astype(BF)
            )[0:1]
            if k < 2:
                sib_send[u, k] = p.astype(BF)
            else:
                part[u % 2, k - 2] = p
        copy_sib(u).start()

    def head_b(u):
        copy_sib(u).wait()
        x_send[u] = (part[u % 2, 1] + sib_recv[u, 1].astype(F32)).astype(BF)
        copy_x(u).start()
        held[u] = part[u % 2, 0] + sib_recv[u, 0].astype(F32)

    def head_c(u):
        copy_x(u).wait()
        total = held[u] + x_recv[u].astype(F32)
        first = u * span
        lanes = q_wide.shape[1]
        cols = pl.ds(pl.multiple_of(who["mine"] * quarter, quarter), quarter)
        for j in range(span // lanes):
            at = slice(first + j * lanes, first + (j + 1) * lanes)
            row, lane = (first + j * lanes) // width, (first + j * lanes) % width
            dots = jnp.transpose(jnp.broadcast_to(row_sums[row : row + 1, lane : lane + lanes], (lanes, lanes)))
            q = q_wide[at, :]
            coef = q * q * (dots / width)
            grad_tokens[at, :] = (
                cot[at, :].astype(F32)
                + q[:, 0:1] * vec[6:7, cols] * total[j * lanes : (j + 1) * lanes]
                - tokens[at, :].astype(F32) * coef[:, 0:1]
            )

    def rows_of(line, pair):
        return pl.ds(pl.multiple_of((2 * line + pair) * block, block), block)

    def grad_a(v):
        left, right = ((normed_t, lpz), (normed_t, lpx))[v // 2]
        cols = slice((v % 2) * (inner // 2), (v % 2 + 1) * (inner // 2))
        for side in (0, 1):
            pair = (1 - who["pair"]) if side == 0 else who["pair"]
            stacked = jnp.concatenate([left[rows_of(l, pair), :] for l in range(lines)], axis=0)
            value = nn(stacked, right[:, cols])
            if side == 0:
                y_send[v] = value.astype(BF)
                copy_y(v).start()
            else:
                g_own[v] = value

    def copy_y(v):
        return push(y_send.at[v], y_recv.at[v], s_y.at[v], r_y.at[v], who["yn"])

    def copy_z(v, k):
        to = (who["line_index"] + k) % lines
        return push(
            z_send.at[v, pl.ds(pl.multiple_of(to * block, block), block)],
            z_recv.at[v, k - 1], s_z.at[v, k - 1], r_z.at[v, k - 1], who["line"](k),
        )

    def each_line(fn):
        def step(k, carry):
            fn(k)
            return carry

        lax.fori_loop(1, lines, step, 0)

    def own_rows():
        return pl.ds(pl.multiple_of(who["line_index"] * block, block), block)

    def grad_b(v):
        copy_y(v).wait()
        g_own[v] = g_own[v] + y_recv[v].astype(F32)
        z_send[v] = g_own[v].astype(BF)
        each_line(lambda k: copy_z(v, k).start())

    def grad_c(v):
        each_line(lambda k: copy_z(v, k).wait())
        total = g_own[v, own_rows(), :]
        for k in range(lines - 1):
            total = total + z_recv[v, k].astype(F32)
        cols = slice((v % 2) * (inner // 2), (v % 2 + 1) * (inner // 2))
        (g_z, g_x)[v // 2][:, cols] = total

    half = bc // 2

    def copy_bh():
        return push(bh_send, bh_recv, s_m.at[0], r_m.at[0], who["sib"])

    def copy_yb():
        return push(yb_send, yb_recv, s_m.at[1], r_m.at[1], who["yn"])

    def copy_zb(k):
        to = (who["line_index"] + k) % lines
        return push(
            zb_send.at[pl.ds(pl.multiple_of(to * block, block), block)],
            zb_recv.at[k - 1], s_sl.at[0, k - 1], r_sl.at[0, k - 1], who["line"](k),
        )

    def copy_bx():
        return push(bx_send, bx_recv, s_m.at[2], r_m.at[2], who["xn"])

    def copy_bs():
        return push(bx_send, bs_recv, s_m.at[3], r_m.at[3], who["sib"])

    def bc_a():
        for side in (0, 1):
            pair = (1 - who["pair"]) if side == 0 else who["pair"]
            stacked = jnp.concatenate([normed_t[rows_of(l, pair), :] for l in range(lines)], axis=0)
            value = nn(stacked, lpbd[:, :bc])
            first = who["core"] == 0
            lo, hi = value[:, :half], value[:, half:]
            at = slice(side * lines * block, (side + 1) * lines * block)
            bh_send[at, :] = jnp.where(first, hi, lo).astype(BF)
            gb_own[at, :] = jnp.where(first, lo, hi)
        copy_bh().start()

    def bc_b():
        copy_bh().wait()
        rows = lines * block
        gb_own[...] = gb_own[...] + bh_recv[...].astype(F32)
        yb_send[...] = gb_own[:rows, :].astype(BF)
        copy_yb().start()

    def bc_c():
        rows = lines * block
        copy_yb().wait()
        gb_own[rows:, :] = gb_own[rows:, :] + yb_recv[...].astype(F32)
        zb_send[...] = gb_own[rows:, :].astype(BF)
        each_line(lambda k: copy_zb(k).start())

    def bc_d():
        each_line(lambda k: copy_zb(k).wait())
        at = pl.ds(pl.multiple_of(lines * block + who["line_index"] * block, block), block)
        total = gb_own[at, :]
        for k in range(lines - 1):
            total = total + zb_recv[k].astype(F32)
        bx_send[...] = total
        copy_bx().start()

    def bc_e():
        copy_bx().wait()
        bx_send[...] = bx_send[...] + bx_recv[...]
        copy_bs().start()

    def bc_f():
        copy_bs().wait()
        mine, theirs = bx_send[...], bs_recv[...]
        first = who["core"] == 0
        g_bc[:, :half] = jnp.where(first, mine, theirs)
        g_bc[:, half:] = jnp.where(first, theirs, mine)

    three = (("sib", 4), ("xn", 5), ("dg", 6))
    token_rows = count // width

    def copy_h(k):
        name, sem = three[k]
        return push(h_send, h_recv.at[k], s_m.at[sem], r_m.at[sem], who[name])

    def small_a():
        h_send[1:2, :] = acc[1:2, :]
        for k in range(3):
            copy_h(k).start()

    def copy_sy():
        return push(sy_send, sy_recv, s_m.at[7], r_m.at[7], who["yn"])

    def copy_dy():
        return push(dy_send, dy_recv, s_m.at[8], r_m.at[8], who["yn"])

    def copy_sz(k):
        return push(sz_send, sz_recv.at[k - 1], s_sl.at[1, k - 1], r_sl.at[1, k - 1], who["line"](k))

    def copy_dz(k):
        return push(dz_send, dz_recv.at[k - 1], s_sl.at[2, k - 1], r_sl.at[2, k - 1], who["line"](k))

    def dt_a():
        dy_send[...] = tn(lpbd[:, bc:], normed[...])[0:16, :].astype(BF)
        copy_dy().start()

    def dt_b():
        copy_dy().wait()
        dz_send[...] = (dy_send[...].astype(F32) + dy_recv[...].astype(F32)).astype(BF)
        each_line(lambda k: copy_dz(k).start())

    def dt_c():
        each_line(lambda k: copy_dz(k).wait())
        total = dz_send[...].astype(F32)
        for k in range(lines - 1):
            total = total + dz_recv[k].astype(F32)
        small_out[8:24, :] = total

    def small_b():
        for k in range(3):
            copy_h(k).wait()
        over_heads = h_send[...] + h_recv[0] + h_recv[1] + h_recv[2]
        row_sums[0:token_rows, :] = over_heads[2 : 2 + token_rows, :]
        sy_send[0:2, :] = over_heads[0:2, :]
        sy_send[2:8, :] = acc[2:8, :]
        copy_sy().start()

    def small_c():
        copy_sy().wait()
        sz_send[...] = sy_send[...] + sy_recv[...]
        each_line(lambda k: copy_sz(k).start())

    def small_d():
        each_line(lambda k: copy_sz(k).wait())
        total = sz_send[...]
        for k in range(lines - 1):
            total = total + sz_recv[k]
        small_out[0:8, :] = total

    h_send[...] = jnp.zeros_like(h_send)

    def seq(*steps):
        for fn, *args in steps:
            fn(*args)

    assert units == 4

    def load(*which):
        for i in which:
            loads[i].wait()

    load(0, 1)
    seq((grad_a, 0), (grad_a, 1))
    load(2, 3, 4, 5, 6, 7)
    seq((head_a, 0), (bc_a,), (head_a, 1), (head_b, 0), (grad_a, 2), (bc_b,), (head_b, 1), (grad_b, 0), (head_a, 2))
    seq((grad_a, 3), (head_b, 2), (dt_a,), (grad_b, 1), (head_a, 3), (small_a,), (bc_c,), (head_b, 3), (dt_b,))
    seq((small_b,), (grad_b, 2), (grad_c, 0), (small_c,), (bc_d,), (dt_c,), (head_c, 0), (grad_b, 3), (grad_c, 1))
    seq((bc_e,), (head_c, 1), (small_d,), (head_c, 2), (grad_c, 2), (bc_f,), (head_c, 3), (grad_c, 3))


def tail(dp_n, units, normed_t, normed, lpx, lpz, lpbd, rows_x, rows_z, rows_bd, tokens, acc, cot, q_wide, vec, bc):
    count, width = normed.shape
    inner = lpx.shape[1]
    quarter = width // 4
    span = count // units
    block = width // dp_n
    lines = dp_n // 2
    half_rows = lines * block
    more = max(lines - 1, 1)
    vm = pltpu.VMEM
    dma = pltpu.SemaphoreType.DMA
    operands = (
        normed_t, lpz, rows_z, lpx, rows_x, lpbd, rows_bd, normed, tokens, acc, cot, q_wide, vec,
    )
    sds = jax.ShapeDtypeStruct
    spec = pl.BlockSpec(memory_space=pltpu.VMEM)
    return pl.pallas_call(
        functools.partial(tail_kernel, dp_n, units),
        out_shape=[
            sds((count, quarter), F32), sds((block, inner), F32), sds((block, inner), F32), sds((block, bc), F32),
            sds((24, width), F32),
        ],
        in_specs=[pl.BlockSpec(memory_space=pl.ANY)] * 8 + [spec] * 5,
        out_specs=[spec] * 5,
        scratch_shapes=[
            vm((units, 2, span, quarter), BF), vm((units, 2, span, quarter), BF),
            vm((units, span, quarter), BF), vm((units, span, quarter), BF),
            vm((2, 2, span, quarter), F32), vm((units, span, quarter), F32),
            vm((4, half_rows, inner // 2), BF), vm((4, half_rows, inner // 2), BF),
            vm((4, half_rows, inner // 2), BF), vm((4, more, block, inner // 2), BF),
            vm((4, half_rows, inner // 2), F32),
            vm((half_rows, bc // 2), BF), vm((half_rows, bc // 2), BF),
            vm((half_rows, bc // 2), BF), vm((more, block, bc // 2), BF),
            vm((2 * half_rows, bc // 2), F32),
            vm((2 * half_rows, bc // 2), BF), vm((2 * half_rows, bc // 2), BF),
            vm((block, bc // 2), F32), vm((block, bc // 2), F32), vm((block, bc // 2), F32),
            vm((8, width), F32), vm((3, 8, width), F32),
            vm((8, width), F32), vm((8, width), F32), vm((8, width), F32), vm((more, 8, width), F32),
            vm((16, width), BF), vm((16, width), BF), vm((16, width), BF), vm((more, 16, width), BF),
            vm((8, width), F32),
        ]
        + [vm(a.shape, a.dtype) for a in operands[:8]]
        + [
            dma((8,)), dma((units,)), dma((units,)), dma((units,)), dma((units,)),
            dma((4,)), dma((4,)), dma((4, more)), dma((4, more)), dma((9,)), dma((9,)),
            dma((3, more)), dma((3, more)),
        ],
        compiler_params=pltpu.CompilerParams(
            collective_id=1, has_side_effects=True, vmem_limit_bytes=62 * 2**20
        ),
        name="tail",
    )(*operands)
def shares(ref_in, block_of, dp_n, width, send, recv, who):
    rows = ref_in.shape[0]
    lines = who["lines"]
    source = ref_in.at[:, width] if ref_in.shape[1] != width.size else ref_in

    def at(dp):
        return block_of.at[pl.ds(pl.multiple_of(dp * rows, rows), rows), width]

    def own():
        return push(source, at(who["dp"]), send.at[0], recv.at[0], who["yn"])

    def along(k):
        return push(source, at(who["dp"]), send.at[k], recv.at[k], who["line"](k))

    def onward(k):
        there = at(2 * ((who["line_index"] - k + lines) % lines) + who["pair"])
        return push(there, there, send.at[lines - 1 + k], recv.at[lines - 1 + k], who["yn"])

    return own, along, onward


def chain(ref_in, block_of, width, send, recv, y_send, y_recv, who):
    rows = ref_in.shape[0]
    lines, line, pair, dp = who["lines"], who["line_index"], who["pair"], who["dp"]

    def at(index):
        return block_of.at[pl.ds(pl.multiple_of((2 * index + pair) * rows, rows), rows), width]

    def hand(sign, j):
        index = line - sign * j
        source = ref_in.at[:, width] if isinstance(j, int) and j == 0 else at(index)
        slot = j + 1 if sign > 0 else lines + j
        to = (2 * (line + sign) + pair, who["mine"])
        return push(source, at(index), send.at[slot], recv.at[slot], to)

    def to_pair(sign, j):
        slot = j if sign > 0 else lines - 1 + j
        index = line - sign * j
        source = ref_in.at[:, width] if isinstance(j, int) and j == 0 else at(index)
        return push(source, at(index), y_send.at[slot], y_recv.at[slot], who["yn"])

    def arrived(sign, j):
        slot = j if sign > 0 else lines - 1 + j
        block = at(line - sign * j)
        return push(block, block, send.at[slot], recv.at[slot], who["yn"])

    def inside(index):
        return jnp.logical_and(index >= 0, index < lines)

    def both(fn):
        for sign in (1, -1):
            fn(sign)

    def begin():
        def one(sign):
            @pl.when(inside(line + sign))
            def _():
                hand(sign, 0).start()

        both(one)

    def begin_pair():
        to_pair(1, 0).start()

    def hop(j):
        def one(sign):
            @pl.when(inside(line - sign * j))
            def _():
                arrived(sign, j).wait_recv()

                @pl.when(inside(line + sign))
                def _():
                    hand(sign, j).start()

                to_pair(sign, j).start()

        both(one)

    def end():
        to_pair(1, 0).wait()

        def one(sign):
            @pl.when(inside(line + sign))
            def _():
                hand(sign, 0).wait_send()

        both(one)

        def later(j):
            def one(sign):
                @pl.when(inside(line - sign * j))
                def _():
                    to_pair(sign, j).wait()

                    @pl.when(inside(line + sign))
                    def _():
                        hand(sign, j).wait_send()

            both(one)

        loop_line(lines, later)

    return begin, begin_pair, hop, end


def loop_line(lines, fn):
    def step(k, carry):
        fn(k)
        return carry

    lax.fori_loop(1, lines, step, 0)


def front_kernel(
    dp_n, heads, units, taps, bc,
    tokens, cot, w_x, w_bc, w_z, w_out, w_dt, conv_x, conv_bc, norm_gain, gate_gain, dt_bias, a_log, skip, starts, fill,
    vec, px_out, pbd_out, normed_out, normed_t_out, q_out, y_out, sin_out, parts, rows_x, rows_bd, rows_z, rows_out,
    own_dt, tok, wx, wbd, px, pbd, normed, normed_t, q, y, sin, own_w, own_cot, state, extx, extb, upper, spread,
    s_loc, s_sib, r_sib, s_x, r_x, s_f, r_f, s_cx, r_cx, s_cf, r_cf, s_w, r_w, s_c, r_c, s_cy, r_cy, s_out, s_y,
):
    who = peers(dp_n)
    count, quarter = tokens.shape
    width = 4 * quarter
    span = count // units
    lines = who["lines"]
    block, inner = w_x.shape
    blocks = sin.shape[0]
    chunk = count // blocks
    per = blocks // units
    pieces = s_cx.shape[0]
    cot_span = count // pieces
    here = pl.ds(pl.multiple_of(who["dp"] * block, block), block)
    own_half = pl.ds(pl.multiple_of(who["core"] * (bc // 2), bc // 2), bc // 2)
    dt_cols = pl.ds(bc, chunk)
    local = [
        pltpu.make_async_copy(src, dst, s_loc.at[k])
        for k, (src, dst) in enumerate((
            (tokens, tok.at[who["mine"]]), (w_x, wx.at[here]), (w_bc.at[:, own_half], wbd.at[here, own_half]),
            (w_z, own_w.at[0]), (w_out, own_w.at[1]), (cot, own_cot),
        ))
    ]
    for copy in local:
        copy.start()
    own_dt[...] = jnp.zeros_like(own_dt)
    own_dt[:, :heads] = w_dt[...]
    wbd[here, dt_cols] = own_dt[...]
    onto = [
        pltpu.make_async_copy(src, dst, s_loc.at[8 + k])
        for k, (src, dst) in enumerate((
            (own_w.at[0], rows_z.at[here]), (own_w.at[1], rows_out.at[here]), (own_cot, parts.at[who["mine"]]),
        ))
    ]
    meet(who)

    def rows(s, n=span):
        return pl.ds(pl.multiple_of(s * n, n), n)

    def to_x(s):
        return push(tokens.at[rows(s)], tok.at[who["mine"], rows(s)], s_x.at[s], r_x.at[s], who["xn"])

    def to_sib():
        return push(tokens, tok.at[who["mine"]], s_sib.at[0], r_sib.at[0], who["sib"])

    def forward(s):
        at = tok.at[who["other"], rows(s)]
        return push(at, at, s_f.at[s], r_f.at[s], who["sib"])

    def cot_x(j):
        at = rows(j, cot_span)
        return push(cot.at[at], parts.at[who["mine"], at], s_cx.at[j], r_cx.at[j], who["xn"])

    def cot_sib():
        return push(cot, parts.at[who["mine"]], s_sib.at[1], r_sib.at[1], who["sib"])

    def cot_forward(j):
        at = parts.at[who["other"], rows(j, cot_span)]
        return push(at, at, s_cf.at[j], r_cf.at[j], who["sib"])

    half = inner // 2
    cuts = [
        shares(ref, to, dp_n, cols, s_w.at[n], r_w.at[n], who)
        for n, (ref, to, cols) in enumerate((
            (w_x, wx, pl.ds(0, half)), (w_x, wx, pl.ds(half, half)), (w_bc, wbd, own_half), (own_dt, wbd, dt_cols),
        ))
    ]
    chains = [
        chain(ref, to, pl.ds(h * half, half), s_c.at[2 * n + h], r_c.at[2 * n + h], s_cy.at[2 * n + h], r_cy.at[2 * n + h], who)
        for n, (ref, to) in enumerate(((w_z, rows_z), (w_out, rows_out)))
        for h in (0, 1)
    ]

    def offer(n):
        loop_line(lines, lambda k: cuts[n][1](k).start())

    def other_half():
        cols = wbd.at[:, own_half]
        return push(cols, cols, s_sib.at[2], r_sib.at[2], who["sib"])

    def pass_rows(n):
        own, along, onward = cuts[n]
        own().start()

        def one(k):
            along(k).wait()
            onward(k).start()

        loop_line(lines, one)

    def have(n):
        own, along, onward = cuts[n]
        own().wait()
        loop_line(lines, lambda k: onward(k).wait())

    def pass_cot(j):
        cot_x(j).wait()
        cot_forward(j).start()

    to_x(0).start()
    offer(0)
    for s in range(1, units):
        to_x(s).start()
    to_sib().start()
    for n in (1, 2, 3):
        offer(n)
    for j in range(pieces):
        cot_x(j).start()
    for begin, begin_pair, hop, end in chains:
        begin()
    pack_vec(vec, conv_x, conv_bc, norm_gain, gate_gain, dt_bias, a_log, skip, starts, fill, chunk)
    set_upper(upper)
    set_spread(spread, heads)
    state[...] = jnp.zeros_like(state)
    extx[...] = jnp.zeros_like(extx)
    extb[...] = jnp.zeros_like(extb)
    par = read_vec(vec, heads, chunk, inner, bc, taps)
    gain = vec[6:7, :width]

    def out_copies(s):
        at = rows(s)
        every = slice(None)
        return [
            pltpu.make_async_copy(ref.at[to], out.at[to], s_out.at[n, s])
            for n, (ref, out, to) in enumerate((
                (normed, normed_out, (at,)), (normed_t, normed_t_out, (every, at)), (q, q_out, (at,)),
                (px, px_out, (at,)), (pbd, pbd_out, (at,)),
            ))
        ]

    def norm(s):
        at = rows(s)
        values = [tok[h, at, :].astype(F32) for h in range(4)]
        total = sum(jnp.sum(p * p, axis=1, keepdims=True) for p in values)
        inv = lax.rsqrt(total / width + EPS)
        q[at, :] = jnp.broadcast_to(inv, (span, q.shape[1]))
        for h in range(4):
            cols = slice(h * quarter, (h + 1) * quarter)
            value = (values[h] * inv * gain[:, cols]).astype(BF)
            normed[at, cols] = value
            normed_t[cols, at] = jnp.transpose(value)
        for copy in out_copies(s)[:3]:
            copy.start()

    def project(s):
        at = rows(s)
        pbd[at, :] = nn(normed[at, :], wbd[...])
        px[at, :] = nn(normed[at, :], wx[...])
        for copy in out_copies(s)[3:]:
            copy.start()

    local[0].wait()
    to_x(0).wait()
    forward(0).start()
    pass_rows(0)
    to_sib().wait()
    forward(0).wait()
    norm(0)
    to_x(1).wait()
    forward(1).start()
    pass_rows(1)
    forward(1).wait()
    norm(1)
    pass_rows(2)
    pass_rows(3)
    have(2)
    local[2].wait()
    other_half().start()
    to_x(2).wait()
    forward(2).start()
    for copy in local[3:]:
        copy.wait()
    for copy in onto:
        copy.start()
    cot_sib().start()
    forward(2).wait()
    norm(2)
    local[1].wait()
    for n in (0, 1, 3):
        have(n)
    other_half().wait()
    keep_rows = [
        pltpu.make_async_copy(wx, rows_x, s_loc.at[6]), pltpu.make_async_copy(wbd, rows_bd, s_loc.at[7]),
    ]
    for copy in keep_rows:
        copy.start()

    def last_tokens(s):
        to_x(s).wait()
        forward(s).start()

    def last_norm(s):
        forward(s).wait()
        norm(s)

    events = {1: [(last_tokens, units - 1)], 2: [(last_norm, units - 1)]}
    late = []
    plan = []
    for n, (begin, begin_pair, hop, end) in enumerate(chains):
        plan.append((lambda k, fn=begin_pair: fn(), 0, 1 + 2 * n))
        for j in range(1, min(lines, 4)):
            plan.append((hop, j, 1 + 2 * n + j))
        if lines > 4:
            plan.append((lambda k, fn=hop: lax.fori_loop(4, lines, lambda j, a: (fn(j), a)[1], 0), 0, 5 + 2 * n))
    plan += [(pass_cot, j, 5 + 2 * j) for j in range(pieces)]
    for fn, k, at in plan:
        if at < blocks:
            events.setdefault(at, []).append((fn, k))
        else:
            late.append((fn, k))

    def y_copies(c):
        at = rows(c, chunk)
        return (
            pltpu.make_async_copy(y.at[at], y_out.at[at], s_y.at[0, c]),
            pltpu.make_async_copy(sin.at[c], sin_out.at[c], s_y.at[1, c]),
        )

    def step(c, carry):
        for at, fns in events.items():

            @pl.when(c == at)
            def _(fns=fns):
                for fn, k in fns:
                    fn(k)

        @pl.when(c % per == 0)
        def _():
            project(c // per)

        at = rows(c, chunk)
        y_c, enter = scan_step(
            heads, par, read_block(vec, c, chunk), px.at[at], pbd.at[at], upper, spread, state, extx, extb
        )
        y[at, :] = y_c
        sin[c] = enter
        for copy in y_copies(c):
            copy.start()
        return carry

    lax.fori_loop(0, blocks, step, 0)
    for fn, k in late:
        fn(k)

    def end_y(c, carry):
        for copy in y_copies(c):
            copy.wait()
        return carry

    lax.fori_loop(0, blocks, end_y, 0)
    for s in range(units):
        for copy in out_copies(s):
            copy.wait()
    for copy in onto + keep_rows:
        copy.wait()
    cot_sib().wait()
    for j in range(pieces):
        cot_forward(j).wait()
    for begin, begin_pair, hop, end in chains:
        end()


def front(dp_n, tokens, cot, w_x, w_bc, w_z, w_out, w_dt, conv_x, conv_bc, norm_gain, gate_gain, *scalars):
    count, quarter = tokens.shape
    width = 4 * quarter
    inner, heads = w_x.shape[1], w_dt.shape[1]
    taps, bc = conv_bc.shape
    blocks = scalars[-1].shape[0]
    chunk = count // blocks
    wide = bc + chunk
    units, pieces = 4, 8
    vm, dma, sds = pltpu.VMEM, pltpu.SemaphoreType.DMA, jax.ShapeDtypeStruct
    hbm, vmem = pl.BlockSpec(memory_space=pl.ANY), pl.BlockSpec(memory_space=pltpu.VMEM)
    ways = dp_n - 1
    outs = [
        sds((24 + blocks, width), F32),
        sds((count, inner), F32), sds((count, wide), F32), sds((count, width), BF), sds((width, count), BF),
        sds((count, 128), F32), sds((count, inner), F32), sds((blocks, bc // 2, inner), BF),
        sds((4, count, quarter), BF), sds((width, inner), BF), sds((width, wide), BF), sds((width, inner), BF),
        sds((width, inner), BF),
    ]
    return pl.pallas_call(
        functools.partial(front_kernel, dp_n, heads, units, taps, bc),
        out_shape=outs,
        in_specs=[hbm] * 6 + [vmem] * 5 + [pl.BlockSpec(memory_space=pltpu.SMEM)] * 5,
        out_specs=[vmem] + [hbm] * (len(outs) - 1),
        scratch_shapes=[
            vm((w_x.shape[0], chunk), BF),
            vm((4, count, quarter), BF), vm((width, inner), BF), vm((width, wide), BF),
            vm((count, inner), F32), vm((count, wide), F32), vm((count, width), BF), vm((width, count), BF),
            vm((count, 128), F32), vm((count, inner), F32), vm((blocks, bc // 2, inner), BF),
            vm((2,) + w_z.shape, BF), vm(cot.shape, BF),
            vm((bc // 2, inner), F32), vm((chunk + 8, inner), F32), vm((chunk + 8, bc), F32),
            vm((chunk, chunk), BF), vm((chunk, 3 * inner), BF),
            dma((11,)), dma((3,)), dma((3,)), dma((units,)), dma((units,)), dma((units,)), dma((units,)),
            dma((pieces,)), dma((pieces,)), dma((pieces,)), dma((pieces,)),
            dma((4, ways)), dma((4, ways)), dma((4, ways + 1)), dma((4, ways + 1)), dma((4, ways)), dma((4, ways)),
            dma((5, units)), dma((2, blocks)),
        ],
        compiler_params=pltpu.CompilerParams(
            collective_id=2, has_side_effects=True, vmem_limit_bytes=58 * 2**20
        ),
        name="front",
    )(
        tokens, cot, w_x, w_bc, w_z, w_out, w_dt, conv_x, conv_bc, norm_gain[None, :], gate_gain[None, :], *scalars
    )
def finish_kernel(heads, taps, bc, bo, gt, gx, gz, go, gb, small, own, o_bo, o_gt, o_gx, o_gz, o_go, o_gb, o_gain, o_cx, o_cb, o_bias, o_alog, o_skip, o_gate):
    o_bo[...] = bo[...]
    o_gt[...] = gt[...]

    @pl.when(pl.program_id(0) == 0)
    def _():
        for src, dst in ((gx, o_gx), (gz, o_gz), (go, o_go), (gb, o_gb)):
            dst[...] = src[...]
        inner = o_cx.shape[1]
        per = small.shape[1] // inner
        for k in range(taps):
            o_cx[k : k + 1, :] = small[2 + k // per : 3 + k // per, (k % per) * inner : (k % per + 1) * inner]
            o_cb[k : k + 1, :] = small[1:2, k * bc : (k + 1) * bc]
        scalars = small[5:6, :128]
        o_bias[...] = scalars[0, :heads]
        o_alog[...] = scalars[0, heads : 2 * heads]
        o_skip[...] = scalars[0, 2 * heads : 3 * heads]
        o_gate[...] = small[4, :inner]
        columns = o_gain.shape[0]
        at = pl.ds(pl.multiple_of(lax.axis_index("heads") * columns, columns), columns)
        o_gain[...] = (small[0:1, at] / own[:, at])[0]


def finish(bo, gt, gx, gz, go, gb, small, norm_gain, heads, taps, bc):
    steps = 4
    sds = jax.ShapeDtypeStruct
    count, quarter = bo.shape
    inner = gx.shape[1]
    rows = pl.BlockSpec((count // steps, quarter), lambda i: (i, 0))
    whole = lambda shape: pl.BlockSpec(shape, lambda i: (0,) * len(shape))
    smalls = [(quarter,), (taps, inner), (taps, bc), (heads,), (heads,), (heads,), (inner,)]
    operands = (bo, gt, gx, gz, go, gb, small, norm_gain[None, :])
    return pl.pallas_call(
        functools.partial(finish_kernel, heads, taps, bc),
        grid=(steps,),
        in_specs=[rows, rows] + [whole(a.shape) for a in operands[2:]],
        out_specs=[rows, rows] + [whole(a.shape) for a in operands[2:6]] + [whole(s) for s in smalls],
        out_shape=[sds(a.shape, a.dtype) for a in operands[:6]] + [sds(s, F32) for s in smalls],
        name="finish",
    )(*operands)


def body(
    tokens, cotangent, starts, fill, norm_gain, w_x, w_z, w_dt, w_bc, conv_x, conv_bc, dt_bias, a_log, skip,
    gate_gain, w_out,
):
    heads_n = lax.axis_size("heads")
    dp_n = lax.axis_size("dp")
    dp_index = lax.axis_index("dp")
    count, columns = tokens.shape
    width = columns * heads_n
    blocks = starts.shape[0]
    chunk = count // blocks
    inner = w_x.shape[1]
    heads = w_dt.shape[1]
    taps, bc = conv_bc.shape
    vec, px, pbd, normed, normed_t, q_wide, y, sin, parts, rows_x, rows_bd, rows_z, rows_out = front(
        dp_n, tokens, cotangent, w_x, w_bc, w_z, w_out, w_dt, conv_x, conv_bc, norm_gain, gate_gain, dt_bias, a_log,
        skip, starts, fill,
    )
    pz, ggn, sums, gn, y_send, g_own = gate(dp_n, blocks, normed, rows_z, rows_out, parts, y, vec)
    lpx, lpz, lpbd, acc, block_out, grad_w_out = scan_backward(
        dp_n, ggn, y, pz, px, pbd, sin, sums, vec, gn, rows_out, tokens, y_send, g_own, heads, taps, bc,
        inner * heads_n,
    )
    grad_tokens, grad_w_x, grad_w_z, grad_w_bc, small = tail(
        dp_n, 4, normed_t, normed, lpx, lpz, lpbd, rows_x, rows_z, rows_bd, tokens, acc, cotangent, q_wide, vec, bc,
    )
    block = width // dp_n
    grad_w_dt = lax.dynamic_slice_in_dim(small[8 : 8 + heads], dp_index * block, block, 1).T
    (
        block_out, grad_tokens, grad_w_x, grad_w_z, grad_w_out, grad_w_bc, grad_norm_gain, grad_conv_x, grad_conv_bc,
        grad_dt_bias, grad_a_log, grad_skip, grad_gate_gain,
    ) = finish(
        block_out, grad_tokens, grad_w_x, grad_w_z, grad_w_out, grad_w_bc, small, norm_gain, heads, taps, bc
    )
    return (
        block_out, grad_tokens, grad_norm_gain, grad_w_x, grad_w_z, grad_w_dt, grad_w_bc, grad_conv_x, grad_conv_bc,
        grad_dt_bias, grad_a_log, grad_skip, grad_gate_gain, grad_w_out,
    )


def solution(mesh):
    placed = (
        P("dp", "heads"),
        P("dp", "heads"),
        P("dp"),
        P("dp"),
        P(),
        P("dp", "heads"),
        P("dp", "heads"),
        P("dp", "heads"),
        P("dp", None),
        P(None, "heads"),
        P(),
        P("heads"),
        P("heads"),
        P("heads"),
        P("heads"),
        P("dp", "heads"),
    )
    return jax.shard_map(
        body,
        mesh=mesh,
        in_specs=placed,
        out_specs=(
            P("dp", "heads"),
            P("dp", "heads"),
            P("heads"),
            P("dp", "heads"),
            P("dp", "heads"),
            P("dp", "heads"),
            P("dp", None),
            P(None, "heads"),
            P(),
            P("heads"),
            P("heads"),
            P("heads"),
            P("heads"),
            P("dp", "heads"),
        ),
        check_vma=False,
    )
```

```python
import functools
import jax
import jax.numpy as jnp
from jax import lax
from jax.experimental import pallas as pl
from jax.experimental.pallas import tpu as pltpu
from jax.sharding import PartitionSpec as P

HD = 64
EPS = 1e-05
F32 = jnp.float32
BF = jnp.bfloat16
NEG = -1e30
MESH = pl.DeviceIdType.MESH


def nn(a, b):
    return lax.dot_general(a, b, (((1,), (0,)), ((), ())), preferred_element_type=F32)


def nt(a, b):
    return lax.dot_general(a, b, (((1,), (1,)), ((), ())), preferred_element_type=F32)


def tn(a, b):
    return lax.dot_general(a, b, (((0,), (0,)), ((), ())), preferred_element_type=F32)


def split2(v):
    hi = v.astype(BF).astype(F32)
    return hi, v - hi


def split3(v):
    hi = v.astype(BF).astype(F32)
    rest = v - hi
    mid = rest.astype(BF).astype(F32)
    return hi, mid, rest - mid


def softplus(v):
    return jnp.maximum(v, 0.0) + jnp.log1p(jnp.exp(-jnp.abs(v)))


def sigmoid(v):
    return 1.0 / (1.0 + jnp.exp(-v))


def iota2(rows, cols, axis):
    return lax.broadcasted_iota(jnp.int32, (rows, cols), axis)


def zero_one(cond):
    return jnp.where(cond, 1.0, 0.0).astype(BF)


def set_upper(upper):
    upper[...] = zero_one(iota2(*upper.shape, 0) <= iota2(*upper.shape, 1))


def set_spread(spread, heads):
    rows, lanes = iota2(*spread.shape, 0), iota2(*spread.shape, 1)
    inner = heads * HD
    base = heads * (1 + 2 * (lanes // inner)) + (lanes % inner) // HD
    spread[...] = zero_one(jnp.logical_or(rows == base, rows == base + heads))


def set_gather(gather, ones_h, heads):
    for q in range(3):
        rows, lanes = iota2(*gather.shape[1:], 0), iota2(*gather.shape[1:], 1)
        gather[q] = zero_one(lanes == q * heads + rows // HD)
    rows, lanes = iota2(*ones_h.shape, 0), iota2(*ones_h.shape, 1)
    ones_h[...] = zero_one(lanes == heads + rows // ones_h.shape[1])


def conv_from(ext, taps, rows, halo):
    n = taps.shape[0]
    out = taps[n - 1 : n, :] * ext[pl.ds(halo, rows), :]
    for k in range(1, n):
        out = out + taps[n - 1 - k : n - k, :] * ext[pl.ds(halo - k, rows), :]
    return out


def dt_rows(pdt, bias, rate, fill, heads, upper):
    chunk = pdt.shape[0]
    pre = jnp.transpose(pdt)[:heads] + bias
    live = (iota2(heads, chunk, 1).astype(F32) < fill).astype(F32)
    dt = softplus(pre) * live
    hi, mid, low = split3(dt * rate)
    stacked = jnp.concatenate([hi, mid, low], axis=0).astype(BF)
    summed = nn(stacked, upper)
    run = summed[:heads] + summed[heads : 2 * heads] + summed[2 * heads :]
    return pre, live, dt, run


def spread_all(run, dt, heads, chunk, spread):
    last = run[:, chunk - 1 : chunk]
    e_in = jnp.exp(run)
    e_out = jnp.exp(last - run)
    parts = [run]
    for v in (dt, e_in, e_out):
        parts.extend(split2(v))
    used = heads * len(parts)
    if used < chunk:
        parts.append(jnp.zeros((chunk - used, chunk), F32))
    cols = jnp.transpose(jnp.concatenate(parts, axis=0))
    return cols, nn(cols.astype(BF), spread)


def pair_stack(v, low_lanes):
    zero = jnp.zeros_like(v)
    return jnp.concatenate([jnp.where(low_lanes, v, zero), jnp.where(low_lanes, zero, v)], axis=0)


def read_vec(vec, heads, chunk, inner, bc, taps):
    return dict(
        convx=vec[0:taps, :inner], skip=vec[4:5, :inner], gain=vec[5:6, :inner],
        bias=vec[8 : 8 + heads, :chunk], rate=vec[8 : 8 + heads, chunk : 2 * chunk], convbc=vec[16 : 16 + taps, :bc],
    )


def read_block(vec, c, chunk):
    row = vec[pl.ds(24 + c, 1), :]
    return row[:, 0:1] > 0.5, row[:, chunk : chunk + 1], row[:, 2 * chunk : 2 * chunk + 1] > 0.5


def pack_vec(vec, conv_x, conv_bc, norm_gain, gate_gain, dt_bias, a_log, skip, starts, fill, chunk):
    taps, inner = conv_x.shape
    vec[...] = jnp.zeros_like(vec)
    vec[0:taps, :inner] = conv_x[...]
    vec[16 : 16 + taps, : conv_bc.shape[1]] = conv_bc[...]
    vec[5:6, :inner] = gate_gain[...]
    vec[6:7, :] = norm_gain[...]
    head = iota2(1, inner, 1) // HD
    skips = jnp.zeros((1, inner), F32)
    for h in range(dt_bias.shape[0]):
        skips = jnp.where(head == h, skip[h], skips)
        vec[8 + h : 9 + h, 0:chunk] = jnp.full((1, chunk), dt_bias[h], F32)
        vec[8 + h : 9 + h, chunk : 2 * chunk] = -jnp.exp(jnp.full((1, chunk), a_log[h], F32))
    vec[4:5, :inner] = skips
    blocks = starts.shape[0]
    for c in range(blocks):
        row = slice(24 + c, 25 + c)
        vec[row, 0:chunk] = jnp.full((1, chunk), 1 - starts[c], jnp.int32).astype(F32)
        vec[row, chunk : 2 * chunk] = jnp.full((1, chunk), fill[c], jnp.int32).astype(F32)
        if c + 1 < blocks:
            vec[row, 2 * chunk : 3 * chunk] = jnp.full((1, chunk), 1 - starts[c + 1], jnp.int32).astype(F32)


def scan_step(heads, par, block, px, pbd, upper, spread, state, extx, extb):
    chunk, inner = px.shape
    bc = par["convbc"].shape[1]
    ns = bc // 2
    keep, n_live, _ = block
    state[...] = jnp.where(keep, state[...], 0.0)
    extx[0:8, :] = jnp.where(keep, extx[chunk : chunk + 8, :], 0.0)
    extb[0:8, :] = jnp.where(keep, extb[chunk : chunk + 8, :], 0.0)
    extx[8 : chunk + 8, :] = px[...]
    extb[8 : chunk + 8, :] = pbd[:, :bc]

    u = conv_from(extx, par["convx"], chunk, 8)
    x = u * sigmoid(u) * (iota2(chunk, inner, 0).astype(F32) < n_live).astype(F32)
    ub = conv_from(extb, par["convbc"], chunk, 8)
    act = (ub * sigmoid(ub) * (iota2(chunk, bc, 0).astype(F32) < n_live).astype(F32)).astype(BF)
    b, cc = act[:, :ns], act[:, ns:]

    _, _, dt, run = dt_rows(pbd[:, bc:], par["bias"], par["rate"], n_live, heads, upper[...])
    cols, wide = spread_all(run, dt, heads, chunk, spread[...])
    dt_w, ein_w, eout_w = wide[:, :inner], wide[:, inner : 2 * inner], wide[:, 2 * inner :]

    xd = x * dt_w
    xdb = xd.astype(BF)
    scores = nt(cc, b)
    tri = iota2(chunk, chunk, 0) >= iota2(chunk, chunk, 1)
    low_lanes = iota2(chunk, 2 * HD, 1) < HD
    diag = []
    for j in range(heads // 2):
        mix = []
        for h in (2 * j, 2 * j + 1):
            spread_h = cols[:, h : h + 1] - run[h : h + 1, :]
            mix.append((scores * jnp.exp(jnp.where(tri, spread_h, NEG))).astype(BF))
        pair = pair_stack(xdb[:, 2 * HD * j : 2 * HD * (j + 1)], low_lanes)
        diag.append(nn(jnp.concatenate(mix, axis=1), pair))
    enter = state[...]
    enter_b = enter.astype(BF)
    y = jnp.concatenate(diag, axis=1) + ein_w * nn(cc, enter_b) + par["skip"] * x
    state[...] = ein_w[chunk - 1 : chunk, :] * enter + tn(b, (xd * eout_w).astype(BF))
    return y, enter_b


def pair_rows(dp_n, block, pair, values):
    return jnp.concatenate(
        [values[pl.ds(pl.multiple_of((2 * l + pair) * block, block), block), :] for l in range(dp_n // 2)], axis=0
    )


def gate_kernel(
    dp_n, normed, rows_z, rows_out, parts, y, vec, normed_t_in, dy_out, lpz, gn, y_send, g_own, gain_grad,
    h_send, h_recv, z_all, g_all, y_all, grad_t, normed_t, s_h, r_h, s_in,
):
    i = pl.program_id(0)
    who = peers(dp_n)
    names = ("sib", "xn", "dg")
    barrier = pltpu.get_barrier_semaphore()
    span, quarter = parts.shape[1:]
    blocks, chunk = h_send.shape[1:]
    inner = y.shape[1]
    here = pl.ds(pl.multiple_of(i * span, span), span)
    load = pltpu.make_async_copy(normed_t_in, normed_t, s_in.at[0])

    @pl.when(i == 0)
    def _():
        load.start()
        for name in names:
            pl.semaphore_signal(barrier, inc=1, device_id=who[name], device_id_type=MESH)

    z = nn(normed[...], rows_z[...])
    z_all[here, :] = z
    y_all[here, :] = y[...]
    g = nn(parts[0], rows_out[0:quarter, :])
    for k in range(1, 4):
        g = g + nn(parts[k], rows_out[k * quarter : (k + 1) * quarter, :])
    g_all[here, :] = g
    for k in range(4):
        grad_t[k * quarter : (k + 1) * quarter, here] = jnp.transpose(parts[k])
    gated = y[...] * (z * sigmoid(z))
    ones = jnp.ones((8, inner), BF)
    for k, value in enumerate((gated * gated, gated * vec[5:6, :inner] * g)):
        row = nt(ones, value.astype(BF))
        for j in range(span // chunk):
            h_send[k, pl.ds(i * (span // chunk) + j, 1), :] = row[0:1, j * chunk : (j + 1) * chunk]

    @pl.when(i == pl.num_programs(0) - 1)
    def _():
        pl.semaphore_wait(barrier, 3)
        copies = [push(h_send, h_recv.at[k], s_h.at[k], r_h.at[k], who[name]) for k, name in enumerate(names)]
        for copy in copies:
            copy.start()
        for copy in copies:
            copy.wait()
        sums = h_send[...] + h_recv[0] + h_recv[1] + h_recv[2]
        gain = vec[5:6, :inner]
        below = jnp.zeros((chunk - blocks, chunk), F32)
        inv = lax.rsqrt(jnp.transpose(jnp.concatenate([sums[0], below], axis=0)) / (4 * inner) + EPS)
        dots = jnp.transpose(jnp.concatenate([sums[1], below], axis=0))
        coef = inv * inv * inv * (dots / (4 * inner))
        gain_grad[...] = jnp.zeros_like(gain_grad)
        for b in range(blocks):
            at = slice(b * chunk, (b + 1) * chunk)
            zb, yb, gb = z_all[at, :], y_all[at, :], g_all[at, :]
            sz = sigmoid(zb)
            silu_z = zb * sz
            gated_b = yb * silu_z
            inv_b = inv[:, b : b + 1]
            scaled = gated_b * inv_b
            gn[at, :] = (scaled * gain).astype(BF)
            gain_grad[0:1, :] += jnp.sum(gb * scaled, axis=0, keepdims=True)
            d_gated = inv_b * (gb * gain) - gated_b * coef[:, b : b + 1]
            lpz[at, :] = (d_gated * yb * (sz * (1.0 + zb * (1.0 - sz)))).astype(BF)
            dy_out[at, :] = d_gated * silu_z
        load.wait()
        block = grad_t.shape[0] // dp_n
        for v in range(4):
            left, right = ((grad_t, gn), (normed_t, lpz))[v // 2]
            cols = slice((v % 2) * (inner // 2), (v % 2 + 1) * (inner // 2))
            y_send[v] = nn(pair_rows(dp_n, block, 1 - who["pair"], left), right[:, cols]).astype(BF)
            g_own[v] = nn(pair_rows(dp_n, block, who["pair"], left), right[:, cols])


def gate(dp_n, blocks, normed, normed_t, rows_z, rows_out, parts, y, vec):
    count, width = normed.shape
    inner = y.shape[1]
    chunk = count // blocks
    steps = 8
    span = count // steps
    quarter = width // 4
    sds = jax.ShapeDtypeStruct
    rows = lambda w: pl.BlockSpec((span, w), lambda i: (i, 0))
    whole = lambda shape: pl.BlockSpec(shape, lambda i: (0,) * len(shape))
    halves = (4, width // 2, inner // 2)
    return pl.pallas_call(
        functools.partial(gate_kernel, dp_n),
        grid=(steps,),
        in_specs=[
            rows(width), whole(rows_z.shape), whole(rows_out.shape),
            pl.BlockSpec((4, span, quarter), lambda i: (0, i, 0)), rows(inner), whole(vec.shape),
            pl.BlockSpec(memory_space=pl.ANY),
        ],
        out_specs=[whole((count, inner))] * 3 + [whole(halves), whole(halves), whole((8, inner))],
        out_shape=[
            sds((count, inner), F32), sds((count, inner), BF), sds((count, inner), BF), sds(halves, BF),
            sds(halves, F32), sds((8, inner), F32),
        ],
        scratch_shapes=[
            pltpu.VMEM((2, blocks, chunk), F32), pltpu.VMEM((3, 2, blocks, chunk), F32),
            pltpu.VMEM((count, inner), F32), pltpu.VMEM((count, inner), F32), pltpu.VMEM((count, inner), F32),
            pltpu.VMEM((width, count), BF), pltpu.VMEM((width, count), BF),
            pltpu.SemaphoreType.DMA((3,)), pltpu.SemaphoreType.DMA((3,)), pltpu.SemaphoreType.DMA((1,)),
        ],
        compiler_params=pltpu.CompilerParams(
            collective_id=4, has_side_effects=True, vmem_limit_bytes=58 * 2**20
        ),
        name="gate",
    )(normed, rows_z, rows_out, parts, y, vec, normed_t)


def sums_beside_scan(
    dp_n, gn_in, rows_out_in, tokens_in, y_send_in, g_in_in, block_out, g_out, g_z,
    gn, rows_out, tokens, y_send, g_in, s_in, sib_send, sib_recv, x_send, x_recv, part, held, y_recv, z_send, z_recv, g_own,
    s_sib, r_sib, s_x, r_x, s_y, r_y, s_z, r_z,
):
    i = pl.program_id(0)
    who = peers(dp_n)
    lines = who["lines"]
    units, span, quarter = held.shape
    block = g_out.shape[0]
    half = g_out.shape[1] // 2

    def copy_sib(k):
        return push(sib_send.at[k], sib_recv.at[k], s_sib.at[k], r_sib.at[k], who["sib"])

    def copy_x(k):
        return push(x_send.at[k], x_recv.at[k], s_x.at[k], r_x.at[k], who["xn"])

    def copy_y(v):
        return push(y_send.at[v], y_recv.at[v], s_y.at[v], r_y.at[v], who["yn"])

    def copy_z(v, k):
        to = (who["line_index"] + k) % lines
        return push(
            z_send.at[v, pl.ds(pl.multiple_of(to * block, block), block)],
            z_recv.at[v, k - 1], s_z.at[v, k - 1], r_z.at[v, k - 1], who["line"](k),
        )

    loads = [
        pltpu.make_async_copy(src, dst, s_in.at[n])
        for n, (src, dst) in enumerate((
            (y_send_in, y_send), (rows_out_in, rows_out), (gn_in, gn), (tokens_in, tokens), (g_in_in, g_in),
        ))
    ]

    @pl.when(i == 0)
    def _():
        for load in loads:
            load.start()
        meet(who)
        loads[0].wait()
        for v in range(4):
            copy_y(v).start()

    @pl.when(i == 1)
    def _():
        for load in loads[1:]:
            load.wait()

    def first(k):
        for n, q in enumerate(("sib_mine", "sib_other", "mine", "other")):
            cols = pl.ds(pl.multiple_of(who[q] * quarter, quarter), quarter)
            p = nt(gn[k * span : (k + 1) * span, :], rows_out[cols, :])
            if n < 2:
                sib_send[k, n] = p.astype(BF)
            else:
                part[n - 2] = p
        copy_sib(k).start()

    def second(k):
        copy_sib(k).wait()
        x_send[k] = (part[1] + sib_recv[k, 1].astype(F32)).astype(BF)
        copy_x(k).start()
        held[k] = part[0] + sib_recv[k, 0].astype(F32)

    def third(k):
        copy_x(k).wait()
        at = slice(k * span, (k + 1) * span)
        block_out[at, :] = (tokens[at, :].astype(F32) + held[k] + x_recv[k].astype(F32)).astype(BF)

    def grad_b(v):
        copy_y(v).wait()
        g_own[v] = g_in[v] + y_recv[v].astype(F32)
        z_send[v] = g_own[v].astype(BF)
        loop_line(lines, lambda k: copy_z(v, k).start())

    def grad_c(v):
        loop_line(lines, lambda k: copy_z(v, k).wait())
        total = g_own[v, pl.ds(pl.multiple_of(who["line_index"] * block, block), block), :]
        for k in range(lines - 1):
            total = total + z_recv[v, k].astype(F32)
        (g_out, g_z)[v // 2][:, (v % 2) * half : (v % 2 + 1) * half] = total

    events = [(grad_b, 0, 3), (grad_b, 1, 6), (grad_b, 2, 8), (grad_b, 3, 11)]
    for k in range(units):
        events += [(first, k, 2 * k + 1), (second, k, 2 * k + 2), (third, k, 2 * k + 7)]
    for at in sorted({e[2] for e in events}):

        @pl.when(i == at)
        def _(at=at):
            for fn, k, when in events:
                if when == at:
                    fn(k)

    def finish():
        for v in range(4):
            grad_c(v)

    return finish


def scan_bwd_kernel(
    heads, taps_n, bc, dp_n, dy_in, px, px_halo, pbd, pbd_halo, sin, gain_grad, vec, gn, rows_out, tokens,
    y_send, g_in,
    lpx, lpbd, acc, block_out, g_out, g_z, dstate, extx, extb, dux, dub, acc_x, acc_bc, acc_s, upper, spread, gather, ones_h,
    *beside,
):
    finish = sums_beside_scan(dp_n, gn, rows_out, tokens, y_send, g_in, block_out, g_out, g_z, *beside)
    i = pl.program_id(0)
    blocks = pl.num_programs(0)
    c = blocks - 1 - i
    chunk, inner = px.shape
    ns = bc // 2
    par = read_vec(vec, heads, chunk, inner, bc, taps_n)
    keep, n_live, keep_next = read_block(vec, c, chunk)
    taps, taps_b, bias, rate, skip = (par[k] for k in ("convx", "convbc", "bias", "rate", "skip"))

    @pl.when(i == 0)
    def _():
        for ref in (dstate, dux, dub, acc_x, acc_bc, acc_s):
            ref[...] = jnp.zeros_like(ref)
        acc_x[taps_n : taps_n + 1, :] = gain_grad[0:1, :]
        set_upper(upper)
        set_spread(spread, heads)
        set_gather(gather, ones_h, heads)

    dy = dy_in[...]

    extx[0:8, :] = jnp.where(keep, px_halo[...], 0.0)
    extb[0:8, :] = jnp.where(keep, pbd_halo[:, :bc], 0.0)
    extx[8 : chunk + 8, :] = px[...]
    extb[8 : chunk + 8, :] = pbd[:, :bc]
    live_x = (iota2(chunk, inner, 0).astype(F32) < n_live).astype(F32)
    live_b = (iota2(chunk, bc, 0).astype(F32) < n_live).astype(F32)
    u = conv_from(extx, taps, chunk, 8)
    su = sigmoid(u)
    x = u * su * live_x
    dx_du = su * (1.0 + u * (1.0 - su)) * live_x
    ub = conv_from(extb, taps_b, chunk, 8)
    sb = sigmoid(ub)
    act = (ub * sb * live_b).astype(BF)
    db_du = sb * (1.0 + ub * (1.0 - sb)) * live_b
    b, cc = act[:, :ns], act[:, ns:]

    pre, live, dt, run = dt_rows(pbd[:, bc:], bias, rate, n_live, heads, upper[...])
    cols, wide = spread_all(run, dt, heads, chunk, spread[...])
    dt_w, ein_w, eout_w = wide[:, :inner], wide[:, inner : 2 * inner], wide[:, 2 * inner :]
    xd = x * dt_w
    xdb = xd.astype(BF)
    dyb = dy.astype(BF)
    acc_x[taps_n + 1 : taps_n + 2, :] += jnp.sum(dy * x, axis=0, keepdims=True)

    scores_t = nt(b, cc)
    tri = iota2(chunk, chunk, 0) <= iota2(chunk, chunk, 1)
    low_lanes = iota2(chunk, 2 * HD, 1) < HD
    d_scores_t = jnp.zeros((chunk, chunk), F32)
    dxd = []
    pulls = []
    read_sums = []
    for j in range(heads // 2):
        span = slice(2 * HD * j, 2 * HD * (j + 1))
        dy_pair = pair_stack(dyb[:, span], low_lanes)
        x_pair = pair_stack(xdb[:, span], low_lanes)
        d_mix = nt(x_pair, dyb[:, span])
        mix = []
        for k in (0, 1):
            h = 2 * j + k
            spread_h = run[h : h + 1, :] - cols[:, h : h + 1]
            fade = jnp.exp(jnp.where(tri, spread_h, NEG))
            m = scores_t * fade
            dm = d_mix[k * chunk : (k + 1) * chunk]
            d_scores_t = d_scores_t + dm * fade
            pull = (dm * m).astype(BF)
            pulls.append(pull)
            read_sums.append(jnp.sum(pull.astype(F32), axis=0, keepdims=True))
            mix.append(m.astype(BF))
        dxd.append(nn(jnp.concatenate(mix, axis=1), dy_pair))
    source_sums = nn(jnp.concatenate(pulls, axis=1), ones_h[...])
    read_rows = jnp.concatenate(read_sums, axis=0)

    d_state = jnp.where(keep_next, dstate[...], 0.0)
    d_state_b = d_state.astype(BF)
    enter_b = sin[0]
    edy = ein_w * dy
    edyb = edy.astype(BF)
    readings = nn(cc, enter_b)
    from_state = nn(b, d_state_b) * eout_w
    d_xd = jnp.concatenate(dxd, axis=1) + from_state
    q1 = edy * readings
    q2 = xd * from_state
    decay = ein_w[chunk - 1 : chunk, :]
    dstate[...] = decay * d_state + tn(cc, edyb)
    d_cb = tn(d_scores_t.astype(BF), b) + nt(edyb, enter_b)
    d_b = nn(d_scores_t.astype(BF), cc) + nt((xd * eout_w).astype(BF), d_state_b)

    sums = (
        nn((d_xd * x).astype(BF), gather[0])
        + nn((q1 - q2).astype(BF), gather[1])
        + nn(q2.astype(BF), gather[2])
        - source_sums
    )
    sums_t = jnp.transpose(sums)
    dt_direct = sums_t[:heads]
    d_run = sums_t[heads : 2 * heads] + read_rows
    whole_q2 = jnp.sum(sums_t[2 * heads : 3 * heads], axis=1, keepdims=True)
    kept = jnp.sum(enter_b.astype(F32) * d_state, axis=0, keepdims=True) * decay
    kept_hi, kept_lo = split2(kept)
    kept_two = jnp.concatenate([kept_hi, kept_lo, jnp.zeros((6, inner), F32)], axis=0).astype(BF)
    kept_rows = nn(kept_two, gather[0])
    kept_cols = jnp.transpose(
        jnp.concatenate([kept_rows[0:1] + kept_rows[1:2], jnp.zeros((chunk - 1, chunk), F32)], axis=0)
    )
    d_last = whole_q2 + kept_cols[:heads, 0:1]
    hi, mid, low = split3(d_run)
    back = nt(jnp.concatenate([hi, mid, low], axis=0).astype(BF), upper[...])
    d_a = back[:heads] + back[heads : 2 * heads] + back[2 * heads :] + d_last
    d_dt = dt_direct + d_a * rate
    d_pre = d_dt * live * sigmoid(pre)
    acc_s[0:heads, :] += d_pre
    acc_s[heads : 2 * heads, :] += d_a * dt * rate

    def conv_back(d_u, du_ref, ext_ref, tap_values, acc):
        du_ref[chunk : chunk + 8, :] = jnp.where(keep_next, du_ref[0:8, :], 0.0)
        du_ref[0:chunk, :] = d_u
        out = tap_values[taps_n - 1 : taps_n, :] * d_u
        acc[taps_n - 1 : taps_n, :] += jnp.sum(d_u * ext_ref[8 : chunk + 8, :], axis=0, keepdims=True)
        for k in range(1, taps_n):
            row = taps_n - 1 - k
            out = out + tap_values[row : row + 1, :] * du_ref[pl.ds(k, chunk), :]
            acc[row : row + 1, :] += jnp.sum(
                d_u * ext_ref[pl.ds(8 - k, chunk), :], axis=0, keepdims=True
            )
        return out

    d_x = d_xd * dt_w + skip * dy
    lpx[...] = conv_back(d_x * dx_du, dux, extx, taps, acc_x).astype(BF)
    d_act = jnp.concatenate([d_b, d_cb], axis=1)
    lpbd[:, :bc] = conv_back(d_act * db_du, dub, extb, taps_b, acc_bc).astype(BF)
    pad = jnp.concatenate([d_pre, jnp.zeros((chunk - heads, chunk), F32)], axis=0)
    lpbd[:, bc:] = jnp.transpose(pad).astype(BF)

    @pl.when(i == blocks - 1)
    def _():
        acc[...] = jnp.zeros_like(acc)
        for k in range(taps_n):
            acc[1:2, k * bc : (k + 1) * bc] = acc_bc[k : k + 1, :]
        per = acc.shape[1] // inner
        for k in range(taps_n + 1):
            acc[2 + k // per : 3 + k // per, (k % per) * inner : (k % per + 1) * inner] = acc_x[k : k + 1, :]
        per_head = jnp.sum(
            jnp.transpose(jnp.concatenate([acc_s[...], jnp.zeros((chunk - 2 * heads, chunk), F32)], axis=0)),
            axis=0, keepdims=True,
        )
        three = jnp.concatenate(split3(acc_x[taps_n + 1 : taps_n + 2, :]) + (jnp.zeros((5, inner), F32),), axis=0)
        skips = jnp.sum(nn(three.astype(BF), gather[2]), axis=0, keepdims=True)
        acc[5:6, 0:chunk] = per_head + skips
        finish()


def scan_backward(
    dp_n, dy, px, pbd, sin, gain_grad, vec, gn, rows_out, tokens, y_send, g_own, heads, taps, bc
):
    count, inner = px.shape
    blocks = sin.shape[0]
    chunk = count // blocks
    whole = lambda a: pl.BlockSpec(a.shape, lambda i: (0,) * a.ndim)
    back = lambda w: pl.BlockSpec((chunk, w), lambda i: (blocks - 1 - i, 0))
    halo = lambda w: pl.BlockSpec((8, w), lambda i: (jnp.maximum((blocks - 1 - i) * (chunk // 8) - 1, 0), 0))
    width = pbd.shape[1]
    lines = dp_n // 2
    more = max(lines - 1, 1)
    block = rows_out.shape[0] // dp_n
    quarter = tokens.shape[1]
    units = 4
    span = count // units
    dma = pltpu.SemaphoreType.DMA
    vm, sds = pltpu.VMEM, jax.ShapeDtypeStruct
    return pl.pallas_call(
        functools.partial(scan_bwd_kernel, heads, taps, bc, dp_n),
        grid=(blocks,),
        in_specs=[
            back(inner), back(inner), halo(inner), back(width), halo(width),
            pl.BlockSpec((1, bc // 2, inner), lambda i: (blocks - 1 - i, 0, 0)), whole(gain_grad), whole(vec),
        ]
        + [pl.BlockSpec(memory_space=pl.ANY)] * 5,
        out_specs=[
            back(inner), back(width), pl.BlockSpec((8, vec.shape[1]), lambda i: (0, 0)),
            whole(tokens), pl.BlockSpec((block, inner), lambda i: (0, 0)), pl.BlockSpec((block, inner), lambda i: (0, 0)),
        ],
        scratch_shapes=[
            vm((bc // 2, inner), F32), vm((chunk + 8, inner), F32), vm((chunk + 8, bc), F32),
            vm((chunk + 8, inner), F32), vm((chunk + 8, bc), F32),
            vm((8, inner), F32), vm((8, bc), F32), vm((2 * heads, chunk), F32),
            vm((chunk, chunk), BF), vm((chunk, 3 * inner), BF), vm((3, inner, chunk), BF), vm((heads * chunk, chunk), BF),
            vm(gn.shape, BF), vm(rows_out.shape, BF), vm(tokens.shape, BF), vm(y_send.shape, BF), vm(g_own.shape, F32),
            dma((5,)),
            vm((units, 2, span, quarter), BF), vm((units, 2, span, quarter), BF),
            vm((units, span, quarter), BF), vm((units, span, quarter), BF),
            vm((2, span, quarter), F32), vm((units, span, quarter), F32),
            vm(y_send.shape, BF), vm(y_send.shape, BF), vm((4, more, block, inner // 2), BF), vm(y_send.shape, F32),
            dma((units,)), dma((units,)), dma((units,)), dma((units,)), dma((4,)), dma((4,)),
            dma((4, more)), dma((4, more)),
        ],
        out_shape=[
            sds((count, inner), BF), sds((count, width), BF),
            sds((8, vec.shape[1]), F32), sds(tokens.shape, BF), sds((block, inner), F32),
            sds((block, inner), F32),
        ],
        compiler_params=pltpu.CompilerParams(
            collective_id=3, has_side_effects=True, vmem_limit_bytes=58 * 2**20
        ),
        name="scan_backward",
    )(dy, px, px, pbd, pbd, sin, gain_grad, vec, gn, rows_out, tokens, y_send, g_own)
def peers(dp_n):
    dp, hm = lax.axis_index("dp"), lax.axis_index("heads")
    across, core = hm // 2, hm % 2
    pair, line, lines = dp % 2, dp // 2, dp_n // 2
    return dict(
        sib=(dp, 2 * across + 1 - core),
        xn=(dp, 2 * (1 - across) + core),
        dg=(dp, 2 * (1 - across) + 1 - core),
        yn=(2 * line + 1 - pair, hm),
        line=lambda k: (2 * ((line + k) % lines) + pair, hm),
        mine=hm,
        other=2 * (1 - across) + core,
        sib_mine=2 * across + 1 - core,
        sib_other=2 * (1 - across) + 1 - core,
        pair=pair, line_index=line, lines=lines, dp=dp, core=core,
    )


def meet(who):
    barrier = pltpu.get_barrier_semaphore()
    for name in ("sib", "xn", "dg", "yn"):
        pl.semaphore_signal(barrier, inc=1, device_id=who[name], device_id_type=MESH)

    def greet(k, carry):
        pl.semaphore_signal(barrier, inc=1, device_id=who["line"](k), device_id_type=MESH)
        return carry

    lax.fori_loop(1, who["lines"], greet, 0)
    pl.semaphore_wait(barrier, 4 + who["lines"] - 1)


def push(src, dst, send, recv, to):
    return pltpu.make_async_remote_copy(
        src_ref=src, dst_ref=dst, send_sem=send, recv_sem=recv, device_id=to, device_id_type=MESH
    )


def tail_kernel(
    dp_n, units,
    normed_t_in, lpx_in, rows_z_in, lpz_in, rows_x_in, lpbd_in, rows_bd_in, normed_in,
    tokens, acc, cot, q_wide, vec,
    grad_tokens, g_x, g_bc, small_out,
    sib_send, sib_recv, x_send, x_recv, part, held,
    y_send, y_recv, z_send, z_recv, g_own, yb_send, yb_recv, zb_send, zb_recv, gb_own, bh_send, bh_recv,
    bx_send, bx_recv, bs_recv, h_send, h_recv, sy_send, sy_recv, sz_send, sz_recv, dy_send, dy_recv, dz_send, dz_recv, row_sums,
    normed_t, lpx, rows_z, lpz, rows_x, lpbd, rows_bd, normed,
    s_in, s_sib, r_sib, s_x, r_x, s_y, r_y, s_z, r_z, s_m, r_m, s_sl, r_sl,
):
    loads = [
        pltpu.make_async_copy(src, dst, s_in.at[i])
        for i, (src, dst) in enumerate((
            (normed_t_in, normed_t), (lpx_in, lpx), (rows_z_in, rows_z), (lpz_in, lpz), (rows_x_in, rows_x),
            (lpbd_in, lpbd), (rows_bd_in, rows_bd), (normed_in, normed),
        ))
    ]
    for load in loads:
        load.start()
    who = peers(dp_n)
    meet(who)
    count = normed.shape[0]
    width = normed.shape[1]
    inner = lpx.shape[1]
    bc = 2 * bh_send.shape[1]
    quarter = width // 4
    span = count // units
    block = width // dp_n
    lines = who["lines"]

    def copy_sib(u):
        return push(sib_send.at[u], sib_recv.at[u], s_sib.at[u], r_sib.at[u], who["sib"])

    def copy_x(u):
        return push(x_send.at[u], x_recv.at[u], s_x.at[u], r_x.at[u], who["xn"])

    def product(u, q):
        cols = pl.ds(pl.multiple_of(q * quarter, quarter), quarter)
        at = slice(u * span, (u + 1) * span)
        return nt(lpx[at, :], rows_x[cols, :]) + nt(lpz[at, :], rows_z[cols, :]) + nt(lpbd[at, :], rows_bd[cols, :])

    def head_a(u):
        for k, q in enumerate(("sib_mine", "sib_other", "mine", "other")):
            p = product(u, who[q])
            at = slice(u * span, (u + 1) * span)
            cols = pl.ds(pl.multiple_of(who[q] * quarter, quarter), quarter)
            inner_p = p * normed[at, cols].astype(F32)
            h_send[0:1, cols] += jnp.sum(inner_p, axis=0, keepdims=True)
            first = u * span
            lanes = slice(first % width, first % width + span)
            h_send[2 + first // width : 3 + first // width, lanes] += nt(
                jnp.ones((8, quarter), BF), inner_p.astype(BF)
            )[0:1]
            if k < 2:
                sib_send[u, k] = p.astype(BF)
            else:
                part[u % 2, k - 2] = p
        copy_sib(u).start()

    def head_b(u):
        copy_sib(u).wait()
        x_send[u] = (part[u % 2, 1] + sib_recv[u, 1].astype(F32)).astype(BF)
        copy_x(u).start()
        held[u] = part[u % 2, 0] + sib_recv[u, 0].astype(F32)

    def head_c(u):
        copy_x(u).wait()
        total = held[u] + x_recv[u].astype(F32)
        first = u * span
        lanes = q_wide.shape[1]
        cols = pl.ds(pl.multiple_of(who["mine"] * quarter, quarter), quarter)
        for j in range(span // lanes):
            at = slice(first + j * lanes, first + (j + 1) * lanes)
            row, lane = (first + j * lanes) // width, (first + j * lanes) % width
            dots = jnp.transpose(jnp.broadcast_to(row_sums[row : row + 1, lane : lane + lanes], (lanes, lanes)))
            q = q_wide[at, :]
            coef = q * q * (dots / width)
            grad_tokens[at, :] = (
                cot[at, :].astype(F32)
                + q[:, 0:1] * vec[6:7, cols] * total[j * lanes : (j + 1) * lanes]
                - tokens[at, :].astype(F32) * coef[:, 0:1]
            )

    def rows_of(line, pair):
        return pl.ds(pl.multiple_of((2 * line + pair) * block, block), block)

    def grad_a(v):
        left, right = (normed_t, lpx)
        cols = slice((v % 2) * (inner // 2), (v % 2 + 1) * (inner // 2))
        for side in (0, 1):
            pair = (1 - who["pair"]) if side == 0 else who["pair"]
            stacked = jnp.concatenate([left[rows_of(l, pair), :] for l in range(lines)], axis=0)
            value = nn(stacked, right[:, cols])
            if side == 0:
                y_send[v] = value.astype(BF)
                copy_y(v).start()
            else:
                g_own[v] = value

    def copy_y(v):
        return push(y_send.at[v], y_recv.at[v], s_y.at[v], r_y.at[v], who["yn"])

    def copy_z(v, k):
        to = (who["line_index"] + k) % lines
        return push(
            z_send.at[v, pl.ds(pl.multiple_of(to * block, block), block)],
            z_recv.at[v, k - 1], s_z.at[v, k - 1], r_z.at[v, k - 1], who["line"](k),
        )

    def each_line(fn):
        def step(k, carry):
            fn(k)
            return carry

        lax.fori_loop(1, lines, step, 0)

    def own_rows():
        return pl.ds(pl.multiple_of(who["line_index"] * block, block), block)

    def grad_b(v):
        copy_y(v).wait()
        g_own[v] = g_own[v] + y_recv[v].astype(F32)
        z_send[v] = g_own[v].astype(BF)
        each_line(lambda k: copy_z(v, k).start())

    def grad_c(v):
        each_line(lambda k: copy_z(v, k).wait())
        total = g_own[v, own_rows(), :]
        for k in range(lines - 1):
            total = total + z_recv[v, k].astype(F32)
        cols = slice((v % 2) * (inner // 2), (v % 2 + 1) * (inner // 2))
        g_x[:, cols] = total

    half = bc // 2

    def copy_bh():
        return push(bh_send, bh_recv, s_m.at[0], r_m.at[0], who["sib"])

    def copy_yb():
        return push(yb_send, yb_recv, s_m.at[1], r_m.at[1], who["yn"])

    def copy_zb(k):
        to = (who["line_index"] + k) % lines
        return push(
            zb_send.at[pl.ds(pl.multiple_of(to * block, block), block)],
            zb_recv.at[k - 1], s_sl.at[0, k - 1], r_sl.at[0, k - 1], who["line"](k),
        )

    def copy_bx():
        return push(bx_send, bx_recv, s_m.at[2], r_m.at[2], who["xn"])

    def copy_bs():
        return push(bx_send, bs_recv, s_m.at[3], r_m.at[3], who["sib"])

    def bc_a():
        for side in (0, 1):
            pair = (1 - who["pair"]) if side == 0 else who["pair"]
            stacked = jnp.concatenate([normed_t[rows_of(l, pair), :] for l in range(lines)], axis=0)
            value = nn(stacked, lpbd[:, :bc])
            first = who["core"] == 0
            lo, hi = value[:, :half], value[:, half:]
            at = slice(side * lines * block, (side + 1) * lines * block)
            bh_send[at, :] = jnp.where(first, hi, lo).astype(BF)
            gb_own[at, :] = jnp.where(first, lo, hi)
        copy_bh().start()

    def bc_b():
        copy_bh().wait()
        rows = lines * block
        gb_own[...] = gb_own[...] + bh_recv[...].astype(F32)
        yb_send[...] = gb_own[:rows, :].astype(BF)
        copy_yb().start()

    def bc_c():
        rows = lines * block
        copy_yb().wait()
        gb_own[rows:, :] = gb_own[rows:, :] + yb_recv[...].astype(F32)
        zb_send[...] = gb_own[rows:, :].astype(BF)
        each_line(lambda k: copy_zb(k).start())

    def bc_d():
        each_line(lambda k: copy_zb(k).wait())
        at = pl.ds(pl.multiple_of(lines * block + who["line_index"] * block, block), block)
        total = gb_own[at, :]
        for k in range(lines - 1):
            total = total + zb_recv[k].astype(F32)
        bx_send[...] = total
        copy_bx().start()

    def bc_e():
        copy_bx().wait()
        bx_send[...] = bx_send[...] + bx_recv[...]
        copy_bs().start()

    def bc_f():
        copy_bs().wait()
        mine, theirs = bx_send[...], bs_recv[...]
        first = who["core"] == 0
        g_bc[:, :half] = jnp.where(first, mine, theirs)
        g_bc[:, half:] = jnp.where(first, theirs, mine)

    three = (("sib", 4), ("xn", 5), ("dg", 6))
    token_rows = count // width

    def copy_h(k):
        name, sem = three[k]
        return push(h_send, h_recv.at[k], s_m.at[sem], r_m.at[sem], who[name])

    def small_a():
        h_send[1:2, :] = acc[1:2, :]
        for k in range(3):
            copy_h(k).start()

    def copy_sy():
        return push(sy_send, sy_recv, s_m.at[7], r_m.at[7], who["yn"])

    def copy_dy():
        return push(dy_send, dy_recv, s_m.at[8], r_m.at[8], who["yn"])

    def copy_sz(k):
        return push(sz_send, sz_recv.at[k - 1], s_sl.at[1, k - 1], r_sl.at[1, k - 1], who["line"](k))

    def copy_dz(k):
        return push(dz_send, dz_recv.at[k - 1], s_sl.at[2, k - 1], r_sl.at[2, k - 1], who["line"](k))

    def dt_a():
        dy_send[...] = tn(lpbd[:, bc:], normed[...])[0:16, :].astype(BF)
        copy_dy().start()

    def dt_b():
        copy_dy().wait()
        dz_send[...] = (dy_send[...].astype(F32) + dy_recv[...].astype(F32)).astype(BF)
        each_line(lambda k: copy_dz(k).start())

    def dt_c():
        each_line(lambda k: copy_dz(k).wait())
        total = dz_send[...].astype(F32)
        for k in range(lines - 1):
            total = total + dz_recv[k].astype(F32)
        small_out[8:24, :] = total

    def small_b():
        for k in range(3):
            copy_h(k).wait()
        over_heads = h_send[...] + h_recv[0] + h_recv[1] + h_recv[2]
        row_sums[0:token_rows, :] = over_heads[2 : 2 + token_rows, :]
        sy_send[0:2, :] = over_heads[0:2, :]
        sy_send[2:8, :] = acc[2:8, :]
        copy_sy().start()

    def small_c():
        copy_sy().wait()
        sz_send[...] = sy_send[...] + sy_recv[...]
        each_line(lambda k: copy_sz(k).start())

    def small_d():
        each_line(lambda k: copy_sz(k).wait())
        total = sz_send[...]
        for k in range(lines - 1):
            total = total + sz_recv[k]
        small_out[0:8, :] = total

    h_send[...] = jnp.zeros_like(h_send)

    def seq(*steps):
        for fn, *args in steps:
            fn(*args)

    assert units == 4

    def load(*which):
        for i in which:
            loads[i].wait()

    load(0, 1)
    grad_a(0)
    load(2, 3, 4, 5, 6, 7)
    seq((head_a, 0), (bc_a,), (head_b, 0), (head_a, 1), (bc_b,), (grad_a, 1), (head_b, 1), (grad_b, 0), (head_a, 2))
    seq((dt_a,), (head_b, 2), (head_a, 3), (small_a,), (bc_c,), (head_b, 3), (grad_b, 1), (dt_b,), (small_b,))
    seq((bc_d,), (head_c, 0), (small_c,), (grad_c, 0), (dt_c,), (head_c, 1), (bc_e,), (small_d,), (bc_f,), (head_c, 2))
    seq((grad_c, 1), (head_c, 3))


def tail(dp_n, units, normed_t, normed, lpx, lpz, lpbd, rows_x, rows_z, rows_bd, tokens, acc, cot, q_wide, vec, bc):
    count, width = normed.shape
    inner = lpx.shape[1]
    quarter = width // 4
    span = count // units
    block = width // dp_n
    lines = dp_n // 2
    half_rows = lines * block
    more = max(lines - 1, 1)
    vm = pltpu.VMEM
    dma = pltpu.SemaphoreType.DMA
    operands = (
        normed_t, lpx, rows_z, lpz, rows_x, lpbd, rows_bd, normed, tokens, acc, cot, q_wide, vec,
    )
    sds = jax.ShapeDtypeStruct
    spec = pl.BlockSpec(memory_space=pltpu.VMEM)
    return pl.pallas_call(
        functools.partial(tail_kernel, dp_n, units),
        out_shape=[
            sds((count, quarter), F32), sds((block, inner), F32), sds((block, bc), F32),
            sds((24, width), F32),
        ],
        in_specs=[pl.BlockSpec(memory_space=pl.ANY)] * 8 + [spec] * 5,
        out_specs=[spec] * 4,
        scratch_shapes=[
            vm((units, 2, span, quarter), BF), vm((units, 2, span, quarter), BF),
            vm((units, span, quarter), BF), vm((units, span, quarter), BF),
            vm((2, 2, span, quarter), F32), vm((units, span, quarter), F32),
            vm((2, half_rows, inner // 2), BF), vm((2, half_rows, inner // 2), BF),
            vm((2, half_rows, inner // 2), BF), vm((2, more, block, inner // 2), BF),
            vm((2, half_rows, inner // 2), F32),
            vm((half_rows, bc // 2), BF), vm((half_rows, bc // 2), BF),
            vm((half_rows, bc // 2), BF), vm((more, block, bc // 2), BF),
            vm((2 * half_rows, bc // 2), F32),
            vm((2 * half_rows, bc // 2), BF), vm((2 * half_rows, bc // 2), BF),
            vm((block, bc // 2), F32), vm((block, bc // 2), F32), vm((block, bc // 2), F32),
            vm((8, width), F32), vm((3, 8, width), F32),
            vm((8, width), F32), vm((8, width), F32), vm((8, width), F32), vm((more, 8, width), F32),
            vm((16, width), BF), vm((16, width), BF), vm((16, width), BF), vm((more, 16, width), BF),
            vm((8, width), F32),
        ]
        + [vm(a.shape, a.dtype) for a in operands[:8]]
        + [
            dma((8,)), dma((units,)), dma((units,)), dma((units,)), dma((units,)),
            dma((2,)), dma((2,)), dma((2, more)), dma((2, more)), dma((9,)), dma((9,)),
            dma((3, more)), dma((3, more)),
        ],
        compiler_params=pltpu.CompilerParams(
            collective_id=1, has_side_effects=True, vmem_limit_bytes=62 * 2**20
        ),
        name="tail",
    )(*operands)
def chain(ref_in, block_of, width, send, recv, y_send, y_recv, who):
    rows = ref_in.shape[0]
    lines, line, pair = who["lines"], who["line_index"], who["pair"]
    own = ref_in.at[:, width] if ref_in.shape[1] != width.size else ref_in

    def at(index):
        return block_of.at[pl.ds(pl.multiple_of((2 * index + pair) * rows, rows), rows), width]

    def hand(sign, j):
        index = line - sign * j
        source = own if isinstance(j, int) and j == 0 else at(index)
        slot = j + 1 if sign > 0 else lines + j
        to = (2 * (line + sign) + pair, who["mine"])
        return push(source, at(index), send.at[slot], recv.at[slot], to)

    def to_pair(sign, j):
        slot = j if sign > 0 else lines - 1 + j
        index = line - sign * j
        source = own if isinstance(j, int) and j == 0 else at(index)
        return push(source, at(index), y_send.at[slot], y_recv.at[slot], who["yn"])

    def arrived(sign, j):
        slot = j if sign > 0 else lines - 1 + j
        block = at(line - sign * j)
        return push(block, block, send.at[slot], recv.at[slot], who["yn"])

    def inside(index):
        return jnp.logical_and(index >= 0, index < lines)

    def both(fn):
        for sign in (1, -1):
            fn(sign)

    def begin():
        def one(sign):
            @pl.when(inside(line + sign))
            def _():
                hand(sign, 0).start()

        both(one)

    def begin_pair():
        to_pair(1, 0).start()

    def hop(j):
        def one(sign):
            @pl.when(inside(line - sign * j))
            def _():
                arrived(sign, j).wait_recv()

                @pl.when(inside(line + sign))
                def _():
                    hand(sign, j).start()

                to_pair(sign, j).start()

        both(one)

    def end():
        to_pair(1, 0).wait()

        def one(sign):
            @pl.when(inside(line + sign))
            def _():
                hand(sign, 0).wait_send()

        both(one)

        def later(j):
            def one(sign):
                @pl.when(inside(line - sign * j))
                def _():
                    to_pair(sign, j).wait()

                    @pl.when(inside(line + sign))
                    def _():
                        hand(sign, j).wait_send()

            both(one)

        loop_line(lines, later)

    return begin, begin_pair, hop, end


def loop_line(lines, fn):
    def step(k, carry):
        fn(k)
        return carry

    lax.fori_loop(1, lines, step, 0)


def front_kernel(
    dp_n, heads, units, taps, bc,
    tokens, cot, w_x, w_bc, w_z, w_out, w_dt, conv_x, conv_bc, norm_gain, gate_gain, dt_bias, a_log, skip, starts, fill,
    vec, px_out, pbd_out, normed_out, normed_t_out, q_out, y_out, sin_out, parts, rows_x, rows_bd, rows_z, rows_out,
    own_dt, tok, wx, wbd, px, pbd, normed, normed_t, q, y, sin, own_w, own_cot, state, extx, extb, upper, spread,
    s_loc, s_sib, r_sib, s_x, r_x, s_f, r_f, s_cx, r_cx, s_cf, r_cf, s_w, r_w, s_wy, r_wy, s_c, r_c, s_cy, r_cy, s_out, s_y,
):
    who = peers(dp_n)
    count, quarter = tokens.shape
    width = 4 * quarter
    span = count // units
    lines = who["lines"]
    block, inner = w_x.shape
    blocks = sin.shape[0]
    chunk = count // blocks
    per = blocks // units
    pieces = s_cx.shape[0]
    cot_span = count // pieces
    here = pl.ds(pl.multiple_of(who["dp"] * block, block), block)
    own_half = pl.ds(pl.multiple_of(who["core"] * (bc // 2), bc // 2), bc // 2)
    dt_cols = pl.ds(bc, chunk)
    local = [
        pltpu.make_async_copy(src, dst, s_loc.at[k])
        for k, (src, dst) in enumerate((
            (tokens, tok.at[who["mine"]]), (w_x, wx.at[here]), (w_bc.at[:, own_half], wbd.at[here, own_half]),
            (w_z, own_w.at[0]), (w_out, own_w.at[1]), (cot, own_cot),
        ))
    ]
    for copy in local:
        copy.start()
    own_dt[...] = jnp.zeros_like(own_dt)
    own_dt[:, :heads] = w_dt[...]
    wbd[here, dt_cols] = own_dt[...]
    onto = [
        pltpu.make_async_copy(src, dst, s_loc.at[8 + k])
        for k, (src, dst) in enumerate((
            (own_w.at[0], rows_z.at[here]), (own_w.at[1], rows_out.at[here]), (own_cot, parts.at[who["mine"]]),
        ))
    ]
    meet(who)

    def rows(s, n=span):
        return pl.ds(pl.multiple_of(s * n, n), n)

    def to_x(s):
        return push(tokens.at[rows(s)], tok.at[who["mine"], rows(s)], s_x.at[s], r_x.at[s], who["xn"])

    def to_sib():
        return push(tokens, tok.at[who["mine"]], s_sib.at[0], r_sib.at[0], who["sib"])

    def forward(s):
        at = tok.at[who["other"], rows(s)]
        return push(at, at, s_f.at[s], r_f.at[s], who["sib"])

    def cot_x(j):
        at = rows(j, cot_span)
        return push(cot.at[at], parts.at[who["mine"], at], s_cx.at[j], r_cx.at[j], who["xn"])

    def cot_sib():
        return push(cot, parts.at[who["mine"]], s_sib.at[1], r_sib.at[1], who["sib"])

    def cot_forward(j):
        at = parts.at[who["other"], rows(j, cot_span)]
        return push(at, at, s_cf.at[j], r_cf.at[j], who["sib"])

    half = inner // 2
    cuts = [
        chain(ref, to, cols, s_w.at[n], r_w.at[n], s_wy.at[n], r_wy.at[n], who)
        for n, (ref, to, cols) in enumerate((
            (w_x, wx, pl.ds(0, half)), (w_x, wx, pl.ds(half, half)), (w_bc, wbd, own_half), (own_dt, wbd, dt_cols),
        ))
    ]
    chains = [
        chain(ref, to, pl.ds(h * half, half), s_c.at[2 * n + h], r_c.at[2 * n + h], s_cy.at[2 * n + h], r_cy.at[2 * n + h], who)
        for n, (ref, to) in enumerate(((w_z, rows_z), (w_out, rows_out)))
        for h in (0, 1)
    ]

    def offer(n):
        cuts[n][0]()

    def other_half():
        cols = wbd.at[:, own_half]
        return push(cols, cols, s_sib.at[2], r_sib.at[2], who["sib"])

    def pass_rows(n):
        begin, begin_pair, hop, end = cuts[n]
        begin_pair()
        loop_line(lines, hop)

    def have(n):
        cuts[n][3]()

    def pass_cot(j):
        cot_x(j).wait()
        cot_forward(j).start()

    to_x(0).start()
    offer(0)
    for s in range(1, units):
        to_x(s).start()
    to_sib().start()
    for n in (1, 2, 3):
        offer(n)
    for j in range(pieces):
        cot_x(j).start()
    for begin, begin_pair, hop, end in chains:
        begin()
    pack_vec(vec, conv_x, conv_bc, norm_gain, gate_gain, dt_bias, a_log, skip, starts, fill, chunk)
    set_upper(upper)
    set_spread(spread, heads)
    state[...] = jnp.zeros_like(state)
    extx[...] = jnp.zeros_like(extx)
    extb[...] = jnp.zeros_like(extb)
    par = read_vec(vec, heads, chunk, inner, bc, taps)
    gain = vec[6:7, :width]

    def out_copies(s):
        at = rows(s)
        every = slice(None)
        return [
            pltpu.make_async_copy(ref.at[to], out.at[to], s_out.at[n, s])
            for n, (ref, out, to) in enumerate((
                (normed, normed_out, (at,)), (normed_t, normed_t_out, (every, at)), (q, q_out, (at,)),
                (px, px_out, (at,)), (pbd, pbd_out, (at,)),
            ))
        ]

    def norm(s):
        at = rows(s)
        values = [tok[h, at, :].astype(F32) for h in range(4)]
        total = sum(jnp.sum(p * p, axis=1, keepdims=True) for p in values)
        inv = lax.rsqrt(total / width + EPS)
        q[at, :] = jnp.broadcast_to(inv, (span, q.shape[1]))
        for h in range(4):
            cols = slice(h * quarter, (h + 1) * quarter)
            value = (values[h] * inv * gain[:, cols]).astype(BF)
            normed[at, cols] = value
            normed_t[cols, at] = jnp.transpose(value)
        for copy in out_copies(s)[:3]:
            copy.start()

    def project(s):
        at = rows(s)
        pbd[at, :] = nn(normed[at, :], wbd[...])
        px[at, :] = nn(normed[at, :], wx[...])
        for copy in out_copies(s)[3:]:
            copy.start()

    local[0].wait()
    to_x(0).wait()
    forward(0).start()
    pass_rows(0)
    to_sib().wait()
    forward(0).wait()
    norm(0)
    to_x(1).wait()
    forward(1).start()
    pass_rows(1)
    forward(1).wait()
    norm(1)
    pass_rows(2)
    pass_rows(3)
    have(2)
    local[2].wait()
    other_half().start()
    to_x(2).wait()
    forward(2).start()
    for copy in local[3:]:
        copy.wait()
    for copy in onto:
        copy.start()
    cot_sib().start()
    forward(2).wait()
    norm(2)
    local[1].wait()
    for n in (0, 1, 3):
        have(n)
    other_half().wait()
    keep_rows = [
        pltpu.make_async_copy(wx, rows_x, s_loc.at[6]), pltpu.make_async_copy(wbd, rows_bd, s_loc.at[7]),
    ]
    for copy in keep_rows:
        copy.start()

    def last_tokens(s):
        to_x(s).wait()
        forward(s).start()

    def last_norm(s):
        forward(s).wait()
        norm(s)

    events = {1: [(last_tokens, units - 1)], 2: [(last_norm, units - 1)]}
    late = []
    plan = []
    for n, (begin, begin_pair, hop, end) in enumerate(chains):
        plan.append((lambda k, fn=begin_pair: fn(), 0, 1 + 2 * n))
        for j in range(1, min(lines, 4)):
            plan.append((hop, j, 1 + 2 * n + j))
        if lines > 4:
            plan.append((lambda k, fn=hop: lax.fori_loop(4, lines, lambda j, a: (fn(j), a)[1], 0), 0, 5 + 2 * n))
    plan += [(pass_cot, j, 5 + 2 * j) for j in range(pieces)]
    for fn, k, at in plan:
        if at < blocks:
            events.setdefault(at, []).append((fn, k))
        else:
            late.append((fn, k))

    def y_copies(c):
        at = rows(c, chunk)
        return (
            pltpu.make_async_copy(y.at[at], y_out.at[at], s_y.at[0, c]),
            pltpu.make_async_copy(sin.at[c], sin_out.at[c], s_y.at[1, c]),
        )

    def step(c, carry):
        for at, fns in events.items():

            @pl.when(c == at)
            def _(fns=fns):
                for fn, k in fns:
                    fn(k)

        @pl.when(c % per == 0)
        def _():
            project(c // per)

        at = rows(c, chunk)
        y_c, enter = scan_step(
            heads, par, read_block(vec, c, chunk), px.at[at], pbd.at[at], upper, spread, state, extx, extb
        )
        y[at, :] = y_c
        sin[c] = enter
        for copy in y_copies(c):
            copy.start()
        return carry

    lax.fori_loop(0, blocks, step, 0)
    for fn, k in late:
        fn(k)

    def end_y(c, carry):
        for copy in y_copies(c):
            copy.wait()
        return carry

    lax.fori_loop(0, blocks, end_y, 0)
    for s in range(units):
        for copy in out_copies(s):
            copy.wait()
    for copy in onto + keep_rows:
        copy.wait()
    cot_sib().wait()
    for j in range(pieces):
        cot_forward(j).wait()
    for begin, begin_pair, hop, end in chains:
        end()


def front(dp_n, tokens, cot, w_x, w_bc, w_z, w_out, w_dt, conv_x, conv_bc, norm_gain, gate_gain, *scalars):
    count, quarter = tokens.shape
    width = 4 * quarter
    inner, heads = w_x.shape[1], w_dt.shape[1]
    taps, bc = conv_bc.shape
    blocks = scalars[-1].shape[0]
    chunk = count // blocks
    wide = bc + chunk
    units, pieces = 4, 8
    vm, dma, sds = pltpu.VMEM, pltpu.SemaphoreType.DMA, jax.ShapeDtypeStruct
    hbm, vmem = pl.BlockSpec(memory_space=pl.ANY), pl.BlockSpec(memory_space=pltpu.VMEM)
    ways = dp_n - 1
    outs = [
        sds((24 + blocks, width), F32),
        sds((count, inner), F32), sds((count, wide), F32), sds((count, width), BF), sds((width, count), BF),
        sds((count, 128), F32), sds((count, inner), F32), sds((blocks, bc // 2, inner), BF),
        sds((4, count, quarter), BF), sds((width, inner), BF), sds((width, wide), BF), sds((width, inner), BF),
        sds((width, inner), BF),
    ]
    return pl.pallas_call(
        functools.partial(front_kernel, dp_n, heads, units, taps, bc),
        out_shape=outs,
        in_specs=[hbm] * 6 + [vmem] * 5 + [pl.BlockSpec(memory_space=pltpu.SMEM)] * 5,
        out_specs=[vmem] + [hbm] * (len(outs) - 1),
        scratch_shapes=[
            vm((w_x.shape[0], chunk), BF),
            vm((4, count, quarter), BF), vm((width, inner), BF), vm((width, wide), BF),
            vm((count, inner), F32), vm((count, wide), F32), vm((count, width), BF), vm((width, count), BF),
            vm((count, 128), F32), vm((count, inner), F32), vm((blocks, bc // 2, inner), BF),
            vm((2,) + w_z.shape, BF), vm(cot.shape, BF),
            vm((bc // 2, inner), F32), vm((chunk + 8, inner), F32), vm((chunk + 8, bc), F32),
            vm((chunk, chunk), BF), vm((chunk, 3 * inner), BF),
            dma((11,)), dma((3,)), dma((3,)), dma((units,)), dma((units,)), dma((units,)), dma((units,)),
            dma((pieces,)), dma((pieces,)), dma((pieces,)), dma((pieces,)),
            dma((4, ways + 1)), dma((4, ways + 1)), dma((4, ways)), dma((4, ways)), dma((4, ways + 1)), dma((4, ways + 1)), dma((4, ways)), dma((4, ways)),
            dma((5, units)), dma((2, blocks)),
        ],
        compiler_params=pltpu.CompilerParams(
            collective_id=2, has_side_effects=True, vmem_limit_bytes=58 * 2**20
        ),
        name="front",
    )(
        tokens, cot, w_x, w_bc, w_z, w_out, w_dt, conv_x, conv_bc, norm_gain[None, :], gate_gain[None, :], *scalars
    )
def finish_kernel(heads, taps, bc, bo, gt, gx, gz, go, gb, small, own, o_bo, o_gt, o_gx, o_gz, o_go, o_gb, o_gain, o_cx, o_cb, o_bias, o_alog, o_skip, o_gate):
    o_bo[...] = bo[...]
    o_gt[...] = gt[...]

    @pl.when(pl.program_id(0) == 0)
    def _():
        for src, dst in ((gx, o_gx), (gz, o_gz), (go, o_go), (gb, o_gb)):
            dst[...] = src[...]
        inner = o_cx.shape[1]
        per = small.shape[1] // inner
        for k in range(taps):
            o_cx[k : k + 1, :] = small[2 + k // per : 3 + k // per, (k % per) * inner : (k % per + 1) * inner]
            o_cb[k : k + 1, :] = small[1:2, k * bc : (k + 1) * bc]
        scalars = small[5:6, :128]
        o_bias[...] = scalars[0, :heads]
        o_alog[...] = scalars[0, heads : 2 * heads]
        o_skip[...] = scalars[0, 2 * heads : 3 * heads]
        o_gate[...] = small[4, :inner]
        columns = o_gain.shape[0]
        at = pl.ds(pl.multiple_of(lax.axis_index("heads") * columns, columns), columns)
        o_gain[...] = (small[0:1, at] / own[:, at])[0]


def finish(bo, gt, gx, gz, go, gb, small, norm_gain, heads, taps, bc):
    steps = 4
    sds = jax.ShapeDtypeStruct
    count, quarter = bo.shape
    inner = gx.shape[1]
    rows = pl.BlockSpec((count // steps, quarter), lambda i: (i, 0))
    whole = lambda shape: pl.BlockSpec(shape, lambda i: (0,) * len(shape))
    smalls = [(quarter,), (taps, inner), (taps, bc), (heads,), (heads,), (heads,), (inner,)]
    operands = (bo, gt, gx, gz, go, gb, small, norm_gain[None, :])
    return pl.pallas_call(
        functools.partial(finish_kernel, heads, taps, bc),
        grid=(steps,),
        in_specs=[rows, rows] + [whole(a.shape) for a in operands[2:]],
        out_specs=[rows, rows] + [whole(a.shape) for a in operands[2:6]] + [whole(s) for s in smalls],
        out_shape=[sds(a.shape, a.dtype) for a in operands[:6]] + [sds(s, F32) for s in smalls],
        name="finish",
    )(*operands)


def body(
    tokens, cotangent, starts, fill, norm_gain, w_x, w_z, w_dt, w_bc, conv_x, conv_bc, dt_bias, a_log, skip,
    gate_gain, w_out,
):
    heads_n = lax.axis_size("heads")
    dp_n = lax.axis_size("dp")
    dp_index = lax.axis_index("dp")
    count, columns = tokens.shape
    width = columns * heads_n
    blocks = starts.shape[0]
    chunk = count // blocks
    inner = w_x.shape[1]
    heads = w_dt.shape[1]
    taps, bc = conv_bc.shape
    vec, px, pbd, normed, normed_t, q_wide, y, sin, parts, rows_x, rows_bd, rows_z, rows_out = front(
        dp_n, tokens, cotangent, w_x, w_bc, w_z, w_out, w_dt, conv_x, conv_bc, norm_gain, gate_gain, dt_bias, a_log,
        skip, starts, fill,
    )
    dy, lpz, gn, y_send, g_own, gain_grad = gate(dp_n, blocks, normed, normed_t, rows_z, rows_out, parts, y, vec)
    lpx, lpbd, acc, block_out, grad_w_out, grad_w_z = scan_backward(
        dp_n, dy, px, pbd, sin, gain_grad, vec, gn, rows_out, tokens, y_send, g_own, heads, taps, bc
    )
    grad_tokens, grad_w_x, grad_w_bc, small = tail(
        dp_n, 4, normed_t, normed, lpx, lpz, lpbd, rows_x, rows_z, rows_bd, tokens, acc, cotangent, q_wide, vec, bc,
    )
    block = width // dp_n
    grad_w_dt = lax.dynamic_slice_in_dim(small[8 : 8 + heads], dp_index * block, block, 1).T
    (
        block_out, grad_tokens, grad_w_x, grad_w_z, grad_w_out, grad_w_bc, grad_norm_gain, grad_conv_x, grad_conv_bc,
        grad_dt_bias, grad_a_log, grad_skip, grad_gate_gain,
    ) = finish(
        block_out, grad_tokens, grad_w_x, grad_w_z, grad_w_out, grad_w_bc, small, norm_gain, heads, taps, bc
    )
    return (
        block_out, grad_tokens, grad_norm_gain, grad_w_x, grad_w_z, grad_w_dt, grad_w_bc, grad_conv_x, grad_conv_bc,
        grad_dt_bias, grad_a_log, grad_skip, grad_gate_gain, grad_w_out,
    )


def solution(mesh):
    placed = (
        P("dp", "heads"),
        P("dp", "heads"),
        P("dp"),
        P("dp"),
        P(),
        P("dp", "heads"),
        P("dp", "heads"),
        P("dp", "heads"),
        P("dp", None),
        P(None, "heads"),
        P(),
        P("heads"),
        P("heads"),
        P("heads"),
        P("heads"),
        P("dp", "heads"),
    )
    return jax.shard_map(
        body,
        mesh=mesh,
        in_specs=placed,
        out_specs=(
            P("dp", "heads"),
            P("dp", "heads"),
            P("heads"),
            P("dp", "heads"),
            P("dp", "heads"),
            P("dp", "heads"),
            P("dp", None),
            P(None, "heads"),
            P(),
            P("heads"),
            P("heads"),
            P("heads"),
            P("heads"),
            P("dp", "heads"),
        ),
        check_vma=False,
    )
```

```python
import functools
import jax
import jax.numpy as jnp
from jax import lax
from jax.experimental import pallas as pl
from jax.experimental.pallas import tpu as pltpu
from jax.sharding import PartitionSpec as P

HD = 64
EPS = 1e-05
F32 = jnp.float32
BF = jnp.bfloat16
NEG = -1e30
MESH = pl.DeviceIdType.MESH


def nn(a, b):
    return lax.dot_general(a, b, (((1,), (0,)), ((), ())), preferred_element_type=F32)


def nt(a, b):
    return lax.dot_general(a, b, (((1,), (1,)), ((), ())), preferred_element_type=F32)


def tn(a, b):
    return lax.dot_general(a, b, (((0,), (0,)), ((), ())), preferred_element_type=F32)


def split2(v):
    hi = v.astype(BF).astype(F32)
    return hi, v - hi


def split3(v):
    hi = v.astype(BF).astype(F32)
    rest = v - hi
    mid = rest.astype(BF).astype(F32)
    return hi, mid, rest - mid


def softplus(v):
    return jnp.maximum(v, 0.0) + jnp.log1p(jnp.exp(-jnp.abs(v)))


def sigmoid(v):
    return 1.0 / (1.0 + jnp.exp(-v))


def iota2(rows, cols, axis):
    return lax.broadcasted_iota(jnp.int32, (rows, cols), axis)


def zero_one(cond):
    return jnp.where(cond, 1.0, 0.0).astype(BF)


def set_upper(upper):
    upper[...] = zero_one(iota2(*upper.shape, 0) <= iota2(*upper.shape, 1))


def set_spread(spread, heads):
    rows, lanes = iota2(*spread.shape, 0), iota2(*spread.shape, 1)
    inner = heads * HD
    base = heads * (1 + 2 * (lanes // inner)) + (lanes % inner) // HD
    spread[...] = zero_one(jnp.logical_or(rows == base, rows == base + heads))


def set_gather(gather, ones_h, heads):
    for q in range(3):
        rows, lanes = iota2(*gather.shape[1:], 0), iota2(*gather.shape[1:], 1)
        gather[q] = zero_one(lanes == q * heads + rows // HD)
    rows, lanes = iota2(*ones_h.shape, 0), iota2(*ones_h.shape, 1)
    ones_h[...] = zero_one(lanes == heads + rows // ones_h.shape[1])


def conv_from(ext, taps, rows, halo):
    n = taps.shape[0]
    out = taps[n - 1 : n, :] * ext[pl.ds(halo, rows), :]
    for k in range(1, n):
        out = out + taps[n - 1 - k : n - k, :] * ext[pl.ds(halo - k, rows), :]
    return out


def dt_rows(pdt, bias, rate, fill, heads, upper):
    chunk = pdt.shape[0]
    pre = jnp.transpose(pdt)[:heads] + bias
    live = (iota2(heads, chunk, 1).astype(F32) < fill).astype(F32)
    dt = softplus(pre) * live
    hi, mid, low = split3(dt * rate)
    stacked = jnp.concatenate([hi, mid, low], axis=0).astype(BF)
    summed = nn(stacked, upper)
    run = summed[:heads] + summed[heads : 2 * heads] + summed[2 * heads :]
    return pre, live, dt, run


def spread_all(run, dt, heads, chunk, spread):
    last = run[:, chunk - 1 : chunk]
    e_in = jnp.exp(run)
    e_out = jnp.exp(last - run)
    parts = [run]
    for v in (dt, e_in, e_out):
        parts.extend(split2(v))
    used = heads * len(parts)
    if used < chunk:
        parts.append(jnp.zeros((chunk - used, chunk), F32))
    cols = jnp.transpose(jnp.concatenate(parts, axis=0))
    return cols, nn(cols.astype(BF), spread)


def pair_stack(v, low_lanes):
    zero = jnp.zeros_like(v)
    return jnp.concatenate([jnp.where(low_lanes, v, zero), jnp.where(low_lanes, zero, v)], axis=0)


def read_vec(vec, heads, chunk, inner, bc, taps):
    return dict(
        convx=vec[0:taps, :inner], skip=vec[4:5, :inner], gain=vec[5:6, :inner],
        bias=vec[8 : 8 + heads, :chunk], rate=vec[8 : 8 + heads, chunk : 2 * chunk], convbc=vec[16 : 16 + taps, :bc],
    )


def read_block(vec, c, chunk):
    row = vec[pl.ds(24 + c, 1), :]
    return row[:, 0:1] > 0.5, row[:, chunk : chunk + 1], row[:, 2 * chunk : 2 * chunk + 1] > 0.5


def pack_vec(vec, conv_x, conv_bc, norm_gain, gate_gain, dt_bias, a_log, skip, starts, fill, chunk):
    taps, inner = conv_x.shape
    vec[...] = jnp.zeros_like(vec)
    vec[0:taps, :inner] = conv_x[...]
    vec[16 : 16 + taps, : conv_bc.shape[1]] = conv_bc[...]
    vec[5:6, :inner] = gate_gain[...]
    vec[6:7, :] = norm_gain[...]
    head = iota2(1, inner, 1) // HD
    skips = jnp.zeros((1, inner), F32)
    for h in range(dt_bias.shape[0]):
        skips = jnp.where(head == h, skip[h], skips)
        vec[8 + h : 9 + h, 0:chunk] = jnp.full((1, chunk), dt_bias[h], F32)
        vec[8 + h : 9 + h, chunk : 2 * chunk] = -jnp.exp(jnp.full((1, chunk), a_log[h], F32))
    vec[4:5, :inner] = skips
    blocks = starts.shape[0]
    for c in range(blocks):
        row = slice(24 + c, 25 + c)
        vec[row, 0:chunk] = jnp.full((1, chunk), 1 - starts[c], jnp.int32).astype(F32)
        vec[row, chunk : 2 * chunk] = jnp.full((1, chunk), fill[c], jnp.int32).astype(F32)
        if c + 1 < blocks:
            vec[row, 2 * chunk : 3 * chunk] = jnp.full((1, chunk), 1 - starts[c + 1], jnp.int32).astype(F32)


def scan_step(heads, par, block, px, pbd, upper, spread, state, extx, extb):
    chunk, inner = px.shape
    bc = par["convbc"].shape[1]
    ns = bc // 2
    keep, n_live, _ = block
    state[...] = jnp.where(keep, state[...], 0.0)
    extx[0:8, :] = jnp.where(keep, extx[chunk : chunk + 8, :], 0.0)
    extb[0:8, :] = jnp.where(keep, extb[chunk : chunk + 8, :], 0.0)
    extx[8 : chunk + 8, :] = px[...]
    extb[8 : chunk + 8, :] = pbd[:, :bc]

    u = conv_from(extx, par["convx"], chunk, 8)
    x = u * sigmoid(u) * (iota2(chunk, inner, 0).astype(F32) < n_live).astype(F32)
    ub = conv_from(extb, par["convbc"], chunk, 8)
    act = (ub * sigmoid(ub) * (iota2(chunk, bc, 0).astype(F32) < n_live).astype(F32)).astype(BF)
    b, cc = act[:, :ns], act[:, ns:]

    _, _, dt, run = dt_rows(pbd[:, bc:], par["bias"], par["rate"], n_live, heads, upper[...])
    cols, wide = spread_all(run, dt, heads, chunk, spread[...])
    dt_w, ein_w, eout_w = wide[:, :inner], wide[:, inner : 2 * inner], wide[:, 2 * inner :]

    xd = x * dt_w
    xdb = xd.astype(BF)
    scores = nt(cc, b)
    tri = iota2(chunk, chunk, 0) >= iota2(chunk, chunk, 1)
    low_lanes = iota2(chunk, 2 * HD, 1) < HD
    diag = []
    for j in range(heads // 2):
        mix = []
        for h in (2 * j, 2 * j + 1):
            spread_h = cols[:, h : h + 1] - run[h : h + 1, :]
            mix.append((scores * jnp.exp(jnp.where(tri, spread_h, NEG))).astype(BF))
        pair = pair_stack(xdb[:, 2 * HD * j : 2 * HD * (j + 1)], low_lanes)
        diag.append(nn(jnp.concatenate(mix, axis=1), pair))
    enter = state[...]
    enter_b = enter.astype(BF)
    y = jnp.concatenate(diag, axis=1) + ein_w * nn(cc, enter_b) + par["skip"] * x
    state[...] = ein_w[chunk - 1 : chunk, :] * enter + tn(b, (xd * eout_w).astype(BF))
    return y, enter_b


def pair_rows(dp_n, block, pair, values):
    return jnp.concatenate(
        [values[pl.ds(pl.multiple_of((2 * l + pair) * block, block), block), :] for l in range(dp_n // 2)], axis=0
    )


def gate_kernel(
    dp_n, normed, rows_z, rows_out, parts, y, vec, normed_t_in, dy_out, lpz, gn, y_send, g_own, gain_grad,
    h_send, h_recv, z_all, g_all, y_all, grad_t, normed_t, s_h, r_h, s_in,
):
    i = pl.program_id(0)
    who = peers(dp_n)
    names = ("sib", "xn", "dg")
    barrier = pltpu.get_barrier_semaphore()
    span, quarter = parts.shape[1:]
    blocks, chunk = h_send.shape[1:]
    inner = y.shape[1]
    here = pl.ds(pl.multiple_of(i * span, span), span)
    load = pltpu.make_async_copy(normed_t_in, normed_t, s_in.at[0])

    @pl.when(i == 0)
    def _():
        load.start()
        for name in names:
            pl.semaphore_signal(barrier, inc=1, device_id=who[name], device_id_type=MESH)

    z = nn(normed[...], rows_z[...])
    z_all[here, :] = z
    y_all[here, :] = y[...]
    g = nn(parts[0], rows_out[0:quarter, :])
    for k in range(1, 4):
        g = g + nn(parts[k], rows_out[k * quarter : (k + 1) * quarter, :])
    g_all[here, :] = g
    for k in range(4):
        grad_t[k * quarter : (k + 1) * quarter, here] = jnp.transpose(parts[k])
    gated = y[...] * (z * sigmoid(z))
    ones = jnp.ones((8, inner), BF)
    for k, value in enumerate((gated * gated, gated * vec[5:6, :inner] * g)):
        row = nt(ones, value.astype(BF))
        for j in range(span // chunk):
            h_send[k, pl.ds(i * (span // chunk) + j, 1), :] = row[0:1, j * chunk : (j + 1) * chunk]

    @pl.when(i == pl.num_programs(0) - 1)
    def _():
        pl.semaphore_wait(barrier, 3)
        copies = [push(h_send, h_recv.at[k], s_h.at[k], r_h.at[k], who[name]) for k, name in enumerate(names)]
        for copy in copies:
            copy.start()
        for copy in copies:
            copy.wait()
        sums = h_send[...] + h_recv[0] + h_recv[1] + h_recv[2]
        gain = vec[5:6, :inner]
        below = jnp.zeros((chunk - blocks, chunk), F32)
        inv = lax.rsqrt(jnp.transpose(jnp.concatenate([sums[0], below], axis=0)) / (4 * inner) + EPS)
        dots = jnp.transpose(jnp.concatenate([sums[1], below], axis=0))
        coef = inv * inv * inv * (dots / (4 * inner))
        gain_grad[...] = jnp.zeros_like(gain_grad)
        for b in range(blocks):
            at = slice(b * chunk, (b + 1) * chunk)
            zb, yb, gb = z_all[at, :], y_all[at, :], g_all[at, :]
            sz = sigmoid(zb)
            silu_z = zb * sz
            gated_b = yb * silu_z
            inv_b = inv[:, b : b + 1]
            scaled = gated_b * inv_b
            gn[at, :] = (scaled * gain).astype(BF)
            gain_grad[0:1, :] += jnp.sum(gb * scaled, axis=0, keepdims=True)
            d_gated = inv_b * (gb * gain) - gated_b * coef[:, b : b + 1]
            lpz[at, :] = (d_gated * yb * (sz * (1.0 + zb * (1.0 - sz)))).astype(BF)
            dy_out[at, :] = d_gated * silu_z
        load.wait()
        block = grad_t.shape[0] // dp_n
        for v in range(4):
            left, right = ((grad_t, gn), (normed_t, lpz))[v // 2]
            cols = slice((v % 2) * (inner // 2), (v % 2 + 1) * (inner // 2))
            y_send[v] = nn(pair_rows(dp_n, block, 1 - who["pair"], left), right[:, cols]).astype(BF)
            g_own[v] = nn(pair_rows(dp_n, block, who["pair"], left), right[:, cols])


def gate(dp_n, blocks, normed, normed_t, rows_z, rows_out, parts, y, vec):
    count, width = normed.shape
    inner = y.shape[1]
    chunk = count // blocks
    steps = 8
    span = count // steps
    quarter = width // 4
    sds = jax.ShapeDtypeStruct
    rows = lambda w: pl.BlockSpec((span, w), lambda i: (i, 0))
    whole = lambda shape: pl.BlockSpec(shape, lambda i: (0,) * len(shape))
    halves = (4, width // 2, inner // 2)
    return pl.pallas_call(
        functools.partial(gate_kernel, dp_n),
        grid=(steps,),
        in_specs=[
            rows(width), whole(rows_z.shape), whole(rows_out.shape),
            pl.BlockSpec((4, span, quarter), lambda i: (0, i, 0)), rows(inner), whole(vec.shape),
            pl.BlockSpec(memory_space=pl.ANY),
        ],
        out_specs=[whole((count, inner))] * 3 + [whole(halves), whole(halves), whole((8, inner))],
        out_shape=[
            sds((count, inner), F32), sds((count, inner), BF), sds((count, inner), BF), sds(halves, BF),
            sds(halves, F32), sds((8, inner), F32),
        ],
        scratch_shapes=[
            pltpu.VMEM((2, blocks, chunk), F32), pltpu.VMEM((3, 2, blocks, chunk), F32),
            pltpu.VMEM((count, inner), F32), pltpu.VMEM((count, inner), F32), pltpu.VMEM((count, inner), F32),
            pltpu.VMEM((width, count), BF), pltpu.VMEM((width, count), BF),
            pltpu.SemaphoreType.DMA((3,)), pltpu.SemaphoreType.DMA((3,)), pltpu.SemaphoreType.DMA((1,)),
        ],
        compiler_params=pltpu.CompilerParams(
            collective_id=4, has_side_effects=True, vmem_limit_bytes=58 * 2**20
        ),
        name="gate",
    )(normed, rows_z, rows_out, parts, y, vec, normed_t)


def sums_beside_scan(
    dp_n, gn_in, rows_out_in, tokens_in, y_send_in, g_in_in, block_out, g_out, g_z,
    gn, rows_out, tokens, y_send, g_in, s_in, sib_send, sib_recv, x_send, x_recv, part, held, y_recv, z_send, z_recv, g_own,
    s_sib, r_sib, s_x, r_x, s_y, r_y, s_z, r_z,
):
    i = pl.program_id(0)
    who = peers(dp_n)
    lines = who["lines"]
    units, span, quarter = held.shape
    block = g_out.shape[0]
    half = g_out.shape[1] // 2

    def copy_sib(k):
        return push(sib_send.at[k], sib_recv.at[k], s_sib.at[k], r_sib.at[k], who["sib"])

    def copy_x(k):
        return push(x_send.at[k], x_recv.at[k], s_x.at[k], r_x.at[k], who["xn"])

    def copy_y(v):
        return push(y_send.at[v], y_recv.at[v], s_y.at[v], r_y.at[v], who["yn"])

    def copy_z(v, k):
        to = (who["line_index"] + k) % lines
        return push(
            z_send.at[v, pl.ds(pl.multiple_of(to * block, block), block)],
            z_recv.at[v, k - 1], s_z.at[v, k - 1], r_z.at[v, k - 1], who["line"](k),
        )

    loads = [
        pltpu.make_async_copy(src, dst, s_in.at[n])
        for n, (src, dst) in enumerate((
            (y_send_in, y_send), (rows_out_in, rows_out), (gn_in, gn), (tokens_in, tokens), (g_in_in, g_in),
        ))
    ]

    @pl.when(i == 0)
    def _():
        for load in loads:
            load.start()
        meet(who)
        loads[0].wait()
        for v in range(4):
            copy_y(v).start()

    @pl.when(i == 1)
    def _():
        for load in loads[1:]:
            load.wait()

    def first(k):
        for n, q in enumerate(("sib_mine", "sib_other", "mine", "other")):
            cols = pl.ds(pl.multiple_of(who[q] * quarter, quarter), quarter)
            p = nt(gn[k * span : (k + 1) * span, :], rows_out[cols, :])
            if n < 2:
                sib_send[k, n] = p.astype(BF)
            else:
                part[n - 2] = p
        copy_sib(k).start()

    def second(k):
        copy_sib(k).wait()
        x_send[k] = (part[1] + sib_recv[k, 1].astype(F32)).astype(BF)
        copy_x(k).start()
        held[k] = part[0] + sib_recv[k, 0].astype(F32)

    def third(k):
        copy_x(k).wait()
        at = slice(k * span, (k + 1) * span)
        block_out[at, :] = (tokens[at, :].astype(F32) + held[k] + x_recv[k].astype(F32)).astype(BF)

    def grad_b(v):
        copy_y(v).wait()
        g_own[v] = g_in[v] + y_recv[v].astype(F32)
        z_send[v] = g_own[v].astype(BF)
        loop_line(lines, lambda k: copy_z(v, k).start())

    def grad_c(v):
        loop_line(lines, lambda k: copy_z(v, k).wait())
        total = g_own[v, pl.ds(pl.multiple_of(who["line_index"] * block, block), block), :]
        for k in range(lines - 1):
            total = total + z_recv[v, k].astype(F32)
        (g_out, g_z)[v // 2][:, (v % 2) * half : (v % 2 + 1) * half] = total

    events = [(grad_b, 0, 3), (grad_b, 1, 6), (grad_b, 2, 8), (grad_b, 3, 11)]
    for k in range(units):
        events += [(first, k, 2 * k + 1), (second, k, 2 * k + 2), (third, k, 2 * k + 7)]
    for at in sorted({e[2] for e in events}):

        @pl.when(i == at)
        def _(at=at):
            for fn, k, when in events:
                if when == at:
                    fn(k)

    def finish():
        for v in range(4):
            grad_c(v)

    return finish


def scan_bwd_kernel(
    heads, taps_n, bc, dp_n, dy_in, px, px_halo, pbd, pbd_halo, sin, gain_grad, vec, gn, rows_out, tokens,
    y_send, g_in,
    lpx, lpbd, acc, block_out, g_out, g_z, dstate, extx, extb, dux, dub, acc_x, acc_bc, acc_s, upper, spread, gather, ones_h,
    *beside,
):
    finish = sums_beside_scan(dp_n, gn, rows_out, tokens, y_send, g_in, block_out, g_out, g_z, *beside)
    i = pl.program_id(0)
    blocks = pl.num_programs(0)
    c = blocks - 1 - i
    chunk, inner = px.shape
    ns = bc // 2
    par = read_vec(vec, heads, chunk, inner, bc, taps_n)
    keep, n_live, keep_next = read_block(vec, c, chunk)
    taps, taps_b, bias, rate, skip = (par[k] for k in ("convx", "convbc", "bias", "rate", "skip"))

    @pl.when(i == 0)
    def _():
        for ref in (dstate, dux, dub, acc_x, acc_bc, acc_s):
            ref[...] = jnp.zeros_like(ref)
        acc_x[taps_n : taps_n + 1, :] = gain_grad[0:1, :]
        set_upper(upper)
        set_spread(spread, heads)
        set_gather(gather, ones_h, heads)

    dy = dy_in[...]

    extx[0:8, :] = jnp.where(keep, px_halo[...], 0.0)
    extb[0:8, :] = jnp.where(keep, pbd_halo[:, :bc], 0.0)
    extx[8 : chunk + 8, :] = px[...]
    extb[8 : chunk + 8, :] = pbd[:, :bc]
    live_x = (iota2(chunk, inner, 0).astype(F32) < n_live).astype(F32)
    live_b = (iota2(chunk, bc, 0).astype(F32) < n_live).astype(F32)
    u = conv_from(extx, taps, chunk, 8)
    su = sigmoid(u)
    x = u * su * live_x
    dx_du = su * (1.0 + u * (1.0 - su)) * live_x
    ub = conv_from(extb, taps_b, chunk, 8)
    sb = sigmoid(ub)
    act = (ub * sb * live_b).astype(BF)
    db_du = sb * (1.0 + ub * (1.0 - sb)) * live_b
    b, cc = act[:, :ns], act[:, ns:]

    pre, live, dt, run = dt_rows(pbd[:, bc:], bias, rate, n_live, heads, upper[...])
    cols, wide = spread_all(run, dt, heads, chunk, spread[...])
    dt_w, ein_w, eout_w = wide[:, :inner], wide[:, inner : 2 * inner], wide[:, 2 * inner :]
    xd = x * dt_w
    xdb = xd.astype(BF)
    dyb = dy.astype(BF)
    acc_x[taps_n + 1 : taps_n + 2, :] += jnp.sum(dy * x, axis=0, keepdims=True)

    scores_t = nt(b, cc)
    tri = iota2(chunk, chunk, 0) <= iota2(chunk, chunk, 1)
    low_lanes = iota2(chunk, 2 * HD, 1) < HD
    d_scores_t = jnp.zeros((chunk, chunk), F32)
    dxd = []
    pulls = []
    read_sums = []
    for j in range(heads // 2):
        span = slice(2 * HD * j, 2 * HD * (j + 1))
        dy_pair = pair_stack(dyb[:, span], low_lanes)
        x_pair = pair_stack(xdb[:, span], low_lanes)
        d_mix = nt(x_pair, dyb[:, span])
        mix = []
        for k in (0, 1):
            h = 2 * j + k
            spread_h = run[h : h + 1, :] - cols[:, h : h + 1]
            fade = jnp.exp(jnp.where(tri, spread_h, NEG))
            m = scores_t * fade
            dm = d_mix[k * chunk : (k + 1) * chunk]
            d_scores_t = d_scores_t + dm * fade
            pull = (dm * m).astype(BF)
            pulls.append(pull)
            read_sums.append(jnp.sum(pull.astype(F32), axis=0, keepdims=True))
            mix.append(m.astype(BF))
        dxd.append(nn(jnp.concatenate(mix, axis=1), dy_pair))
    source_sums = nn(jnp.concatenate(pulls, axis=1), ones_h[...])
    read_rows = jnp.concatenate(read_sums, axis=0)

    d_state = jnp.where(keep_next, dstate[...], 0.0)
    d_state_b = d_state.astype(BF)
    enter_b = sin[0]
    edy = ein_w * dy
    edyb = edy.astype(BF)
    readings = nn(cc, enter_b)
    from_state = nn(b, d_state_b) * eout_w
    d_xd = jnp.concatenate(dxd, axis=1) + from_state
    q1 = edy * readings
    q2 = xd * from_state
    decay = ein_w[chunk - 1 : chunk, :]
    dstate[...] = decay * d_state + tn(cc, edyb)
    d_cb = tn(d_scores_t.astype(BF), b) + nt(edyb, enter_b)
    d_b = nn(d_scores_t.astype(BF), cc) + nt((xd * eout_w).astype(BF), d_state_b)

    sums = (
        nn((d_xd * x).astype(BF), gather[0])
        + nn((q1 - q2).astype(BF), gather[1])
        + nn(q2.astype(BF), gather[2])
        - source_sums
    )
    sums_t = jnp.transpose(sums)
    dt_direct = sums_t[:heads]
    d_run = sums_t[heads : 2 * heads] + read_rows
    whole_q2 = jnp.sum(sums_t[2 * heads : 3 * heads], axis=1, keepdims=True)
    kept = jnp.sum(enter_b.astype(F32) * d_state, axis=0, keepdims=True) * decay
    kept_hi, kept_lo = split2(kept)
    kept_two = jnp.concatenate([kept_hi, kept_lo, jnp.zeros((6, inner), F32)], axis=0).astype(BF)
    kept_rows = nn(kept_two, gather[0])
    kept_cols = jnp.transpose(
        jnp.concatenate([kept_rows[0:1] + kept_rows[1:2], jnp.zeros((chunk - 1, chunk), F32)], axis=0)
    )
    d_last = whole_q2 + kept_cols[:heads, 0:1]
    hi, mid, low = split3(d_run)
    back = nt(jnp.concatenate([hi, mid, low], axis=0).astype(BF), upper[...])
    d_a = back[:heads] + back[heads : 2 * heads] + back[2 * heads :] + d_last
    d_dt = dt_direct + d_a * rate
    d_pre = d_dt * live * sigmoid(pre)
    acc_s[0:heads, :] += d_pre
    acc_s[heads : 2 * heads, :] += d_a * dt * rate

    def conv_back(d_u, du_ref, ext_ref, tap_values, acc):
        du_ref[chunk : chunk + 8, :] = jnp.where(keep_next, du_ref[0:8, :], 0.0)
        du_ref[0:chunk, :] = d_u
        out = tap_values[taps_n - 1 : taps_n, :] * d_u
        acc[taps_n - 1 : taps_n, :] += jnp.sum(d_u * ext_ref[8 : chunk + 8, :], axis=0, keepdims=True)
        for k in range(1, taps_n):
            row = taps_n - 1 - k
            out = out + tap_values[row : row + 1, :] * du_ref[pl.ds(k, chunk), :]
            acc[row : row + 1, :] += jnp.sum(
                d_u * ext_ref[pl.ds(8 - k, chunk), :], axis=0, keepdims=True
            )
        return out

    d_x = d_xd * dt_w + skip * dy
    lpx[...] = conv_back(d_x * dx_du, dux, extx, taps, acc_x).astype(BF)
    d_act = jnp.concatenate([d_b, d_cb], axis=1)
    lpbd[:, :bc] = conv_back(d_act * db_du, dub, extb, taps_b, acc_bc).astype(BF)
    pad = jnp.concatenate([d_pre, jnp.zeros((chunk - heads, chunk), F32)], axis=0)
    lpbd[:, bc:] = jnp.transpose(pad).astype(BF)

    @pl.when(i == blocks - 1)
    def _():
        acc[...] = jnp.zeros_like(acc)
        for k in range(taps_n):
            acc[1:2, k * bc : (k + 1) * bc] = acc_bc[k : k + 1, :]
        per = acc.shape[1] // inner
        for k in range(taps_n + 1):
            acc[2 + k // per : 3 + k // per, (k % per) * inner : (k % per + 1) * inner] = acc_x[k : k + 1, :]
        per_head = jnp.sum(
            jnp.transpose(jnp.concatenate([acc_s[...], jnp.zeros((chunk - 2 * heads, chunk), F32)], axis=0)),
            axis=0, keepdims=True,
        )
        three = jnp.concatenate(split3(acc_x[taps_n + 1 : taps_n + 2, :]) + (jnp.zeros((5, inner), F32),), axis=0)
        skips = jnp.sum(nn(three.astype(BF), gather[2]), axis=0, keepdims=True)
        acc[5:6, 0:chunk] = per_head + skips
        finish()


def scan_backward(
    dp_n, dy, px, pbd, sin, gain_grad, vec, gn, rows_out, tokens, y_send, g_own, heads, taps, bc
):
    count, inner = px.shape
    blocks = sin.shape[0]
    chunk = count // blocks
    whole = lambda a: pl.BlockSpec(a.shape, lambda i: (0,) * a.ndim)
    back = lambda w: pl.BlockSpec((chunk, w), lambda i: (blocks - 1 - i, 0))
    halo = lambda w: pl.BlockSpec((8, w), lambda i: (jnp.maximum((blocks - 1 - i) * (chunk // 8) - 1, 0), 0))
    width = pbd.shape[1]
    lines = dp_n // 2
    more = max(lines - 1, 1)
    block = rows_out.shape[0] // dp_n
    quarter = tokens.shape[1]
    units = 4
    span = count // units
    dma = pltpu.SemaphoreType.DMA
    vm, sds = pltpu.VMEM, jax.ShapeDtypeStruct
    return pl.pallas_call(
        functools.partial(scan_bwd_kernel, heads, taps, bc, dp_n),
        grid=(blocks,),
        in_specs=[
            back(inner), back(inner), halo(inner), back(width), halo(width),
            pl.BlockSpec((1, bc // 2, inner), lambda i: (blocks - 1 - i, 0, 0)), whole(gain_grad), whole(vec),
        ]
        + [pl.BlockSpec(memory_space=pl.ANY)] * 5,
        out_specs=[
            back(inner), back(width), pl.BlockSpec((8, vec.shape[1]), lambda i: (0, 0)),
            whole(tokens), pl.BlockSpec((block, inner), lambda i: (0, 0)), pl.BlockSpec((block, inner), lambda i: (0, 0)),
        ],
        scratch_shapes=[
            vm((bc // 2, inner), F32), vm((chunk + 8, inner), F32), vm((chunk + 8, bc), F32),
            vm((chunk + 8, inner), F32), vm((chunk + 8, bc), F32),
            vm((8, inner), F32), vm((8, bc), F32), vm((2 * heads, chunk), F32),
            vm((chunk, chunk), BF), vm((chunk, 3 * inner), BF), vm((3, inner, chunk), BF), vm((heads * chunk, chunk), BF),
            vm(gn.shape, BF), vm(rows_out.shape, BF), vm(tokens.shape, BF), vm(y_send.shape, BF), vm(g_own.shape, F32),
            dma((5,)),
            vm((units, 2, span, quarter), BF), vm((units, 2, span, quarter), BF),
            vm((units, span, quarter), BF), vm((units, span, quarter), BF),
            vm((2, span, quarter), F32), vm((units, span, quarter), F32),
            vm(y_send.shape, BF), vm(y_send.shape, BF), vm((4, more, block, inner // 2), BF), vm(y_send.shape, F32),
            dma((units,)), dma((units,)), dma((units,)), dma((units,)), dma((4,)), dma((4,)),
            dma((4, more)), dma((4, more)),
        ],
        out_shape=[
            sds((count, inner), BF), sds((count, width), BF),
            sds((8, vec.shape[1]), F32), sds(tokens.shape, BF), sds((block, inner), F32),
            sds((block, inner), F32),
        ],
        compiler_params=pltpu.CompilerParams(
            collective_id=3, has_side_effects=True, vmem_limit_bytes=58 * 2**20
        ),
        name="scan_backward",
    )(dy, px, px, pbd, pbd, sin, gain_grad, vec, gn, rows_out, tokens, y_send, g_own)
def peers(dp_n):
    dp, hm = lax.axis_index("dp"), lax.axis_index("heads")
    across, core = hm // 2, hm % 2
    pair, line, lines = dp % 2, dp // 2, dp_n // 2
    return dict(
        sib=(dp, 2 * across + 1 - core),
        xn=(dp, 2 * (1 - across) + core),
        dg=(dp, 2 * (1 - across) + 1 - core),
        yn=(2 * line + 1 - pair, hm),
        line=lambda k: (2 * ((line + k) % lines) + pair, hm),
        mine=hm,
        other=2 * (1 - across) + core,
        sib_mine=2 * across + 1 - core,
        sib_other=2 * (1 - across) + 1 - core,
        pair=pair, line_index=line, lines=lines, dp=dp, core=core,
    )


def meet(who):
    barrier = pltpu.get_barrier_semaphore()
    for name in ("sib", "xn", "dg", "yn"):
        pl.semaphore_signal(barrier, inc=1, device_id=who[name], device_id_type=MESH)

    def greet(k, carry):
        pl.semaphore_signal(barrier, inc=1, device_id=who["line"](k), device_id_type=MESH)
        return carry

    lax.fori_loop(1, who["lines"], greet, 0)
    pl.semaphore_wait(barrier, 4 + who["lines"] - 1)


def push(src, dst, send, recv, to):
    return pltpu.make_async_remote_copy(
        src_ref=src, dst_ref=dst, send_sem=send, recv_sem=recv, device_id=to, device_id_type=MESH
    )


def tail_kernel(
    dp_n, units,
    normed_t_in, lpx_in, rows_z_in, lpz_in, rows_x_in, lpbd_in, rows_bd_in, normed_in,
    tokens, acc, cot, q_wide, vec,
    grad_tokens, g_x, g_bc, small_out,
    sib_send, sib_recv, x_send, x_recv, part, held,
    y_send, y_recv, z_send, z_recv, g_own, yb_send, yb_recv, zb_send, zb_recv, gb_own, bh_send, bh_recv,
    bx_send, bx_recv, bs_recv, h_send, h_recv, sy_send, sy_recv, sz_send, sz_recv, dy_send, dy_recv, dz_send, dz_recv, row_sums,
    normed_t, lpx, rows_z, lpz, rows_x, lpbd, rows_bd, normed,
    s_in, s_sib, r_sib, s_x, r_x, s_y, r_y, s_z, r_z, s_m, r_m, s_sl, r_sl,
):
    loads = [
        pltpu.make_async_copy(src, dst, s_in.at[i])
        for i, (src, dst) in enumerate((
            (normed_t_in, normed_t), (lpx_in, lpx), (rows_z_in, rows_z), (lpz_in, lpz), (rows_x_in, rows_x),
            (lpbd_in, lpbd), (rows_bd_in, rows_bd), (normed_in, normed),
        ))
    ]
    for load in loads:
        load.start()
    who = peers(dp_n)
    meet(who)
    count = normed.shape[0]
    width = normed.shape[1]
    inner = lpx.shape[1]
    bc = 2 * bh_send.shape[1]
    quarter = width // 4
    span = count // units
    block = width // dp_n
    lines = who["lines"]

    def copy_sib(u):
        return push(sib_send.at[u], sib_recv.at[u], s_sib.at[u], r_sib.at[u], who["sib"])

    def copy_x(u):
        return push(x_send.at[u], x_recv.at[u], s_x.at[u], r_x.at[u], who["xn"])

    def product(u, q):
        cols = pl.ds(pl.multiple_of(q * quarter, quarter), quarter)
        at = slice(u * span, (u + 1) * span)
        return nt(lpx[at, :], rows_x[cols, :]) + nt(lpz[at, :], rows_z[cols, :]) + nt(lpbd[at, :], rows_bd[cols, :])

    def head_a(u):
        for k, q in enumerate(("sib_mine", "sib_other", "mine", "other")):
            p = product(u, who[q])
            at = slice(u * span, (u + 1) * span)
            cols = pl.ds(pl.multiple_of(who[q] * quarter, quarter), quarter)
            inner_p = p * normed[at, cols].astype(F32)
            h_send[0:1, cols] += jnp.sum(inner_p, axis=0, keepdims=True)
            first = u * span
            lanes = slice(first % width, first % width + span)
            h_send[2 + first // width : 3 + first // width, lanes] += nt(
                jnp.ones((8, quarter), BF), inner_p.astype(BF)
            )[0:1]
            if k < 2:
                sib_send[u, k] = p.astype(BF)
            else:
                part[u % 2, k - 2] = p
        copy_sib(u).start()

    def head_b(u):
        copy_sib(u).wait()
        x_send[u] = (part[u % 2, 1] + sib_recv[u, 1].astype(F32)).astype(BF)
        copy_x(u).start()
        held[u] = part[u % 2, 0] + sib_recv[u, 0].astype(F32)

    def head_c(u):
        copy_x(u).wait()
        total = held[u] + x_recv[u].astype(F32)
        first = u * span
        lanes = q_wide.shape[1]
        cols = pl.ds(pl.multiple_of(who["mine"] * quarter, quarter), quarter)
        for j in range(span // lanes):
            at = slice(first + j * lanes, first + (j + 1) * lanes)
            row, lane = (first + j * lanes) // width, (first + j * lanes) % width
            dots = jnp.transpose(jnp.broadcast_to(row_sums[row : row + 1, lane : lane + lanes], (lanes, lanes)))
            q = q_wide[at, :]
            coef = q * q * (dots / width)
            grad_tokens[at, :] = (
                cot[at, :].astype(F32)
                + q[:, 0:1] * vec[6:7, cols] * total[j * lanes : (j + 1) * lanes]
                - tokens[at, :].astype(F32) * coef[:, 0:1]
            )

    def rows_of(line, pair):
        return pl.ds(pl.multiple_of((2 * line + pair) * block, block), block)

    def grad_a(v):
        left, right = (normed_t, lpx)
        cols = slice((v % 2) * (inner // 2), (v % 2 + 1) * (inner // 2))
        for side in (0, 1):
            pair = (1 - who["pair"]) if side == 0 else who["pair"]
            stacked = jnp.concatenate([left[rows_of(l, pair), :] for l in range(lines)], axis=0)
            value = nn(stacked, right[:, cols])
            if side == 0:
                y_send[v] = value.astype(BF)
                copy_y(v).start()
            else:
                g_own[v] = value

    def copy_y(v):
        return push(y_send.at[v], y_recv.at[v], s_y.at[v], r_y.at[v], who["yn"])

    def copy_z(v, k):
        to = (who["line_index"] + k) % lines
        return push(
            z_send.at[v, pl.ds(pl.multiple_of(to * block, block), block)],
            z_recv.at[v, k - 1], s_z.at[v, k - 1], r_z.at[v, k - 1], who["line"](k),
        )

    def each_line(fn):
        def step(k, carry):
            fn(k)
            return carry

        lax.fori_loop(1, lines, step, 0)

    def own_rows():
        return pl.ds(pl.multiple_of(who["line_index"] * block, block), block)

    def grad_b(v):
        copy_y(v).wait()
        g_own[v] = g_own[v] + y_recv[v].astype(F32)
        z_send[v] = g_own[v].astype(BF)
        each_line(lambda k: copy_z(v, k).start())

    def grad_c(v):
        each_line(lambda k: copy_z(v, k).wait())
        total = g_own[v, own_rows(), :]
        for k in range(lines - 1):
            total = total + z_recv[v, k].astype(F32)
        cols = slice((v % 2) * (inner // 2), (v % 2 + 1) * (inner // 2))
        g_x[:, cols] = total

    half = bc // 2

    def copy_bh():
        return push(bh_send, bh_recv, s_m.at[0], r_m.at[0], who["sib"])

    def copy_yb():
        return push(yb_send, yb_recv, s_m.at[1], r_m.at[1], who["yn"])

    def copy_zb(k):
        to = (who["line_index"] + k) % lines
        return push(
            zb_send.at[pl.ds(pl.multiple_of(to * block, block), block)],
            zb_recv.at[k - 1], s_sl.at[0, k - 1], r_sl.at[0, k - 1], who["line"](k),
        )

    def copy_bx():
        return push(bx_send, bx_recv, s_m.at[2], r_m.at[2], who["xn"])

    def copy_bs():
        return push(bx_send, bs_recv, s_m.at[3], r_m.at[3], who["sib"])

    def bc_a():
        for side in (0, 1):
            pair = (1 - who["pair"]) if side == 0 else who["pair"]
            stacked = jnp.concatenate([normed_t[rows_of(l, pair), :] for l in range(lines)], axis=0)
            value = nn(stacked, lpbd[:, :bc])
            first = who["core"] == 0
            lo, hi = value[:, :half], value[:, half:]
            at = slice(side * lines * block, (side + 1) * lines * block)
            bh_send[at, :] = jnp.where(first, hi, lo).astype(BF)
            gb_own[at, :] = jnp.where(first, lo, hi)
        copy_bh().start()

    def bc_b():
        copy_bh().wait()
        rows = lines * block
        gb_own[...] = gb_own[...] + bh_recv[...].astype(F32)
        yb_send[...] = gb_own[:rows, :].astype(BF)
        copy_yb().start()

    def bc_c():
        rows = lines * block
        copy_yb().wait()
        gb_own[rows:, :] = gb_own[rows:, :] + yb_recv[...].astype(F32)
        zb_send[...] = gb_own[rows:, :].astype(BF)
        each_line(lambda k: copy_zb(k).start())

    def bc_d():
        each_line(lambda k: copy_zb(k).wait())
        at = pl.ds(pl.multiple_of(lines * block + who["line_index"] * block, block), block)
        total = gb_own[at, :]
        for k in range(lines - 1):
            total = total + zb_recv[k].astype(F32)
        bx_send[...] = total
        copy_bx().start()

    def bc_e():
        copy_bx().wait()
        bx_send[...] = bx_send[...] + bx_recv[...]
        copy_bs().start()

    def bc_f():
        copy_bs().wait()
        mine, theirs = bx_send[...], bs_recv[...]
        first = who["core"] == 0
        g_bc[:, :half] = jnp.where(first, mine, theirs)
        g_bc[:, half:] = jnp.where(first, theirs, mine)

    three = (("sib", 4), ("xn", 5), ("dg", 6))
    token_rows = count // width

    def copy_h(k):
        name, sem = three[k]
        return push(h_send, h_recv.at[k], s_m.at[sem], r_m.at[sem], who[name])

    def small_a():
        h_send[1:2, :] = acc[1:2, :]
        for k in range(3):
            copy_h(k).start()

    def copy_sy():
        return push(sy_send, sy_recv, s_m.at[7], r_m.at[7], who["yn"])

    def copy_dy():
        return push(dy_send, dy_recv, s_m.at[8], r_m.at[8], who["yn"])

    def copy_sz(k):
        return push(sz_send, sz_recv.at[k - 1], s_sl.at[1, k - 1], r_sl.at[1, k - 1], who["line"](k))

    def copy_dz(k):
        return push(dz_send, dz_recv.at[k - 1], s_sl.at[2, k - 1], r_sl.at[2, k - 1], who["line"](k))

    def dt_a():
        dy_send[...] = tn(lpbd[:, bc:], normed[...])[0:16, :].astype(BF)
        copy_dy().start()

    def dt_b():
        copy_dy().wait()
        dz_send[...] = (dy_send[...].astype(F32) + dy_recv[...].astype(F32)).astype(BF)
        each_line(lambda k: copy_dz(k).start())

    def dt_c():
        each_line(lambda k: copy_dz(k).wait())
        total = dz_send[...].astype(F32)
        for k in range(lines - 1):
            total = total + dz_recv[k].astype(F32)
        small_out[8:24, :] = total

    def small_b():
        for k in range(3):
            copy_h(k).wait()
        over_heads = h_send[...] + h_recv[0] + h_recv[1] + h_recv[2]
        row_sums[0:token_rows, :] = over_heads[2 : 2 + token_rows, :]
        sy_send[0:2, :] = over_heads[0:2, :]
        sy_send[2:8, :] = acc[2:8, :]
        copy_sy().start()

    def small_c():
        copy_sy().wait()
        sz_send[...] = sy_send[...] + sy_recv[...]
        each_line(lambda k: copy_sz(k).start())

    def small_d():
        each_line(lambda k: copy_sz(k).wait())
        total = sz_send[...]
        for k in range(lines - 1):
            total = total + sz_recv[k]
        small_out[0:8, :] = total

    h_send[...] = jnp.zeros_like(h_send)

    def seq(*steps):
        for fn, *args in steps:
            fn(*args)

    assert units == 4

    def load(*which):
        for i in which:
            loads[i].wait()

    load(0, 1)
    grad_a(0)
    load(2, 3, 4, 5, 6, 7)
    seq((head_a, 0), (bc_a,), (head_b, 0), (head_a, 1), (bc_b,), (grad_a, 1), (head_b, 1), (grad_b, 0), (head_a, 2))
    seq((dt_a,), (head_b, 2), (head_a, 3), (small_a,), (bc_c,), (head_b, 3), (grad_b, 1), (dt_b,), (small_b,))
    seq((bc_d,), (head_c, 0), (small_c,), (grad_c, 0), (dt_c,), (head_c, 1), (bc_e,), (small_d,), (bc_f,), (head_c, 2))
    seq((grad_c, 1), (head_c, 3))


def tail(dp_n, units, normed_t, normed, lpx, lpz, lpbd, rows_x, rows_z, rows_bd, tokens, acc, cot, q_wide, vec, bc):
    count, width = normed.shape
    inner = lpx.shape[1]
    quarter = width // 4
    span = count // units
    block = width // dp_n
    lines = dp_n // 2
    half_rows = lines * block
    more = max(lines - 1, 1)
    vm = pltpu.VMEM
    dma = pltpu.SemaphoreType.DMA
    operands = (
        normed_t, lpx, rows_z, lpz, rows_x, lpbd, rows_bd, normed, tokens, acc, cot, q_wide, vec,
    )
    sds = jax.ShapeDtypeStruct
    spec = pl.BlockSpec(memory_space=pltpu.VMEM)
    return pl.pallas_call(
        functools.partial(tail_kernel, dp_n, units),
        out_shape=[
            sds((count, quarter), F32), sds((block, inner), F32), sds((block, bc), F32),
            sds((24, width), F32),
        ],
        in_specs=[pl.BlockSpec(memory_space=pl.ANY)] * 8 + [spec] * 5,
        out_specs=[spec] * 4,
        scratch_shapes=[
            vm((units, 2, span, quarter), BF), vm((units, 2, span, quarter), BF),
            vm((units, span, quarter), BF), vm((units, span, quarter), BF),
            vm((2, 2, span, quarter), F32), vm((units, span, quarter), F32),
            vm((2, half_rows, inner // 2), BF), vm((2, half_rows, inner // 2), BF),
            vm((2, half_rows, inner // 2), BF), vm((2, more, block, inner // 2), BF),
            vm((2, half_rows, inner // 2), F32),
            vm((half_rows, bc // 2), BF), vm((half_rows, bc // 2), BF),
            vm((half_rows, bc // 2), BF), vm((more, block, bc // 2), BF),
            vm((2 * half_rows, bc // 2), F32),
            vm((2 * half_rows, bc // 2), BF), vm((2 * half_rows, bc // 2), BF),
            vm((block, bc // 2), F32), vm((block, bc // 2), F32), vm((block, bc // 2), F32),
            vm((8, width), F32), vm((3, 8, width), F32),
            vm((8, width), F32), vm((8, width), F32), vm((8, width), F32), vm((more, 8, width), F32),
            vm((16, width), BF), vm((16, width), BF), vm((16, width), BF), vm((more, 16, width), BF),
            vm((8, width), F32),
        ]
        + [vm(a.shape, a.dtype) for a in operands[:8]]
        + [
            dma((8,)), dma((units,)), dma((units,)), dma((units,)), dma((units,)),
            dma((2,)), dma((2,)), dma((2, more)), dma((2, more)), dma((9,)), dma((9,)),
            dma((3, more)), dma((3, more)),
        ],
        compiler_params=pltpu.CompilerParams(
            collective_id=1, has_side_effects=True, vmem_limit_bytes=62 * 2**20
        ),
        name="tail",
    )(*operands)
def chain(ref_in, block_of, width, send, recv, y_send, y_recv, who):
    rows = ref_in.shape[0]
    lines, line, pair = who["lines"], who["line_index"], who["pair"]
    own = ref_in.at[:, width] if ref_in.shape[1] != width.size else ref_in

    def at(index):
        return block_of.at[pl.ds(pl.multiple_of((2 * index + pair) * rows, rows), rows), width]

    def hand(sign, j):
        index = line - sign * j
        source = own if isinstance(j, int) and j == 0 else at(index)
        slot = j + 1 if sign > 0 else lines + j
        to = (2 * (line + sign) + pair, who["mine"])
        return push(source, at(index), send.at[slot], recv.at[slot], to)

    def to_pair(sign, j):
        slot = j if sign > 0 else lines - 1 + j
        index = line - sign * j
        source = own if isinstance(j, int) and j == 0 else at(index)
        return push(source, at(index), y_send.at[slot], y_recv.at[slot], who["yn"])

    def arrived(sign, j):
        slot = j if sign > 0 else lines - 1 + j
        block = at(line - sign * j)
        return push(block, block, send.at[slot], recv.at[slot], who["yn"])

    def inside(index):
        return jnp.logical_and(index >= 0, index < lines)

    def both(fn):
        for sign in (1, -1):
            fn(sign)

    def begin():
        def one(sign):
            @pl.when(inside(line + sign))
            def _():
                hand(sign, 0).start()

        both(one)

    def begin_pair():
        to_pair(1, 0).start()

    def hop(j):
        def one(sign):
            @pl.when(inside(line - sign * j))
            def _():
                arrived(sign, j).wait_recv()

                @pl.when(inside(line + sign))
                def _():
                    hand(sign, j).start()

                to_pair(sign, j).start()

        both(one)

    def end():
        to_pair(1, 0).wait()

        def one(sign):
            @pl.when(inside(line + sign))
            def _():
                hand(sign, 0).wait_send()

        both(one)

        def later(j):
            def one(sign):
                @pl.when(inside(line - sign * j))
                def _():
                    to_pair(sign, j).wait()

                    @pl.when(inside(line + sign))
                    def _():
                        hand(sign, j).wait_send()

            both(one)

        loop_line(lines, later)

    return begin, begin_pair, hop, end


def loop_line(lines, fn):
    def step(k, carry):
        fn(k)
        return carry

    lax.fori_loop(1, lines, step, 0)


def front_kernel(
    dp_n, heads, units, taps, bc,
    tokens, cot, w_x, w_bc, w_z, w_out, w_dt, conv_x, conv_bc, norm_gain, gate_gain, dt_bias, a_log, skip, starts, fill,
    vec, px_out, pbd_out, normed_out, normed_t_out, q_out, y_out, sin_out, parts, rows_x, rows_bd, rows_z, rows_out,
    own_dt, tok, wx, wbd, px, pbd, normed, normed_t, q, y, sin, own_w, own_cot, state, extx, extb, upper, spread,
    s_loc, s_sib, r_sib, s_x, r_x, s_f, r_f, s_cx, r_cx, s_cf, r_cf, s_w, r_w, s_wy, r_wy, s_c, r_c, s_cy, r_cy, s_out, s_y,
):
    who = peers(dp_n)
    count, quarter = tokens.shape
    width = 4 * quarter
    span = count // units
    lines = who["lines"]
    block, inner = w_x.shape
    blocks = sin.shape[0]
    chunk = count // blocks
    per = blocks // units
    pieces = s_cx.shape[0]
    cot_span = count // pieces
    here = pl.ds(pl.multiple_of(who["dp"] * block, block), block)
    own_half = pl.ds(pl.multiple_of(who["core"] * (bc // 2), bc // 2), bc // 2)
    dt_cols = pl.ds(bc, chunk)
    local = [
        pltpu.make_async_copy(src, dst, s_loc.at[k])
        for k, (src, dst) in enumerate((
            (tokens, tok.at[who["mine"]]), (w_x, wx.at[here]), (w_bc.at[:, own_half], wbd.at[here, own_half]),
            (w_z, own_w.at[0]), (w_out, own_w.at[1]), (cot, own_cot),
        ))
    ]
    for copy in local:
        copy.start()
    own_dt[...] = jnp.zeros_like(own_dt)
    own_dt[:, :heads] = w_dt[...]
    wbd[here, dt_cols] = own_dt[...]
    onto = [
        pltpu.make_async_copy(src, dst, s_loc.at[8 + k])
        for k, (src, dst) in enumerate((
            (own_w.at[0], rows_z.at[here]), (own_w.at[1], rows_out.at[here]), (own_cot, parts.at[who["mine"]]),
        ))
    ]
    meet(who)

    def rows(s, n=span):
        return pl.ds(pl.multiple_of(s * n, n), n)

    def to_x(s):
        return push(tokens.at[rows(s)], tok.at[who["mine"], rows(s)], s_x.at[s], r_x.at[s], who["xn"])

    def to_sib():
        return push(tokens, tok.at[who["mine"]], s_sib.at[0], r_sib.at[0], who["sib"])

    def forward(s):
        at = tok.at[who["other"], rows(s)]
        return push(at, at, s_f.at[s], r_f.at[s], who["sib"])

    def cot_x(j):
        at = rows(j, cot_span)
        return push(cot.at[at], parts.at[who["mine"], at], s_cx.at[j], r_cx.at[j], who["xn"])

    def cot_sib():
        return push(cot, parts.at[who["mine"]], s_sib.at[1], r_sib.at[1], who["sib"])

    def cot_forward(j):
        at = parts.at[who["other"], rows(j, cot_span)]
        return push(at, at, s_cf.at[j], r_cf.at[j], who["sib"])

    half = inner // 2
    cuts = [
        chain(ref, to, cols, s_w.at[n], r_w.at[n], s_wy.at[n], r_wy.at[n], who)
        for n, (ref, to, cols) in enumerate((
            (w_x, wx, pl.ds(0, half)), (w_x, wx, pl.ds(half, half)), (w_bc, wbd, own_half), (own_dt, wbd, dt_cols),
        ))
    ]
    chains = [
        chain(ref, to, pl.ds(h * half, half), s_c.at[2 * n + h], r_c.at[2 * n + h], s_cy.at[2 * n + h], r_cy.at[2 * n + h], who)
        for n, (ref, to) in enumerate(((w_z, rows_z), (w_out, rows_out)))
        for h in (0, 1)
    ]

    def other_half():
        cols = wbd.at[:, own_half]
        return push(cols, cols, s_sib.at[2], r_sib.at[2], who["sib"])

    def have(n):
        cuts[n][3]()

    def pass_cot(j):
        cot_x(j).wait()
        cot_forward(j).start()

    to_x(0).start()
    for begin, begin_pair, hop, end in cuts:
        begin()
        begin_pair()
    for s in range(1, units):
        to_x(s).start()
    to_sib().start()
    for j in range(pieces):
        cot_x(j).start()
    pack_vec(vec, conv_x, conv_bc, norm_gain, gate_gain, dt_bias, a_log, skip, starts, fill, chunk)
    set_upper(upper)
    set_spread(spread, heads)
    state[...] = jnp.zeros_like(state)
    extx[...] = jnp.zeros_like(extx)
    extb[...] = jnp.zeros_like(extb)
    par = read_vec(vec, heads, chunk, inner, bc, taps)
    gain = vec[6:7, :width]

    def out_copies(s):
        at = rows(s)
        every = slice(None)
        return [
            pltpu.make_async_copy(ref.at[to], out.at[to], s_out.at[n, s])
            for n, (ref, out, to) in enumerate((
                (normed, normed_out, (at,)), (normed_t, normed_t_out, (every, at)), (q, q_out, (at,)),
                (px, px_out, (at,)), (pbd, pbd_out, (at,)),
            ))
        ]

    def norm(s):
        at = rows(s)
        values = [tok[h, at, :].astype(F32) for h in range(4)]
        total = sum(jnp.sum(p * p, axis=1, keepdims=True) for p in values)
        inv = lax.rsqrt(total / width + EPS)
        q[at, :] = jnp.broadcast_to(inv, (span, q.shape[1]))
        for h in range(4):
            cols = slice(h * quarter, (h + 1) * quarter)
            value = (values[h] * inv * gain[:, cols]).astype(BF)
            normed[at, cols] = value
            normed_t[cols, at] = jnp.transpose(value)
        for copy in out_copies(s)[:3]:
            copy.start()

    def project(s):
        at = rows(s)
        pbd[at, :] = nn(normed[at, :], wbd[...])
        px[at, :] = nn(normed[at, :], wx[...])
        for copy in out_copies(s)[3:]:
            copy.start()

    def hops(group, j):
        if j < lines:
            for begin, begin_pair, hop, end in group:
                hop(j)

    local[0].wait()
    hops(cuts, 1)
    to_x(0).wait()
    forward(0).start()
    hops(cuts, 2)
    for begin, begin_pair, hop, end in chains:
        begin()
    to_sib().wait()
    forward(0).wait()
    norm(0)
    to_x(1).wait()
    forward(1).start()
    hops(cuts, 3)
    if lines > 4:
        for begin, begin_pair, hop, end in cuts:
            lax.fori_loop(4, lines, lambda j, a, fn=hop: (fn(j), a)[1], 0)
    for begin, begin_pair, hop, end in chains:
        begin_pair()
    forward(1).wait()
    norm(1)
    have(2)
    local[2].wait()
    other_half().start()
    to_x(2).wait()
    forward(2).start()
    for copy in local[3:]:
        copy.wait()
    for copy in onto:
        copy.start()
    cot_sib().start()
    forward(2).wait()
    norm(2)
    local[1].wait()
    for n in (0, 1, 3):
        have(n)
    other_half().wait()
    hops(chains, 1)
    keep_rows = [
        pltpu.make_async_copy(wx, rows_x, s_loc.at[6]), pltpu.make_async_copy(wbd, rows_bd, s_loc.at[7]),
    ]
    for copy in keep_rows:
        copy.start()

    def last_tokens(s):
        to_x(s).wait()
        forward(s).start()

    def last_norm(s):
        forward(s).wait()
        norm(s)

    events = {1: [(last_tokens, units - 1)], 2: [(last_norm, units - 1)]}
    late = []
    plan = []
    for n, (begin, begin_pair, hop, end) in enumerate(chains):
        if lines > 2:
            plan.append((hop, 2, 1 + n // 2))
        if lines > 3:
            plan.append((hop, 3, 3 + n))
        if lines > 4:
            plan.append((lambda k, fn=hop: lax.fori_loop(4, lines, lambda j, a: (fn(j), a)[1], 0), 0, 7 + n))
    plan += [(pass_cot, j, 5 + 2 * j) for j in range(pieces)]
    for fn, k, at in plan:
        if at < blocks:
            events.setdefault(at, []).append((fn, k))
        else:
            late.append((fn, k))

    def y_copies(c):
        at = rows(c, chunk)
        return (
            pltpu.make_async_copy(y.at[at], y_out.at[at], s_y.at[0, c]),
            pltpu.make_async_copy(sin.at[c], sin_out.at[c], s_y.at[1, c]),
        )

    def step(c, carry):
        for at, fns in events.items():

            @pl.when(c == at)
            def _(fns=fns):
                for fn, k in fns:
                    fn(k)

        @pl.when(c % per == 0)
        def _():
            project(c // per)

        at = rows(c, chunk)
        y_c, enter = scan_step(
            heads, par, read_block(vec, c, chunk), px.at[at], pbd.at[at], upper, spread, state, extx, extb
        )
        y[at, :] = y_c
        sin[c] = enter
        for copy in y_copies(c):
            copy.start()
        return carry

    lax.fori_loop(0, blocks, step, 0)
    for fn, k in late:
        fn(k)

    def end_y(c, carry):
        for copy in y_copies(c):
            copy.wait()
        return carry

    lax.fori_loop(0, blocks, end_y, 0)
    for s in range(units):
        for copy in out_copies(s):
            copy.wait()
    for copy in onto + keep_rows:
        copy.wait()
    cot_sib().wait()
    for j in range(pieces):
        cot_forward(j).wait()
    for begin, begin_pair, hop, end in chains:
        end()


def front(dp_n, tokens, cot, w_x, w_bc, w_z, w_out, w_dt, conv_x, conv_bc, norm_gain, gate_gain, *scalars):
    count, quarter = tokens.shape
    width = 4 * quarter
    inner, heads = w_x.shape[1], w_dt.shape[1]
    taps, bc = conv_bc.shape
    blocks = scalars[-1].shape[0]
    chunk = count // blocks
    wide = bc + chunk
    units, pieces = 4, 8
    vm, dma, sds = pltpu.VMEM, pltpu.SemaphoreType.DMA, jax.ShapeDtypeStruct
    hbm, vmem = pl.BlockSpec(memory_space=pl.ANY), pl.BlockSpec(memory_space=pltpu.VMEM)
    ways = dp_n - 1
    outs = [
        sds((24 + blocks, width), F32),
        sds((count, inner), F32), sds((count, wide), F32), sds((count, width), BF), sds((width, count), BF),
        sds((count, 128), F32), sds((count, inner), F32), sds((blocks, bc // 2, inner), BF),
        sds((4, count, quarter), BF), sds((width, inner), BF), sds((width, wide), BF), sds((width, inner), BF),
        sds((width, inner), BF),
    ]
    return pl.pallas_call(
        functools.partial(front_kernel, dp_n, heads, units, taps, bc),
        out_shape=outs,
        in_specs=[hbm] * 6 + [vmem] * 5 + [pl.BlockSpec(memory_space=pltpu.SMEM)] * 5,
        out_specs=[vmem] + [hbm] * (len(outs) - 1),
        scratch_shapes=[
            vm((w_x.shape[0], chunk), BF),
            vm((4, count, quarter), BF), vm((width, inner), BF), vm((width, wide), BF),
            vm((count, inner), F32), vm((count, wide), F32), vm((count, width), BF), vm((width, count), BF),
            vm((count, 128), F32), vm((count, inner), F32), vm((blocks, bc // 2, inner), BF),
            vm((2,) + w_z.shape, BF), vm(cot.shape, BF),
            vm((bc // 2, inner), F32), vm((chunk + 8, inner), F32), vm((chunk + 8, bc), F32),
            vm((chunk, chunk), BF), vm((chunk, 3 * inner), BF),
            dma((11,)), dma((3,)), dma((3,)), dma((units,)), dma((units,)), dma((units,)), dma((units,)),
            dma((pieces,)), dma((pieces,)), dma((pieces,)), dma((pieces,)),
            dma((4, ways + 1)), dma((4, ways + 1)), dma((4, ways)), dma((4, ways)), dma((4, ways + 1)), dma((4, ways + 1)), dma((4, ways)), dma((4, ways)),
            dma((5, units)), dma((2, blocks)),
        ],
        compiler_params=pltpu.CompilerParams(
            collective_id=2, has_side_effects=True, vmem_limit_bytes=58 * 2**20
        ),
        name="front",
    )(
        tokens, cot, w_x, w_bc, w_z, w_out, w_dt, conv_x, conv_bc, norm_gain[None, :], gate_gain[None, :], *scalars
    )
def finish_kernel(heads, taps, bc, bo, gt, gx, gz, go, gb, small, own, o_bo, o_gt, o_gx, o_gz, o_go, o_gb, o_gain, o_cx, o_cb, o_bias, o_alog, o_skip, o_gate):
    o_bo[...] = bo[...]
    o_gt[...] = gt[...]

    @pl.when(pl.program_id(0) == 0)
    def _():
        for src, dst in ((gx, o_gx), (gz, o_gz), (go, o_go), (gb, o_gb)):
            dst[...] = src[...]
        inner = o_cx.shape[1]
        per = small.shape[1] // inner
        for k in range(taps):
            o_cx[k : k + 1, :] = small[2 + k // per : 3 + k // per, (k % per) * inner : (k % per + 1) * inner]
            o_cb[k : k + 1, :] = small[1:2, k * bc : (k + 1) * bc]
        scalars = small[5:6, :128]
        o_bias[...] = scalars[0, :heads]
        o_alog[...] = scalars[0, heads : 2 * heads]
        o_skip[...] = scalars[0, 2 * heads : 3 * heads]
        o_gate[...] = small[4, :inner]
        columns = o_gain.shape[0]
        at = pl.ds(pl.multiple_of(lax.axis_index("heads") * columns, columns), columns)
        o_gain[...] = (small[0:1, at] / own[:, at])[0]


def finish(bo, gt, gx, gz, go, gb, small, norm_gain, heads, taps, bc):
    steps = 4
    sds = jax.ShapeDtypeStruct
    count, quarter = bo.shape
    inner = gx.shape[1]
    rows = pl.BlockSpec((count // steps, quarter), lambda i: (i, 0))
    whole = lambda shape: pl.BlockSpec(shape, lambda i: (0,) * len(shape))
    smalls = [(quarter,), (taps, inner), (taps, bc), (heads,), (heads,), (heads,), (inner,)]
    operands = (bo, gt, gx, gz, go, gb, small, norm_gain[None, :])
    return pl.pallas_call(
        functools.partial(finish_kernel, heads, taps, bc),
        grid=(steps,),
        in_specs=[rows, rows] + [whole(a.shape) for a in operands[2:]],
        out_specs=[rows, rows] + [whole(a.shape) for a in operands[2:6]] + [whole(s) for s in smalls],
        out_shape=[sds(a.shape, a.dtype) for a in operands[:6]] + [sds(s, F32) for s in smalls],
        name="finish",
    )(*operands)


def body(
    tokens, cotangent, starts, fill, norm_gain, w_x, w_z, w_dt, w_bc, conv_x, conv_bc, dt_bias, a_log, skip,
    gate_gain, w_out,
):
    heads_n = lax.axis_size("heads")
    dp_n = lax.axis_size("dp")
    dp_index = lax.axis_index("dp")
    count, columns = tokens.shape
    width = columns * heads_n
    blocks = starts.shape[0]
    chunk = count // blocks
    inner = w_x.shape[1]
    heads = w_dt.shape[1]
    taps, bc = conv_bc.shape
    vec, px, pbd, normed, normed_t, q_wide, y, sin, parts, rows_x, rows_bd, rows_z, rows_out = front(
        dp_n, tokens, cotangent, w_x, w_bc, w_z, w_out, w_dt, conv_x, conv_bc, norm_gain, gate_gain, dt_bias, a_log,
        skip, starts, fill,
    )
    dy, lpz, gn, y_send, g_own, gain_grad = gate(dp_n, blocks, normed, normed_t, rows_z, rows_out, parts, y, vec)
    lpx, lpbd, acc, block_out, grad_w_out, grad_w_z = scan_backward(
        dp_n, dy, px, pbd, sin, gain_grad, vec, gn, rows_out, tokens, y_send, g_own, heads, taps, bc
    )
    grad_tokens, grad_w_x, grad_w_bc, small = tail(
        dp_n, 4, normed_t, normed, lpx, lpz, lpbd, rows_x, rows_z, rows_bd, tokens, acc, cotangent, q_wide, vec, bc,
    )
    block = width // dp_n
    grad_w_dt = lax.dynamic_slice_in_dim(small[8 : 8 + heads], dp_index * block, block, 1).T
    (
        block_out, grad_tokens, grad_w_x, grad_w_z, grad_w_out, grad_w_bc, grad_norm_gain, grad_conv_x, grad_conv_bc,
        grad_dt_bias, grad_a_log, grad_skip, grad_gate_gain,
    ) = finish(
        block_out, grad_tokens, grad_w_x, grad_w_z, grad_w_out, grad_w_bc, small, norm_gain, heads, taps, bc
    )
    return (
        block_out, grad_tokens, grad_norm_gain, grad_w_x, grad_w_z, grad_w_dt, grad_w_bc, grad_conv_x, grad_conv_bc,
        grad_dt_bias, grad_a_log, grad_skip, grad_gate_gain, grad_w_out,
    )


def solution(mesh):
    placed = (
        P("dp", "heads"),
        P("dp", "heads"),
        P("dp"),
        P("dp"),
        P(),
        P("dp", "heads"),
        P("dp", "heads"),
        P("dp", "heads"),
        P("dp", None),
        P(None, "heads"),
        P(),
        P("heads"),
        P("heads"),
        P("heads"),
        P("heads"),
        P("dp", "heads"),
    )
    return jax.shard_map(
        body,
        mesh=mesh,
        in_specs=placed,
        out_specs=(
            P("dp", "heads"),
            P("dp", "heads"),
            P("heads"),
            P("dp", "heads"),
            P("dp", "heads"),
            P("dp", "heads"),
            P("dp", None),
            P(None, "heads"),
            P(),
            P("heads"),
            P("heads"),
            P("heads"),
            P("heads"),
            P("dp", "heads"),
        ),
        check_vma=False,
    )
```

```python
import functools
import jax
import jax.numpy as jnp
from jax import lax
from jax.experimental import pallas as pl
from jax.experimental.pallas import tpu as pltpu
from jax.sharding import PartitionSpec as P

HD = 64
EPS = 1e-05
F32 = jnp.float32
BF = jnp.bfloat16
NEG = -1e30
MESH = pl.DeviceIdType.MESH


def nn(a, b):
    return lax.dot_general(a, b, (((1,), (0,)), ((), ())), preferred_element_type=F32)


def nt(a, b):
    return lax.dot_general(a, b, (((1,), (1,)), ((), ())), preferred_element_type=F32)


def tn(a, b):
    return lax.dot_general(a, b, (((0,), (0,)), ((), ())), preferred_element_type=F32)


def split2(v):
    hi = v.astype(BF).astype(F32)
    return hi, v - hi


def split3(v):
    hi = v.astype(BF).astype(F32)
    rest = v - hi
    mid = rest.astype(BF).astype(F32)
    return hi, mid, rest - mid


def softplus(v):
    return jnp.maximum(v, 0.0) + jnp.log1p(jnp.exp(-jnp.abs(v)))


def sigmoid(v):
    return 1.0 / (1.0 + jnp.exp(-v))


def iota2(rows, cols, axis):
    return lax.broadcasted_iota(jnp.int32, (rows, cols), axis)


def zero_one(cond):
    return jnp.where(cond, 1.0, 0.0).astype(BF)


def set_upper(upper):
    upper[...] = zero_one(iota2(*upper.shape, 0) <= iota2(*upper.shape, 1))


def set_spread(spread, heads):
    rows, lanes = iota2(*spread.shape, 0), iota2(*spread.shape, 1)
    inner = heads * HD
    base = heads * (1 + 2 * (lanes // inner)) + (lanes % inner) // HD
    spread[...] = zero_one(jnp.logical_or(rows == base, rows == base + heads))


def set_gather(gather, ones_h, heads):
    for q in range(3):
        rows, lanes = iota2(*gather.shape[1:], 0), iota2(*gather.shape[1:], 1)
        gather[q] = zero_one(lanes == q * heads + rows // HD)
    rows, lanes = iota2(*ones_h.shape, 0), iota2(*ones_h.shape, 1)
    ones_h[...] = zero_one(lanes == heads + rows // ones_h.shape[1])


def conv_from(ext, taps, rows, halo):
    n = taps.shape[0]
    moved = [ext[pl.ds(halo - k, rows), :] for k in range(n)]
    out = taps[n - 1 : n, :] * moved[0]
    for k in range(1, n):
        out = out + taps[n - 1 - k : n - k, :] * moved[k]
    return out, moved


def dt_rows(pdt, bias, rate, fill, heads, upper):
    chunk = pdt.shape[0]
    pre = jnp.transpose(pdt)[:heads] + bias
    live = (iota2(heads, chunk, 1).astype(F32) < fill).astype(F32)
    dt = softplus(pre) * live
    hi, mid, low = split3(dt * rate)
    stacked = jnp.concatenate([hi, mid, low], axis=0).astype(BF)
    summed = nn(stacked, upper)
    run = summed[:heads] + summed[heads : 2 * heads] + summed[2 * heads :]
    return pre, live, dt, run


def spread_all(run, dt, heads, chunk, spread):
    last = run[:, chunk - 1 : chunk]
    e_in = jnp.exp(run)
    e_out = jnp.exp(last - run)
    parts = [run]
    for v in (dt, e_in, e_out):
        parts.extend(split2(v))
    used = heads * len(parts)
    if used < chunk:
        parts.append(jnp.zeros((chunk - used, chunk), F32))
    cols = jnp.transpose(jnp.concatenate(parts, axis=0))
    return cols, nn(cols.astype(BF), spread)


def pair_stack(v, low_lanes):
    zero = jnp.zeros_like(v)
    return jnp.concatenate([jnp.where(low_lanes, v, zero), jnp.where(low_lanes, zero, v)], axis=0)


def read_vec(vec, heads, chunk, inner, bc, taps):
    return dict(
        convx=vec[0:taps, :inner], skip=vec[4:5, :inner], gain=vec[5:6, :inner],
        bias=vec[8 : 8 + heads, :chunk], rate=vec[8 : 8 + heads, chunk : 2 * chunk], convbc=vec[16 : 16 + taps, :bc],
    )


def read_block(vec, c, chunk):
    row = vec[pl.ds(24 + c, 1), :]
    return row[:, 0:1] > 0.5, row[:, chunk : chunk + 1], row[:, 2 * chunk : 2 * chunk + 1] > 0.5


def pack_vec(vec, conv_x, conv_bc, norm_gain, gate_gain, dt_bias, a_log, skip, starts, fill, chunk):
    taps, inner = conv_x.shape
    vec[...] = jnp.zeros_like(vec)
    vec[0:taps, :inner] = conv_x[...]
    vec[16 : 16 + taps, : conv_bc.shape[1]] = conv_bc[...]
    vec[5:6, :inner] = gate_gain[...]
    vec[6:7, :] = norm_gain[...]
    head = iota2(1, inner, 1) // HD
    skips = jnp.zeros((1, inner), F32)
    for h in range(dt_bias.shape[0]):
        skips = jnp.where(head == h, skip[h], skips)
        vec[8 + h : 9 + h, 0:chunk] = jnp.full((1, chunk), dt_bias[h], F32)
        vec[8 + h : 9 + h, chunk : 2 * chunk] = -jnp.exp(jnp.full((1, chunk), a_log[h], F32))
    vec[4:5, :inner] = skips
    blocks = starts.shape[0]
    for c in range(blocks):
        row = slice(24 + c, 25 + c)
        vec[row, 0:chunk] = jnp.full((1, chunk), 1 - starts[c], jnp.int32).astype(F32)
        vec[row, chunk : 2 * chunk] = jnp.full((1, chunk), fill[c], jnp.int32).astype(F32)
        if c + 1 < blocks:
            vec[row, 2 * chunk : 3 * chunk] = jnp.full((1, chunk), 1 - starts[c + 1], jnp.int32).astype(F32)


def scan_step(heads, par, block, px, pbd, upper, spread, state, extx, extb):
    chunk, inner = px.shape
    bc = par["convbc"].shape[1]
    ns = bc // 2
    keep, n_live, _ = block
    state[...] = jnp.where(keep, state[...], 0.0)
    extx[0:8, :] = jnp.where(keep, extx[chunk : chunk + 8, :], 0.0)
    extb[0:8, :] = jnp.where(keep, extb[chunk : chunk + 8, :], 0.0)
    extx[8 : chunk + 8, :] = px[...]
    extb[8 : chunk + 8, :] = pbd[:, :bc]

    u, _ = conv_from(extx, par["convx"], chunk, 8)
    x = u * sigmoid(u) * (iota2(chunk, inner, 0).astype(F32) < n_live).astype(F32)
    ub, _ = conv_from(extb, par["convbc"], chunk, 8)
    act = (ub * sigmoid(ub) * (iota2(chunk, bc, 0).astype(F32) < n_live).astype(F32)).astype(BF)
    b, cc = act[:, :ns], act[:, ns:]

    _, _, dt, run = dt_rows(pbd[:, bc:], par["bias"], par["rate"], n_live, heads, upper[...])
    cols, wide = spread_all(run, dt, heads, chunk, spread[...])
    dt_w, ein_w, eout_w = wide[:, :inner], wide[:, inner : 2 * inner], wide[:, 2 * inner :]

    xd = x * dt_w
    xdb = xd.astype(BF)
    scores = nt(cc, b)
    tri = iota2(chunk, chunk, 0) >= iota2(chunk, chunk, 1)
    low_lanes = iota2(chunk, 2 * HD, 1) < HD
    diag = []
    for j in range(heads // 2):
        mix = []
        for h in (2 * j, 2 * j + 1):
            spread_h = cols[:, h : h + 1] - run[h : h + 1, :]
            mix.append((scores * jnp.exp(jnp.where(tri, spread_h, NEG))).astype(BF))
        pair = pair_stack(xdb[:, 2 * HD * j : 2 * HD * (j + 1)], low_lanes)
        diag.append(nn(jnp.concatenate(mix, axis=1), pair))
    enter = state[...]
    enter_b = enter.astype(BF)
    y = jnp.concatenate(diag, axis=1) + ein_w * nn(cc, enter_b) + par["skip"] * x
    state[...] = ein_w[chunk - 1 : chunk, :] * enter + tn(b, (xd * eout_w).astype(BF))
    return y, enter_b


def pair_rows(dp_n, block, pair, values):
    return jnp.concatenate(
        [values[pl.ds(pl.multiple_of((2 * l + pair) * block, block), block), :] for l in range(dp_n // 2)], axis=0
    )


def gate_kernel(
    dp_n, normed, rows_z, rows_out, parts, y, vec, normed_t_in, dy_out, lpz, gn, y_send, g_own, gain_grad,
    h_send, h_recv, z_all, g_all, y_all, grad_t, normed_t, s_h, r_h, s_in,
):
    i = pl.program_id(0)
    who = peers(dp_n)
    names = ("sib", "xn", "dg")
    barrier = pltpu.get_barrier_semaphore()
    span, quarter = parts.shape[1:]
    blocks, chunk = h_send.shape[1:]
    inner = y.shape[1]
    here = pl.ds(pl.multiple_of(i * span, span), span)
    load = pltpu.make_async_copy(normed_t_in, normed_t, s_in.at[0])

    @pl.when(i == 0)
    def _():
        load.start()
        for name in names:
            pl.semaphore_signal(barrier, inc=1, device_id=who[name], device_id_type=MESH)

    z = nn(normed[...], rows_z[...])
    z_all[here, :] = z
    y_all[here, :] = y[...]
    g = nn(parts[0], rows_out[0:quarter, :])
    for k in range(1, 4):
        g = g + nn(parts[k], rows_out[k * quarter : (k + 1) * quarter, :])
    g_all[here, :] = g
    for k in range(4):
        grad_t[k * quarter : (k + 1) * quarter, here] = jnp.transpose(parts[k])
    gated = y[...] * (z * sigmoid(z))
    ones = jnp.ones((8, inner), BF)
    for k, value in enumerate((gated * gated, gated * vec[5:6, :inner] * g)):
        row = nt(ones, value.astype(BF))
        for j in range(span // chunk):
            h_send[k, pl.ds(i * (span // chunk) + j, 1), :] = row[0:1, j * chunk : (j + 1) * chunk]

    @pl.when(i == pl.num_programs(0) - 1)
    def _():
        pl.semaphore_wait(barrier, 3)
        copies = [push(h_send, h_recv.at[k], s_h.at[k], r_h.at[k], who[name]) for k, name in enumerate(names)]
        for copy in copies:
            copy.start()
        for copy in copies:
            copy.wait()
        sums = h_send[...] + h_recv[0] + h_recv[1] + h_recv[2]
        gain = vec[5:6, :inner]
        below = jnp.zeros((chunk - blocks, chunk), F32)
        inv = lax.rsqrt(jnp.transpose(jnp.concatenate([sums[0], below], axis=0)) / (4 * inner) + EPS)
        dots = jnp.transpose(jnp.concatenate([sums[1], below], axis=0))
        coef = inv * inv * inv * (dots / (4 * inner))
        gain_grad[...] = jnp.zeros_like(gain_grad)
        for b in range(blocks):
            at = slice(b * chunk, (b + 1) * chunk)
            zb, yb, gb = z_all[at, :], y_all[at, :], g_all[at, :]
            sz = sigmoid(zb)
            silu_z = zb * sz
            gated_b = yb * silu_z
            inv_b = inv[:, b : b + 1]
            scaled = gated_b * inv_b
            gn[at, :] = (scaled * gain).astype(BF)
            gain_grad[0:1, :] += jnp.sum(gb * scaled, axis=0, keepdims=True)
            d_gated = inv_b * (gb * gain) - gated_b * coef[:, b : b + 1]
            lpz[at, :] = (d_gated * yb * (sz * (1.0 + zb * (1.0 - sz)))).astype(BF)
            dy_out[at, :] = d_gated * silu_z
        load.wait()
        block = grad_t.shape[0] // dp_n
        for v, (left, right) in enumerate(((grad_t, gn), (normed_t, lpz))):
            theirs = nn(pair_rows(dp_n, block, 1 - who["pair"], left), right[...])
            ours = nn(pair_rows(dp_n, block, who["pair"], left), right[...])
            for h in (0, 1):
                cols = slice(h * (inner // 2), (h + 1) * (inner // 2))
                y_send[2 * v + h] = theirs[:, cols].astype(BF)
                g_own[2 * v + h] = ours[:, cols]


def gate(dp_n, blocks, normed, normed_t, rows_z, rows_out, parts, y, vec):
    count, width = normed.shape
    inner = y.shape[1]
    chunk = count // blocks
    steps = 8
    span = count // steps
    quarter = width // 4
    sds = jax.ShapeDtypeStruct
    rows = lambda w: pl.BlockSpec((span, w), lambda i: (i, 0))
    whole = lambda shape: pl.BlockSpec(shape, lambda i: (0,) * len(shape))
    halves = (4, width // 2, inner // 2)
    return pl.pallas_call(
        functools.partial(gate_kernel, dp_n),
        grid=(steps,),
        in_specs=[
            rows(width), whole(rows_z.shape), whole(rows_out.shape),
            pl.BlockSpec((4, span, quarter), lambda i: (0, i, 0)), rows(inner), whole(vec.shape),
            pl.BlockSpec(memory_space=pl.ANY),
        ],
        out_specs=[whole((count, inner))] * 3 + [whole(halves), whole(halves), whole((8, inner))],
        out_shape=[
            sds((count, inner), F32), sds((count, inner), BF), sds((count, inner), BF), sds(halves, BF),
            sds(halves, F32), sds((8, inner), F32),
        ],
        scratch_shapes=[
            pltpu.VMEM((2, blocks, chunk), F32), pltpu.VMEM((3, 2, blocks, chunk), F32),
            pltpu.VMEM((count, inner), F32), pltpu.VMEM((count, inner), F32), pltpu.VMEM((count, inner), F32),
            pltpu.VMEM((width, count), BF), pltpu.VMEM((width, count), BF),
            pltpu.SemaphoreType.DMA((3,)), pltpu.SemaphoreType.DMA((3,)), pltpu.SemaphoreType.DMA((1,)),
        ],
        compiler_params=pltpu.CompilerParams(
            collective_id=4, has_side_effects=True, vmem_limit_bytes=58 * 2**20
        ),
        name="gate",
    )(normed, rows_z, rows_out, parts, y, vec, normed_t)


def sums_beside_scan(
    dp_n, gn_in, rows_out_in, tokens_in, y_send_in, g_in_in, block_out, g_out, g_z,
    gn, rows_out, tokens, y_send, g_in, s_in, sib_send, sib_recv, x_send, x_recv, part, held, y_recv, z_send, z_recv, g_own,
    s_sib, r_sib, s_x, r_x, s_y, r_y, s_z, r_z,
):
    i = pl.program_id(0)
    who = peers(dp_n)
    lines = who["lines"]
    units, span, quarter = held.shape
    block = g_out.shape[0]
    half = g_out.shape[1] // 2

    def copy_sib(k):
        return push(sib_send.at[k], sib_recv.at[k], s_sib.at[k], r_sib.at[k], who["sib"])

    def copy_x(k):
        return push(x_send.at[k], x_recv.at[k], s_x.at[k], r_x.at[k], who["xn"])

    def copy_y(v):
        return push(y_send.at[v], y_recv.at[v], s_y.at[v], r_y.at[v], who["yn"])

    def copy_z(v, k):
        to = (who["line_index"] + k) % lines
        return push(
            z_send.at[v, pl.ds(pl.multiple_of(to * block, block), block)],
            z_recv.at[v, k - 1], s_z.at[v, k - 1], r_z.at[v, k - 1], who["line"](k),
        )

    loads = [
        pltpu.make_async_copy(src, dst, s_in.at[n])
        for n, (src, dst) in enumerate((
            (y_send_in, y_send), (rows_out_in, rows_out), (gn_in, gn), (tokens_in, tokens), (g_in_in, g_in),
        ))
    ]

    @pl.when(i == 0)
    def _():
        for load in loads:
            load.start()
        meet(who)
        loads[0].wait()
        for v in range(4):
            copy_y(v).start()

    @pl.when(i == 1)
    def _():
        for load in loads[1:]:
            load.wait()

    def first(k):
        for n, q in enumerate(("sib_mine", "sib_other", "mine", "other")):
            cols = pl.ds(pl.multiple_of(who[q] * quarter, quarter), quarter)
            p = nt(gn[k * span : (k + 1) * span, :], rows_out[cols, :])
            if n < 2:
                sib_send[k, n] = p.astype(BF)
            else:
                part[n - 2] = p
        copy_sib(k).start()

    def second(k):
        copy_sib(k).wait()
        x_send[k] = (part[1] + sib_recv[k, 1].astype(F32)).astype(BF)
        copy_x(k).start()
        held[k] = part[0] + sib_recv[k, 0].astype(F32)

    def third(k):
        copy_x(k).wait()
        at = slice(k * span, (k + 1) * span)
        block_out[at, :] = (tokens[at, :].astype(F32) + held[k] + x_recv[k].astype(F32)).astype(BF)

    def grad_b(v):
        copy_y(v).wait()
        g_own[v] = g_in[v] + y_recv[v].astype(F32)
        z_send[v] = g_own[v].astype(BF)
        loop_line(lines, lambda k: copy_z(v, k).start())

    def grad_c(v):
        loop_line(lines, lambda k: copy_z(v, k).wait())
        total = g_own[v, pl.ds(pl.multiple_of(who["line_index"] * block, block), block), :]
        for k in range(lines - 1):
            total = total + z_recv[v, k].astype(F32)
        (g_out, g_z)[v // 2][:, (v % 2) * half : (v % 2 + 1) * half] = total

    events = [(grad_b, 0, 3), (grad_b, 1, 6), (grad_b, 2, 8), (grad_b, 3, 11)]
    for k in range(units):
        events += [(first, k, 2 * k + 1), (second, k, 2 * k + 2), (third, k, 2 * k + 7)]
    for at in sorted({e[2] for e in events}):

        @pl.when(i == at)
        def _(at=at):
            for fn, k, when in events:
                if when == at:
                    fn(k)

    def finish():
        for v in range(4):
            grad_c(v)

    return finish


def scan_bwd_kernel(
    heads, taps_n, bc, dp_n, dy_in, px, px_halo, pbd, pbd_halo, sin, gain_grad, vec, gn, rows_out, tokens,
    y_send, g_in,
    lpx, lpbd, acc, block_out, g_out, g_z, dstate, extx, extb, dux, dub, acc_x, acc_bc, acc_s, upper, spread, gather, ones_h,
    *beside,
):
    finish = sums_beside_scan(dp_n, gn, rows_out, tokens, y_send, g_in, block_out, g_out, g_z, *beside)
    i = pl.program_id(0)
    blocks = pl.num_programs(0)
    c = blocks - 1 - i
    chunk, inner = px.shape
    ns = bc // 2
    par = read_vec(vec, heads, chunk, inner, bc, taps_n)
    keep, n_live, keep_next = read_block(vec, c, chunk)
    taps, taps_b, bias, rate, skip = (par[k] for k in ("convx", "convbc", "bias", "rate", "skip"))

    @pl.when(i == 0)
    def _():
        for ref in (dstate, dux, dub, acc_x, acc_bc, acc_s):
            ref[...] = jnp.zeros_like(ref)
        acc_x[taps_n : taps_n + 1, :] = gain_grad[0:1, :]
        set_upper(upper)
        set_spread(spread, heads)
        set_gather(gather, ones_h, heads)

    dy = dy_in[...]

    extx[0:8, :] = jnp.where(keep, px_halo[...], 0.0)
    extb[0:8, :] = jnp.where(keep, pbd_halo[:, :bc], 0.0)
    extx[8 : chunk + 8, :] = px[...]
    extb[8 : chunk + 8, :] = pbd[:, :bc]
    live_x = (iota2(chunk, inner, 0).astype(F32) < n_live).astype(F32)
    live_b = (iota2(chunk, bc, 0).astype(F32) < n_live).astype(F32)
    u, moved_x = conv_from(extx, taps, chunk, 8)
    su = sigmoid(u)
    x = u * su * live_x
    dx_du = su * (1.0 + u * (1.0 - su)) * live_x
    ub, moved_b = conv_from(extb, taps_b, chunk, 8)
    sb = sigmoid(ub)
    act = (ub * sb * live_b).astype(BF)
    db_du = sb * (1.0 + ub * (1.0 - sb)) * live_b
    b, cc = act[:, :ns], act[:, ns:]

    pre, live, dt, run = dt_rows(pbd[:, bc:], bias, rate, n_live, heads, upper[...])
    cols, wide = spread_all(run, dt, heads, chunk, spread[...])
    dt_w, ein_w, eout_w = wide[:, :inner], wide[:, inner : 2 * inner], wide[:, 2 * inner :]
    xd = x * dt_w
    xdb = xd.astype(BF)
    dyb = dy.astype(BF)
    acc_x[taps_n + 1 : taps_n + 2, :] += jnp.sum(dy * x, axis=0, keepdims=True)

    scores_t = nt(b, cc)
    tri = iota2(chunk, chunk, 0) <= iota2(chunk, chunk, 1)
    low_lanes = iota2(chunk, 2 * HD, 1) < HD
    d_scores_t = jnp.zeros((chunk, chunk), F32)
    dxd = []
    pulls = []
    read_sums = []
    for j in range(heads // 2):
        span = slice(2 * HD * j, 2 * HD * (j + 1))
        dy_pair = pair_stack(dyb[:, span], low_lanes)
        x_pair = pair_stack(xdb[:, span], low_lanes)
        d_mix = nt(x_pair, dyb[:, span])
        mix = []
        for k in (0, 1):
            h = 2 * j + k
            spread_h = run[h : h + 1, :] - cols[:, h : h + 1]
            fade = jnp.exp(jnp.where(tri, spread_h, NEG))
            m = scores_t * fade
            dm = d_mix[k * chunk : (k + 1) * chunk]
            d_scores_t = d_scores_t + dm * fade
            pull = (dm * m).astype(BF)
            pulls.append(pull)
            read_sums.append(jnp.sum(pull.astype(F32), axis=0, keepdims=True))
            mix.append(m.astype(BF))
        dxd.append(nn(jnp.concatenate(mix, axis=1), dy_pair))
    source_sums = nn(jnp.concatenate(pulls, axis=1), ones_h[...])
    read_rows = jnp.concatenate(read_sums, axis=0)

    d_state = jnp.where(keep_next, dstate[...], 0.0)
    d_state_b = d_state.astype(BF)
    enter_b = sin[0]
    edy = ein_w * dy
    edyb = edy.astype(BF)
    readings = nn(cc, enter_b)
    from_state = nn(b, d_state_b) * eout_w
    d_xd = jnp.concatenate(dxd, axis=1) + from_state
    q1 = edy * readings
    q2 = xd * from_state
    decay = ein_w[chunk - 1 : chunk, :]
    dstate[...] = decay * d_state + tn(cc, edyb)
    d_cb = tn(d_scores_t.astype(BF), b) + nt(edyb, enter_b)
    d_b = nn(d_scores_t.astype(BF), cc) + nt((xd * eout_w).astype(BF), d_state_b)

    sums = (
        nn((d_xd * x).astype(BF), gather[0])
        + nn((q1 - q2).astype(BF), gather[1])
        + nn(q2.astype(BF), gather[2])
        - source_sums
    )
    sums_t = jnp.transpose(sums)
    dt_direct = sums_t[:heads]
    d_run = sums_t[heads : 2 * heads] + read_rows
    whole_q2 = jnp.sum(sums_t[2 * heads : 3 * heads], axis=1, keepdims=True)
    kept = jnp.sum(enter_b.astype(F32) * d_state, axis=0, keepdims=True) * decay
    kept_hi, kept_lo = split2(kept)
    kept_two = jnp.concatenate([kept_hi, kept_lo, jnp.zeros((6, inner), F32)], axis=0).astype(BF)
    kept_rows = nn(kept_two, gather[0])
    kept_cols = jnp.transpose(
        jnp.concatenate([kept_rows[0:1] + kept_rows[1:2], jnp.zeros((chunk - 1, chunk), F32)], axis=0)
    )
    d_last = whole_q2 + kept_cols[:heads, 0:1]
    hi, mid, low = split3(d_run)
    back = nt(jnp.concatenate([hi, mid, low], axis=0).astype(BF), upper[...])
    d_a = back[:heads] + back[heads : 2 * heads] + back[2 * heads :] + d_last
    d_dt = dt_direct + d_a * rate
    d_pre = d_dt * live * sigmoid(pre)
    acc_s[0:heads, :] += d_pre
    acc_s[heads : 2 * heads, :] += d_a * dt * rate

    def conv_back(d_u, du_ref, moved, tap_values, acc):
        du_ref[chunk : chunk + 8, :] = jnp.where(keep_next, du_ref[0:8, :], 0.0)
        du_ref[0:chunk, :] = d_u
        out = tap_values[taps_n - 1 : taps_n, :] * d_u
        acc[taps_n - 1 : taps_n, :] += jnp.sum(d_u * moved[0], axis=0, keepdims=True)
        for k in range(1, taps_n):
            row = taps_n - 1 - k
            out = out + tap_values[row : row + 1, :] * du_ref[pl.ds(k, chunk), :]
            acc[row : row + 1, :] += jnp.sum(d_u * moved[k], axis=0, keepdims=True)
        return out

    d_x = d_xd * dt_w + skip * dy
    lpx[...] = conv_back(d_x * dx_du, dux, moved_x, taps, acc_x).astype(BF)
    d_act = jnp.concatenate([d_b, d_cb], axis=1)
    lpbd[:, :bc] = conv_back(d_act * db_du, dub, moved_b, taps_b, acc_bc).astype(BF)
    pad = jnp.concatenate([d_pre, jnp.zeros((chunk - heads, chunk), F32)], axis=0)
    lpbd[:, bc:] = jnp.transpose(pad).astype(BF)

    @pl.when(i == blocks - 1)
    def _():
        acc[...] = jnp.zeros_like(acc)
        for k in range(taps_n):
            acc[1:2, k * bc : (k + 1) * bc] = acc_bc[k : k + 1, :]
        per = acc.shape[1] // inner
        for k in range(taps_n + 1):
            acc[2 + k // per : 3 + k // per, (k % per) * inner : (k % per + 1) * inner] = acc_x[k : k + 1, :]
        per_head = jnp.sum(
            jnp.transpose(jnp.concatenate([acc_s[...], jnp.zeros((chunk - 2 * heads, chunk), F32)], axis=0)),
            axis=0, keepdims=True,
        )
        three = jnp.concatenate(split3(acc_x[taps_n + 1 : taps_n + 2, :]) + (jnp.zeros((5, inner), F32),), axis=0)
        skips = jnp.sum(nn(three.astype(BF), gather[2]), axis=0, keepdims=True)
        acc[5:6, 0:chunk] = per_head + skips
        finish()


def scan_backward(
    dp_n, dy, px, pbd, sin, gain_grad, vec, gn, rows_out, tokens, y_send, g_own, heads, taps, bc
):
    count, inner = px.shape
    blocks = sin.shape[0]
    chunk = count // blocks
    whole = lambda a: pl.BlockSpec(a.shape, lambda i: (0,) * a.ndim)
    back = lambda w: pl.BlockSpec((chunk, w), lambda i: (blocks - 1 - i, 0))
    halo = lambda w: pl.BlockSpec((8, w), lambda i: (jnp.maximum((blocks - 1 - i) * (chunk // 8) - 1, 0), 0))
    width = pbd.shape[1]
    lines = dp_n // 2
    more = max(lines - 1, 1)
    block = rows_out.shape[0] // dp_n
    quarter = tokens.shape[1]
    units = 4
    span = count // units
    dma = pltpu.SemaphoreType.DMA
    vm, sds = pltpu.VMEM, jax.ShapeDtypeStruct
    return pl.pallas_call(
        functools.partial(scan_bwd_kernel, heads, taps, bc, dp_n),
        grid=(blocks,),
        in_specs=[
            back(inner), back(inner), halo(inner), back(width), halo(width),
            pl.BlockSpec((1, bc // 2, inner), lambda i: (blocks - 1 - i, 0, 0)), whole(gain_grad), whole(vec),
        ]
        + [pl.BlockSpec(memory_space=pl.ANY)] * 5,
        out_specs=[
            back(inner), back(width), pl.BlockSpec((8, vec.shape[1]), lambda i: (0, 0)),
            whole(tokens), pl.BlockSpec((block, inner), lambda i: (0, 0)), pl.BlockSpec((block, inner), lambda i: (0, 0)),
        ],
        scratch_shapes=[
            vm((bc // 2, inner), F32), vm((chunk + 8, inner), F32), vm((chunk + 8, bc), F32),
            vm((chunk + 8, inner), F32), vm((chunk + 8, bc), F32),
            vm((8, inner), F32), vm((8, bc), F32), vm((2 * heads, chunk), F32),
            vm((chunk, chunk), BF), vm((chunk, 3 * inner), BF), vm((3, inner, chunk), BF), vm((heads * chunk, chunk), BF),
            vm(gn.shape, BF), vm(rows_out.shape, BF), vm(tokens.shape, BF), vm(y_send.shape, BF), vm(g_own.shape, F32),
            dma((5,)),
            vm((units, 2, span, quarter), BF), vm((units, 2, span, quarter), BF),
            vm((units, span, quarter), BF), vm((units, span, quarter), BF),
            vm((2, span, quarter), F32), vm((units, span, quarter), F32),
            vm(y_send.shape, BF), vm(y_send.shape, BF), vm((4, more, block, inner // 2), BF), vm(y_send.shape, F32),
            dma((units,)), dma((units,)), dma((units,)), dma((units,)), dma((4,)), dma((4,)),
            dma((4, more)), dma((4, more)),
        ],
        out_shape=[
            sds((count, inner), BF), sds((count, width), BF),
            sds((8, vec.shape[1]), F32), sds(tokens.shape, BF), sds((block, inner), F32),
            sds((block, inner), F32),
        ],
        compiler_params=pltpu.CompilerParams(
            collective_id=3, has_side_effects=True, vmem_limit_bytes=58 * 2**20
        ),
        name="scan_backward",
    )(dy, px, px, pbd, pbd, sin, gain_grad, vec, gn, rows_out, tokens, y_send, g_own)
def peers(dp_n):
    dp, hm = lax.axis_index("dp"), lax.axis_index("heads")
    across, core = hm // 2, hm % 2
    pair, line, lines = dp % 2, dp // 2, dp_n // 2
    return dict(
        sib=(dp, 2 * across + 1 - core),
        xn=(dp, 2 * (1 - across) + core),
        dg=(dp, 2 * (1 - across) + 1 - core),
        yn=(2 * line + 1 - pair, hm),
        line=lambda k: (2 * ((line + k) % lines) + pair, hm),
        mine=hm,
        other=2 * (1 - across) + core,
        sib_mine=2 * across + 1 - core,
        sib_other=2 * (1 - across) + 1 - core,
        pair=pair, line_index=line, lines=lines, dp=dp, core=core,
    )


def meet(who):
    barrier = pltpu.get_barrier_semaphore()
    for name in ("sib", "xn", "dg", "yn"):
        pl.semaphore_signal(barrier, inc=1, device_id=who[name], device_id_type=MESH)

    def greet(k, carry):
        pl.semaphore_signal(barrier, inc=1, device_id=who["line"](k), device_id_type=MESH)
        return carry

    lax.fori_loop(1, who["lines"], greet, 0)
    pl.semaphore_wait(barrier, 4 + who["lines"] - 1)


def push(src, dst, send, recv, to):
    return pltpu.make_async_remote_copy(
        src_ref=src, dst_ref=dst, send_sem=send, recv_sem=recv, device_id=to, device_id_type=MESH
    )


def tail_kernel(
    dp_n, units,
    normed_t_in, lpx_in, rows_z_in, lpz_in, rows_x_in, lpbd_in, rows_bd_in, normed_in,
    tokens, acc, cot, q_wide, vec,
    grad_tokens, g_x, g_bc, small_out,
    sib_send, sib_recv, x_send, x_recv, part, held,
    y_send, y_recv, z_send, z_recv, g_own, yb_send, yb_recv, zb_send, zb_recv, gb_own, bh_send, bh_recv,
    bx_send, bx_recv, bs_recv, h_send, h_recv, sy_send, sy_recv, sz_send, sz_recv, dy_send, dy_recv, dz_send, dz_recv, row_sums,
    normed_t, lpx, rows_z, lpz, rows_x, lpbd, rows_bd, normed,
    s_in, s_sib, r_sib, s_x, r_x, s_y, r_y, s_z, r_z, s_m, r_m, s_sl, r_sl,
):
    loads = [
        pltpu.make_async_copy(src, dst, s_in.at[i])
        for i, (src, dst) in enumerate((
            (normed_t_in, normed_t), (lpx_in, lpx), (rows_z_in, rows_z), (lpz_in, lpz), (rows_x_in, rows_x),
            (lpbd_in, lpbd), (rows_bd_in, rows_bd), (normed_in, normed),
        ))
    ]
    for load in loads:
        load.start()
    who = peers(dp_n)
    meet(who)
    count = normed.shape[0]
    width = normed.shape[1]
    inner = lpx.shape[1]
    bc = 2 * bh_send.shape[1]
    quarter = width // 4
    span = count // units
    block = width // dp_n
    lines = who["lines"]

    def copy_sib(u):
        return push(sib_send.at[u], sib_recv.at[u], s_sib.at[u], r_sib.at[u], who["sib"])

    def copy_x(u):
        return push(x_send.at[u], x_recv.at[u], s_x.at[u], r_x.at[u], who["xn"])

    def product(u, q):
        cols = pl.ds(pl.multiple_of(q * quarter, quarter), quarter)
        at = slice(u * span, (u + 1) * span)
        return nt(lpx[at, :], rows_x[cols, :]) + nt(lpz[at, :], rows_z[cols, :]) + nt(lpbd[at, :], rows_bd[cols, :])

    def head_a(u):
        for k, q in enumerate(("sib_mine", "sib_other", "mine", "other")):
            p = product(u, who[q])
            at = slice(u * span, (u + 1) * span)
            cols = pl.ds(pl.multiple_of(who[q] * quarter, quarter), quarter)
            inner_p = p * normed[at, cols].astype(F32)
            h_send[0:1, cols] += jnp.sum(inner_p, axis=0, keepdims=True)
            first = u * span
            lanes = slice(first % width, first % width + span)
            h_send[2 + first // width : 3 + first // width, lanes] += nt(
                jnp.ones((8, quarter), BF), inner_p.astype(BF)
            )[0:1]
            if k < 2:
                sib_send[u, k] = p.astype(BF)
            else:
                part[u % 2, k - 2] = p
        copy_sib(u).start()

    def head_b(u):
        copy_sib(u).wait()
        x_send[u] = (part[u % 2, 1] + sib_recv[u, 1].astype(F32)).astype(BF)
        copy_x(u).start()
        held[u] = part[u % 2, 0] + sib_recv[u, 0].astype(F32)

    def head_c(u):
        copy_x(u).wait()
        total = held[u] + x_recv[u].astype(F32)
        first = u * span
        lanes = q_wide.shape[1]
        cols = pl.ds(pl.multiple_of(who["mine"] * quarter, quarter), quarter)
        for j in range(span // lanes):
            at = slice(first + j * lanes, first + (j + 1) * lanes)
            row, lane = (first + j * lanes) // width, (first + j * lanes) % width
            dots = jnp.transpose(jnp.broadcast_to(row_sums[row : row + 1, lane : lane + lanes], (lanes, lanes)))
            q = q_wide[at, :]
            coef = q * q * (dots / width)
            grad_tokens[at, :] = (
                cot[at, :].astype(F32)
                + q[:, 0:1] * vec[6:7, cols] * total[j * lanes : (j + 1) * lanes]
                - tokens[at, :].astype(F32) * coef[:, 0:1]
            )

    def rows_of(line, pair):
        return pl.ds(pl.multiple_of((2 * line + pair) * block, block), block)

    def grad_a(v):
        left, right = (normed_t, lpx)
        cols = slice((v % 2) * (inner // 2), (v % 2 + 1) * (inner // 2))
        for side in (0, 1):
            pair = (1 - who["pair"]) if side == 0 else who["pair"]
            stacked = jnp.concatenate([left[rows_of(l, pair), :] for l in range(lines)], axis=0)
            value = nn(stacked, right[:, cols])
            if side == 0:
                y_send[v] = value.astype(BF)
                copy_y(v).start()
            else:
                g_own[v] = value

    def copy_y(v):
        return push(y_send.at[v], y_recv.at[v], s_y.at[v], r_y.at[v], who["yn"])

    def copy_z(v, k):
        to = (who["line_index"] + k) % lines
        return push(
            z_send.at[v, pl.ds(pl.multiple_of(to * block, block), block)],
            z_recv.at[v, k - 1], s_z.at[v, k - 1], r_z.at[v, k - 1], who["line"](k),
        )

    def each_line(fn):
        def step(k, carry):
            fn(k)
            return carry

        lax.fori_loop(1, lines, step, 0)

    def own_rows():
        return pl.ds(pl.multiple_of(who["line_index"] * block, block), block)

    def grad_b(v):
        copy_y(v).wait()
        g_own[v] = g_own[v] + y_recv[v].astype(F32)
        z_send[v] = g_own[v].astype(BF)
        each_line(lambda k: copy_z(v, k).start())

    def grad_c(v):
        each_line(lambda k: copy_z(v, k).wait())
        total = g_own[v, own_rows(), :]
        for k in range(lines - 1):
            total = total + z_recv[v, k].astype(F32)
        cols = slice((v % 2) * (inner // 2), (v % 2 + 1) * (inner // 2))
        g_x[:, cols] = total

    half = bc // 2

    def copy_bh():
        return push(bh_send, bh_recv, s_m.at[0], r_m.at[0], who["sib"])

    def copy_yb():
        return push(yb_send, yb_recv, s_m.at[1], r_m.at[1], who["yn"])

    def copy_zb(k):
        to = (who["line_index"] + k) % lines
        return push(
            zb_send.at[pl.ds(pl.multiple_of(to * block, block), block)],
            zb_recv.at[k - 1], s_sl.at[0, k - 1], r_sl.at[0, k - 1], who["line"](k),
        )

    def copy_bx():
        return push(bx_send, bx_recv, s_m.at[2], r_m.at[2], who["xn"])

    def copy_bs():
        return push(bx_send, bs_recv, s_m.at[3], r_m.at[3], who["sib"])

    def bc_a():
        for side in (0, 1):
            pair = (1 - who["pair"]) if side == 0 else who["pair"]
            stacked = jnp.concatenate([normed_t[rows_of(l, pair), :] for l in range(lines)], axis=0)
            value = nn(stacked, lpbd[:, :bc])
            first = who["core"] == 0
            lo, hi = value[:, :half], value[:, half:]
            at = slice(side * lines * block, (side + 1) * lines * block)
            bh_send[at, :] = jnp.where(first, hi, lo).astype(BF)
            gb_own[at, :] = jnp.where(first, lo, hi)
        copy_bh().start()

    def bc_b():
        copy_bh().wait()
        rows = lines * block
        gb_own[...] = gb_own[...] + bh_recv[...].astype(F32)
        yb_send[...] = gb_own[:rows, :].astype(BF)
        copy_yb().start()

    def bc_c():
        rows = lines * block
        copy_yb().wait()
        gb_own[rows:, :] = gb_own[rows:, :] + yb_recv[...].astype(F32)
        zb_send[...] = gb_own[rows:, :].astype(BF)
        each_line(lambda k: copy_zb(k).start())

    def bc_d():
        each_line(lambda k: copy_zb(k).wait())
        at = pl.ds(pl.multiple_of(lines * block + who["line_index"] * block, block), block)
        total = gb_own[at, :]
        for k in range(lines - 1):
            total = total + zb_recv[k].astype(F32)
        bx_send[...] = total
        copy_bx().start()

    def bc_e():
        copy_bx().wait()
        bx_send[...] = bx_send[...] + bx_recv[...]
        copy_bs().start()

    def bc_f():
        copy_bs().wait()
        mine, theirs = bx_send[...], bs_recv[...]
        first = who["core"] == 0
        g_bc[:, :half] = jnp.where(first, mine, theirs)
        g_bc[:, half:] = jnp.where(first, theirs, mine)

    three = (("sib", 4), ("xn", 5), ("dg", 6))
    token_rows = count // width

    def copy_h(k):
        name, sem = three[k]
        return push(h_send, h_recv.at[k], s_m.at[sem], r_m.at[sem], who[name])

    def small_a():
        h_send[1:2, :] = acc[1:2, :]
        for k in range(3):
            copy_h(k).start()

    def copy_sy():
        return push(sy_send, sy_recv, s_m.at[7], r_m.at[7], who["yn"])

    def copy_dy():
        return push(dy_send, dy_recv, s_m.at[8], r_m.at[8], who["yn"])

    def copy_sz(k):
        return push(sz_send, sz_recv.at[k - 1], s_sl.at[1, k - 1], r_sl.at[1, k - 1], who["line"](k))

    def copy_dz(k):
        return push(dz_send, dz_recv.at[k - 1], s_sl.at[2, k - 1], r_sl.at[2, k - 1], who["line"](k))

    def dt_a():
        dy_send[...] = tn(lpbd[:, bc:], normed[...])[0:16, :].astype(BF)
        copy_dy().start()

    def dt_b():
        copy_dy().wait()
        dz_send[...] = (dy_send[...].astype(F32) + dy_recv[...].astype(F32)).astype(BF)
        each_line(lambda k: copy_dz(k).start())

    def dt_c():
        each_line(lambda k: copy_dz(k).wait())
        total = dz_send[...].astype(F32)
        for k in range(lines - 1):
            total = total + dz_recv[k].astype(F32)
        small_out[8:24, :] = total

    def small_b():
        for k in range(3):
            copy_h(k).wait()
        over_heads = h_send[...] + h_recv[0] + h_recv[1] + h_recv[2]
        row_sums[0:token_rows, :] = over_heads[2 : 2 + token_rows, :]
        sy_send[0:2, :] = over_heads[0:2, :]
        sy_send[2:8, :] = acc[2:8, :]
        copy_sy().start()

    def small_c():
        copy_sy().wait()
        sz_send[...] = sy_send[...] + sy_recv[...]
        each_line(lambda k: copy_sz(k).start())

    def small_d():
        each_line(lambda k: copy_sz(k).wait())
        total = sz_send[...]
        for k in range(lines - 1):
            total = total + sz_recv[k]
        small_out[0:8, :] = total

    h_send[...] = jnp.zeros_like(h_send)

    def seq(*steps):
        for fn, *args in steps:
            fn(*args)

    assert units == 4

    def load(*which):
        for i in which:
            loads[i].wait()

    load(0, 1)
    grad_a(0)
    load(2, 3, 4, 5, 6, 7)
    seq((head_a, 0), (bc_a,), (head_b, 0), (head_a, 1), (bc_b,), (grad_a, 1), (head_b, 1), (grad_b, 0), (head_a, 2))
    seq((dt_a,), (head_b, 2), (head_a, 3), (small_a,), (bc_c,), (head_b, 3), (grad_b, 1), (dt_b,), (small_b,))
    seq((bc_d,), (head_c, 0), (small_c,), (grad_c, 0), (dt_c,), (head_c, 1), (bc_e,), (small_d,), (bc_f,), (head_c, 2))
    seq((grad_c, 1), (head_c, 3))


def tail(dp_n, units, normed_t, normed, lpx, lpz, lpbd, rows_x, rows_z, rows_bd, tokens, acc, cot, q_wide, vec, bc):
    count, width = normed.shape
    inner = lpx.shape[1]
    quarter = width // 4
    span = count // units
    block = width // dp_n
    lines = dp_n // 2
    half_rows = lines * block
    more = max(lines - 1, 1)
    vm = pltpu.VMEM
    dma = pltpu.SemaphoreType.DMA
    operands = (
        normed_t, lpx, rows_z, lpz, rows_x, lpbd, rows_bd, normed, tokens, acc, cot, q_wide, vec,
    )
    sds = jax.ShapeDtypeStruct
    spec = pl.BlockSpec(memory_space=pltpu.VMEM)
    return pl.pallas_call(
        functools.partial(tail_kernel, dp_n, units),
        out_shape=[
            sds((count, quarter), F32), sds((block, inner), F32), sds((block, bc), F32),
            sds((24, width), F32),
        ],
        in_specs=[pl.BlockSpec(memory_space=pl.ANY)] * 8 + [spec] * 5,
        out_specs=[spec] * 4,
        scratch_shapes=[
            vm((units, 2, span, quarter), BF), vm((units, 2, span, quarter), BF),
            vm((units, span, quarter), BF), vm((units, span, quarter), BF),
            vm((2, 2, span, quarter), F32), vm((units, span, quarter), F32),
            vm((2, half_rows, inner // 2), BF), vm((2, half_rows, inner // 2), BF),
            vm((2, half_rows, inner // 2), BF), vm((2, more, block, inner // 2), BF),
            vm((2, half_rows, inner // 2), F32),
            vm((half_rows, bc // 2), BF), vm((half_rows, bc // 2), BF),
            vm((half_rows, bc // 2), BF), vm((more, block, bc // 2), BF),
            vm((2 * half_rows, bc // 2), F32),
            vm((2 * half_rows, bc // 2), BF), vm((2 * half_rows, bc // 2), BF),
            vm((block, bc // 2), F32), vm((block, bc // 2), F32), vm((block, bc // 2), F32),
            vm((8, width), F32), vm((3, 8, width), F32),
            vm((8, width), F32), vm((8, width), F32), vm((8, width), F32), vm((more, 8, width), F32),
            vm((16, width), BF), vm((16, width), BF), vm((16, width), BF), vm((more, 16, width), BF),
            vm((8, width), F32),
        ]
        + [vm(a.shape, a.dtype) for a in operands[:8]]
        + [
            dma((8,)), dma((units,)), dma((units,)), dma((units,)), dma((units,)),
            dma((2,)), dma((2,)), dma((2, more)), dma((2, more)), dma((9,)), dma((9,)),
            dma((3, more)), dma((3, more)),
        ],
        compiler_params=pltpu.CompilerParams(
            collective_id=1, has_side_effects=True, vmem_limit_bytes=62 * 2**20
        ),
        name="tail",
    )(*operands)
def chain(ref_in, block_of, width, send, recv, y_send, y_recv, who):
    rows = ref_in.shape[0]
    lines, line, pair = who["lines"], who["line_index"], who["pair"]
    own = ref_in.at[:, width] if ref_in.shape[1] != width.size else ref_in

    def at(index):
        return block_of.at[pl.ds(pl.multiple_of((2 * index + pair) * rows, rows), rows), width]

    def hand(sign, j):
        index = line - sign * j
        source = own if isinstance(j, int) and j == 0 else at(index)
        slot = j + 1 if sign > 0 else lines + j
        to = (2 * (line + sign) + pair, who["mine"])
        return push(source, at(index), send.at[slot], recv.at[slot], to)

    def to_pair(sign, j):
        slot = j if sign > 0 else lines - 1 + j
        index = line - sign * j
        source = own if isinstance(j, int) and j == 0 else at(index)
        return push(source, at(index), y_send.at[slot], y_recv.at[slot], who["yn"])

    def arrived(sign, j):
        slot = j if sign > 0 else lines - 1 + j
        block = at(line - sign * j)
        return push(block, block, send.at[slot], recv.at[slot], who["yn"])

    def inside(index):
        return jnp.logical_and(index >= 0, index < lines)

    def both(fn):
        for sign in (1, -1):
            fn(sign)

    def begin():
        def one(sign):
            @pl.when(inside(line + sign))
            def _():
                hand(sign, 0).start()

        both(one)

    def begin_pair():
        to_pair(1, 0).start()

    def hop(j):
        def one(sign):
            @pl.when(inside(line - sign * j))
            def _():
                arrived(sign, j).wait_recv()

                @pl.when(inside(line + sign))
                def _():
                    hand(sign, j).start()

                to_pair(sign, j).start()

        both(one)

    def end():
        to_pair(1, 0).wait()

        def one(sign):
            @pl.when(inside(line + sign))
            def _():
                hand(sign, 0).wait_send()

        both(one)

        def later(j):
            def one(sign):
                @pl.when(inside(line - sign * j))
                def _():
                    to_pair(sign, j).wait()

                    @pl.when(inside(line + sign))
                    def _():
                        hand(sign, j).wait_send()

            both(one)

        loop_line(lines, later)

    return begin, begin_pair, hop, end


def loop_line(lines, fn):
    def step(k, carry):
        fn(k)
        return carry

    lax.fori_loop(1, lines, step, 0)


def front_kernel(
    dp_n, heads, units, taps, bc,
    tokens, cot, w_x, w_bc, w_z, w_out, w_dt, conv_x, conv_bc, norm_gain, gate_gain, dt_bias, a_log, skip, starts, fill,
    vec, px_out, pbd_out, normed_out, normed_t_out, q_out, y_out, sin_out, parts, rows_x, rows_bd, rows_z, rows_out,
    own_dt, tok, wx, wbd, px, pbd, normed, normed_t, q, y, sin, own_w, own_cot, state, extx, extb, upper, spread,
    s_loc, s_sib, r_sib, s_x, r_x, s_f, r_f, s_cx, r_cx, s_cf, r_cf, s_w, r_w, s_wy, r_wy, s_c, r_c, s_cy, r_cy, s_out, s_y,
):
    who = peers(dp_n)
    count, quarter = tokens.shape
    width = 4 * quarter
    span = count // units
    lines = who["lines"]
    block, inner = w_x.shape
    blocks = sin.shape[0]
    chunk = count // blocks
    per = blocks // units
    pieces = s_cx.shape[0]
    cot_span = count // pieces
    here = pl.ds(pl.multiple_of(who["dp"] * block, block), block)
    own_half = pl.ds(pl.multiple_of(who["core"] * (bc // 2), bc // 2), bc // 2)
    dt_cols = pl.ds(bc, chunk)
    local = [
        pltpu.make_async_copy(src, dst, s_loc.at[k])
        for k, (src, dst) in enumerate((
            (tokens, tok.at[who["mine"]]), (w_x, wx.at[here]), (w_bc.at[:, own_half], wbd.at[here, own_half]),
            (w_z, own_w.at[0]), (w_out, own_w.at[1]), (cot, own_cot),
        ))
    ]
    for copy in local:
        copy.start()
    own_dt[...] = jnp.zeros_like(own_dt)
    own_dt[:, :heads] = w_dt[...]
    wbd[here, dt_cols] = own_dt[...]
    onto = [
        pltpu.make_async_copy(src, dst, s_loc.at[8 + k])
        for k, (src, dst) in enumerate((
            (own_w.at[0], rows_z.at[here]), (own_w.at[1], rows_out.at[here]), (own_cot, parts.at[who["mine"]]),
        ))
    ]
    meet(who)

    def rows(s, n=span):
        return pl.ds(pl.multiple_of(s * n, n), n)

    def to_x(s):
        return push(tokens.at[rows(s)], tok.at[who["mine"], rows(s)], s_x.at[s], r_x.at[s], who["xn"])

    def to_sib():
        return push(tokens, tok.at[who["mine"]], s_sib.at[0], r_sib.at[0], who["sib"])

    def forward(s):
        at = tok.at[who["other"], rows(s)]
        return push(at, at, s_f.at[s], r_f.at[s], who["sib"])

    def cot_x(j):
        at = rows(j, cot_span)
        return push(cot.at[at], parts.at[who["mine"], at], s_cx.at[j], r_cx.at[j], who["xn"])

    def cot_sib():
        return push(cot, parts.at[who["mine"]], s_sib.at[1], r_sib.at[1], who["sib"])

    def cot_forward(j):
        at = parts.at[who["other"], rows(j, cot_span)]
        return push(at, at, s_cf.at[j], r_cf.at[j], who["sib"])

    half = inner // 2
    cuts = [
        chain(ref, to, cols, s_w.at[n], r_w.at[n], s_wy.at[n], r_wy.at[n], who)
        for n, (ref, to, cols) in enumerate((
            (w_x, wx, pl.ds(0, half)), (w_x, wx, pl.ds(half, half)), (w_bc, wbd, own_half), (own_dt, wbd, dt_cols),
        ))
    ]
    chains = [
        chain(ref, to, pl.ds(h * half, half), s_c.at[2 * n + h], r_c.at[2 * n + h], s_cy.at[2 * n + h], r_cy.at[2 * n + h], who)
        for n, (ref, to) in enumerate(((w_z, rows_z), (w_out, rows_out)))
        for h in (0, 1)
    ]

    def other_half():
        cols = wbd.at[:, own_half]
        return push(cols, cols, s_sib.at[2], r_sib.at[2], who["sib"])

    def have(n):
        cuts[n][3]()

    def pass_cot(j):
        cot_x(j).wait()
        cot_forward(j).start()

    to_x(0).start()
    for begin, begin_pair, hop, end in cuts:
        begin()
        begin_pair()
    for s in range(1, units):
        to_x(s).start()
    to_sib().start()
    for j in range(pieces):
        cot_x(j).start()
    pack_vec(vec, conv_x, conv_bc, norm_gain, gate_gain, dt_bias, a_log, skip, starts, fill, chunk)
    set_upper(upper)
    set_spread(spread, heads)
    state[...] = jnp.zeros_like(state)
    extx[...] = jnp.zeros_like(extx)
    extb[...] = jnp.zeros_like(extb)
    par = read_vec(vec, heads, chunk, inner, bc, taps)
    gain = vec[6:7, :width]

    def out_copies(s):
        at = rows(s)
        every = slice(None)
        return [
            pltpu.make_async_copy(ref.at[to], out.at[to], s_out.at[n, s])
            for n, (ref, out, to) in enumerate((
                (normed, normed_out, (at,)), (normed_t, normed_t_out, (every, at)), (q, q_out, (at,)),
                (px, px_out, (at,)), (pbd, pbd_out, (at,)),
            ))
        ]

    def norm(s):
        at = rows(s)
        values = [tok[h, at, :].astype(F32) for h in range(4)]
        total = sum(jnp.sum(p * p, axis=1, keepdims=True) for p in values)
        inv = lax.rsqrt(total / width + EPS)
        q[at, :] = jnp.broadcast_to(inv, (span, q.shape[1]))
        for h in range(4):
            cols = slice(h * quarter, (h + 1) * quarter)
            value = (values[h] * inv * gain[:, cols]).astype(BF)
            normed[at, cols] = value
            normed_t[cols, at] = jnp.transpose(value)
        for copy in out_copies(s)[:3]:
            copy.start()

    def project(s):
        at = rows(s)
        pbd[at, :] = nn(normed[at, :], wbd[...])
        px[at, :] = nn(normed[at, :], wx[...])
        for copy in out_copies(s)[3:]:
            copy.start()

    def hops(group, j):
        if j < lines:
            for begin, begin_pair, hop, end in group:
                hop(j)

    local[0].wait()
    hops(cuts, 1)
    to_x(0).wait()
    forward(0).start()
    hops(cuts, 2)
    for begin, begin_pair, hop, end in chains:
        begin()
    to_sib().wait()
    forward(0).wait()
    norm(0)
    to_x(1).wait()
    forward(1).start()
    hops(cuts, 3)
    if lines > 4:
        for begin, begin_pair, hop, end in cuts:
            lax.fori_loop(4, lines, lambda j, a, fn=hop: (fn(j), a)[1], 0)
    for begin, begin_pair, hop, end in chains:
        begin_pair()
    forward(1).wait()
    norm(1)
    have(2)
    local[2].wait()
    other_half().start()
    to_x(2).wait()
    forward(2).start()
    for copy in local[3:]:
        copy.wait()
    for copy in onto:
        copy.start()
    cot_sib().start()
    forward(2).wait()
    norm(2)
    local[1].wait()
    for n in (0, 1, 3):
        have(n)
    other_half().wait()
    hops(chains, 1)
    keep_rows = [
        pltpu.make_async_copy(wx, rows_x, s_loc.at[6]), pltpu.make_async_copy(wbd, rows_bd, s_loc.at[7]),
    ]
    for copy in keep_rows:
        copy.start()

    def last_tokens(s):
        to_x(s).wait()
        forward(s).start()

    def last_norm(s):
        forward(s).wait()
        norm(s)

    events = {1: [(last_tokens, units - 1)], 2: [(last_norm, units - 1)]}
    late = []
    plan = []
    for n, (begin, begin_pair, hop, end) in enumerate(chains):
        if lines > 2:
            plan.append((hop, 2, 1 + n // 2))
        if lines > 3:
            plan.append((hop, 3, 3 + n))
        if lines > 4:
            plan.append((lambda k, fn=hop: lax.fori_loop(4, lines, lambda j, a: (fn(j), a)[1], 0), 0, 7 + n))
    plan += [(pass_cot, j, 5 + 2 * j) for j in range(pieces)]
    for fn, k, at in plan:
        if at < blocks:
            events.setdefault(at, []).append((fn, k))
        else:
            late.append((fn, k))

    def y_copies(c):
        at = rows(c, chunk)
        return (
            pltpu.make_async_copy(y.at[at], y_out.at[at], s_y.at[0, c]),
            pltpu.make_async_copy(sin.at[c], sin_out.at[c], s_y.at[1, c]),
        )

    def step(c, carry):
        for at, fns in events.items():

            @pl.when(c == at)
            def _(fns=fns):
                for fn, k in fns:
                    fn(k)

        @pl.when(c % per == 0)
        def _():
            project(c // per)

        at = rows(c, chunk)
        y_c, enter = scan_step(
            heads, par, read_block(vec, c, chunk), px.at[at], pbd.at[at], upper, spread, state, extx, extb
        )
        y[at, :] = y_c
        sin[c] = enter
        for copy in y_copies(c):
            copy.start()
        return carry

    lax.fori_loop(0, blocks, step, 0)
    for fn, k in late:
        fn(k)

    def end_y(c, carry):
        for copy in y_copies(c):
            copy.wait()
        return carry

    lax.fori_loop(0, blocks, end_y, 0)
    for s in range(units):
        for copy in out_copies(s):
            copy.wait()
    for copy in onto + keep_rows:
        copy.wait()
    cot_sib().wait()
    for j in range(pieces):
        cot_forward(j).wait()
    for begin, begin_pair, hop, end in chains:
        end()


def front(dp_n, tokens, cot, w_x, w_bc, w_z, w_out, w_dt, conv_x, conv_bc, norm_gain, gate_gain, *scalars):
    count, quarter = tokens.shape
    width = 4 * quarter
    inner, heads = w_x.shape[1], w_dt.shape[1]
    taps, bc = conv_bc.shape
    blocks = scalars[-1].shape[0]
    chunk = count // blocks
    wide = bc + chunk
    units, pieces = 4, 8
    vm, dma, sds = pltpu.VMEM, pltpu.SemaphoreType.DMA, jax.ShapeDtypeStruct
    hbm, vmem = pl.BlockSpec(memory_space=pl.ANY), pl.BlockSpec(memory_space=pltpu.VMEM)
    ways = dp_n - 1
    outs = [
        sds((24 + blocks, width), F32),
        sds((count, inner), F32), sds((count, wide), F32), sds((count, width), BF), sds((width, count), BF),
        sds((count, 128), F32), sds((count, inner), F32), sds((blocks, bc // 2, inner), BF),
        sds((4, count, quarter), BF), sds((width, inner), BF), sds((width, wide), BF), sds((width, inner), BF),
        sds((width, inner), BF),
    ]
    return pl.pallas_call(
        functools.partial(front_kernel, dp_n, heads, units, taps, bc),
        out_shape=outs,
        in_specs=[hbm] * 6 + [vmem] * 5 + [pl.BlockSpec(memory_space=pltpu.SMEM)] * 5,
        out_specs=[vmem] + [hbm] * (len(outs) - 1),
        scratch_shapes=[
            vm((w_x.shape[0], chunk), BF),
            vm((4, count, quarter), BF), vm((width, inner), BF), vm((width, wide), BF),
            vm((count, inner), F32), vm((count, wide), F32), vm((count, width), BF), vm((width, count), BF),
            vm((count, 128), F32), vm((count, inner), F32), vm((blocks, bc // 2, inner), BF),
            vm((2,) + w_z.shape, BF), vm(cot.shape, BF),
            vm((bc // 2, inner), F32), vm((chunk + 8, inner), F32), vm((chunk + 8, bc), F32),
            vm((chunk, chunk), BF), vm((chunk, 3 * inner), BF),
            dma((11,)), dma((3,)), dma((3,)), dma((units,)), dma((units,)), dma((units,)), dma((units,)),
            dma((pieces,)), dma((pieces,)), dma((pieces,)), dma((pieces,)),
            dma((4, ways + 1)), dma((4, ways + 1)), dma((4, ways)), dma((4, ways)), dma((4, ways + 1)), dma((4, ways + 1)), dma((4, ways)), dma((4, ways)),
            dma((5, units)), dma((2, blocks)),
        ],
        compiler_params=pltpu.CompilerParams(
            collective_id=2, has_side_effects=True, vmem_limit_bytes=58 * 2**20
        ),
        name="front",
    )(
        tokens, cot, w_x, w_bc, w_z, w_out, w_dt, conv_x, conv_bc, norm_gain[None, :], gate_gain[None, :], *scalars
    )
def finish_kernel(heads, taps, bc, bo, gt, gx, gz, go, gb, small, own, o_bo, o_gt, o_gx, o_gz, o_go, o_gb, o_gain, o_cx, o_cb, o_bias, o_alog, o_skip, o_gate):
    o_bo[...] = bo[...]
    o_gt[...] = gt[...]

    @pl.when(pl.program_id(0) == 0)
    def _():
        for src, dst in ((gx, o_gx), (gz, o_gz), (go, o_go), (gb, o_gb)):
            dst[...] = src[...]
        inner = o_cx.shape[1]
        per = small.shape[1] // inner
        for k in range(taps):
            o_cx[k : k + 1, :] = small[2 + k // per : 3 + k // per, (k % per) * inner : (k % per + 1) * inner]
            o_cb[k : k + 1, :] = small[1:2, k * bc : (k + 1) * bc]
        scalars = small[5:6, :128]
        o_bias[...] = scalars[0, :heads]
        o_alog[...] = scalars[0, heads : 2 * heads]
        o_skip[...] = scalars[0, 2 * heads : 3 * heads]
        o_gate[...] = small[4, :inner]
        columns = o_gain.shape[0]
        at = pl.ds(pl.multiple_of(lax.axis_index("heads") * columns, columns), columns)
        o_gain[...] = (small[0:1, at] / own[:, at])[0]


def finish(bo, gt, gx, gz, go, gb, small, norm_gain, heads, taps, bc):
    steps = 4
    sds = jax.ShapeDtypeStruct
    count, quarter = bo.shape
    inner = gx.shape[1]
    rows = pl.BlockSpec((count // steps, quarter), lambda i: (i, 0))
    whole = lambda shape: pl.BlockSpec(shape, lambda i: (0,) * len(shape))
    smalls = [(quarter,), (taps, inner), (taps, bc), (heads,), (heads,), (heads,), (inner,)]
    operands = (bo, gt, gx, gz, go, gb, small, norm_gain[None, :])
    return pl.pallas_call(
        functools.partial(finish_kernel, heads, taps, bc),
        grid=(steps,),
        in_specs=[rows, rows] + [whole(a.shape) for a in operands[2:]],
        out_specs=[rows, rows] + [whole(a.shape) for a in operands[2:6]] + [whole(s) for s in smalls],
        out_shape=[sds(a.shape, a.dtype) for a in operands[:6]] + [sds(s, F32) for s in smalls],
        name="finish",
    )(*operands)


def body(
    tokens, cotangent, starts, fill, norm_gain, w_x, w_z, w_dt, w_bc, conv_x, conv_bc, dt_bias, a_log, skip,
    gate_gain, w_out,
):
    heads_n = lax.axis_size("heads")
    dp_n = lax.axis_size("dp")
    dp_index = lax.axis_index("dp")
    count, columns = tokens.shape
    width = columns * heads_n
    blocks = starts.shape[0]
    chunk = count // blocks
    inner = w_x.shape[1]
    heads = w_dt.shape[1]
    taps, bc = conv_bc.shape
    vec, px, pbd, normed, normed_t, q_wide, y, sin, parts, rows_x, rows_bd, rows_z, rows_out = front(
        dp_n, tokens, cotangent, w_x, w_bc, w_z, w_out, w_dt, conv_x, conv_bc, norm_gain, gate_gain, dt_bias, a_log,
        skip, starts, fill,
    )
    dy, lpz, gn, y_send, g_own, gain_grad = gate(dp_n, blocks, normed, normed_t, rows_z, rows_out, parts, y, vec)
    lpx, lpbd, acc, block_out, grad_w_out, grad_w_z = scan_backward(
        dp_n, dy, px, pbd, sin, gain_grad, vec, gn, rows_out, tokens, y_send, g_own, heads, taps, bc
    )
    grad_tokens, grad_w_x, grad_w_bc, small = tail(
        dp_n, 4, normed_t, normed, lpx, lpz, lpbd, rows_x, rows_z, rows_bd, tokens, acc, cotangent, q_wide, vec, bc,
    )
    block = width // dp_n
    grad_w_dt = lax.dynamic_slice_in_dim(small[8 : 8 + heads], dp_index * block, block, 1).T
    (
        block_out, grad_tokens, grad_w_x, grad_w_z, grad_w_out, grad_w_bc, grad_norm_gain, grad_conv_x, grad_conv_bc,
        grad_dt_bias, grad_a_log, grad_skip, grad_gate_gain,
    ) = finish(
        block_out, grad_tokens, grad_w_x, grad_w_z, grad_w_out, grad_w_bc, small, norm_gain, heads, taps, bc
    )
    return (
        block_out, grad_tokens, grad_norm_gain, grad_w_x, grad_w_z, grad_w_dt, grad_w_bc, grad_conv_x, grad_conv_bc,
        grad_dt_bias, grad_a_log, grad_skip, grad_gate_gain, grad_w_out,
    )


def solution(mesh):
    placed = (
        P("dp", "heads"),
        P("dp", "heads"),
        P("dp"),
        P("dp"),
        P(),
        P("dp", "heads"),
        P("dp", "heads"),
        P("dp", "heads"),
        P("dp", None),
        P(None, "heads"),
        P(),
        P("heads"),
        P("heads"),
        P("heads"),
        P("heads"),
        P("dp", "heads"),
    )
    return jax.shard_map(
        body,
        mesh=mesh,
        in_specs=placed,
        out_specs=(
            P("dp", "heads"),
            P("dp", "heads"),
            P("heads"),
            P("dp", "heads"),
            P("dp", "heads"),
            P("dp", "heads"),
            P("dp", None),
            P(None, "heads"),
            P(),
            P("heads"),
            P("heads"),
            P("heads"),
            P("heads"),
            P("dp", "heads"),
        ),
        check_vma=False,
    )
```

```python
import functools
import jax
import jax.numpy as jnp
from jax import lax
from jax.experimental import pallas as pl
from jax.experimental.pallas import tpu as pltpu
from jax.sharding import PartitionSpec as P

HD = 64
EPS = 1e-05
F32 = jnp.float32
BF = jnp.bfloat16
NEG = -1e30
MESH = pl.DeviceIdType.MESH


def nn(a, b):
    return lax.dot_general(a, b, (((1,), (0,)), ((), ())), preferred_element_type=F32)


def nt(a, b):
    return lax.dot_general(a, b, (((1,), (1,)), ((), ())), preferred_element_type=F32)


def tn(a, b):
    return lax.dot_general(a, b, (((0,), (0,)), ((), ())), preferred_element_type=F32)


def split2(v):
    hi = v.astype(BF).astype(F32)
    return hi, v - hi


def split3(v):
    hi = v.astype(BF).astype(F32)
    rest = v - hi
    mid = rest.astype(BF).astype(F32)
    return hi, mid, rest - mid


def softplus(v):
    return jnp.maximum(v, 0.0) + jnp.log1p(jnp.exp(-jnp.abs(v)))


def sigmoid(v):
    return 1.0 / (1.0 + jnp.exp(-v))


def iota2(rows, cols, axis):
    return lax.broadcasted_iota(jnp.int32, (rows, cols), axis)


def zero_one(cond):
    return jnp.where(cond, 1.0, 0.0).astype(BF)


def set_upper(upper):
    upper[...] = zero_one(iota2(*upper.shape, 0) <= iota2(*upper.shape, 1))


def set_spread(spread, heads):
    rows, lanes = iota2(*spread.shape, 0), iota2(*spread.shape, 1)
    inner = heads * HD
    base = heads * (1 + 2 * (lanes // inner)) + (lanes % inner) // HD
    spread[...] = zero_one(jnp.logical_or(rows == base, rows == base + heads))


def set_gather(gather, ones_h, heads):
    for q in range(3):
        rows, lanes = iota2(*gather.shape[1:], 0), iota2(*gather.shape[1:], 1)
        gather[q] = zero_one(lanes == q * heads + rows // HD)
    rows, lanes = iota2(*ones_h.shape, 0), iota2(*ones_h.shape, 1)
    ones_h[...] = zero_one(lanes == heads + rows // ones_h.shape[1])


def conv_from(ext, taps, rows, halo):
    n = taps.shape[0]
    moved = [ext[pl.ds(halo - k, rows), :] for k in range(n)]
    out = taps[n - 1 : n, :] * moved[0]
    for k in range(1, n):
        out = out + taps[n - 1 - k : n - k, :] * moved[k]
    return out, moved


def dt_rows(pdt, bias, rate, fill, heads, upper):
    chunk = pdt.shape[0]
    pre = jnp.transpose(pdt)[:heads] + bias
    live = (iota2(heads, chunk, 1).astype(F32) < fill).astype(F32)
    dt = softplus(pre) * live
    hi, mid, low = split3(dt * rate)
    stacked = jnp.concatenate([hi, mid, low], axis=0).astype(BF)
    summed = nn(stacked, upper)
    run = summed[:heads] + summed[heads : 2 * heads] + summed[2 * heads :]
    return pre, live, dt, run


def spread_all(run, dt, heads, chunk, spread):
    last = run[:, chunk - 1 : chunk]
    e_in = jnp.exp(run)
    e_out = jnp.exp(last - run)
    parts = [run]
    for v in (dt, e_in, e_out):
        parts.extend(split2(v))
    used = heads * len(parts)
    if used < chunk:
        parts.append(jnp.zeros((chunk - used, chunk), F32))
    cols = jnp.transpose(jnp.concatenate(parts, axis=0))
    return cols, nn(cols.astype(BF), spread)


def pair_stack(v, low_lanes):
    zero = jnp.zeros_like(v)
    return jnp.concatenate([jnp.where(low_lanes, v, zero), jnp.where(low_lanes, zero, v)], axis=0)


def read_vec(vec, heads, chunk, inner, bc, taps):
    return dict(
        convx=vec[0:taps, :inner], skip=vec[4:5, :inner], gain=vec[5:6, :inner],
        bias=vec[8 : 8 + heads, :chunk], rate=vec[8 : 8 + heads, chunk : 2 * chunk], convbc=vec[16 : 16 + taps, :bc],
    )


def read_block(vec, c, chunk):
    row = vec[pl.ds(24 + c, 1), :]
    return row[:, 0:1] > 0.5, row[:, chunk : chunk + 1], row[:, 2 * chunk : 2 * chunk + 1] > 0.5


def pack_vec(vec, conv_x, conv_bc, norm_gain, gate_gain, dt_bias, a_log, skip, starts, fill, chunk):
    taps, inner = conv_x.shape
    vec[...] = jnp.zeros_like(vec)
    vec[0:taps, :inner] = conv_x[...]
    vec[16 : 16 + taps, : conv_bc.shape[1]] = conv_bc[...]
    vec[5:6, :inner] = gate_gain[...]
    vec[6:7, :] = norm_gain[...]
    head = iota2(1, inner, 1) // HD
    skips = jnp.zeros((1, inner), F32)
    for h in range(dt_bias.shape[0]):
        skips = jnp.where(head == h, skip[h], skips)
        vec[8 + h : 9 + h, 0:chunk] = jnp.full((1, chunk), dt_bias[h], F32)
        vec[8 + h : 9 + h, chunk : 2 * chunk] = -jnp.exp(jnp.full((1, chunk), a_log[h], F32))
    vec[4:5, :inner] = skips
    blocks = starts.shape[0]
    for c in range(blocks):
        row = slice(24 + c, 25 + c)
        vec[row, 0:chunk] = jnp.full((1, chunk), 1 - starts[c], jnp.int32).astype(F32)
        vec[row, chunk : 2 * chunk] = jnp.full((1, chunk), fill[c], jnp.int32).astype(F32)
        if c + 1 < blocks:
            vec[row, 2 * chunk : 3 * chunk] = jnp.full((1, chunk), 1 - starts[c + 1], jnp.int32).astype(F32)


def scan_step(heads, par, block, px, pbd, upper, spread, state, extx, extb):
    chunk, inner = px.shape
    bc = par["convbc"].shape[1]
    ns = bc // 2
    keep, n_live, _ = block
    state[...] = jnp.where(keep, state[...], 0.0)
    extx[0:8, :] = jnp.where(keep, extx[chunk : chunk + 8, :], 0.0)
    extb[0:8, :] = jnp.where(keep, extb[chunk : chunk + 8, :], 0.0)
    extx[8 : chunk + 8, :] = px[...]
    extb[8 : chunk + 8, :] = pbd[:, :bc]

    u, _ = conv_from(extx, par["convx"], chunk, 8)
    x = u * sigmoid(u) * (iota2(chunk, inner, 0).astype(F32) < n_live).astype(F32)
    ub, _ = conv_from(extb, par["convbc"], chunk, 8)
    act = (ub * sigmoid(ub) * (iota2(chunk, bc, 0).astype(F32) < n_live).astype(F32)).astype(BF)
    b, cc = act[:, :ns], act[:, ns:]

    _, _, dt, run = dt_rows(pbd[:, bc:], par["bias"], par["rate"], n_live, heads, upper[...])
    cols, wide = spread_all(run, dt, heads, chunk, spread[...])
    dt_w, ein_w, eout_w = wide[:, :inner], wide[:, inner : 2 * inner], wide[:, 2 * inner :]

    xd = x * dt_w
    xdb = xd.astype(BF)
    scores = nt(cc, b)
    tri = iota2(chunk, chunk, 0) >= iota2(chunk, chunk, 1)
    low_lanes = iota2(chunk, 2 * HD, 1) < HD
    diag = []
    for j in range(heads // 2):
        mix = []
        for h in (2 * j, 2 * j + 1):
            spread_h = cols[:, h : h + 1] - run[h : h + 1, :]
            mix.append((scores * jnp.exp(jnp.where(tri, spread_h, NEG))).astype(BF))
        pair = pair_stack(xdb[:, 2 * HD * j : 2 * HD * (j + 1)], low_lanes)
        diag.append(nn(jnp.concatenate(mix, axis=1), pair))
    enter = state[...]
    enter_b = enter.astype(BF)
    y = jnp.concatenate(diag, axis=1) + ein_w * nn(cc, enter_b) + par["skip"] * x
    state[...] = ein_w[chunk - 1 : chunk, :] * enter + tn(b, (xd * eout_w).astype(BF))
    return y, enter_b


def pair_rows(dp_n, block, pair, values):
    return jnp.concatenate(
        [values[pl.ds(pl.multiple_of((2 * l + pair) * block, block), block), :] for l in range(dp_n // 2)], axis=0
    )


def gate_kernel(
    dp_n, normed, rows_z, rows_out, parts, y, vec, normed_t_in, dy_out, lpz, gn, y_send, g_own, gain_grad,
    h_send, h_recv, z_all, g_all, y_all, grad_t, normed_t, s_h, r_h, s_in,
):
    i = pl.program_id(0)
    who = peers(dp_n)
    names = ("sib", "xn", "dg")
    barrier = pltpu.get_barrier_semaphore()
    span, quarter = parts.shape[1:]
    blocks, chunk = h_send.shape[1:]
    inner = y.shape[1]
    here = pl.ds(pl.multiple_of(i * span, span), span)
    load = pltpu.make_async_copy(normed_t_in, normed_t, s_in.at[0])

    @pl.when(i == 0)
    def _():
        load.start()
        for name in names:
            pl.semaphore_signal(barrier, inc=1, device_id=who[name], device_id_type=MESH)

    z = nn(normed[...], rows_z[...])
    z_all[here, :] = z
    y_all[here, :] = y[...]
    g = nn(parts[0], rows_out[0:quarter, :])
    for k in range(1, 4):
        g = g + nn(parts[k], rows_out[k * quarter : (k + 1) * quarter, :])
    g_all[here, :] = g
    for k in range(4):
        grad_t[k * quarter : (k + 1) * quarter, here] = jnp.transpose(parts[k])
    gated = y[...] * (z * sigmoid(z))
    ones = jnp.ones((8, inner), BF)
    for k, value in enumerate((gated * gated, gated * vec[5:6, :inner] * g)):
        row = nt(ones, value.astype(BF))
        for j in range(span // chunk):
            h_send[k, pl.ds(i * (span // chunk) + j, 1), :] = row[0:1, j * chunk : (j + 1) * chunk]

    @pl.when(i == pl.num_programs(0) - 1)
    def _():
        pl.semaphore_wait(barrier, 3)
        copies = [push(h_send, h_recv.at[k], s_h.at[k], r_h.at[k], who[name]) for k, name in enumerate(names)]
        for copy in copies:
            copy.start()
        for copy in copies:
            copy.wait()
        sums = h_send[...] + h_recv[0] + h_recv[1] + h_recv[2]
        gain = vec[5:6, :inner]
        below = jnp.zeros((chunk - blocks, chunk), F32)
        inv = lax.rsqrt(jnp.transpose(jnp.concatenate([sums[0], below], axis=0)) / (4 * inner) + EPS)
        dots = jnp.transpose(jnp.concatenate([sums[1], below], axis=0))
        coef = inv * inv * inv * (dots / (4 * inner))
        gain_grad[...] = jnp.zeros_like(gain_grad)
        for b in range(blocks):
            at = slice(b * chunk, (b + 1) * chunk)
            zb, yb, gb = z_all[at, :], y_all[at, :], g_all[at, :]
            sz = sigmoid(zb)
            silu_z = zb * sz
            gated_b = yb * silu_z
            inv_b = inv[:, b : b + 1]
            scaled = gated_b * inv_b
            gn[at, :] = (scaled * gain).astype(BF)
            gain_grad[0:1, :] += jnp.sum(gb * scaled, axis=0, keepdims=True)
            d_gated = inv_b * (gb * gain) - gated_b * coef[:, b : b + 1]
            lpz[at, :] = (d_gated * yb * (sz * (1.0 + zb * (1.0 - sz)))).astype(BF)
            dy_out[at, :] = d_gated * silu_z
        load.wait()
        block = grad_t.shape[0] // dp_n
        for v, (left, right) in enumerate(((grad_t, gn), (normed_t, lpz))):
            theirs = nn(pair_rows(dp_n, block, 1 - who["pair"], left), right[...])
            ours = nn(pair_rows(dp_n, block, who["pair"], left), right[...])
            for h in (0, 1):
                cols = slice(h * (inner // 2), (h + 1) * (inner // 2))
                y_send[2 * v + h] = theirs[:, cols].astype(BF)
                g_own[2 * v + h] = ours[:, cols]


def gate(dp_n, blocks, normed, normed_t, rows_z, rows_out, parts, y, vec):
    count, width = normed.shape
    inner = y.shape[1]
    chunk = count // blocks
    steps = 4
    span = count // steps
    quarter = width // 4
    sds = jax.ShapeDtypeStruct
    rows = lambda w: pl.BlockSpec((span, w), lambda i: (i, 0))
    whole = lambda shape: pl.BlockSpec(shape, lambda i: (0,) * len(shape))
    halves = (4, width // 2, inner // 2)
    return pl.pallas_call(
        functools.partial(gate_kernel, dp_n),
        grid=(steps,),
        in_specs=[
            rows(width), whole(rows_z.shape), whole(rows_out.shape),
            pl.BlockSpec((4, span, quarter), lambda i: (0, i, 0)), rows(inner), whole(vec.shape),
            pl.BlockSpec(memory_space=pl.ANY),
        ],
        out_specs=[whole((count, inner))] * 3 + [whole(halves), whole(halves), whole((8, inner))],
        out_shape=[
            sds((count, inner), F32), sds((count, inner), BF), sds((count, inner), BF), sds(halves, BF),
            sds(halves, F32), sds((8, inner), F32),
        ],
        scratch_shapes=[
            pltpu.VMEM((2, blocks, chunk), F32), pltpu.VMEM((3, 2, blocks, chunk), F32),
            pltpu.VMEM((count, inner), F32), pltpu.VMEM((count, inner), F32), pltpu.VMEM((count, inner), F32),
            pltpu.VMEM((width, count), BF), pltpu.VMEM((width, count), BF),
            pltpu.SemaphoreType.DMA((3,)), pltpu.SemaphoreType.DMA((3,)), pltpu.SemaphoreType.DMA((1,)),
        ],
        compiler_params=pltpu.CompilerParams(
            collective_id=4, has_side_effects=True, vmem_limit_bytes=58 * 2**20
        ),
        name="gate",
    )(normed, rows_z, rows_out, parts, y, vec, normed_t)


def sums_beside_scan(
    dp_n, gn_in, rows_out_in, tokens_in, y_send_in, g_in_in, block_out, g_out, g_z,
    gn, rows_out, tokens, y_send, g_in, s_in, sib_send, sib_recv, x_send, x_recv, part, held, y_recv, z_send, z_recv, g_own,
    s_sib, r_sib, s_x, r_x, s_y, r_y, s_z, r_z,
):
    i = pl.program_id(0)
    who = peers(dp_n)
    lines = who["lines"]
    units, span, quarter = held.shape
    block = g_out.shape[0]
    half = g_out.shape[1] // 2

    def copy_sib(k):
        return push(sib_send.at[k], sib_recv.at[k], s_sib.at[k], r_sib.at[k], who["sib"])

    def copy_x(k):
        return push(x_send.at[k], x_recv.at[k], s_x.at[k], r_x.at[k], who["xn"])

    def copy_y(v):
        return push(y_send.at[v], y_recv.at[v], s_y.at[v], r_y.at[v], who["yn"])

    def copy_z(v, k):
        to = (who["line_index"] + k) % lines
        return push(
            z_send.at[v, pl.ds(pl.multiple_of(to * block, block), block)],
            z_recv.at[v, k - 1], s_z.at[v, k - 1], r_z.at[v, k - 1], who["line"](k),
        )

    loads = [
        pltpu.make_async_copy(src, dst, s_in.at[n])
        for n, (src, dst) in enumerate((
            (y_send_in, y_send), (rows_out_in, rows_out), (gn_in, gn), (tokens_in, tokens), (g_in_in, g_in),
        ))
    ]

    @pl.when(i == 0)
    def _():
        for load in loads:
            load.start()
        meet(who)
        loads[0].wait()
        for v in range(4):
            copy_y(v).start()

    @pl.when(i == 1)
    def _():
        for load in loads[1:]:
            load.wait()

    def first(k):
        for n, q in enumerate(("sib_mine", "sib_other", "mine", "other")):
            cols = pl.ds(pl.multiple_of(who[q] * quarter, quarter), quarter)
            p = nt(gn[k * span : (k + 1) * span, :], rows_out[cols, :])
            if n < 2:
                sib_send[k, n] = p.astype(BF)
            else:
                part[n - 2] = p
        copy_sib(k).start()

    def second(k):
        copy_sib(k).wait()
        x_send[k] = (part[1] + sib_recv[k, 1].astype(F32)).astype(BF)
        copy_x(k).start()
        held[k] = part[0] + sib_recv[k, 0].astype(F32)

    def third(k):
        copy_x(k).wait()
        at = slice(k * span, (k + 1) * span)
        block_out[at, :] = (tokens[at, :].astype(F32) + held[k] + x_recv[k].astype(F32)).astype(BF)

    def grad_b(v):
        copy_y(v).wait()
        g_own[v] = g_in[v] + y_recv[v].astype(F32)
        z_send[v] = g_own[v].astype(BF)
        loop_line(lines, lambda k: copy_z(v, k).start())

    def grad_c(v):
        loop_line(lines, lambda k: copy_z(v, k).wait())
        total = g_own[v, pl.ds(pl.multiple_of(who["line_index"] * block, block), block), :]
        for k in range(lines - 1):
            total = total + z_recv[v, k].astype(F32)
        (g_out, g_z)[v // 2][:, (v % 2) * half : (v % 2 + 1) * half] = total

    events = [(grad_b, 0, 3), (grad_b, 1, 6), (grad_b, 2, 8), (grad_b, 3, 11)]
    for k in range(units):
        events += [(first, k, 2 * k + 1), (second, k, 2 * k + 2), (third, k, 2 * k + 7)]
    for at in sorted({e[2] for e in events}):

        @pl.when(i == at)
        def _(at=at):
            for fn, k, when in events:
                if when == at:
                    fn(k)

    def finish():
        for v in range(4):
            grad_c(v)

    return finish


def scan_bwd_kernel(
    heads, taps_n, bc, dp_n, dy_in, px, px_halo, pbd, pbd_halo, sin, gain_grad, vec, gn, rows_out, tokens,
    y_send, g_in,
    lpx, lpbd, acc, block_out, g_out, g_z, dstate, extx, extb, dux, dub, acc_x, acc_bc, acc_s, upper, spread, gather, ones_h,
    *beside,
):
    finish = sums_beside_scan(dp_n, gn, rows_out, tokens, y_send, g_in, block_out, g_out, g_z, *beside)
    i = pl.program_id(0)
    blocks = pl.num_programs(0)
    c = blocks - 1 - i
    chunk, inner = px.shape
    ns = bc // 2
    par = read_vec(vec, heads, chunk, inner, bc, taps_n)
    keep, n_live, keep_next = read_block(vec, c, chunk)
    taps, taps_b, bias, rate, skip = (par[k] for k in ("convx", "convbc", "bias", "rate", "skip"))

    @pl.when(i == 0)
    def _():
        for ref in (dstate, dux, dub, acc_x, acc_bc, acc_s):
            ref[...] = jnp.zeros_like(ref)
        acc_x[taps_n : taps_n + 1, :] = gain_grad[0:1, :]
        set_upper(upper)
        set_spread(spread, heads)
        set_gather(gather, ones_h, heads)

    dy = dy_in[...]

    extx[0:8, :] = jnp.where(keep, px_halo[...], 0.0)
    extb[0:8, :] = jnp.where(keep, pbd_halo[:, :bc], 0.0)
    extx[8 : chunk + 8, :] = px[...]
    extb[8 : chunk + 8, :] = pbd[:, :bc]
    live_x = (iota2(chunk, inner, 0).astype(F32) < n_live).astype(F32)
    live_b = (iota2(chunk, bc, 0).astype(F32) < n_live).astype(F32)
    u, moved_x = conv_from(extx, taps, chunk, 8)
    su = sigmoid(u)
    x = u * su * live_x
    dx_du = su * (1.0 + u * (1.0 - su)) * live_x
    ub, moved_b = conv_from(extb, taps_b, chunk, 8)
    sb = sigmoid(ub)
    act = (ub * sb * live_b).astype(BF)
    db_du = sb * (1.0 + ub * (1.0 - sb)) * live_b
    b, cc = act[:, :ns], act[:, ns:]

    pre, live, dt, run = dt_rows(pbd[:, bc:], bias, rate, n_live, heads, upper[...])
    cols, wide = spread_all(run, dt, heads, chunk, spread[...])
    dt_w, ein_w, eout_w = wide[:, :inner], wide[:, inner : 2 * inner], wide[:, 2 * inner :]
    xd = x * dt_w
    xdb = xd.astype(BF)
    dyb = dy.astype(BF)
    acc_x[taps_n + 1 : taps_n + 2, :] += jnp.sum(dy * x, axis=0, keepdims=True)

    scores_t = nt(b, cc)
    tri = iota2(chunk, chunk, 0) <= iota2(chunk, chunk, 1)
    low_lanes = iota2(chunk, 2 * HD, 1) < HD
    d_scores_t = jnp.zeros((chunk, chunk), F32)
    dxd = []
    pulls = []
    read_sums = []
    for j in range(heads // 2):
        span = slice(2 * HD * j, 2 * HD * (j + 1))
        dy_pair = pair_stack(dyb[:, span], low_lanes)
        x_pair = pair_stack(xdb[:, span], low_lanes)
        d_mix = nt(x_pair, dyb[:, span])
        mix = []
        for k in (0, 1):
            h = 2 * j + k
            spread_h = run[h : h + 1, :] - cols[:, h : h + 1]
            fade = jnp.exp(jnp.where(tri, spread_h, NEG))
            m = scores_t * fade
            dm = d_mix[k * chunk : (k + 1) * chunk]
            d_scores_t = d_scores_t + dm * fade
            pull = (dm * m).astype(BF)
            pulls.append(pull)
            read_sums.append(jnp.sum(pull.astype(F32), axis=0, keepdims=True))
            mix.append(m.astype(BF))
        dxd.append(nn(jnp.concatenate(mix, axis=1), dy_pair))
    source_sums = nn(jnp.concatenate(pulls, axis=1), ones_h[...])
    read_rows = jnp.concatenate(read_sums, axis=0)

    d_state = jnp.where(keep_next, dstate[...], 0.0)
    d_state_b = d_state.astype(BF)
    enter_b = sin[0]
    edy = ein_w * dy
    edyb = edy.astype(BF)
    readings = nn(cc, enter_b)
    from_state = nn(b, d_state_b) * eout_w
    d_xd = jnp.concatenate(dxd, axis=1) + from_state
    q1 = edy * readings
    q2 = xd * from_state
    decay = ein_w[chunk - 1 : chunk, :]
    dstate[...] = decay * d_state + tn(cc, edyb)
    d_cb = tn(d_scores_t.astype(BF), b) + nt(edyb, enter_b)
    d_b = nn(d_scores_t.astype(BF), cc) + nt((xd * eout_w).astype(BF), d_state_b)

    sums = (
        nn((d_xd * x).astype(BF), gather[0])
        + nn((q1 - q2).astype(BF), gather[1])
        + nn(q2.astype(BF), gather[2])
        - source_sums
    )
    sums_t = jnp.transpose(sums)
    dt_direct = sums_t[:heads]
    d_run = sums_t[heads : 2 * heads] + read_rows
    whole_q2 = jnp.sum(sums_t[2 * heads : 3 * heads], axis=1, keepdims=True)
    kept = jnp.sum(enter_b.astype(F32) * d_state, axis=0, keepdims=True) * decay
    kept_hi, kept_lo = split2(kept)
    kept_two = jnp.concatenate([kept_hi, kept_lo, jnp.zeros((6, inner), F32)], axis=0).astype(BF)
    kept_rows = nn(kept_two, gather[0])
    kept_cols = jnp.transpose(
        jnp.concatenate([kept_rows[0:1] + kept_rows[1:2], jnp.zeros((chunk - 1, chunk), F32)], axis=0)
    )
    d_last = whole_q2 + kept_cols[:heads, 0:1]
    hi, mid, low = split3(d_run)
    back = nt(jnp.concatenate([hi, mid, low], axis=0).astype(BF), upper[...])
    d_a = back[:heads] + back[heads : 2 * heads] + back[2 * heads :] + d_last
    d_dt = dt_direct + d_a * rate
    d_pre = d_dt * live * sigmoid(pre)
    acc_s[0:heads, :] += d_pre
    acc_s[heads : 2 * heads, :] += d_a * dt * rate

    def conv_back(d_u, du_ref, moved, tap_values, acc):
        du_ref[chunk : chunk + 8, :] = jnp.where(keep_next, du_ref[0:8, :], 0.0)
        du_ref[0:chunk, :] = d_u
        out = tap_values[taps_n - 1 : taps_n, :] * d_u
        acc[taps_n - 1 : taps_n, :] += jnp.sum(d_u * moved[0], axis=0, keepdims=True)
        for k in range(1, taps_n):
            row = taps_n - 1 - k
            out = out + tap_values[row : row + 1, :] * du_ref[pl.ds(k, chunk), :]
            acc[row : row + 1, :] += jnp.sum(d_u * moved[k], axis=0, keepdims=True)
        return out

    d_x = d_xd * dt_w + skip * dy
    lpx[...] = conv_back(d_x * dx_du, dux, moved_x, taps, acc_x).astype(BF)
    d_act = jnp.concatenate([d_b, d_cb], axis=1)
    lpbd[:, :bc] = conv_back(d_act * db_du, dub, moved_b, taps_b, acc_bc).astype(BF)
    pad = jnp.concatenate([d_pre, jnp.zeros((chunk - heads, chunk), F32)], axis=0)
    lpbd[:, bc:] = jnp.transpose(pad).astype(BF)

    @pl.when(i == blocks - 1)
    def _():
        acc[...] = jnp.zeros_like(acc)
        for k in range(taps_n):
            acc[1:2, k * bc : (k + 1) * bc] = acc_bc[k : k + 1, :]
        per = acc.shape[1] // inner
        for k in range(taps_n + 1):
            acc[2 + k // per : 3 + k // per, (k % per) * inner : (k % per + 1) * inner] = acc_x[k : k + 1, :]
        per_head = jnp.sum(
            jnp.transpose(jnp.concatenate([acc_s[...], jnp.zeros((chunk - 2 * heads, chunk), F32)], axis=0)),
            axis=0, keepdims=True,
        )
        three = jnp.concatenate(split3(acc_x[taps_n + 1 : taps_n + 2, :]) + (jnp.zeros((5, inner), F32),), axis=0)
        skips = jnp.sum(nn(three.astype(BF), gather[2]), axis=0, keepdims=True)
        acc[5:6, 0:chunk] = per_head + skips
        finish()


def scan_backward(
    dp_n, dy, px, pbd, sin, gain_grad, vec, gn, rows_out, tokens, y_send, g_own, heads, taps, bc
):
    count, inner = px.shape
    blocks = sin.shape[0]
    chunk = count // blocks
    whole = lambda a: pl.BlockSpec(a.shape, lambda i: (0,) * a.ndim)
    back = lambda w: pl.BlockSpec((chunk, w), lambda i: (blocks - 1 - i, 0))
    halo = lambda w: pl.BlockSpec((8, w), lambda i: (jnp.maximum((blocks - 1 - i) * (chunk // 8) - 1, 0), 0))
    width = pbd.shape[1]
    lines = dp_n // 2
    more = max(lines - 1, 1)
    block = rows_out.shape[0] // dp_n
    quarter = tokens.shape[1]
    units = 4
    span = count // units
    dma = pltpu.SemaphoreType.DMA
    vm, sds = pltpu.VMEM, jax.ShapeDtypeStruct
    return pl.pallas_call(
        functools.partial(scan_bwd_kernel, heads, taps, bc, dp_n),
        grid=(blocks,),
        in_specs=[
            back(inner), back(inner), halo(inner), back(width), halo(width),
            pl.BlockSpec((1, bc // 2, inner), lambda i: (blocks - 1 - i, 0, 0)), whole(gain_grad), whole(vec),
        ]
        + [pl.BlockSpec(memory_space=pl.ANY)] * 5,
        out_specs=[
            back(inner), back(width), pl.BlockSpec((8, vec.shape[1]), lambda i: (0, 0)),
            whole(tokens), pl.BlockSpec((block, inner), lambda i: (0, 0)), pl.BlockSpec((block, inner), lambda i: (0, 0)),
        ],
        scratch_shapes=[
            vm((bc // 2, inner), F32), vm((chunk + 8, inner), F32), vm((chunk + 8, bc), F32),
            vm((chunk + 8, inner), F32), vm((chunk + 8, bc), F32),
            vm((8, inner), F32), vm((8, bc), F32), vm((2 * heads, chunk), F32),
            vm((chunk, chunk), BF), vm((chunk, 3 * inner), BF), vm((3, inner, chunk), BF), vm((heads * chunk, chunk), BF),
            vm(gn.shape, BF), vm(rows_out.shape, BF), vm(tokens.shape, BF), vm(y_send.shape, BF), vm(g_own.shape, F32),
            dma((5,)),
            vm((units, 2, span, quarter), BF), vm((units, 2, span, quarter), BF),
            vm((units, span, quarter), BF), vm((units, span, quarter), BF),
            vm((2, span, quarter), F32), vm((units, span, quarter), F32),
            vm(y_send.shape, BF), vm(y_send.shape, BF), vm((4, more, block, inner // 2), BF), vm(y_send.shape, F32),
            dma((units,)), dma((units,)), dma((units,)), dma((units,)), dma((4,)), dma((4,)),
            dma((4, more)), dma((4, more)),
        ],
        out_shape=[
            sds((count, inner), BF), sds((count, width), BF),
            sds((8, vec.shape[1]), F32), sds(tokens.shape, BF), sds((block, inner), F32),
            sds((block, inner), F32),
        ],
        compiler_params=pltpu.CompilerParams(
            collective_id=3, has_side_effects=True, vmem_limit_bytes=58 * 2**20
        ),
        name="scan_backward",
    )(dy, px, px, pbd, pbd, sin, gain_grad, vec, gn, rows_out, tokens, y_send, g_own)
def peers(dp_n):
    dp, hm = lax.axis_index("dp"), lax.axis_index("heads")
    across, core = hm // 2, hm % 2
    pair, line, lines = dp % 2, dp // 2, dp_n // 2
    return dict(
        sib=(dp, 2 * across + 1 - core),
        xn=(dp, 2 * (1 - across) + core),
        dg=(dp, 2 * (1 - across) + 1 - core),
        yn=(2 * line + 1 - pair, hm),
        line=lambda k: (2 * ((line + k) % lines) + pair, hm),
        mine=hm,
        other=2 * (1 - across) + core,
        sib_mine=2 * across + 1 - core,
        sib_other=2 * (1 - across) + 1 - core,
        pair=pair, line_index=line, lines=lines, dp=dp, core=core,
    )


def meet(who):
    barrier = pltpu.get_barrier_semaphore()
    for name in ("sib", "xn", "dg", "yn"):
        pl.semaphore_signal(barrier, inc=1, device_id=who[name], device_id_type=MESH)

    def greet(k, carry):
        pl.semaphore_signal(barrier, inc=1, device_id=who["line"](k), device_id_type=MESH)
        return carry

    lax.fori_loop(1, who["lines"], greet, 0)
    pl.semaphore_wait(barrier, 4 + who["lines"] - 1)


def push(src, dst, send, recv, to):
    return pltpu.make_async_remote_copy(
        src_ref=src, dst_ref=dst, send_sem=send, recv_sem=recv, device_id=to, device_id_type=MESH
    )


def tail_kernel(
    dp_n, units,
    normed_t_in, lpx_in, rows_z_in, lpz_in, rows_x_in, lpbd_in, rows_bd_in, normed_in,
    tokens, acc, cot, q_wide, vec,
    grad_tokens, g_x, g_bc, small_out,
    sib_send, sib_recv, x_send, x_recv, part, held,
    y_send, y_recv, z_send, z_recv, g_own, yb_send, yb_recv, zb_send, zb_recv, gb_own, bh_send, bh_recv,
    bx_send, bx_recv, bs_recv, h_send, h_recv, sy_send, sy_recv, sz_send, sz_recv, dy_send, dy_recv, dz_send, dz_recv, row_sums,
    normed_t, lpx, rows_z, lpz, rows_x, lpbd, rows_bd, normed,
    s_in, s_sib, r_sib, s_x, r_x, s_y, r_y, s_z, r_z, s_m, r_m, s_sl, r_sl,
):
    loads = [
        pltpu.make_async_copy(src, dst, s_in.at[i])
        for i, (src, dst) in enumerate((
            (normed_t_in, normed_t), (lpx_in, lpx), (rows_z_in, rows_z), (lpz_in, lpz), (rows_x_in, rows_x),
            (lpbd_in, lpbd), (rows_bd_in, rows_bd), (normed_in, normed),
        ))
    ]
    for load in loads:
        load.start()
    who = peers(dp_n)
    meet(who)
    count = normed.shape[0]
    width = normed.shape[1]
    inner = lpx.shape[1]
    bc = 2 * bh_send.shape[1]
    quarter = width // 4
    span = count // units
    block = width // dp_n
    lines = who["lines"]

    def copy_sib(u):
        return push(sib_send.at[u], sib_recv.at[u], s_sib.at[u], r_sib.at[u], who["sib"])

    def copy_x(u):
        return push(x_send.at[u], x_recv.at[u], s_x.at[u], r_x.at[u], who["xn"])

    def product(u, q):
        cols = pl.ds(pl.multiple_of(q * quarter, quarter), quarter)
        at = slice(u * span, (u + 1) * span)
        return nt(lpx[at, :], rows_x[cols, :]) + nt(lpz[at, :], rows_z[cols, :]) + nt(lpbd[at, :], rows_bd[cols, :])

    def head_a(u):
        for k, q in enumerate(("sib_mine", "sib_other", "mine", "other")):
            p = product(u, who[q])
            at = slice(u * span, (u + 1) * span)
            cols = pl.ds(pl.multiple_of(who[q] * quarter, quarter), quarter)
            inner_p = p * normed[at, cols].astype(F32)
            h_send[0:1, cols] += jnp.sum(inner_p, axis=0, keepdims=True)
            first = u * span
            lanes = slice(first % width, first % width + span)
            h_send[2 + first // width : 3 + first // width, lanes] += nt(
                jnp.ones((8, quarter), BF), inner_p.astype(BF)
            )[0:1]
            if k < 2:
                sib_send[u, k] = p.astype(BF)
            else:
                part[u % 2, k - 2] = p
        copy_sib(u).start()

    def head_b(u):
        copy_sib(u).wait()
        x_send[u] = (part[u % 2, 1] + sib_recv[u, 1].astype(F32)).astype(BF)
        copy_x(u).start()
        held[u] = part[u % 2, 0] + sib_recv[u, 0].astype(F32)

    def head_c(u):
        copy_x(u).wait()
        total = held[u] + x_recv[u].astype(F32)
        first = u * span
        lanes = q_wide.shape[1]
        cols = pl.ds(pl.multiple_of(who["mine"] * quarter, quarter), quarter)
        for j in range(span // lanes):
            at = slice(first + j * lanes, first + (j + 1) * lanes)
            row, lane = (first + j * lanes) // width, (first + j * lanes) % width
            dots = jnp.transpose(jnp.broadcast_to(row_sums[row : row + 1, lane : lane + lanes], (lanes, lanes)))
            q = q_wide[at, :]
            coef = q * q * (dots / width)
            grad_tokens[at, :] = (
                cot[at, :].astype(F32)
                + q[:, 0:1] * vec[6:7, cols] * total[j * lanes : (j + 1) * lanes]
                - tokens[at, :].astype(F32) * coef[:, 0:1]
            )

    def rows_of(line, pair):
        return pl.ds(pl.multiple_of((2 * line + pair) * block, block), block)

    def grad_a(v):
        left, right = (normed_t, lpx)
        cols = slice((v % 2) * (inner // 2), (v % 2 + 1) * (inner // 2))
        for side in (0, 1):
            pair = (1 - who["pair"]) if side == 0 else who["pair"]
            stacked = jnp.concatenate([left[rows_of(l, pair), :] for l in range(lines)], axis=0)
            value = nn(stacked, right[:, cols])
            if side == 0:
                y_send[v] = value.astype(BF)
                copy_y(v).start()
            else:
                g_own[v] = value

    def copy_y(v):
        return push(y_send.at[v], y_recv.at[v], s_y.at[v], r_y.at[v], who["yn"])

    def copy_z(v, k):
        to = (who["line_index"] + k) % lines
        return push(
            z_send.at[v, pl.ds(pl.multiple_of(to * block, block), block)],
            z_recv.at[v, k - 1], s_z.at[v, k - 1], r_z.at[v, k - 1], who["line"](k),
        )

    def each_line(fn):
        def step(k, carry):
            fn(k)
            return carry

        lax.fori_loop(1, lines, step, 0)

    def own_rows():
        return pl.ds(pl.multiple_of(who["line_index"] * block, block), block)

    def grad_b(v):
        copy_y(v).wait()
        g_own[v] = g_own[v] + y_recv[v].astype(F32)
        z_send[v] = g_own[v].astype(BF)
        each_line(lambda k: copy_z(v, k).start())

    def grad_c(v):
        each_line(lambda k: copy_z(v, k).wait())
        total = g_own[v, own_rows(), :]
        for k in range(lines - 1):
            total = total + z_recv[v, k].astype(F32)
        cols = slice((v % 2) * (inner // 2), (v % 2 + 1) * (inner // 2))
        g_x[:, cols] = total

    half = bc // 2

    def copy_bh():
        return push(bh_send, bh_recv, s_m.at[0], r_m.at[0], who["sib"])

    def copy_yb():
        return push(yb_send, yb_recv, s_m.at[1], r_m.at[1], who["yn"])

    def copy_zb(k):
        to = (who["line_index"] + k) % lines
        return push(
            zb_send.at[pl.ds(pl.multiple_of(to * block, block), block)],
            zb_recv.at[k - 1], s_sl.at[0, k - 1], r_sl.at[0, k - 1], who["line"](k),
        )

    def copy_bx():
        return push(bx_send, bx_recv, s_m.at[2], r_m.at[2], who["xn"])

    def copy_bs():
        return push(bx_send, bs_recv, s_m.at[3], r_m.at[3], who["sib"])

    def bc_a():
        for side in (0, 1):
            pair = (1 - who["pair"]) if side == 0 else who["pair"]
            stacked = jnp.concatenate([normed_t[rows_of(l, pair), :] for l in range(lines)], axis=0)
            value = nn(stacked, lpbd[:, :bc])
            first = who["core"] == 0
            lo, hi = value[:, :half], value[:, half:]
            at = slice(side * lines * block, (side + 1) * lines * block)
            bh_send[at, :] = jnp.where(first, hi, lo).astype(BF)
            gb_own[at, :] = jnp.where(first, lo, hi)
        copy_bh().start()

    def bc_b():
        copy_bh().wait()
        rows = lines * block
        gb_own[...] = gb_own[...] + bh_recv[...].astype(F32)
        yb_send[...] = gb_own[:rows, :].astype(BF)
        copy_yb().start()

    def bc_c():
        rows = lines * block
        copy_yb().wait()
        gb_own[rows:, :] = gb_own[rows:, :] + yb_recv[...].astype(F32)
        zb_send[...] = gb_own[rows:, :].astype(BF)
        each_line(lambda k: copy_zb(k).start())

    def bc_d():
        each_line(lambda k: copy_zb(k).wait())
        at = pl.ds(pl.multiple_of(lines * block + who["line_index"] * block, block), block)
        total = gb_own[at, :]
        for k in range(lines - 1):
            total = total + zb_recv[k].astype(F32)
        bx_send[...] = total
        copy_bx().start()

    def bc_e():
        copy_bx().wait()
        bx_send[...] = bx_send[...] + bx_recv[...]
        copy_bs().start()

    def bc_f():
        copy_bs().wait()
        mine, theirs = bx_send[...], bs_recv[...]
        first = who["core"] == 0
        g_bc[:, :half] = jnp.where(first, mine, theirs)
        g_bc[:, half:] = jnp.where(first, theirs, mine)

    three = (("sib", 4), ("xn", 5), ("dg", 6))
    token_rows = count // width

    def copy_h(k):
        name, sem = three[k]
        return push(h_send, h_recv.at[k], s_m.at[sem], r_m.at[sem], who[name])

    def small_a():
        h_send[1:2, :] = acc[1:2, :]
        for k in range(3):
            copy_h(k).start()

    def copy_sy():
        return push(sy_send, sy_recv, s_m.at[7], r_m.at[7], who["yn"])

    def copy_dy():
        return push(dy_send, dy_recv, s_m.at[8], r_m.at[8], who["yn"])

    def copy_sz(k):
        return push(sz_send, sz_recv.at[k - 1], s_sl.at[1, k - 1], r_sl.at[1, k - 1], who["line"](k))

    def copy_dz(k):
        return push(dz_send, dz_recv.at[k - 1], s_sl.at[2, k - 1], r_sl.at[2, k - 1], who["line"](k))

    def dt_a():
        dy_send[...] = tn(lpbd[:, bc:], normed[...])[0:16, :].astype(BF)
        copy_dy().start()

    def dt_b():
        copy_dy().wait()
        dz_send[...] = (dy_send[...].astype(F32) + dy_recv[...].astype(F32)).astype(BF)
        each_line(lambda k: copy_dz(k).start())

    def dt_c():
        each_line(lambda k: copy_dz(k).wait())
        total = dz_send[...].astype(F32)
        for k in range(lines - 1):
            total = total + dz_recv[k].astype(F32)
        small_out[8:24, :] = total

    def small_b():
        for k in range(3):
            copy_h(k).wait()
        over_heads = h_send[...] + h_recv[0] + h_recv[1] + h_recv[2]
        row_sums[0:token_rows, :] = over_heads[2 : 2 + token_rows, :]
        sy_send[0:2, :] = over_heads[0:2, :]
        sy_send[2:8, :] = acc[2:8, :]
        copy_sy().start()

    def small_c():
        copy_sy().wait()
        sz_send[...] = sy_send[...] + sy_recv[...]
        each_line(lambda k: copy_sz(k).start())

    def small_d():
        each_line(lambda k: copy_sz(k).wait())
        total = sz_send[...]
        for k in range(lines - 1):
            total = total + sz_recv[k]
        small_out[0:8, :] = total

    h_send[...] = jnp.zeros_like(h_send)

    def seq(*steps):
        for fn, *args in steps:
            fn(*args)

    assert units == 4

    def load(*which):
        for i in which:
            loads[i].wait()

    load(0, 1)
    grad_a(0)
    load(2, 3, 4, 5, 6, 7)
    seq((head_a, 0), (bc_a,), (head_b, 0), (head_a, 1), (bc_b,), (grad_a, 1), (head_b, 1), (grad_b, 0), (head_a, 2))
    seq((dt_a,), (head_b, 2), (head_a, 3), (small_a,), (bc_c,), (head_b, 3), (grad_b, 1), (dt_b,), (small_b,))
    seq((bc_d,), (head_c, 0), (small_c,), (grad_c, 0), (dt_c,), (head_c, 1), (bc_e,), (small_d,), (bc_f,), (head_c, 2))
    seq((grad_c, 1), (head_c, 3))


def tail(dp_n, units, normed_t, normed, lpx, lpz, lpbd, rows_x, rows_z, rows_bd, tokens, acc, cot, q_wide, vec, bc):
    count, width = normed.shape
    inner = lpx.shape[1]
    quarter = width // 4
    span = count // units
    block = width // dp_n
    lines = dp_n // 2
    half_rows = lines * block
    more = max(lines - 1, 1)
    vm = pltpu.VMEM
    dma = pltpu.SemaphoreType.DMA
    operands = (
        normed_t, lpx, rows_z, lpz, rows_x, lpbd, rows_bd, normed, tokens, acc, cot, q_wide, vec,
    )
    sds = jax.ShapeDtypeStruct
    spec = pl.BlockSpec(memory_space=pltpu.VMEM)
    return pl.pallas_call(
        functools.partial(tail_kernel, dp_n, units),
        out_shape=[
            sds((count, quarter), F32), sds((block, inner), F32), sds((block, bc), F32),
            sds((24, width), F32),
        ],
        in_specs=[pl.BlockSpec(memory_space=pl.ANY)] * 8 + [spec] * 5,
        out_specs=[spec] * 4,
        scratch_shapes=[
            vm((units, 2, span, quarter), BF), vm((units, 2, span, quarter), BF),
            vm((units, span, quarter), BF), vm((units, span, quarter), BF),
            vm((2, 2, span, quarter), F32), vm((units, span, quarter), F32),
            vm((2, half_rows, inner // 2), BF), vm((2, half_rows, inner // 2), BF),
            vm((2, half_rows, inner // 2), BF), vm((2, more, block, inner // 2), BF),
            vm((2, half_rows, inner // 2), F32),
            vm((half_rows, bc // 2), BF), vm((half_rows, bc // 2), BF),
            vm((half_rows, bc // 2), BF), vm((more, block, bc // 2), BF),
            vm((2 * half_rows, bc // 2), F32),
            vm((2 * half_rows, bc // 2), BF), vm((2 * half_rows, bc // 2), BF),
            vm((block, bc // 2), F32), vm((block, bc // 2), F32), vm((block, bc // 2), F32),
            vm((8, width), F32), vm((3, 8, width), F32),
            vm((8, width), F32), vm((8, width), F32), vm((8, width), F32), vm((more, 8, width), F32),
            vm((16, width), BF), vm((16, width), BF), vm((16, width), BF), vm((more, 16, width), BF),
            vm((8, width), F32),
        ]
        + [vm(a.shape, a.dtype) for a in operands[:8]]
        + [
            dma((8,)), dma((units,)), dma((units,)), dma((units,)), dma((units,)),
            dma((2,)), dma((2,)), dma((2, more)), dma((2, more)), dma((9,)), dma((9,)),
            dma((3, more)), dma((3, more)),
        ],
        compiler_params=pltpu.CompilerParams(
            collective_id=1, has_side_effects=True, vmem_limit_bytes=62 * 2**20
        ),
        name="tail",
    )(*operands)
def chain(ref_in, block_of, width, send, recv, y_send, y_recv, who):
    rows = ref_in.shape[0]
    lines, line, pair = who["lines"], who["line_index"], who["pair"]
    own = ref_in.at[:, width] if ref_in.shape[1] != width.size else ref_in

    def at(index):
        return block_of.at[pl.ds(pl.multiple_of((2 * index + pair) * rows, rows), rows), width]

    def hand(sign, j):
        index = line - sign * j
        source = own if isinstance(j, int) and j == 0 else at(index)
        slot = j + 1 if sign > 0 else lines + j
        to = (2 * (line + sign) + pair, who["mine"])
        return push(source, at(index), send.at[slot], recv.at[slot], to)

    def to_pair(sign, j):
        slot = j if sign > 0 else lines - 1 + j
        index = line - sign * j
        source = own if isinstance(j, int) and j == 0 else at(index)
        return push(source, at(index), y_send.at[slot], y_recv.at[slot], who["yn"])

    def arrived(sign, j):
        slot = j if sign > 0 else lines - 1 + j
        block = at(line - sign * j)
        return push(block, block, send.at[slot], recv.at[slot], who["yn"])

    def inside(index):
        return jnp.logical_and(index >= 0, index < lines)

    def both(fn):
        for sign in (1, -1):
            fn(sign)

    def begin():
        def one(sign):
            @pl.when(inside(line + sign))
            def _():
                hand(sign, 0).start()

        both(one)

    def begin_pair():
        to_pair(1, 0).start()

    def hop(j):
        def one(sign):
            @pl.when(inside(line - sign * j))
            def _():
                arrived(sign, j).wait_recv()

                @pl.when(inside(line + sign))
                def _():
                    hand(sign, j).start()

                to_pair(sign, j).start()

        both(one)

    def end():
        to_pair(1, 0).wait()

        def one(sign):
            @pl.when(inside(line + sign))
            def _():
                hand(sign, 0).wait_send()

        both(one)

        def later(j):
            def one(sign):
                @pl.when(inside(line - sign * j))
                def _():
                    to_pair(sign, j).wait()

                    @pl.when(inside(line + sign))
                    def _():
                        hand(sign, j).wait_send()

            both(one)

        loop_line(lines, later)

    return begin, begin_pair, hop, end


def loop_line(lines, fn):
    def step(k, carry):
        fn(k)
        return carry

    lax.fori_loop(1, lines, step, 0)


def front_kernel(
    dp_n, heads, units, taps, bc,
    tokens, cot, w_x, w_bc, w_z, w_out, w_dt, conv_x, conv_bc, norm_gain, gate_gain, dt_bias, a_log, skip, starts, fill,
    vec, px_out, pbd_out, normed_out, normed_t_out, q_out, y_out, sin_out, parts, rows_x, rows_bd, rows_z, rows_out,
    own_dt, tok, wx, wbd, px, pbd, normed, normed_t, q, y, sin, own_w, own_cot, state, extx, extb, upper, spread,
    s_loc, s_sib, r_sib, s_x, r_x, s_f, r_f, s_cx, r_cx, s_cf, r_cf, s_w, r_w, s_wy, r_wy, s_c, r_c, s_cy, r_cy, s_out, s_y,
):
    who = peers(dp_n)
    count, quarter = tokens.shape
    width = 4 * quarter
    span = count // units
    lines = who["lines"]
    block, inner = w_x.shape
    blocks = sin.shape[0]
    chunk = count // blocks
    per = blocks // units
    pieces = s_cx.shape[0]
    cot_span = count // pieces
    here = pl.ds(pl.multiple_of(who["dp"] * block, block), block)
    own_half = pl.ds(pl.multiple_of(who["core"] * (bc // 2), bc // 2), bc // 2)
    dt_cols = pl.ds(bc, chunk)
    local = [
        pltpu.make_async_copy(src, dst, s_loc.at[k])
        for k, (src, dst) in enumerate((
            (tokens, tok.at[who["mine"]]), (w_x, wx.at[here]), (w_bc.at[:, own_half], wbd.at[here, own_half]),
            (w_z, own_w.at[0]), (w_out, own_w.at[1]), (cot, own_cot),
        ))
    ]
    for copy in local:
        copy.start()
    own_dt[...] = jnp.zeros_like(own_dt)
    own_dt[:, :heads] = w_dt[...]
    wbd[here, dt_cols] = own_dt[...]
    onto = [
        pltpu.make_async_copy(src, dst, s_loc.at[8 + k])
        for k, (src, dst) in enumerate((
            (own_w.at[0], rows_z.at[here]), (own_w.at[1], rows_out.at[here]), (own_cot, parts.at[who["mine"]]),
        ))
    ]
    meet(who)

    def rows(s, n=span):
        return pl.ds(pl.multiple_of(s * n, n), n)

    def to_x(s):
        return push(tokens.at[rows(s)], tok.at[who["mine"], rows(s)], s_x.at[s], r_x.at[s], who["xn"])

    def to_sib():
        return push(tokens, tok.at[who["mine"]], s_sib.at[0], r_sib.at[0], who["sib"])

    def forward(s):
        at = tok.at[who["other"], rows(s)]
        return push(at, at, s_f.at[s], r_f.at[s], who["sib"])

    def cot_x(j):
        at = rows(j, cot_span)
        return push(cot.at[at], parts.at[who["mine"], at], s_cx.at[j], r_cx.at[j], who["xn"])

    def cot_sib():
        return push(cot, parts.at[who["mine"]], s_sib.at[1], r_sib.at[1], who["sib"])

    def cot_forward(j):
        at = parts.at[who["other"], rows(j, cot_span)]
        return push(at, at, s_cf.at[j], r_cf.at[j], who["sib"])

    half = inner // 2
    cuts = [
        chain(ref, to, cols, s_w.at[n], r_w.at[n], s_wy.at[n], r_wy.at[n], who)
        for n, (ref, to, cols) in enumerate((
            (w_x, wx, pl.ds(0, half)), (w_x, wx, pl.ds(half, half)), (w_bc, wbd, own_half), (own_dt, wbd, dt_cols),
        ))
    ]
    chains = [
        chain(ref, to, pl.ds(h * half, half), s_c.at[2 * n + h], r_c.at[2 * n + h], s_cy.at[2 * n + h], r_cy.at[2 * n + h], who)
        for n, (ref, to) in enumerate(((w_z, rows_z), (w_out, rows_out)))
        for h in (0, 1)
    ]

    def other_half():
        cols = wbd.at[:, own_half]
        return push(cols, cols, s_sib.at[2], r_sib.at[2], who["sib"])

    def have(n):
        cuts[n][3]()

    def pass_cot(j):
        cot_x(j).wait()
        cot_forward(j).start()

    to_x(0).start()
    for begin, begin_pair, hop, end in cuts:
        begin()
        begin_pair()
    for s in range(1, units):
        to_x(s).start()
    to_sib().start()
    for j in range(pieces):
        cot_x(j).start()
    pack_vec(vec, conv_x, conv_bc, norm_gain, gate_gain, dt_bias, a_log, skip, starts, fill, chunk)
    set_upper(upper)
    set_spread(spread, heads)
    state[...] = jnp.zeros_like(state)
    extx[...] = jnp.zeros_like(extx)
    extb[...] = jnp.zeros_like(extb)
    par = read_vec(vec, heads, chunk, inner, bc, taps)
    gain = vec[6:7, :width]

    def out_copies(s):
        at = rows(s)
        every = slice(None)
        return [
            pltpu.make_async_copy(ref.at[to], out.at[to], s_out.at[n, s])
            for n, (ref, out, to) in enumerate((
                (normed, normed_out, (at,)), (normed_t, normed_t_out, (every, at)), (q, q_out, (at,)),
                (px, px_out, (at,)), (pbd, pbd_out, (at,)),
            ))
        ]

    def norm(s):
        at = rows(s)
        values = [tok[h, at, :].astype(F32) for h in range(4)]
        total = sum(jnp.sum(p * p, axis=1, keepdims=True) for p in values)
        inv = lax.rsqrt(total / width + EPS)
        q[at, :] = jnp.broadcast_to(inv, (span, q.shape[1]))
        for h in range(4):
            cols = slice(h * quarter, (h + 1) * quarter)
            value = (values[h] * inv * gain[:, cols]).astype(BF)
            normed[at, cols] = value
            normed_t[cols, at] = jnp.transpose(value)
        for copy in out_copies(s)[:3]:
            copy.start()

    def project(s):
        at = rows(s)
        pbd[at, :] = nn(normed[at, :], wbd[...])
        px[at, :] = nn(normed[at, :], wx[...])
        for copy in out_copies(s)[3:]:
            copy.start()

    def hops(group, j):
        if j < lines:
            for begin, begin_pair, hop, end in group:
                hop(j)

    local[0].wait()
    hops(cuts, 1)
    to_x(0).wait()
    forward(0).start()
    hops(cuts, 2)
    for begin, begin_pair, hop, end in chains:
        begin()
    to_sib().wait()
    forward(0).wait()
    norm(0)
    to_x(1).wait()
    forward(1).start()
    hops(cuts, 3)
    if lines > 4:
        for begin, begin_pair, hop, end in cuts:
            lax.fori_loop(4, lines, lambda j, a, fn=hop: (fn(j), a)[1], 0)
    for begin, begin_pair, hop, end in chains:
        begin_pair()
    forward(1).wait()
    norm(1)
    have(2)
    local[2].wait()
    other_half().start()
    to_x(2).wait()
    forward(2).start()
    for copy in local[3:]:
        copy.wait()
    for copy in onto:
        copy.start()
    cot_sib().start()
    forward(2).wait()
    norm(2)
    local[1].wait()
    for n in (0, 1, 3):
        have(n)
    other_half().wait()
    hops(chains, 1)
    keep_rows = [
        pltpu.make_async_copy(wx, rows_x, s_loc.at[6]), pltpu.make_async_copy(wbd, rows_bd, s_loc.at[7]),
    ]
    for copy in keep_rows:
        copy.start()

    def last_tokens(s):
        to_x(s).wait()
        forward(s).start()

    def last_norm(s):
        forward(s).wait()
        norm(s)

    events = {1: [(last_tokens, units - 1)], 2: [(last_norm, units - 1)]}
    late = []
    plan = []
    for n, (begin, begin_pair, hop, end) in enumerate(chains):
        if lines > 2:
            plan.append((hop, 2, 1 + n // 2))
        if lines > 3:
            plan.append((hop, 3, 3 + n))
        if lines > 4:
            plan.append((lambda k, fn=hop: lax.fori_loop(4, lines, lambda j, a: (fn(j), a)[1], 0), 0, 7 + n))
    plan += [(pass_cot, j, 5 + 2 * j) for j in range(pieces)]
    for fn, k, at in plan:
        if at < blocks:
            events.setdefault(at, []).append((fn, k))
        else:
            late.append((fn, k))

    def y_copies(c):
        at = rows(c, chunk)
        return (
            pltpu.make_async_copy(y.at[at], y_out.at[at], s_y.at[0, c]),
            pltpu.make_async_copy(sin.at[c], sin_out.at[c], s_y.at[1, c]),
        )

    def step(c, carry):
        for at, fns in events.items():

            @pl.when(c == at)
            def _(fns=fns):
                for fn, k in fns:
                    fn(k)

        @pl.when(c % per == 0)
        def _():
            project(c // per)

        at = rows(c, chunk)
        y_c, enter = scan_step(
            heads, par, read_block(vec, c, chunk), px.at[at], pbd.at[at], upper, spread, state, extx, extb
        )
        y[at, :] = y_c
        sin[c] = enter
        for copy in y_copies(c):
            copy.start()
        return carry

    lax.fori_loop(0, blocks, step, 0)
    for fn, k in late:
        fn(k)

    def end_y(c, carry):
        for copy in y_copies(c):
            copy.wait()
        return carry

    lax.fori_loop(0, blocks, end_y, 0)
    for s in range(units):
        for copy in out_copies(s):
            copy.wait()
    for copy in onto + keep_rows:
        copy.wait()
    cot_sib().wait()
    for j in range(pieces):
        cot_forward(j).wait()
    for begin, begin_pair, hop, end in chains:
        end()


def front(dp_n, tokens, cot, w_x, w_bc, w_z, w_out, w_dt, conv_x, conv_bc, norm_gain, gate_gain, *scalars):
    count, quarter = tokens.shape
    width = 4 * quarter
    inner, heads = w_x.shape[1], w_dt.shape[1]
    taps, bc = conv_bc.shape
    blocks = scalars[-1].shape[0]
    chunk = count // blocks
    wide = bc + chunk
    units, pieces = 4, 8
    vm, dma, sds = pltpu.VMEM, pltpu.SemaphoreType.DMA, jax.ShapeDtypeStruct
    hbm, vmem = pl.BlockSpec(memory_space=pl.ANY), pl.BlockSpec(memory_space=pltpu.VMEM)
    ways = dp_n - 1
    outs = [
        sds((24 + blocks, width), F32),
        sds((count, inner), F32), sds((count, wide), F32), sds((count, width), BF), sds((width, count), BF),
        sds((count, 128), F32), sds((count, inner), F32), sds((blocks, bc // 2, inner), BF),
        sds((4, count, quarter), BF), sds((width, inner), BF), sds((width, wide), BF), sds((width, inner), BF),
        sds((width, inner), BF),
    ]
    return pl.pallas_call(
        functools.partial(front_kernel, dp_n, heads, units, taps, bc),
        out_shape=outs,
        in_specs=[hbm] * 6 + [vmem] * 5 + [pl.BlockSpec(memory_space=pltpu.SMEM)] * 5,
        out_specs=[vmem] + [hbm] * (len(outs) - 1),
        scratch_shapes=[
            vm((w_x.shape[0], chunk), BF),
            vm((4, count, quarter), BF), vm((width, inner), BF), vm((width, wide), BF),
            vm((count, inner), F32), vm((count, wide), F32), vm((count, width), BF), vm((width, count), BF),
            vm((count, 128), F32), vm((count, inner), F32), vm((blocks, bc // 2, inner), BF),
            vm((2,) + w_z.shape, BF), vm(cot.shape, BF),
            vm((bc // 2, inner), F32), vm((chunk + 8, inner), F32), vm((chunk + 8, bc), F32),
            vm((chunk, chunk), BF), vm((chunk, 3 * inner), BF),
            dma((11,)), dma((3,)), dma((3,)), dma((units,)), dma((units,)), dma((units,)), dma((units,)),
            dma((pieces,)), dma((pieces,)), dma((pieces,)), dma((pieces,)),
            dma((4, ways + 1)), dma((4, ways + 1)), dma((4, ways)), dma((4, ways)), dma((4, ways + 1)), dma((4, ways + 1)), dma((4, ways)), dma((4, ways)),
            dma((5, units)), dma((2, blocks)),
        ],
        compiler_params=pltpu.CompilerParams(
            collective_id=2, has_side_effects=True, vmem_limit_bytes=58 * 2**20
        ),
        name="front",
    )(
        tokens, cot, w_x, w_bc, w_z, w_out, w_dt, conv_x, conv_bc, norm_gain[None, :], gate_gain[None, :], *scalars
    )
def finish_kernel(heads, taps, bc, bo, gt, gx, gz, go, gb, small, own, o_bo, o_gt, o_gx, o_gz, o_go, o_gb, o_gain, o_cx, o_cb, o_bias, o_alog, o_skip, o_gate):
    o_bo[...] = bo[...]
    o_gt[...] = gt[...]

    @pl.when(pl.program_id(0) == 0)
    def _():
        for src, dst in ((gx, o_gx), (gz, o_gz), (go, o_go), (gb, o_gb)):
            dst[...] = src[...]
        inner = o_cx.shape[1]
        per = small.shape[1] // inner
        for k in range(taps):
            o_cx[k : k + 1, :] = small[2 + k // per : 3 + k // per, (k % per) * inner : (k % per + 1) * inner]
            o_cb[k : k + 1, :] = small[1:2, k * bc : (k + 1) * bc]
        scalars = small[5:6, :128]
        o_bias[...] = scalars[0, :heads]
        o_alog[...] = scalars[0, heads : 2 * heads]
        o_skip[...] = scalars[0, 2 * heads : 3 * heads]
        o_gate[...] = small[4, :inner]
        columns = o_gain.shape[0]
        at = pl.ds(pl.multiple_of(lax.axis_index("heads") * columns, columns), columns)
        o_gain[...] = (small[0:1, at] / own[:, at])[0]


def finish(bo, gt, gx, gz, go, gb, small, norm_gain, heads, taps, bc):
    steps = 4
    sds = jax.ShapeDtypeStruct
    count, quarter = bo.shape
    inner = gx.shape[1]
    rows = pl.BlockSpec((count // steps, quarter), lambda i: (i, 0))
    whole = lambda shape: pl.BlockSpec(shape, lambda i: (0,) * len(shape))
    smalls = [(quarter,), (taps, inner), (taps, bc), (heads,), (heads,), (heads,), (inner,)]
    operands = (bo, gt, gx, gz, go, gb, small, norm_gain[None, :])
    return pl.pallas_call(
        functools.partial(finish_kernel, heads, taps, bc),
        grid=(steps,),
        in_specs=[rows, rows] + [whole(a.shape) for a in operands[2:]],
        out_specs=[rows, rows] + [whole(a.shape) for a in operands[2:6]] + [whole(s) for s in smalls],
        out_shape=[sds(a.shape, a.dtype) for a in operands[:6]] + [sds(s, F32) for s in smalls],
        name="finish",
    )(*operands)


def body(
    tokens, cotangent, starts, fill, norm_gain, w_x, w_z, w_dt, w_bc, conv_x, conv_bc, dt_bias, a_log, skip,
    gate_gain, w_out,
):
    heads_n = lax.axis_size("heads")
    dp_n = lax.axis_size("dp")
    dp_index = lax.axis_index("dp")
    count, columns = tokens.shape
    width = columns * heads_n
    blocks = starts.shape[0]
    chunk = count // blocks
    inner = w_x.shape[1]
    heads = w_dt.shape[1]
    taps, bc = conv_bc.shape
    vec, px, pbd, normed, normed_t, q_wide, y, sin, parts, rows_x, rows_bd, rows_z, rows_out = front(
        dp_n, tokens, cotangent, w_x, w_bc, w_z, w_out, w_dt, conv_x, conv_bc, norm_gain, gate_gain, dt_bias, a_log,
        skip, starts, fill,
    )
    dy, lpz, gn, y_send, g_own, gain_grad = gate(dp_n, blocks, normed, normed_t, rows_z, rows_out, parts, y, vec)
    lpx, lpbd, acc, block_out, grad_w_out, grad_w_z = scan_backward(
        dp_n, dy, px, pbd, sin, gain_grad, vec, gn, rows_out, tokens, y_send, g_own, heads, taps, bc
    )
    grad_tokens, grad_w_x, grad_w_bc, small = tail(
        dp_n, 4, normed_t, normed, lpx, lpz, lpbd, rows_x, rows_z, rows_bd, tokens, acc, cotangent, q_wide, vec, bc,
    )
    block = width // dp_n
    grad_w_dt = lax.dynamic_slice_in_dim(small[8 : 8 + heads], dp_index * block, block, 1).T
    (
        block_out, grad_tokens, grad_w_x, grad_w_z, grad_w_out, grad_w_bc, grad_norm_gain, grad_conv_x, grad_conv_bc,
        grad_dt_bias, grad_a_log, grad_skip, grad_gate_gain,
    ) = finish(
        block_out, grad_tokens, grad_w_x, grad_w_z, grad_w_out, grad_w_bc, small, norm_gain, heads, taps, bc
    )
    return (
        block_out, grad_tokens, grad_norm_gain, grad_w_x, grad_w_z, grad_w_dt, grad_w_bc, grad_conv_x, grad_conv_bc,
        grad_dt_bias, grad_a_log, grad_skip, grad_gate_gain, grad_w_out,
    )


def solution(mesh):
    placed = (
        P("dp", "heads"),
        P("dp", "heads"),
        P("dp"),
        P("dp"),
        P(),
        P("dp", "heads"),
        P("dp", "heads"),
        P("dp", "heads"),
        P("dp", None),
        P(None, "heads"),
        P(),
        P("heads"),
        P("heads"),
        P("heads"),
        P("heads"),
        P("dp", "heads"),
    )
    return jax.shard_map(
        body,
        mesh=mesh,
        in_specs=placed,
        out_specs=(
            P("dp", "heads"),
            P("dp", "heads"),
            P("heads"),
            P("dp", "heads"),
            P("dp", "heads"),
            P("dp", "heads"),
            P("dp", None),
            P(None, "heads"),
            P(),
            P("heads"),
            P("heads"),
            P("heads"),
            P("heads"),
            P("dp", "heads"),
        ),
        check_vma=False,
    )
```
